32 devices in a mesh: ep: 8 (over z, y), tp: 4 (over x, core).
Axes of the slice: x: 2, y: 2, z: 4, core: 2. Of those that a mesh axis runs over, the one named last changes fastest.
Arguments:
- layer_input: bfloat16 [4096, 2048], P('ep'), may hold values from -6 to 6
- attention_gain: float32 [2048], replicated, may hold values from 0.5 to 1.5
- attention_in: bfloat16 [3, 2048, 2048], P(None, 'ep', 'tp'), may hold values from -0.125 to 0.125
- attention_bias: float32 [3, 2048], P(None, 'tp'), may hold values from -1.75 to 1.75
- attention_out: bfloat16 [2048, 2048], P('tp', 'ep'), may hold values from -1 to 1
- feedforward_gain: float32 [2048], replicated, may hold values from 0.5 to 1.5
- shared_in: bfloat16 [2, 2048, 5632], P(None, 'ep', 'tp'), may hold values from -0.125 to 0.125
- shared_down: bfloat16 [5632, 2048], P('tp', 'ep'), may hold values from -0.15625 to 0.15625
- shared_gate: float32 [2048], replicated, may hold values from -0.125 to 0.125
- router: float32 [2048, 16], replicated, may hold values from -0.0625 to 0.0625
- expert_in: bfloat16 [16, 2, 2048, 1408], P('ep', None, None, 'tp'), may hold values from -0.125 to 0.125
- expert_down: bfloat16 [16, 1408, 2048], P('ep', 'tp'), may hold values from -0.3125 to 0.3125
- routes: int32 [4096, 4], P('ep'), may hold values from 0 to 15, all different within a row
- document_lengths: int32 [8], replicated, may hold values from 1 to 3871, as said below
- cotangent: bfloat16 [4096, 2048], P('ep'), may hold values from -6 to 6
Outputs:
- layer_output: bfloat16 [4096, 2048], P('ep')
- grad_input: bfloat16 [4096, 2048], P('ep')
- grad_attention_gain: float32 [2048], replicated
- grad_attention_in: float32 [3, 2048, 2048], P(None, 'ep', 'tp')
- grad_attention_bias: float32 [3, 2048], P(None, 'tp')
- grad_attention_out: float32 [2048, 2048], P('tp', 'ep')
- grad_feedforward_gain: float32 [2048], replicated
- grad_shared_in: float32 [2, 2048, 5632], P(None, 'ep', 'tp')
- grad_shared_down: float32 [5632, 2048], P('tp', 'ep')
- grad_shared_gate: float32 [2048], replicated
- grad_router: float32 [2048, 16], replicated
- grad_expert_in: float32 [16, 2, 2048, 1408], P('ep', None, None, 'tp')
- grad_expert_down: float32 [16, 1408, 2048], P('ep', 'tp')
The draws below stay inside these ranges and needn't reach their ends.
Inputs may be any that keep to these rules, and one draw needn't show every extreme that they name: `document_lengths`: 8 document lengths in order, followed by a padded tail of one or more positions; one document, at a place drawn from the seed, has the largest length, begins within the first 512 positions and ends within the last 512; some document has length 1.
All inputs are finite; a program needn't handle non-finite values.
Results may differ from the reference program's by a relative error of at most 0.02.
Values may be sent and summed in bfloat16 or wider, within the bound.
A program may use at most 320 MiB of HBM per device.

```python
import math
import jax
import jax.numpy as jnp
from jax import lax

D = 2048
HEADS = 16
HD = 128
FS = 5632
FE = 1408
TOP = 4
TOK_DEV = 512
WINDOW = 1024
DOCS = 8
TOKENS = 4096
EXPERTS = 16
C = 160
REACH = 2


def draw_document_lengths(key, part):
    key = jax.random.fold_in(key, 11)
    key_big, key_small = jax.random.split(key, 2)
    index_range = jnp.arange(DOCS, dtype=jnp.int32)
    big_index = jax.random.randint(key_big, (), 0, DOCS, dtype=jnp.int32)
    unit_index = (big_index + 1) % DOCS
    most_small = max(1, TOK_DEV // (2 * DOCS))
    small_lengths = jax.random.randint(key_small, (DOCS,), 1, most_small + 1, dtype=jnp.int32)
    small_lengths = jnp.where(index_range == unit_index, 1, small_lengths).astype(jnp.int32)
    big_length = TOKENS - 1 - (DOCS - 1) * most_small
    return jnp.where(index_range == big_index, big_length, small_lengths).astype(jnp.int32)


def block_levels(own_key, shape, shards, least, largest):
    loudness, own = 1.0, jax.random.fold_in(own_key, 6)
    for dim, shards_of in shards:
        heights = jnp.exp(jax.random.uniform(jax.random.fold_in(own, dim), (shards_of,), jnp.float32, least / len(shards), largest / len(shards)))
        loudness = loudness * jnp.repeat(heights, shape[dim] // shards_of).reshape([-1 if axis == dim else 1 for axis in range(len(shape))])
    return loudness


def different_ones(rng, rows, number_of, top, lift):
    ranking = jax.random.permutation(jax.random.fold_in(rng, 1), number_of)
    boost = ranking
    for power in range(3):
        boost = boost * boost // number_of
    boost = boost * lift // number_of
    tickets = jax.random.randint(jax.random.fold_in(rng, 2), (rows, number_of), 0, 4096) + boost
    holders = jax.random.permutation(jax.random.fold_in(rng, 3), rows)[jnp.arange(number_of) % rows]
    tickets = jnp.where(jnp.arange(rows)[:, None] == holders[None, :], 1 << 14, tickets)
    priority = tickets * number_of + jnp.arange(number_of)
    return lax.top_k(priority.astype(jnp.int32), top)[1].astype(jnp.int32)


def gaussian(stream_key, shape, deviation, reach, pieces=(), kind=jnp.bfloat16):
    array = deviation * jax.random.normal(stream_key, shape, jnp.float32)
    if pieces:
        array = array * block_levels(stream_key, shape, pieces, -0.22, 0.18)
    return jnp.clip(array, -reach, reach).astype(kind)


def setup_inputs(seed: int = 0) -> dict:
    streams_of = jax.random.split(jax.random.key(seed), 16)
    return {
        "layer_input": gaussian(streams_of[0], (TOKENS, D), 1.0, 6.0, ((0, 8),)),
        "attention_gain": jnp.clip(1.0 + 0.1 * jax.random.normal(streams_of[1], (D,), jnp.float32), 0.5, 1.5),
        "attention_in": gaussian(streams_of[2], (3, D, D), D ** -0.5, 0.125, ((1, 8), (2, 4))),
        "attention_bias": gaussian(streams_of[3], (3, D), 0.3, 1.75, ((1, 4),), jnp.float32),
        "attention_out": gaussian(streams_of[4], (D, D), (D // 64) ** -0.5, 1.0, ((0, 4), (1, 8))),
        "feedforward_gain": jnp.clip(1.0 + 0.1 * jax.random.normal(streams_of[5], (D,), jnp.float32), 0.5, 1.5),
        "shared_in": gaussian(streams_of[6], (2, D, FS), D ** -0.5, 0.125, ((1, 8), (2, 4))),
        "shared_down": gaussian(streams_of[7], (FS, D), (FS // 4) ** -0.5, 0.15625, ((0, 4), (1, 8))),
        "shared_gate": gaussian(streams_of[8], (D,), 0.022, 0.125, (), jnp.float32),
        "router": gaussian(streams_of[9], (D, EXPERTS), 0.011, 0.0625, (), jnp.float32),
        "expert_in": gaussian(streams_of[10], (EXPERTS, 2, D, FE), D ** -0.5, 0.125, ((0, 8), (3, 4))),
        "expert_down": gaussian(streams_of[11], (EXPERTS, FE, D), (FE // 4) ** -0.5, 0.3125, ((0, 8), (1, 4))),
        "routes": different_ones(streams_of[12], TOKENS, EXPERTS, TOP, 2048),
        "document_lengths": draw_document_lengths(jax.random.fold_in(streams_of[15], 71), 0),
        "cotangent": gaussian(streams_of[14], (TOKENS, D), 1.0, 6.0, ((0, 8),)),
    }


@jax.custom_vjp
def low(v):
    return lax.optimization_barrier(v.astype(jnp.bfloat16)).astype(jnp.float32)

@jax.custom_vjp
def low_back(v):
    return v

def low_keep(v):
    return (low(v), None)

def low_pass(kept, grad):
    return (grad,)

def back_keep(v):
    return (v, None)

def back_low(kept, grad):
    return (low(grad),)
low.defvjp(low_keep, low_pass)
low_back.defvjp(back_keep, back_low)
HIGHEST = lax.Precision.HIGHEST
EPSILON = 1e-06
ROPE_BASE = 1000000.0
MASKED = -1000000000.0

def rms_norm(values, gain_vec):
    return values * lax.rsqrt(lax.optimization_barrier(jnp.mean(values * values, axis=-1, keepdims=True)) + EPSILON) * gain_vec

def doc_table(document_lengths, positions):
    doc_ends = jnp.cumsum(document_lengths).astype(jnp.int32)
    starts_all = jnp.concatenate([doc_ends - document_lengths, doc_ends[-1:]])
    doc_ids = lax.optimization_barrier(jnp.sum((positions[:, None] >= doc_ends[None, :]).astype(jnp.int32), axis=1)).astype(jnp.int32)
    matches = doc_ids[:, None] == jnp.arange(DOCS + 1, dtype=jnp.int32)[None, :]
    doc_begin = lax.optimization_barrier(jnp.sum(jnp.where(matches, starts_all[None, :], 0), axis=1)).astype(jnp.int32)
    rope_pos = positions - doc_begin
    valid_mask = positions < doc_ends[-1]
    doc_ids = jnp.where(positions < 0, -1, doc_ids)
    return (doc_ids, rope_pos, valid_mask)

def rope_angles(rope_pos, head_dim):
    half_width = head_dim // 2
    freqs = jnp.power(ROPE_BASE, -2.0 * jnp.arange(half_width, dtype=jnp.float32) / head_dim)
    angles = rope_pos.astype(jnp.float32)[:, None] * freqs[None, :]
    return (jnp.cos(angles)[:, None, :], jnp.sin(angles)[:, None, :])

def rotate(values, cosine, sine_part, turn_sign):
    half_width = values.shape[-1] // 2
    first_part = values[..., :half_width]
    second_part = values[..., half_width:]
    return jnp.concatenate([first_part * cosine - turn_sign * second_part * sine_part, second_part * cosine + turn_sign * first_part * sine_part], axis=-1)

def slot_table(routes):
    blocks = TOKENS // TOK_DEV
    flat_routes = routes.reshape(blocks, TOK_DEV * TOP)
    one_hot = (flat_routes[:, :, None] == jnp.arange(EXPERTS, dtype=jnp.int32)[None, None, :]).astype(jnp.int32)
    earlier = jnp.cumsum(one_hot, axis=1).astype(jnp.int32) - one_hot
    arrival_rank = lax.optimization_barrier(jnp.sum(earlier * one_hot, axis=2)).astype(jnp.int32)
    block_ids = jnp.arange(blocks, dtype=jnp.int32)[:, None]
    slot_index = flat_routes * (blocks * C) + block_ids * C + arrival_rank
    slot_index = jnp.where(arrival_rank < C, slot_index, EXPERTS * blocks * C)
    return slot_index.reshape(-1).astype(jnp.int32)

def block_forward(layer_input, attention_gain, attention_in, attention_bias, attention_out, feedforward_gain, shared_in, shared_down, shared_gate, router, expert_in, expert_down, routes, document_lengths):
    score_scale = 1.0 / math.sqrt(HD)
    positions = jnp.arange(TOKENS, dtype=jnp.int32)
    doc_ids, rope_pos, valid_mask = doc_table(document_lengths, positions)
    cosine, sine_part = rope_angles(rope_pos, HD)
    normed_attention = low(rms_norm(layer_input, attention_gain))
    raw_proj = jnp.einsum('td,sde->ste', normed_attention, attention_in, precision=HIGHEST) + attention_bias[:, None, :]
    raw_proj = low_back(raw_proj)
    queries = low(rotate(raw_proj[0].reshape(TOKENS, HEADS, HD), cosine, sine_part, 1.0))
    keys = low(rotate(raw_proj[1].reshape(TOKENS, HEADS, HD), cosine, sine_part, 1.0))
    values = low(raw_proj[2].reshape(TOKENS, HEADS, HD))
    lead_rows = REACH * TOK_DEV
    key_pad = jnp.concatenate([jnp.zeros((lead_rows, HEADS, HD), jnp.float32), keys])
    value_pad = jnp.concatenate([jnp.zeros((lead_rows, HEADS, HD), jnp.float32), values])
    blocks = TOKENS // TOK_DEV

    def attend(block_index):
        query_start = (block_index * TOK_DEV).astype(jnp.int32)
        query_block = lax.dynamic_slice_in_dim(queries, query_start, TOK_DEV, 0)
        key_block = lax.dynamic_slice_in_dim(key_pad, query_start, lead_rows + TOK_DEV, 0)
        value_block = lax.dynamic_slice_in_dim(value_pad, query_start, lead_rows + TOK_DEV, 0)
        query_pos = query_start + jnp.arange(TOK_DEV, dtype=jnp.int32)
        key_pos = query_start - lead_rows + jnp.arange(lead_rows + TOK_DEV, dtype=jnp.int32)
        query_doc = doc_table(document_lengths, query_pos)[0]
        key_doc = doc_table(document_lengths, key_pos)[0]
        distance = query_pos[:, None] - key_pos[None, :]
        allowed = (query_doc[:, None] == key_doc[None, :]) & (distance >= 0) & (distance < WINDOW)
        scores = jnp.einsum('qhe,khe->hqk', query_block, key_block, precision=HIGHEST) * score_scale
        scores = low_back(jnp.where(allowed[None], scores, MASKED))
        weights = low(jax.nn.softmax(scores, axis=-1))
        return jnp.einsum('hqk,khe->qhe', weights, value_block, precision=HIGHEST)
    heads_out = lax.map(jax.checkpoint(attend), jnp.arange(blocks, dtype=jnp.int32)).reshape(TOKENS, D)
    heads_out = low_back(low(heads_out * valid_mask.astype(jnp.float32)[:, None]))
    attention_sum = low_back(jnp.dot(heads_out, attention_out, precision=HIGHEST))
    residual = layer_input + attention_sum
    normed_ffn = rms_norm(residual, feedforward_gain)
    normed_low = low(normed_ffn)
    shared_pre = low_back(jnp.einsum('td,sdf->stf', normed_low, shared_in, precision=HIGHEST))
    shared_hidden = low(jax.nn.silu(shared_pre[0]) * shared_pre[1])
    shared_out = low_back(jnp.dot(shared_hidden, shared_down, precision=HIGHEST))
    shared_scale = jax.nn.sigmoid(jnp.dot(normed_ffn, shared_gate, precision=HIGHEST))
    router_probs = jax.nn.softmax(jnp.dot(normed_ffn, router, precision=HIGHEST), axis=-1)
    chosen = jnp.take_along_axis(router_probs, routes, axis=1)
    gate_values = chosen / lax.optimization_barrier(jnp.sum(chosen, axis=1, keepdims=True))
    slot_index = slot_table(routes)
    expert_rows = blocks * C
    token_rows = jnp.repeat(normed_low, TOP, axis=0)
    dispatched = jnp.zeros((EXPERTS * expert_rows, D), jnp.float32).at[slot_index].set(token_rows, mode='drop')
    dispatched = low_back(dispatched).reshape(EXPERTS, expert_rows, D)
    expert_pre = low_back(jnp.einsum('erd,esdf->serf', dispatched, expert_in, precision=HIGHEST))
    expert_hidden = low(jax.nn.silu(expert_pre[0]) * expert_pre[1])
    expert_out = low_back(low(jnp.einsum('erf,efd->erd', expert_hidden, expert_down, precision=HIGHEST)))
    padded_out = jnp.concatenate([expert_out.reshape(EXPERTS * expert_rows, D), jnp.zeros((1, D), jnp.float32)])
    picked = padded_out[slot_index].reshape(TOKENS, TOP, D)
    moe_sum = lax.optimization_barrier(jnp.sum(gate_values[:, :, None] * picked, axis=1))
    return residual + shared_scale[:, None] * shared_out + moe_sum

def reference(layer_input, attention_gain, attention_in, attention_bias, attention_out, feedforward_gain, shared_in, shared_down, shared_gate, router, expert_in, expert_down, routes, document_lengths, cotangent):
    floats = tuple((argument.astype(jnp.float32) for argument in (layer_input, attention_gain, attention_in, attention_bias, attention_out, feedforward_gain, shared_in, shared_down, shared_gate, router, expert_in, expert_down)))

    def forward(input_rows, gain_one, proj_in, proj_bias, proj_out, gain_two, shared_one, shared_two, shared_vec, router_mat, experts_one, experts_two):
        return block_forward(input_rows, gain_one, proj_in, proj_bias, proj_out, gain_two, shared_one, shared_two, shared_vec, router_mat, experts_one, experts_two, routes, document_lengths)
    result, pullback = jax.vjp(forward, floats[0], floats[1], floats[2], floats[3], floats[4], floats[5], floats[6], floats[7], floats[8], floats[9], floats[10], floats[11])
    grads = pullback(cotangent.astype(jnp.float32))
    return (result.astype(jnp.bfloat16), grads[0].astype(jnp.bfloat16), grads[1], grads[2], grads[3], grads[4], grads[5], grads[6], grads[7], grads[8], grads[9], grads[10], grads[11])
```

```python
import functools
import math

import jax
import jax.numpy as jnp
from jax import lax
from jax.experimental import pallas as pl
from jax.experimental.pallas import tpu as pltpu
from jax.sharding import PartitionSpec as P

EP, TP = "ep", "tp"
HD = 128
WINDOW = 1024


HIGHEST = lax.Precision.HIGHEST
EPSILON = 1e-06
ROPE_BASE = 1000000.0
MASKED = -1000000000.0


def shifted(value, axis, steps):
    count = lax.axis_size(axis)
    leading, last = (max(0, -steps), min(count, count - steps))
    return lax.ppermute(value, axis, [(source, source + steps) for source in range(leading, last)])


def tensor_total(partial_sum):
    return lax.psum(partial_sum, TP)


def rms_parts(values):
    inverse = lax.rsqrt(jnp.mean(values * values, axis=-1, keepdims=True) + EPSILON)
    return (inverse, values * inverse)


def norm_back(grad_rows, gain_vec, inverse, normed):
    scaled = grad_rows * gain_vec
    grad_in = inverse * (scaled - normed * jnp.mean(scaled * normed, axis=-1, keepdims=True))
    return (grad_in, jnp.sum(grad_rows * normed, axis=0))


def doc_table(document_lengths, positions):
    doc_ends = jnp.cumsum(document_lengths)
    starts_all = jnp.concatenate([doc_ends - document_lengths, doc_ends[-1:]])
    doc_ids = jnp.sum((positions[:, None] >= doc_ends[None, :]).astype(jnp.int32), axis=1)
    matches = (
        doc_ids[:, None] == jnp.arange(document_lengths.shape[0] + 1, dtype=jnp.int32)[None, :]
    )
    doc_begin = jnp.sum(jnp.where(matches, starts_all[None, :], 0), axis=1)
    rope_pos = positions - doc_begin
    valid_mask = positions < doc_ends[-1]
    doc_ids = jnp.where(positions < 0, -1, doc_ids)
    return (doc_ids, rope_pos, valid_mask)


def rope_angles(rope_pos, head_dim):
    half_width = head_dim // 2
    freqs = jnp.power(ROPE_BASE, -2.0 * jnp.arange(half_width, dtype=jnp.float32) / head_dim)
    angles = rope_pos.astype(jnp.float32)[:, None] * freqs[None, :]
    return (jnp.cos(angles)[:, None, :], jnp.sin(angles)[:, None, :])


def rotate(values, cosine, sine_part, turn_sign):
    half_width = values.shape[-1] // 2
    first_part = values[..., :half_width]
    second_part = values[..., half_width:]
    return jnp.concatenate(
        [
            first_part * cosine - turn_sign * second_part * sine_part,
            second_part * cosine + turn_sign * first_part * sine_part,
        ],
        axis=-1,
    )


def silu_parts(gate_pre):
    sig_gate = jax.nn.sigmoid(gate_pre)
    return (gate_pre * sig_gate, sig_gate * (1.0 + gate_pre * (1.0 - sig_gate)))


NN = (((1,), (0,)), ((), ()))
NT = (((1,), (1,)), ((), ()))
TN = (((0,), (0,)), ((), ()))


def product(left, right, dims=NN):
    return lax.dot_general(left, right, dims, preferred_element_type=jnp.float32)


def feed_kernel(
    rank_row, rank_column, gate_row, scale_column, rows, cotangent,
    expert_in, expert_down, shared,
    out_part, back_part, slot_rows, slot_cotangent, grad_pre, gated,
    grad_shared_pre, scaled, token_grad, scale_grad, out_terms, back_terms,
):
    bf16, f32 = jnp.bfloat16, jnp.float32
    experts, _, slots, _ = slot_rows.shape
    tokens = rows.shape[1]
    hidden_count = gated.shape[3]
    all_slots = experts * slots
    token_rows, token_cotangent = rows[0], cotangent[0]
    shared_count = scaled.shape[2]

    @pl.when(pl.program_id(0) == 0)
    def _():
        out_terms[all_slots:, :] = shared[2]
        back_terms[all_slots : all_slots + shared_count, :] = shared[0]
        back_terms[all_slots + shared_count :, :] = shared[1]

    silu, slope = silu_parts(product(token_rows, shared[0], NT))
    up = product(token_rows, shared[1], NT)
    hidden = (silu * up).astype(bf16).astype(f32)
    scale = scale_column[0]
    scaled_hidden = (scale * hidden).astype(bf16)
    scaled[0] = scaled_hidden
    back = product(token_cotangent, shared[2], NT)
    scale_grad[0] = jnp.sum(hidden * back, axis=1, keepdims=True)
    back = scale * back
    gate_grad = (back * up * slope).astype(bf16)
    up_grad = (back * silu).astype(bf16)
    grad_shared_pre[0, 0] = gate_grad
    grad_shared_pre[1, 0] = up_grad
    order = lax.broadcasted_iota(jnp.int32, (all_slots, tokens), 0)
    spread_order = lax.broadcasted_iota(jnp.int32, (tokens, all_slots), 1)
    hits, spread = None, None
    for expert in range(experts):
        row_hits = order == rank_row[0, expert : expert + 1, :] + expert * slots
        column_hits = spread_order == rank_column[0, :, expert : expert + 1] + expert * slots
        hits = row_hits if hits is None else hits | row_hits
        spread = column_hits if spread is None else spread | column_hits
    place = hits.astype(bf16)
    taken = product(place, token_rows).astype(bf16)
    taken_cotangent = product(place, token_cotangent).astype(bf16)
    for expert in range(experts):
        mine = slice(expert * slots, (expert + 1) * slots)
        slot_rows[expert, 0] = taken[mine]
        slot_cotangent[expert, 0] = taken_cotangent[mine]
        gate = jnp.sum(
            jnp.where(hits[mine], gate_row[0, expert : expert + 1, :], 0.0), axis=1, keepdims=True
        )
        pre = product(taken[mine], expert_in[expert])
        silu, slope = silu_parts(pre[:, :hidden_count])
        up = pre[:, hidden_count:]
        hidden = (silu * up).astype(bf16).astype(f32)
        gated_hidden = (gate * hidden).astype(bf16)
        gated[expert, 0] = gated_hidden
        back = product(taken_cotangent[mine], expert_down[expert], NT)
        slot_grad = jnp.sum(hidden * back, axis=1, keepdims=True)
        token_grad[0, expert : expert + 1, :] = jnp.sum(
            jnp.where(hits[mine], slot_grad, 0.0), axis=0, keepdims=True
        )
        back = gate * back
        gate_grad_e = (back * up * slope).astype(bf16)
        up_grad_e = (back * silu).astype(bf16)
        grad_pre[0, expert, 0] = gate_grad_e
        grad_pre[1, expert, 0] = up_grad_e
        out_terms[mine, :] = product(gated_hidden, expert_down[expert]).astype(bf16)
        both_grads = jnp.concatenate([gate_grad_e, up_grad_e], axis=1)
        back_terms[mine, :] = product(both_grads, expert_in[expert], NT).astype(bf16)
    spread = spread.astype(bf16)
    out_part[0] = product(
        jnp.concatenate([spread, scaled_hidden], axis=1), out_terms[...]
    ).astype(bf16)
    back_part[0] = product(
        jnp.concatenate([spread, gate_grad, up_grad], axis=1), back_terms[...]
    ).astype(bf16)


def feed(rank, gates, scale, rows, cotangent, expert_in, expert_down, shared, capacity):
    bf16, f32 = jnp.bfloat16, jnp.float32
    blocks, experts, tokens = rank.shape
    width = rows.shape[2]
    hidden = expert_in.shape[2] // 2
    slice_hidden = shared.shape[1]
    once = pl.Buffered(1)

    def whole(array):
        return pl.BlockSpec(array.shape, lambda b: (0,) * array.ndim, pipeline_mode=once)

    row_spec = pl.BlockSpec((1, experts, tokens), lambda b: (b, 0, 0))
    token_spec = pl.BlockSpec((1, tokens, width), lambda b: (b, 0, 0))
    slot_spec = pl.BlockSpec((experts, 1, capacity, width), lambda b: (0, b, 0, 0))
    shape = jax.ShapeDtypeStruct
    return pl.pallas_call(
        feed_kernel,
        grid=(blocks,),
        in_specs=[
            row_spec,
            pl.BlockSpec((1, tokens, experts), lambda b: (b, 0, 0)),
            row_spec,
            pl.BlockSpec((1, tokens, 1), lambda b: (b, 0, 0)),
            token_spec,
            token_spec,
            whole(expert_in),
            whole(expert_down),
            whole(shared),
        ],
        out_specs=(
            token_spec,
            token_spec,
            slot_spec,
            slot_spec,
            pl.BlockSpec((2, experts, 1, capacity, hidden), lambda b: (0, 0, b, 0, 0)),
            pl.BlockSpec((experts, 1, capacity, hidden), lambda b: (0, b, 0, 0)),
            pl.BlockSpec((2, 1, tokens, slice_hidden), lambda b: (0, b, 0, 0)),
            pl.BlockSpec((1, tokens, slice_hidden), lambda b: (b, 0, 0)),
            row_spec,
            pl.BlockSpec((1, tokens, 1), lambda b: (b, 0, 0)),
        ),
        out_shape=(
            shape((blocks, tokens, width), bf16),
            shape((blocks, tokens, width), bf16),
            shape((experts, blocks, capacity, width), bf16),
            shape((experts, blocks, capacity, width), bf16),
            shape((2, experts, blocks, capacity, hidden), bf16),
            shape((experts, blocks, capacity, hidden), bf16),
            shape((2, blocks, tokens, slice_hidden), bf16),
            shape((blocks, tokens, slice_hidden), bf16),
            shape((blocks, experts, tokens), f32),
            shape((blocks, tokens, 1), f32),
        ),
        scratch_shapes=[
            pltpu.VMEM((experts * capacity + slice_hidden, width), bf16),
            pltpu.VMEM((experts * capacity + 2 * slice_hidden, width), bf16),
        ],
        compiler_params=pltpu.CompilerParams(vmem_limit_bytes=60 * 2**20),
        name="feed",
    )(rank, jnp.swapaxes(rank, 1, 2), gates, scale, rows, cotangent, expert_in, expert_down, shared)


def turned(values, cosine, sine):
    half = values.shape[1] // 2
    swapped = jnp.concatenate([values[:, half:], values[:, :half]], axis=1)
    return values * cosine + swapped * sine


def project_kernel(rows, gain, weights, bias, cosine, sine, normed, queries, keys_values):
    bf16, f32 = jnp.bfloat16, jnp.float32

    @pl.when(pl.program_id(0) == 0)
    def _():
        _, scaled = rms_parts(rows[...].astype(f32))
        normed[...] = (scaled * gain[...]).astype(bf16)

    columns = queries.shape[1]
    for kind in range(3):
        raw = product(normed[...], weights[kind]) + bias[kind : kind + 1, :]
        for start in range(0, columns, HD):
            head = slice(start, start + HD)
            part = raw[:, head]
            if kind < 2:
                part = turned(part, cosine[...], sine[...])
            if kind == 0:
                queries[:, head] = part.astype(bf16)
            else:
                keys_values[kind - 1, :, head] = part.astype(bf16)


def project(rows, gain, weights, bias, cosine, sine):
    tokens, width = rows.shape
    columns = weights.shape[2]
    step = min(2 * HD, columns)
    shape = jax.ShapeDtypeStruct
    bf16 = jnp.bfloat16

    def whole(*dims):
        return pl.BlockSpec(dims, lambda h: (0,) * len(dims))

    return pl.pallas_call(
        project_kernel,
        grid=(columns // step,),
        in_specs=[
            whole(tokens, width),
            whole(1, width),
            pl.BlockSpec((3, width, step), lambda h: (0, 0, h)),
            pl.BlockSpec((3, step), lambda h: (0, h)),
            whole(tokens, HD),
            whole(tokens, HD),
        ],
        out_specs=(
            whole(tokens, width),
            pl.BlockSpec((tokens, step), lambda h: (0, h)),
            pl.BlockSpec((2, tokens, step), lambda h: (0, 0, h)),
        ),
        out_shape=(
            shape((tokens, width), bf16),
            shape((tokens, columns), bf16),
            shape((2, tokens, columns), bf16),
        ),
        compiler_params=pltpu.CompilerParams(vmem_limit_bytes=40 * 2**20),
        name="project",
    )(rows, gain[None], weights, bias, cosine, sine)


def masked_scores(queries, keys, query_doc, key_doc):
    tokens, count = queries.shape[0], keys.shape[0]
    scores = product(queries, keys, NT) * (1.0 / math.sqrt(HD))
    ahead = lax.broadcasted_iota(jnp.int32, (tokens, count), 0) + (count - tokens)
    distance = ahead - lax.broadcasted_iota(jnp.int32, (tokens, count), 1)
    allowed = (query_doc == key_doc) & (distance >= 0) & (distance < WINDOW)
    return jnp.where(allowed, scores, MASKED)


def attend_kernel(queries, keys, values, query_doc, key_doc, valid, heads, log_totals):
    count = keys.shape[1] * keys.shape[2]
    keys, values = keys[0].reshape(count, HD), values[0].reshape(count, HD)
    scores = masked_scores(queries[...], keys, query_doc[...], key_doc[...])
    row_max = jnp.max(scores, axis=1, keepdims=True)
    terms = jnp.exp(scores - row_max)
    total = jnp.sum(terms, axis=1, keepdims=True)
    weights = (terms / total).astype(jnp.bfloat16)
    heads[...] = (product(weights, values) * valid[...]).astype(jnp.bfloat16)
    log_totals[0] = row_max + jnp.log(total)


def attention_specs(tokens, blocks):
    def column(*dims):
        return pl.BlockSpec(dims, lambda h: (0,) * len(dims))

    head = pl.BlockSpec((tokens, HD), lambda h: (0, h))
    keys = pl.BlockSpec((1, blocks, tokens, HD), lambda h: (0, 0, 0, h))
    values = pl.BlockSpec((1, blocks, tokens, HD), lambda h: (1, 0, 0, h))
    logs = pl.BlockSpec((1, tokens, 1), lambda h: (h, 0, 0))
    return head, keys, values, column(tokens, 1), column(1, blocks * tokens), logs


def attend(queries, keys_values, query_doc, key_doc, valid):
    tokens, columns = queries.shape
    blocks = keys_values.shape[1]
    head, keys, values, column, row, logs = attention_specs(tokens, blocks)
    shape = jax.ShapeDtypeStruct
    return pl.pallas_call(
        attend_kernel,
        grid=(columns // HD,),
        in_specs=[head, keys, values, column, row, column],
        out_specs=(head, logs),
        out_shape=(
            shape((tokens, columns), jnp.bfloat16),
            shape((columns // HD, tokens, 1), jnp.float32),
        ),
        compiler_params=pltpu.CompilerParams(vmem_limit_bytes=40 * 2**20),
        name="attend",
    )(queries, keys_values, keys_values, query_doc, key_doc, valid)


def attend_back_kernel(
    queries, keys, values, query_doc, key_doc, log_totals, grad_heads, cosine, sine,
    grad_queries, grad_keys_values,
):
    bf16 = jnp.bfloat16
    scale = 1.0 / math.sqrt(HD)
    blocks, tokens = keys.shape[1], keys.shape[2]
    keys, values = (ref[0].reshape(blocks * tokens, HD) for ref in (keys, values))
    scores = masked_scores(queries[...], keys, query_doc[...], key_doc[...])
    probs = jnp.exp(scores - log_totals[0])
    grads = grad_heads[...]
    slopes = product(grads, values, NT)
    slopes = probs * (slopes - jnp.sum(probs * slopes, axis=1, keepdims=True))
    grad_scores = slopes.astype(bf16)
    turned_back = turned(product(grad_scores, keys) * scale, cosine[...], -sine[...])
    grad_queries[...] = turned_back.astype(bf16)
    grad_keys = product(grad_scores, queries[...], TN) * scale
    grad_keys_values[0] = grad_keys.astype(bf16).reshape(blocks, tokens, HD)
    grad_values = product(probs.astype(bf16), grads, TN)
    grad_keys_values[1] = grad_values.astype(bf16).reshape(blocks, tokens, HD)


def attend_back(queries, keys_values, query_doc, key_doc, log_totals, grad_heads, cosine, sine):
    tokens, columns = queries.shape
    blocks = keys_values.shape[1]
    head, keys, values, column, row, logs = attention_specs(tokens, blocks)
    angle = pl.BlockSpec((tokens, HD), lambda h: (0, 0))
    shape = jax.ShapeDtypeStruct
    return pl.pallas_call(
        attend_back_kernel,
        grid=(columns // HD,),
        in_specs=[head, keys, values, column, row, logs, head, angle, angle],
        out_specs=(head, pl.BlockSpec((2, blocks, tokens, HD), lambda h: (0, 0, 0, h))),
        out_shape=(
            shape((tokens, columns), jnp.bfloat16),
            shape(keys_values.shape, jnp.bfloat16),
        ),
        compiler_params=pltpu.CompilerParams(vmem_limit_bytes=48 * 2**20),
        name="attend_back",
    )(queries, keys_values, keys_values, query_doc, key_doc, log_totals, grad_heads, cosine, sine)


RING = 8
NO_SLOT = 1 << 20
RIGHT, LEFT, OVER_X, OVER_CORE, OVER_FAR, OVER_Y, OVER_Z, LOCAL = range(8)
MESH_ID = pl.DeviceIdType.MESH


def ring_place(ep):
    z, y = ep // 2, ep % 2
    return z + y * (7 - 2 * z)


def ring_member(place):
    upper = place // 4
    return 2 * place + upper * (15 - 4 * place)


class Peers:
    def __init__(self):
        self.ep, self.tp = lax.axis_index(EP), lax.axis_index(TP)
        self.x, self.core = self.tp // 2, self.tp % 2
        self.z, self.y = self.ep // 2, self.ep % 2
        self.place = ring_place(self.ep)
        self.right = (self.block(1), self.tp)
        self.left = (self.block(RING - 1), self.tp)
        self.quarter = self.tp
        self.x_quarter = (1 - self.x) * 2 + self.core
        self.core_quarter = self.x * 2 + 1 - self.core
        self.far_quarter = (1 - self.x) * 2 + 1 - self.core
        self.x_peer = (self.ep, self.x_quarter)
        self.core_peer = (self.ep, self.core_quarter)
        self.far_peer = (self.ep, self.far_quarter)
        self.y_peer = (self.z * 2 + 1 - self.y, self.tp)

    def block(self, step):
        return ring_member((self.place + step + RING) % RING)


def greet(peers):
    barrier = pltpu.get_barrier_semaphore()
    for peer in peers:
        pl.semaphore_signal(barrier, inc=1, device_id=peer, device_id_type=MESH_ID)
    pl.semaphore_wait(barrier, len(peers))


class Copies:
    def __init__(self, send_sems, recv_sems):
        self.send_sems, self.recv_sems = send_sems, recv_sems
        self.count = 0
        self.sent = []
        self.landing = {}

    def describe(self, source, target, peer, index):
        return pltpu.make_async_remote_copy(
            src_ref=source,
            dst_ref=target,
            send_sem=self.send_sems.at[index],
            recv_sem=self.recv_sems.at[index],
            device_id=peer,
            device_id_type=MESH_ID,
        )

    def send(self, key, source, target, landing, peer):
        index = self.count
        self.count += 1
        copy = self.describe(source, target, peer, index)
        copy.start()
        self.sent.append(copy)
        self.landing[key] = self.describe(landing, landing, peer, index).wait_recv

    def local(self, key, source, target):
        index = self.count
        self.count += 1
        copy = pltpu.make_async_copy(source, target, self.send_sems.at[index])
        copy.start()
        self.landing[key] = copy.wait

    def arrive(self, *key):
        self.landing.pop(key)()

    def finish(self):
        for wait in self.landing.values():
            wait()
        for copy in self.sent:
            copy.wait_send()


def remote_params(collective_id, vmem=48):
    return pltpu.CompilerParams(
        collective_id=collective_id, has_side_effects=True, vmem_limit_bytes=vmem * 2**20
    )


def semaphores(count):
    return [pltpu.SemaphoreType.DMA((count,))] * 2


IN_PLACE = pl.BlockSpec(memory_space=pl.ANY)
IN_VMEM = pl.BlockSpec(memory_space=pltpu.VMEM)


def gather_kernel(rows, scales, out, out_scales, send_sems, recv_sems):
    me = Peers()
    copies = Copies(send_sems, recv_sems)
    count = rows.shape[0]
    half, part = count // 2, count // 4
    q, qx, qc, qd = me.quarter, me.x_quarter, me.core_quarter, me.far_quarter
    here = me.block(0)
    low, high, whole = pl.ds(0, half), pl.ds(half, half), pl.ds(0, count)
    own, other, scale = range(3)
    sides = ((RIGHT, me.right, -1, 0), (LEFT, me.left, 1, 1))
    greet([me.right, me.left, me.x_peer, me.core_peer, me.far_peer])

    def cells(step, quarter, which):
        return out.at[me.block(step), quarter, which]

    def push(key, step, quarter, which, peer, landing_step, landing_quarter, source=None):
        cell = cells(step, quarter, which)
        copies.send(
            key,
            cell if source is None else source,
            cell,
            cells(landing_step, landing_quarter, which),
            peer,
        )

    push((OVER_X, other, 0), 0, q, low, me.x_peer, 0, qx, rows.at[low])
    push((RIGHT, own, 1), 0, q, whole, me.right, -1, q, rows)
    push((LEFT, own, 1), 0, q, whole, me.left, 1, q, rows)
    push((OVER_X, own, 0), 0, q, high, me.x_peer, 0, qx, rows.at[high])
    push((OVER_CORE, own, 0), 0, q, whole, me.core_peer, 0, qc, rows)
    copies.local((LOCAL, own), rows, out.at[here, q])
    for way, peer, quarter in (
        (OVER_X, me.x_peer, qx),
        (OVER_CORE, me.core_peer, qc),
        (OVER_FAR, me.far_peer, qd),
    ):
        copies.send(
            (way, scale, 0), scales, out_scales.at[here, q], out_scales.at[here, quarter], peer
        )
    copies.local((LOCAL, scale), scales, out_scales.at[here, q])
    copies.arrive(OVER_X, other, 0)
    for side, peer, sign, keep in sides:
        push((side, other, 1), 0, qx, low, peer, sign, qx)
    for way in (OVER_X, OVER_CORE, OVER_FAR):
        copies.arrive(way, scale, 0)
    copies.arrive(LOCAL, scale)

    def push_scales(step, side, peer, sign):
        blocks = out_scales.at[me.block(step)]
        copies.send(
            (side, scale, abs(step) + 1), blocks, blocks, out_scales.at[me.block(step + sign)], peer
        )

    for side, peer, sign, keep in sides:
        push_scales(0, side, peer, sign)
    copies.arrive(OVER_X, own, 0)
    push((OVER_CORE, other, 0), 0, qx, whole, me.core_peer, 0, qd)
    waiting = []
    for hop in (1, 2, 3):
        for side, peer, sign, keep in sides:
            step = sign * hop
            copies.arrive(side, own, hop)
            which = whole if hop < 3 else pl.ds(keep * half, half)
            push((side, own, hop + 1), step, q, which, peer, step + sign, q)
            push((OVER_X, own, step), step, q, high, me.x_peer, step, qx)
            push((OVER_CORE, own, step), step, q, whole, me.core_peer, step, qc)
        for side, peer, sign, keep in sides:
            step = sign * hop
            copies.arrive(side, other, hop)
            which = low if hop < 3 else pl.ds(keep * part, part)
            push((side, other, hop + 1), step, qx, which, peer, step + sign, qx)
            push((OVER_CORE, other, step), step, qx, low, me.core_peer, step, qd)
            copies.arrive(side, scale, hop)
            if hop < 3 or side == RIGHT:
                push_scales(step, side, peer, sign)
        for step in waiting:
            copies.arrive(OVER_X, own, step)
            push((OVER_CORE, scale, step), step, qx, high, me.core_peer, step, qd)
        waiting = [-hop, hop]
    copies.arrive(LEFT, own, 4)
    push((OVER_X, own, 4), 4, q, high, me.x_peer, 4, qx)
    copies.arrive(RIGHT, own, 4)
    push((OVER_CORE, own, 4), 4, q, whole, me.core_peer, 4, qc)
    copies.arrive(LEFT, other, 4)
    copies.arrive(RIGHT, other, 4)
    push((OVER_CORE, other, 4), 4, qx, low, me.core_peer, 4, qd)
    for step in waiting + [4]:
        copies.arrive(OVER_X, own, step)
        push((OVER_CORE, scale, step), step, qx, high, me.core_peer, step, qd)
    copies.finish()


def gather_rows(rows, scales, collective_id):
    return pl.pallas_call(
        gather_kernel,
        out_shape=(
            jax.ShapeDtypeStruct((RING, 4) + rows.shape, rows.dtype),
            jax.ShapeDtypeStruct((RING, 4) + scales.shape, scales.dtype),
        ),
        in_specs=[IN_PLACE] * 2,
        out_specs=(IN_PLACE,) * 2,
        scratch_shapes=semaphores(80),
        compiler_params=remote_params(collective_id),
        name="gather_rows",
    )(rows, scales)


def add_into(total, term, rows, tile=32):
    tile = min(tile, rows)

    def step(index, carry):
        here = pl.ds(pl.multiple_of(index * tile, tile), tile)
        summed = total[here, :].astype(jnp.float32) + term[here, :].astype(jnp.float32)
        total[here, :] = summed.astype(total.dtype)
        return carry

    lax.fori_loop(0, rows // tile, step, 0)


def scatter_kernel(
    part, scalars, out, out_scalars,
    held, core_in, x_in, ring_q, ring_x, last_in,
    s_held, s_core, s_x, s_ring,
    send_sems, recv_sems,
):
    me = Peers()
    copies = Copies(send_sems, recv_sems)
    count = part.shape[2]
    half, piece = count // 2, count // 4
    q, qx, qc, qd = me.quarter, me.x_quarter, me.core_quarter, me.far_quarter
    own, other, scale, last = range(4)
    peers = {RIGHT: me.right, LEFT: me.left}
    greet([me.right, me.left, me.x_peer, me.core_peer])
    order = (4, 3, 5, 2, 6, 1, 7, 0)
    for k in order:
        for slot, mine, theirs in ((0, q, qc), (1, qx, qd)):
            copies.local((LOCAL, k, slot), part.at[me.block(k), mine], held.at[k, slot])
            target = core_in.at[k, slot]
            copies.send(
                (OVER_CORE, k, slot), part.at[me.block(k), theirs], target, target, me.core_peer
            )
    for k in range(RING):
        for slot, mine, theirs in ((0, q, qc), (1, qx, qd)):
            copies.local((LOCAL, scale, k, slot), scalars.at[me.block(k), mine], s_held.at[slot, k])
            target = s_core.at[slot, k]
            copies.send(
                (OVER_CORE, scale, k, slot),
                scalars.at[me.block(k), theirs],
                target,
                target,
                me.core_peer,
            )

    def prepare(k):
        for slot in (1, 0):
            copies.arrive(LOCAL, k, slot)
            copies.arrive(OVER_CORE, k, slot)
            add_into(held.at[k, slot], core_in.at[k, slot], count)
            if slot == 1:
                source = held.at[k, 1, pl.ds(half, half)]
                copies.send((OVER_X, k), source, x_in.at[k], x_in.at[k], me.x_peer)

    def over_x(k):
        copies.arrive(OVER_X, k)
        add_into(held.at[k, 0, pl.ds(half, half)], x_in.at[k], half)

    def pass_on(side, hop, k):
        if hop == 0:
            rows_q, rows_x = pl.ds(side * half, half), pl.ds(side * piece, piece)
        else:
            rows_q, rows_x = pl.ds(0, count), pl.ds(0, half)
        for kind, landing, rows in ((own, ring_q, rows_q), (other, ring_x, rows_x)):
            target = landing.at[side, hop, rows]
            copies.send((side, kind, hop), held.at[k, kind].at[rows], target, target, peers[side])

    def take_in(side, hop, k):
        if hop == 0:
            span_q, span_x, at_q, at_x = half, piece, side * half, side * piece
        else:
            span_q, span_x, at_q, at_x = count, half, 0, 0
        for kind, landing, span, at in ((own, ring_q, span_q, at_q), (other, ring_x, span_x, at_x)):
            copies.arrive(side, kind, hop)
            rows = pl.ds(at, span)
            add_into(held.at[k, kind, rows], landing.at[side, hop, rows], span)

    def pass_scalars(side, hop, k):
        target = s_ring.at[side, hop]
        copies.send((side, scale, hop), s_held.at[0, k], target, target, peers[side])

    def take_scalars(side, hop, k):
        copies.arrive(side, scale, hop)
        s_held[0, k] += s_ring[side, hop]

    prepare(4)
    prepare(3)
    prepare(5)
    over_x(4)
    pass_on(RIGHT, 0, 4)
    pass_on(LEFT, 0, 4)
    prepare(2)
    prepare(6)
    for k in range(RING):
        for slot in (0, 1):
            copies.arrive(LOCAL, scale, k, slot)
            copies.arrive(OVER_CORE, scale, k, slot)
    s_held[...] += s_core[...]
    copies.send((OVER_X, scale, scale), s_held.at[1], s_x, s_x, me.x_peer)
    over_x(3)
    over_x(5)
    for hop, right_block, left_block, later in ((1, 3, 5, (1, 7)), (2, 2, 6, (0,)), (3, 1, 7, ())):
        take_in(RIGHT, hop - 1, right_block)
        pass_on(RIGHT, hop, right_block)
        take_in(LEFT, hop - 1, left_block)
        pass_on(LEFT, hop, left_block)
        if hop == 1:
            copies.arrive(OVER_X, scale, scale)
            s_held[0] += s_x[...]
            pass_scalars(RIGHT, 0, 4)
        else:
            take_scalars(RIGHT, hop - 2, right_block + 1)
            if hop == 3:
                take_scalars(LEFT, hop - 2, left_block - 1)
            pass_scalars(RIGHT, hop - 1, right_block + 1)
            pass_scalars(LEFT, hop - 1, left_block - 1)
        for k in later:
            prepare(k)
        if hop == 1:
            over_x(2)
            over_x(6)
        elif hop == 2:
            over_x(1)
            over_x(7)
    over_x(0)
    take_in(RIGHT, 3, 0)
    for side, k in ((RIGHT, 1), (LEFT, 7)):
        take_scalars(side, 2, k)
        pass_scalars(side, 3, k)
    take_in(LEFT, 3, 0)
    copies.send((OVER_X, last, last), held.at[0, 1, pl.ds(0, half)], last_in, last_in, me.x_peer)
    take_scalars(RIGHT, 3, 0)
    take_scalars(LEFT, 3, 0)
    out_scalars[...] = s_held[0, 0]
    out[pl.ds(half, half), :] = held[0, 0, pl.ds(half, half), :].astype(out.dtype)
    copies.arrive(OVER_X, last, last)
    out[pl.ds(0, half), :] = (
        held[0, 0, pl.ds(0, half), :].astype(jnp.float32) + last_in[...].astype(jnp.float32)
    ).astype(out.dtype)
    copies.finish()


def scatter_rows(part, scalars, collective_id):
    ring, quarters, count, width = part.shape
    half = count // 2
    dtype = part.dtype
    s_shape = scalars.shape[2:]
    return pl.pallas_call(
        scatter_kernel,
        out_shape=(
            jax.ShapeDtypeStruct((count, width), jnp.float32),
            jax.ShapeDtypeStruct(s_shape, jnp.float32),
        ),
        in_specs=[IN_PLACE] * 2,
        out_specs=(IN_VMEM,) * 2,
        scratch_shapes=[
            pltpu.VMEM((RING, 2, count, width), dtype),
            pltpu.VMEM((RING, 2, count, width), dtype),
            pltpu.VMEM((RING, half, width), dtype),
            pltpu.VMEM((2, 4, count, width), dtype),
            pltpu.VMEM((2, 4, half, width), dtype),
            pltpu.VMEM((half, width), dtype),
            pltpu.VMEM((2, RING) + s_shape, jnp.float32),
            pltpu.VMEM((2, RING) + s_shape, jnp.float32),
            pltpu.VMEM((RING,) + s_shape, jnp.float32),
            pltpu.VMEM((2, 4) + s_shape, jnp.float32),
        ]
        + semaphores(112),
        compiler_params=remote_params(collective_id),
        name="scatter_rows",
    )(part, scalars)


def spread_kernel(shard_in, shard_out, full_in, full_out, send_sems, recv_sems):
    me = Peers()
    copies = Copies(send_sems, recv_sems)
    kinds, depth, _ = shard_in.shape
    rows, columns = shard_out.shape
    sides = ((RIGHT, me.right, -1), (LEFT, me.left, 1))
    greet([me.right, me.left])

    def cell(kind, step, part, parts):
        block = me.block(step)
        if kind < kinds:
            return full_in.at[kind, block, pl.ds(part * (depth // parts), depth // parts)]
        across = pl.ds(pl.multiple_of(block * columns, columns), columns)
        return full_out.at[pl.ds(part * (rows // parts), rows // parts), across]

    def pass_on(side, peer, sign, kind, hop, source=None):
        parts = 2 if hop == 3 else 1
        part = side if hop == 3 else 0
        step = sign * hop
        here = cell(kind, step, part, parts)
        copies.send(
            (side, kind, hop + 1),
            here if source is None else source,
            here,
            cell(kind, step + sign, part, parts),
            peer,
        )

    order = tuple(range(kinds - 1, -1, -1)) + (kinds,)
    for kind in order:
        source = shard_in.at[kind] if kind < kinds else shard_out
        for side, peer, sign in sides:
            pass_on(side, peer, sign, kind, 0, source)
        copies.local((LOCAL, kind), source, cell(kind, 0, 0, 1))
    for hop in (1, 2, 3):
        for kind in order:
            for side, peer, sign in sides:
                copies.arrive(side, kind, hop)
                pass_on(side, peer, sign, kind, hop)
    copies.finish()


def spread_weights(shard_in, shard_out, collective_id):
    kinds, depth, width = shard_in.shape
    rows, columns = shard_out.shape
    return pl.pallas_call(
        spread_kernel,
        out_shape=(
            jax.ShapeDtypeStruct((kinds, RING, depth, width), shard_in.dtype),
            jax.ShapeDtypeStruct((rows, RING * columns), shard_out.dtype),
        ),
        in_specs=[IN_PLACE] * 2,
        out_specs=(IN_PLACE,) * 2,
        scratch_shapes=semaphores(9 * (kinds + 1)),
        compiler_params=remote_params(collective_id),
        name="spread_weights",
    )(shard_in, shard_out)


def collect_kernel(
    grad_in, grad_out, tail, sum_in, sum_out, sum_tail,
    held_in, held_out, ring_in, ring_out, tails, tail_sums,
    send_sems, recv_sems,
):
    me = Peers()
    copies = Copies(send_sems, recv_sems)
    kinds, _, depth, width = grad_in.shape
    rows, columns = sum_out.shape
    peers = {RIGHT: me.right, LEFT: me.left}
    tail_kind = kinds + 1
    greet([me.right, me.left, me.x_peer, me.core_peer, me.far_peer])
    order = (4, 3, 5, 2, 6, 1, 7, 0)

    def held(kind, k):
        return held_in.at[k, kind] if kind < kinds else held_out.at[k]

    def ring(kind, side, hop):
        return ring_in.at[side, hop, kind] if kind < kinds else ring_out.at[side, hop]

    def span(kind, side, hop):
        whole = depth if kind < kinds else rows
        return (side * (whole // 2), whole // 2) if hop == 0 else (0, whole)

    def pass_on(side, hop, k, kind):
        at = pl.ds(*span(kind, side, hop))
        target = ring(kind, side, hop).at[at]
        copies.send((side, kind, hop), held(kind, k).at[at], target, target, peers[side])

    def take_in(side, hop, k, kind):
        copies.arrive(side, kind, hop)
        start, size = span(kind, side, hop)
        at = pl.ds(start, size)
        add_into(held(kind, k).at[at], ring(kind, side, hop).at[at], size)

    tails[0] = tail[...]
    for side, place in ((RIGHT, 7), (LEFT, 1)):
        copies.send((side, tail_kind, 0), tail, tails.at[place], tails.at[place], peers[side])
    for k in order:
        block = me.block(k)
        for kind in range(kinds):
            copies.local((LOCAL, kind, k), grad_in.at[kind, block], held(kind, k))
        across = pl.ds(pl.multiple_of(block * columns, columns), columns)
        copies.local((LOCAL, kinds, k), grad_out.at[:, across], held(kinds, k))

    def ready(*blocks):
        for k in blocks:
            for kind in range(kinds + 1):
                copies.arrive(LOCAL, kind, k)

    ready(4)
    for kind in range(kinds + 1):
        for side in (RIGHT, LEFT):
            pass_on(side, 0, 4, kind)
    for hop, right_block, left_block in ((1, 3, 5), (2, 2, 6), (3, 1, 7)):
        ready(right_block, left_block)
        for kind in range(kinds + 1):
            for side, k in ((RIGHT, right_block), (LEFT, left_block)):
                take_in(side, hop - 1, k, kind)
                pass_on(side, hop, k, kind)
        for side, place, sign in ((RIGHT, 8 - hop, -1), (LEFT, hop, 1)):
            copies.arrive(side, tail_kind, hop - 1)
            if hop < 3 or side == RIGHT:
                target = tails.at[place + sign]
                copies.send((side, tail_kind, hop), tails.at[place], target, target, peers[side])
    copies.arrive(RIGHT, tail_kind, 3)
    total = tails[0]
    for place in range(1, RING):
        total = total + tails[place]
    tail_sums[me.tp] = total
    for way, peer, quarter in (
        (OVER_X, me.x_peer, me.x_quarter),
        (OVER_CORE, me.core_peer, me.core_quarter),
        (OVER_FAR, me.far_peer, me.far_quarter),
    ):
        copies.send(
            (way, tail_kind), tail_sums.at[me.tp], tail_sums.at[me.tp], tail_sums.at[quarter], peer
        )
    ready(0)
    for kind in range(kinds + 1):
        for side in (RIGHT, LEFT):
            take_in(side, 3, 0, kind)
    for kind in range(kinds):
        sum_in[kind] = held_in[0, kind].astype(jnp.float32)
    sum_out[...] = held_out[0].astype(jnp.float32)
    for way in (OVER_X, OVER_CORE, OVER_FAR):
        copies.arrive(way, tail_kind)
    sum_tail[...] = tail_sums[...]
    copies.finish()


def collect_weights(grad_in, grad_out, tail, collective_id):
    kinds, ring, depth, width = grad_in.shape
    rows, columns = grad_out.shape[0], grad_out.shape[1] // ring
    f32 = jnp.float32
    return pl.pallas_call(
        collect_kernel,
        out_shape=(
            jax.ShapeDtypeStruct((kinds, depth, width), f32),
            jax.ShapeDtypeStruct((rows, columns), f32),
            jax.ShapeDtypeStruct((4,) + tail.shape, f32),
        ),
        in_specs=[IN_PLACE, IN_PLACE, IN_VMEM],
        out_specs=(IN_VMEM,) * 3,
        scratch_shapes=[
            pltpu.VMEM((RING, kinds, depth, width), grad_in.dtype),
            pltpu.VMEM((RING, rows, columns), grad_out.dtype),
            pltpu.VMEM((2, 4, kinds, depth, width), grad_in.dtype),
            pltpu.VMEM((2, 4, rows, columns), grad_out.dtype),
            pltpu.VMEM((RING,) + tail.shape, f32),
            pltpu.VMEM((4,) + tail.shape, f32),
        ]
        + semaphores(96),
        compiler_params=remote_params(collective_id),
        name="collect_weights",
    )(grad_in, grad_out, tail)


def greet_along_z(me):
    barrier = pltpu.get_barrier_semaphore()
    pl.semaphore_signal(barrier, inc=1, device_id=me.y_peer, device_id_type=MESH_ID)

    @pl.when(me.z > 0)
    def _():
        peer = (me.ep - 2, me.tp)
        pl.semaphore_signal(barrier, inc=1, device_id=peer, device_id_type=MESH_ID)

    @pl.when(me.z < 3)
    def _():
        peer = (me.ep + 2, me.tp)
        pl.semaphore_signal(barrier, inc=1, device_id=peer, device_id_type=MESH_ID)

    pl.semaphore_wait(barrier, 1 + (me.z + 2) // 3 + (5 - me.z) // 3)


def share_kernel(own, out, send_sems, recv_sems):
    me = Peers()
    kinds, tokens, _ = own.shape
    pieces = 2
    size = tokens // pieces
    parts = [(kind, pl.ds(piece * size, size)) for kind in range(kinds) for piece in range(pieces)]
    count = len(parts)
    greet_along_z(me)

    def copy(index, source, target, peer):
        return Copies(send_sems, recv_sems).describe(source, target, peer, index)

    def upward(index, kind, rows):
        return copy(index, own.at[kind, rows], out.at[kind, 0, rows], (me.ep + 2, me.tp))

    def sideways(index, kind, rows):
        return copy(count + index, own.at[kind, rows], out.at[kind, 1, rows], me.y_peer)

    def onward(index, kind, rows):
        return copy(count + index, out.at[kind, 0, rows], out.at[kind, 1, rows], me.y_peer)

    @pl.when(me.z < 3)
    def _():
        for index, (kind, rows) in enumerate(parts):
            upward(index, kind, rows).start()

    @pl.when(me.y == 0)
    def _():
        for index, (kind, rows) in enumerate(parts):
            sideways(index, kind, rows).start()

    out[:, 2] = own[...]

    @pl.when(me.z == 0)
    def _():
        out[:, 0] = jnp.zeros_like(own)

    @pl.when((me.z == 0) & (me.y == 0))
    def _():
        out[:, 1] = jnp.zeros_like(own)

    @pl.when(me.z > 0)
    def _():
        for index, (kind, rows) in enumerate(parts):
            upward(index, kind, rows).wait_recv()

            @pl.when(me.y == 1)
            def _():
                onward(index, kind, rows).start()

    @pl.when(me.y == 1)
    def _():
        for index, (kind, rows) in enumerate(parts):
            sideways(index, kind, rows).wait_recv()

    @pl.when((me.y == 0) & (me.z > 0))
    def _():
        for index, (kind, rows) in enumerate(parts):
            onward(index, kind, rows).wait_recv()

    @pl.when(me.z < 3)
    def _():
        for index, (kind, rows) in enumerate(parts):
            upward(index, kind, rows).wait_send()

    @pl.when((me.y == 0) | (me.z > 0))
    def _():
        for index, (kind, rows) in enumerate(parts):
            sideways(index, kind, rows).wait_send()


def share_keys(own, collective_id):
    kinds, tokens, width = own.shape
    return pl.pallas_call(
        share_kernel,
        out_shape=jax.ShapeDtypeStruct((kinds, 3, tokens, width), own.dtype),
        in_specs=[IN_VMEM],
        out_specs=IN_VMEM,
        scratch_shapes=semaphores(8),
        compiler_params=remote_params(collective_id),
        name="share_keys",
    )(own)


def return_kernel(grads, cosine, sine, out, total, from_y, from_z, send_sems, recv_sems):
    me = Peers()
    kinds, _, tokens, _ = grads.shape
    pieces = 2
    size = tokens // pieces
    parts = [(kind, pl.ds(piece * size, size)) for kind in range(kinds) for piece in range(pieces)]
    count = len(parts)
    greet_along_z(me)

    def copy(index, source, target, peer):
        return Copies(send_sems, recv_sems).describe(source, target, peer, index)

    def sideways(index, kind, rows):
        return copy(index, grads.at[kind, 1, rows], from_y.at[kind, rows], me.y_peer)

    def downward(index, kind, rows, source):
        return copy(count + index, source.at[kind, rows], from_z.at[kind, rows], (me.ep - 2, me.tp))

    for index, (kind, rows) in enumerate(parts):
        sideways(index, kind, rows).start()

    @pl.when((me.z > 0) & (me.y == 0))
    def _():
        for index, (kind, rows) in enumerate(parts):
            downward(index, kind, rows, grads.at[:, 0]).start()

    for index, (kind, rows) in enumerate(parts):
        sideways(index, kind, rows).wait_recv()
        here = grads[kind, 2, rows, :].astype(jnp.float32)

        @pl.when(me.y == 0)
        def _():
            total[kind, rows, :] = here + from_y[kind, rows, :].astype(jnp.float32)

        @pl.when(me.y == 1)
        def _():
            total[kind, rows, :] = here
            two_back = grads[kind, 0, rows, :].astype(jnp.float32)
            summed = two_back + from_y[kind, rows, :].astype(jnp.float32)
            from_y[kind, rows, :] = summed.astype(from_y.dtype)

        @pl.when((me.z > 0) & (me.y == 1))
        def _():
            downward(index, kind, rows, from_y).start()

    @pl.when(me.z < 3)
    def _():
        for index, (kind, rows) in enumerate(parts):
            downward(index, kind, rows, from_y).wait_recv()
            total[kind, rows, :] += from_z[kind, rows, :].astype(jnp.float32)

    for start in range(0, total.shape[2], HD):
        head = slice(start, start + HD)
        out[0, :, head] = turned(total[0, :, head], cosine[...], -sine[...]).astype(out.dtype)
    out[1] = total[1].astype(out.dtype)
    for index, (kind, rows) in enumerate(parts):
        sideways(index, kind, rows).wait_send()

    @pl.when(me.z > 0)
    def _():
        for index, (kind, rows) in enumerate(parts):
            downward(index, kind, rows, from_y).wait_send()


def return_keys(grads, cosine, sine, collective_id):
    kinds, _, tokens, width = grads.shape
    return pl.pallas_call(
        return_kernel,
        out_shape=jax.ShapeDtypeStruct((kinds, tokens, width), grads.dtype),
        in_specs=[IN_VMEM] * 3,
        out_specs=IN_VMEM,
        scratch_shapes=[
            pltpu.VMEM((kinds, tokens, width), jnp.float32),
            pltpu.VMEM((kinds, tokens, width), grads.dtype),
            pltpu.VMEM((kinds, tokens, width), grads.dtype),
        ]
        + semaphores(8),
        compiler_params=remote_params(collective_id),
        name="return_keys",
    )(grads, cosine, sine)


def reduce_kernel(flip, left, right, out, core_out, core_in, x_out, x_in, send_sems, recv_sems):
    me = Peers()
    copies = Copies(send_sems, recv_sems)
    terms = left.shape[0]
    count = out.shape[0]
    f32 = jnp.float32
    greet([me.x_peer, me.core_peer])

    def quarter(index):
        rows = pl.ds(pl.multiple_of(index * count, count), count)
        total = None
        for term in range(terms):
            one = product(left[term, rows, :], right[term], NT if flip else NN)
            total = one if total is None else total + one
        return total

    for slot, index in ((1, me.far_quarter), (0, me.core_quarter)):
        core_out[slot] = quarter(index).astype(core_out.dtype)
        target = core_in.at[slot]
        copies.send((OVER_CORE, slot), core_out.at[slot], target, target, me.core_peer)
    mine = quarter(me.x_quarter)
    copies.arrive(OVER_CORE, 1)
    x_out[...] = (mine + core_in[1].astype(f32)).astype(x_out.dtype)
    copies.send((OVER_X,), x_out, x_in, x_in, me.x_peer)
    mine = quarter(me.quarter)
    copies.arrive(OVER_CORE, 0)
    out[...] = mine + core_in[0].astype(f32)
    copies.arrive(OVER_X)
    out[...] += x_in[...].astype(f32)
    copies.finish()


def product_to_owner(left, right, flip, collective_id):
    tokens = left.shape[1]
    width = right.shape[1] if flip else right.shape[2]
    count = tokens // 4
    bf16 = jnp.bfloat16
    return pl.pallas_call(
        functools.partial(reduce_kernel, flip),
        out_shape=jax.ShapeDtypeStruct((count, width), jnp.float32),
        in_specs=[IN_VMEM] * 2,
        out_specs=IN_VMEM,
        scratch_shapes=[
            pltpu.VMEM((2, count, width), bf16),
            pltpu.VMEM((2, count, width), bf16),
            pltpu.VMEM((count, width), bf16),
            pltpu.VMEM((count, width), bf16),
        ]
        + semaphores(3),
        compiler_params=remote_params(collective_id),
        name="product_to_owner",
    )(left, right)


def tensor_kernel(rows, out, send_sems, recv_sems):
    me = Peers()
    copies = Copies(send_sems, recv_sems)
    greet([me.x_peer, me.core_peer])
    mine = out.at[me.quarter]
    copies.send((OVER_X,), rows, mine, out.at[me.x_quarter], me.x_peer)
    copies.send((OVER_CORE, 0), rows, mine, out.at[me.core_quarter], me.core_peer)
    copies.local((LOCAL,), rows, mine)
    copies.arrive(OVER_X)
    beside = out.at[me.x_quarter]
    copies.send((OVER_CORE, 1), beside, beside, out.at[me.far_quarter], me.core_peer)
    copies.finish()


def tensor_gather(rows, collective_id):
    return pl.pallas_call(
        tensor_kernel,
        out_shape=jax.ShapeDtypeStruct((4,) + rows.shape, rows.dtype),
        in_specs=[IN_PLACE],
        out_specs=IN_PLACE,
        scratch_shapes=semaphores(4),
        compiler_params=remote_params(collective_id),
        name="tensor_gather",
    )(rows)


def own_rows(block, tp_index, count):
    return lax.dynamic_slice_in_dim(block, tp_index * count, count, 0)


def after(value, earlier):
    return lax.optimization_barrier((value, earlier))[0]


def per_device_dense(
    layer_input,
    attention_gain,
    attention_in,
    attention_bias,
    attention_out,
    feedforward_gain,
    shared_in,
    shared_down,
    shared_gate,
    router,
    expert_in,
    expert_down,
    routes,
    document_lengths,
    cotangent,
):
    bf16 = jnp.bfloat16
    f32 = jnp.float32
    both = (EP, TP)
    tok_count, model_width = layer_input.shape
    expert_count = router.shape[1]
    top_count = routes.shape[1]
    ep_size = lax.axis_size(EP)
    tp_size = lax.axis_size(TP)
    ep_index = lax.axis_index(EP)
    tp_index = lax.axis_index(TP)
    own_count = tok_count // tp_size
    all_count = tok_count * ep_size
    capacity = tp_size * (
        (5 * tok_count * top_count + 4 * expert_count * tp_size - 1) // (4 * expert_count * tp_size)
    )
    reach_back = min((WINDOW + tok_count - 2) // tok_count, ep_size - 1)
    local_experts = expert_in.shape[0]
    in_blocks, out_full = spread_weights(attention_in, attention_out, 0)
    in_full = in_blocks.reshape(3, model_width, -1)
    all_cotangent = lax.all_gather(
        after(own_rows(cotangent, tp_index, own_count), in_blocks), both, axis=0, tiled=True
    )
    shard_width = shared_in.shape[1]
    slice_hidden = shared_in.shape[2] // ep_size
    shared_shards = jnp.concatenate([jnp.swapaxes(shared_in, 1, 2), shared_down[None]])
    shared_shards = jnp.swapaxes(
        shared_shards.reshape(3, ep_size, slice_hidden, shard_width), 0, 1
    )
    shared_slices = lax.all_to_all(
        after(shared_shards, in_blocks), EP, split_axis=0, concat_axis=0, tiled=True
    )
    shared_slices = jnp.transpose(shared_slices, (1, 2, 0, 3)).reshape(
        3, slice_hidden, model_width
    )
    expert_both = jnp.swapaxes(expert_in, 1, 2).reshape(local_experts, model_width, -1)

    positions = ep_index * tok_count + jnp.arange(tok_count, dtype=jnp.int32)
    key_count = (reach_back + 1) * tok_count
    key_positions = (ep_index - reach_back) * tok_count + jnp.arange(key_count, dtype=jnp.int32)
    query_doc, rope_pos, valid_mask = doc_table(document_lengths, positions)
    query_doc = query_doc[:, None]
    key_doc = doc_table(document_lengths, key_positions)[0][None, :]
    valid_rows = valid_mask.astype(f32)[:, None]
    cosine, sine = (part[:, 0] for part in rope_angles(rope_pos, HD))
    cosine = jnp.concatenate([cosine, cosine], axis=1)
    sine = jnp.concatenate([-sine, sine], axis=1)
    normed_attention, queries, own_kv = project(
        layer_input, attention_gain, in_full, attention_bias, cosine, sine
    )
    keys_values = share_keys(own_kv, 1)
    heads_low, log_totals = attend(queries, keys_values, query_doc, key_doc, valid_rows)
    attention_sum = product_to_owner(heads_low[None], out_full[None], False, 2)
    input_rows = own_rows(layer_input, tp_index, own_count).astype(f32)
    residual = input_rows + attention_sum
    inverse_two, normed_two = rms_parts(residual)
    normed_ffn = normed_two * feedforward_gain
    normed_low = normed_ffn.astype(bf16)
    shared_scale = jax.nn.sigmoid(jnp.dot(normed_ffn, shared_gate, precision=HIGHEST))
    router_probs = jax.nn.softmax(jnp.dot(normed_ffn, router, precision=HIGHEST), axis=-1)
    routes_own = own_rows(routes, tp_index, own_count)
    expert_ids = jnp.arange(expert_count, dtype=jnp.int32)
    picked = jnp.any(routes_own[:, :, None] == expert_ids[None, None, :], axis=1)
    chosen = jnp.where(picked, router_probs, 0.0)
    chosen_total = jnp.sum(chosen, axis=1, keepdims=True)
    gates = chosen / chosen_total
    scale_count = -(-(expert_count + 1 + top_count) // 8) * 8
    scale_rows = jnp.zeros((scale_count, own_count), f32)
    scale_rows = scale_rows.at[:expert_count].set(gates.T).at[expert_count].set(shared_scale)
    scale_rows = scale_rows.at[expert_count + 1 : expert_count + 1 + top_count].set(
        routes_own.T.astype(f32)
    )
    all_rows, all_scales = gather_rows(normed_low, scale_rows, 3)
    all_rows = all_rows.reshape(ep_size, tok_count, model_width)
    all_cotangent = all_cotangent.reshape(ep_size, tok_count, model_width)
    all_scales = jnp.swapaxes(all_scales, 1, 2).reshape(ep_size, scale_count, tok_count)
    my_gates = lax.dynamic_slice_in_dim(all_scales, ep_index * local_experts, local_experts, 1)
    my_ids = ep_index * local_experts + jnp.arange(local_experts, dtype=jnp.int32)
    all_routes = all_scales[:, expert_count + 1 : expert_count + 1 + top_count].astype(jnp.int32)
    taken = jnp.any(all_routes[:, None] == my_ids[None, :, None, None], axis=2)
    earlier_mask = jnp.tril(jnp.ones((tok_count, tok_count), bf16), -1)
    rank = product(
        taken.astype(bf16).reshape(-1, tok_count), earlier_mask, NT
    ).astype(jnp.int32).reshape(taken.shape)
    rank = jnp.where(taken & (rank < capacity), rank, NO_SLOT)
    (
        ffn_part,
        back_part,
        slot_rows,
        slot_cotangent,
        grad_pre,
        gated,
        grad_shared_pre,
        scaled_hidden,
        token_grad,
        scale_grad,
    ) = feed(
        rank,
        my_gates,
        all_scales[:, expert_count][:, :, None],
        all_rows,
        all_cotangent,
        expert_both,
        expert_down,
        shared_slices,
        capacity,
    )
    ffn_sum = lax.psum_scatter(
        ffn_part.reshape(all_count, model_width), both, scatter_dimension=0, tiled=True
    )
    layer_output = lax.all_gather(
        (residual + ffn_sum.astype(f32)).astype(bf16), TP, axis=0, tiled=True
    )
    scalar_part = jnp.zeros((ep_size, scale_count, tok_count), f32)
    scalar_part = lax.dynamic_update_slice(
        scalar_part, token_grad, (0, ep_index * local_experts, 0)
    )
    scalar_part = scalar_part.at[:, expert_count].set(scale_grad[:, :, 0])
    scalar_part = jnp.swapaxes(
        scalar_part.reshape(ep_size, scale_count, tp_size, own_count), 1, 2
    )
    back_sum, scalar_sum = scatter_rows(
        back_part.reshape(ep_size, tp_size, own_count, model_width), scalar_part, 4
    )
    scalar_sum = scalar_sum.T
    slot_rows = slot_rows.reshape(local_experts, -1, model_width)
    slot_cotangent = slot_cotangent.reshape(slot_rows.shape)
    grad_pre = grad_pre.reshape(2, local_experts, slot_rows.shape[1], -1)
    gated = gated.reshape(local_experts, slot_rows.shape[1], -1)
    grad_expert_down = jnp.einsum(
        "erf,erd->efd", gated, slot_cotangent, preferred_element_type=f32
    )
    grad_expert_in = jnp.einsum(
        "erd,serf->esdf", slot_rows, grad_pre, preferred_element_type=f32
    )
    flat_rows = all_rows.reshape(all_count, model_width)
    flat_cotangent = all_cotangent.reshape(all_count, model_width)
    shared_grads = [
        product(flat_rows, grad_shared_pre[0].reshape(all_count, -1), TN),
        product(flat_rows, grad_shared_pre[1].reshape(all_count, -1), TN),
        product(flat_cotangent, scaled_hidden.reshape(all_count, -1), TN),
    ]
    shared_grads = jnp.stack([grad.astype(bf16) for grad in shared_grads])
    shared_grads = jnp.transpose(
        shared_grads.reshape(3, ep_size, shard_width, slice_hidden), (1, 0, 3, 2)
    )
    shared_grads = lax.all_to_all(shared_grads, EP, split_axis=0, concat_axis=0, tiled=True)
    shared_grads = (
        jnp.swapaxes(shared_grads, 0, 1).reshape(3, -1, shard_width).astype(f32)
    )
    grad_shared_in = jnp.swapaxes(shared_grads[:2], 1, 2)
    grad_shared_down = shared_grads[2]

    grad_gates = scalar_sum[:, :expert_count]
    grad_probs = jnp.where(
        picked,
        (grad_gates - jnp.sum(grad_gates * gates, axis=1, keepdims=True)) / chosen_total,
        0.0,
    )
    grad_logits = router_probs * (
        grad_probs - jnp.sum(grad_probs * router_probs, axis=1, keepdims=True)
    )
    grad_router = jnp.einsum("td,te->de", normed_ffn, grad_logits, precision=HIGHEST)
    grad_scale_pre = scalar_sum[:, expert_count] * shared_scale * (1.0 - shared_scale)
    grad_shared_gate = jnp.dot(grad_scale_pre, normed_ffn, precision=HIGHEST)
    grad_normed = (
        back_sum
        + jnp.einsum("te,de->td", grad_logits, router, precision=HIGHEST)
        + grad_scale_pre[:, None] * shared_gate[None, :]
    )
    grad_mid_norm, grad_feedforward_gain = norm_back(
        grad_normed, feedforward_gain, inverse_two, normed_two
    )
    small = jnp.concatenate([grad_feedforward_gain[None], grad_shared_gate[None], grad_router.T])
    small = lax.psum(small, both)
    grad_residual = own_rows(cotangent, tp_index, own_count).astype(f32) + grad_mid_norm
    grad_attention = tensor_gather(grad_residual.astype(bf16), 5).reshape(tok_count, model_width)
    grad_attention_out = product(heads_low, grad_attention, TN)
    grad_heads = (product(grad_attention, out_full, NT) * valid_rows).astype(bf16)
    grad_queries, grad_kv = attend_back(
        queries, keys_values, query_doc, key_doc, log_totals, grad_heads, cosine, sine
    )
    grad_own_kv = return_keys(grad_kv, cosine, sine, 6)
    grad_raw = jnp.concatenate([grad_queries[None], grad_own_kv])
    grad_attention_bias = jnp.sum(grad_raw.astype(f32), axis=1)
    grad_normed_attention = product_to_owner(grad_raw, in_full, True, 7)
    inverse_one, normed_one = rms_parts(input_rows)
    grad_in_norm, grad_attention_gain = norm_back(
        grad_normed_attention, attention_gain, inverse_one, normed_one
    )
    grad_input = tensor_gather((grad_residual + grad_in_norm).astype(bf16), 8)
    grad_attention_in = jnp.einsum(
        "td,ste->sde", normed_attention, grad_raw, preferred_element_type=f32
    )
    columns = grad_attention_bias.shape[1]
    tail = jnp.concatenate(
        [
            grad_attention_bias,
            grad_attention_gain.reshape(-1, columns),
            jnp.zeros((8 - 3 - model_width // columns, columns), f32),
        ]
    )
    grad_attention_in, grad_attention_out, tails = collect_weights(
        grad_attention_in.astype(bf16).reshape(in_blocks.shape),
        grad_attention_out.astype(bf16),
        tail,
        9,
    )
    grad_attention_bias = lax.dynamic_index_in_dim(tails, tp_index, 0, keepdims=False)[:3]
    grad_attention_gain = jnp.sum(tails[:, 3:], axis=0)[: model_width // columns].reshape(-1)
    return (
        layer_output,
        grad_input.reshape(tok_count, model_width),
        grad_attention_gain,
        grad_attention_in,
        grad_attention_bias,
        grad_attention_out,
        small[0],
        grad_shared_in,
        grad_shared_down,
        small[1],
        small[2:].T,
        grad_expert_in,
        grad_expert_down,
    )


def per_device(*arguments):
    small_slice = lax.axis_size(EP) == RING and lax.axis_size(TP) == 4
    return (per_device_dense if small_slice else per_device_sparse)(*arguments)


def per_device_sparse(
    layer_input,
    attention_gain,
    attention_in,
    attention_bias,
    attention_out,
    feedforward_gain,
    shared_in,
    shared_down,
    shared_gate,
    router,
    expert_in,
    expert_down,
    routes,
    document_lengths,
    cotangent,
):
    bf16 = jnp.bfloat16
    f32 = jnp.float32
    tok_count = layer_input.shape[0]
    model_width = layer_input.shape[1]
    expert_count = router.shape[1]
    top_count = routes.shape[1]
    ep_size = lax.axis_size(EP)
    tp_size = lax.axis_size(TP)
    capacity = tp_size * (
        (5 * tok_count * top_count + 4 * expert_count * tp_size - 1) // (4 * expert_count * tp_size)
    )
    reach_back = min((WINDOW + tok_count - 2) // tok_count, ep_size - 1)
    head_dim = HD
    local_heads = attention_in.shape[2] // head_dim
    score_scale = 1.0 / math.sqrt(head_dim)
    in_full, out_full, shared_in_full, shared_down_full = (
        lax.all_gather(attention_in, EP, axis=1, tiled=True),
        lax.all_gather(attention_out, EP, axis=1, tiled=True),
        lax.all_gather(shared_in, EP, axis=1, tiled=True),
        lax.all_gather(shared_down, EP, axis=1, tiled=True),
    )
    ep_index = lax.axis_index(EP)
    positions = ep_index * tok_count + jnp.arange(tok_count, dtype=jnp.int32)
    key_count = (reach_back + 1) * tok_count
    key_positions = (ep_index - reach_back) * tok_count + jnp.arange(key_count, dtype=jnp.int32)
    query_doc, rope_pos, valid_mask = doc_table(document_lengths, positions)
    key_doc = doc_table(document_lengths, key_positions)[0]
    distance = positions[:, None] - key_positions[None, :]
    allowed = (query_doc[:, None] == key_doc[None, :]) & (distance >= 0) & (distance < WINDOW)
    valid_rows = valid_mask.astype(f32)[:, None]
    cosine, sine_part = rope_angles(rope_pos, head_dim)
    input_rows = layer_input.astype(f32)
    inverse_one, normed_one = rms_parts(input_rows)
    normed_attention = (normed_one * attention_gain).astype(bf16)
    raw_proj = (
        jnp.einsum("td,sde->ste", normed_attention, in_full, preferred_element_type=f32)
        + attention_bias[:, None, :]
    )
    queries = rotate(
        raw_proj[0].reshape(tok_count, local_heads, head_dim), cosine, sine_part, 1.0
    ).astype(bf16)
    keys_own = rotate(
        raw_proj[1].reshape(tok_count, local_heads, head_dim), cosine, sine_part, 1.0
    ).astype(bf16)
    values_own = raw_proj[2].reshape(tok_count, local_heads, head_dim).astype(bf16)
    key_value = jnp.stack([keys_own, values_own])
    earlier = []
    for hop_count in range(reach_back, 0, -1):
        earlier.append(shifted(key_value, EP, hop_count))
    all_kv = jnp.concatenate(earlier + [key_value], axis=1)
    all_keys = all_kv[0]
    all_values = all_kv[1]
    scores = jnp.einsum("qhe,khe->hqk", queries, all_keys, preferred_element_type=f32) * score_scale
    scores = jnp.where(allowed[None], scores, MASKED)
    row_max = jnp.max(scores, axis=-1, keepdims=True)
    exp_terms = jnp.exp(scores - row_max)
    row_total = jnp.sum(exp_terms, axis=-1, keepdims=True)
    log_total = row_max + jnp.log(row_total)
    weights = (exp_terms / row_total).astype(bf16)
    heads_out = jnp.einsum("hqk,khe->qhe", weights, all_values, preferred_element_type=f32).reshape(
        tok_count, -1
    )
    heads_low = (heads_out * valid_rows).astype(bf16)
    attention_sum = tensor_total(jnp.dot(heads_low, out_full, preferred_element_type=f32))
    residual = input_rows + attention_sum
    inverse_two, normed_two = rms_parts(residual)
    normed_ffn = normed_two * feedforward_gain
    normed_low = normed_ffn.astype(bf16)
    shared_pre = jnp.einsum("td,sdf->stf", normed_low, shared_in_full, preferred_element_type=f32)
    shared_silu, shared_slope = silu_parts(shared_pre[0])
    shared_hidden = (shared_silu * shared_pre[1]).astype(bf16)
    shared_out = tensor_total(jnp.dot(shared_hidden, shared_down_full, preferred_element_type=f32))
    shared_scale = jax.nn.sigmoid(jnp.dot(normed_ffn, shared_gate, precision=HIGHEST))
    router_probs = jax.nn.softmax(jnp.dot(normed_ffn, router, precision=HIGHEST), axis=-1)
    chosen = jnp.take_along_axis(router_probs, routes, axis=1)
    chosen_total = jnp.sum(chosen, axis=1, keepdims=True)
    gate_values = chosen / chosen_total
    assign_count = tok_count * top_count
    flat_routes = routes.reshape(-1)
    expert_ids = jnp.arange(expert_count, dtype=jnp.int32)
    one_hot = (flat_routes[:, None] == expert_ids[None, :]).astype(jnp.int32)
    arrival_rank = jnp.sum((jnp.cumsum(one_hot, axis=0) - one_hot) * one_hot, axis=1)
    slot_count = expert_count * capacity
    slot_index = jnp.where(
        arrival_rank < capacity, flat_routes * capacity + arrival_rank, slot_count
    )
    slot_assign = (
        jnp.full((slot_count + 1,), assign_count, jnp.int32)
        .at[slot_index]
        .set(jnp.arange(assign_count, dtype=jnp.int32))[:slot_count]
    )
    slot_token = slot_assign // top_count
    padded_rows = jnp.concatenate([normed_low, jnp.zeros((1, model_width), bf16)])
    send_rows = padded_rows[slot_token].reshape(expert_count, capacity, model_width)

    def expert_trip(outgoing, work):
        row_block = lax.all_to_all(outgoing, EP, split_axis=0, concat_axis=1, tiled=True)
        partial_rows, extras = work(row_block)
        share_rows = lax.psum_scatter(partial_rows, TP, scatter_dimension=1, tiled=True).astype(
            bf16
        )
        whole_rows = lax.all_gather(share_rows, TP, axis=1, tiled=True)
        return (lax.all_to_all(whole_rows, EP, split_axis=1, concat_axis=0, tiled=True), extras)

    def expert_forward(row_block):
        pre_acts = jnp.einsum("erd,esdf->serf", row_block, expert_in, preferred_element_type=f32)
        gate_silu, gate_slope = silu_parts(pre_acts[0])
        hidden = (gate_silu * pre_acts[1]).astype(bf16)
        partial_rows = jnp.einsum("erf,efd->erd", hidden, expert_down, preferred_element_type=f32)
        return (partial_rows, (row_block, pre_acts, hidden, gate_silu, gate_slope))

    returned_rows, kept_state = expert_trip(send_rows, expert_forward)
    expert_rows, expert_pre, expert_hidden, expert_silu, expert_slope = kept_state
    padded_back = jnp.concatenate(
        [returned_rows.reshape(slot_count, model_width), jnp.zeros((1, model_width), bf16)]
    )
    picked = padded_back[slot_index].reshape(tok_count, top_count, model_width).astype(f32)
    moe_sum = jnp.sum(gate_values[:, :, None] * picked, axis=1)
    layer_output = (residual + shared_scale[:, None] * shared_out + moe_sum).astype(bf16)
    grad_rows = cotangent.astype(f32)
    padded_grad = jnp.concatenate([grad_rows, jnp.zeros((1, model_width), f32)])
    padded_gates = jnp.concatenate([gate_values.reshape(-1), jnp.zeros((1,), f32)])
    grad_send = (padded_gates[slot_assign][:, None] * padded_grad[slot_token]).astype(bf16)
    grad_send = grad_send.reshape(expert_count, capacity, model_width)

    def expert_backward(grad_block):
        grad_down = jnp.einsum(
            "erf,erd->efd", expert_hidden, grad_block, preferred_element_type=f32
        )
        grad_hidden = jnp.einsum(
            "erd,efd->erf", grad_block, expert_down, preferred_element_type=f32
        )
        grad_pre = jnp.stack(
            [grad_hidden * expert_pre[1] * expert_slope, grad_hidden * expert_silu]
        ).astype(bf16)
        grad_weights_in = jnp.einsum(
            "erd,serf->esdf", expert_rows, grad_pre, preferred_element_type=f32
        )
        grad_back_rows = jnp.einsum(
            "serf,esdf->erd", grad_pre, expert_in, preferred_element_type=f32
        )
        return (grad_back_rows, (grad_weights_in, grad_down))

    grad_returned, expert_grads = expert_trip(grad_send, expert_backward)
    grad_expert_in, grad_expert_down = expert_grads
    grad_gate_values = jnp.sum(picked * grad_rows[:, None, :], axis=2)
    grad_chosen = (
        grad_gate_values - jnp.sum(grad_gate_values * gate_values, axis=1, keepdims=True)
    ) / chosen_total
    grad_probs = jnp.sum(
        jnp.where(routes[:, :, None] == expert_ids[None, None, :], grad_chosen[:, :, None], 0.0),
        axis=1,
    )
    grad_logits = router_probs * (
        grad_probs - jnp.sum(grad_probs * router_probs, axis=1, keepdims=True)
    )
    grad_router = jnp.einsum("td,te->de", normed_ffn, grad_logits, precision=HIGHEST)
    grad_shared_out = (shared_scale[:, None] * grad_rows).astype(bf16)
    grad_shared_down = jnp.einsum(
        "tf,td->fd", shared_hidden, grad_shared_out, preferred_element_type=f32
    )
    grad_shared_hidden = jnp.einsum(
        "td,fd->tf", grad_shared_out, shared_down_full, preferred_element_type=f32
    )
    grad_shared_pre = jnp.stack(
        [grad_shared_hidden * shared_pre[1] * shared_slope, grad_shared_hidden * shared_silu]
    ).astype(bf16)
    grad_shared_in = jnp.einsum(
        "td,stf->sdf", normed_low, grad_shared_pre, preferred_element_type=f32
    )
    shared_back = jnp.einsum(
        "stf,sdf->td", grad_shared_pre, shared_in_full, preferred_element_type=f32
    )
    grad_scale_pre = jnp.sum(grad_rows * shared_out, axis=1) * shared_scale * (1.0 - shared_scale)
    grad_shared_gate = jnp.dot(grad_scale_pre, normed_ffn, precision=HIGHEST)
    padded_return = jnp.concatenate(
        [grad_returned.reshape(slot_count, model_width), jnp.zeros((1, model_width), bf16)]
    )
    moe_back = jnp.sum(
        padded_return[slot_index].reshape(tok_count, top_count, model_width).astype(f32), axis=1
    )
    grad_normed = (
        tensor_total(shared_back)
        + moe_back
        + jnp.einsum("te,de->td", grad_logits, router, precision=HIGHEST)
        + grad_scale_pre[:, None] * shared_gate[None, :]
    )
    grad_mid_norm, grad_feedforward_gain = norm_back(
        grad_normed, feedforward_gain, inverse_two, normed_two
    )
    grad_residual = grad_rows + grad_mid_norm
    grad_attention = grad_residual.astype(bf16)
    grad_attention_out = jnp.einsum(
        "tf,td->fd", heads_low, grad_attention, preferred_element_type=f32
    )
    grad_heads = jnp.einsum(
        "td,fd->tf", grad_attention, out_full, preferred_element_type=f32
    ).astype(bf16)
    grad_heads = (grad_heads * valid_rows.astype(bf16)).reshape(tok_count, local_heads, head_dim)
    scores_again = (
        jnp.einsum("qhe,khe->hqk", queries, all_keys, preferred_element_type=f32) * score_scale
    )
    scores_again = jnp.where(allowed[None], scores_again, MASKED)
    softmax_out = jnp.exp(scores_again - log_total)
    weights_again = softmax_out.astype(bf16)
    grad_weights = jnp.einsum("qhe,khe->hqk", grad_heads, all_values, preferred_element_type=f32)
    grad_scores = (
        softmax_out * (grad_weights - jnp.sum(softmax_out * grad_weights, axis=-1, keepdims=True))
    ).astype(bf16)
    grad_queries = (
        jnp.einsum("hqk,khe->qhe", grad_scores, all_keys, preferred_element_type=f32) * score_scale
    )
    grad_keys = (
        jnp.einsum("hqk,qhe->khe", grad_scores, queries, preferred_element_type=f32) * score_scale
    )
    grad_values = jnp.einsum("hqk,qhe->khe", weights_again, grad_heads, preferred_element_type=f32)
    grad_kv = jnp.stack([grad_keys, grad_values])
    own_part = grad_kv[:, reach_back * tok_count :]
    for hop_count in range(1, reach_back + 1):
        segment_start = (reach_back - hop_count) * tok_count
        segment = grad_kv[:, segment_start : segment_start + tok_count]
        own_part = own_part + shifted(segment, EP, -hop_count)
    grad_raw = (
        jnp.stack(
            [
                rotate(grad_queries, cosine, sine_part, -1.0),
                rotate(own_part[0], cosine, sine_part, -1.0),
                own_part[1],
            ]
        )
        .reshape(3, tok_count, -1)
        .astype(bf16)
    )
    grad_attention_bias = jnp.sum(grad_raw.astype(f32), axis=1)
    grad_attention_in = jnp.einsum(
        "td,ste->sde", normed_attention, grad_raw, preferred_element_type=f32
    )
    grad_normed_attention = tensor_total(
        jnp.einsum("ste,sde->td", grad_raw, in_full, preferred_element_type=f32)
    )
    grad_in_norm, grad_attention_gain = norm_back(
        grad_normed_attention, attention_gain, inverse_one, normed_one
    )
    grad_input = (grad_residual + grad_in_norm).astype(bf16)
    grad_attention_in, grad_attention_out, grad_shared_in, grad_shared_down = (
        lax.psum_scatter(
            grad_attention_in.astype(jnp.bfloat16), EP, scatter_dimension=1, tiled=True
        ).astype(jnp.float32),
        lax.psum_scatter(
            grad_attention_out.astype(jnp.bfloat16), EP, scatter_dimension=1, tiled=True
        ).astype(jnp.float32),
        lax.psum_scatter(
            grad_shared_in.astype(jnp.bfloat16), EP, scatter_dimension=1, tiled=True
        ).astype(jnp.float32),
        lax.psum_scatter(
            grad_shared_down.astype(jnp.bfloat16), EP, scatter_dimension=1, tiled=True
        ).astype(jnp.float32),
    )
    (
        grad_attention_gain,
        grad_attention_bias,
        grad_feedforward_gain,
        grad_shared_gate,
        grad_router,
    ) = (
        lax.psum(grad_attention_gain.astype(jnp.bfloat16), EP).astype(jnp.float32),
        lax.psum(grad_attention_bias.astype(jnp.bfloat16), EP).astype(jnp.float32),
        lax.psum(grad_feedforward_gain.astype(jnp.bfloat16), EP).astype(jnp.float32),
        lax.psum(grad_shared_gate.astype(jnp.bfloat16), EP).astype(jnp.float32),
        lax.psum(grad_router.astype(jnp.bfloat16), EP).astype(jnp.float32),
    )
    return (
        layer_output,
        grad_input,
        grad_attention_gain,
        grad_attention_in,
        grad_attention_bias,
        grad_attention_out,
        grad_feedforward_gain,
        grad_shared_in,
        grad_shared_down,
        grad_shared_gate,
        grad_router,
        grad_expert_in,
        grad_expert_down,
    )


def solution(mesh):
    return jax.shard_map(
        per_device,
        mesh=mesh,
        in_specs=(
            P(EP, None),
            P(),
            P(None, EP, TP),
            P(None, TP),
            P(TP, EP),
            P(),
            P(None, EP, TP),
            P(TP, EP),
            P(),
            P(),
            P(EP, None, None, TP),
            P(EP, TP, None),
            P(EP, None),
            P(),
            P(EP, None),
        ),
        out_specs=(
            P(EP, None),
            P(EP, None),
            P(),
            P(None, EP, TP),
            P(None, TP),
            P(TP, EP),
            P(),
            P(None, EP, TP),
            P(TP, EP),
            P(),
            P(),
            P(EP, None, None, TP),
            P(EP, TP, None),
        ),
        check_vma=False,
    )
```

```python
import functools
import math

import jax
import jax.numpy as jnp
from jax import lax
from jax.experimental import pallas as pl
from jax.experimental.pallas import tpu as pltpu
from jax.sharding import PartitionSpec as P

EP, TP = "ep", "tp"
HD = 128
WINDOW = 1024


HIGHEST = lax.Precision.HIGHEST
EPSILON = 1e-06
ROPE_BASE = 1000000.0
MASKED = -1000000000.0


def shifted(value, axis, steps):
    count = lax.axis_size(axis)
    leading, last = (max(0, -steps), min(count, count - steps))
    return lax.ppermute(value, axis, [(source, source + steps) for source in range(leading, last)])


def tensor_total(partial_sum):
    return lax.psum(partial_sum, TP)


def rms_parts(values):
    inverse = lax.rsqrt(jnp.mean(values * values, axis=-1, keepdims=True) + EPSILON)
    return (inverse, values * inverse)


def norm_back(grad_rows, gain_vec, inverse, normed):
    scaled = grad_rows * gain_vec
    grad_in = inverse * (scaled - normed * jnp.mean(scaled * normed, axis=-1, keepdims=True))
    return (grad_in, jnp.sum(grad_rows * normed, axis=0))


def doc_table(document_lengths, positions):
    doc_ends = jnp.cumsum(document_lengths)
    starts_all = jnp.concatenate([doc_ends - document_lengths, doc_ends[-1:]])
    doc_ids = jnp.sum((positions[:, None] >= doc_ends[None, :]).astype(jnp.int32), axis=1)
    matches = (
        doc_ids[:, None] == jnp.arange(document_lengths.shape[0] + 1, dtype=jnp.int32)[None, :]
    )
    doc_begin = jnp.sum(jnp.where(matches, starts_all[None, :], 0), axis=1)
    rope_pos = positions - doc_begin
    valid_mask = positions < doc_ends[-1]
    doc_ids = jnp.where(positions < 0, -1, doc_ids)
    return (doc_ids, rope_pos, valid_mask)


def rope_angles(rope_pos, head_dim):
    half_width = head_dim // 2
    freqs = jnp.power(ROPE_BASE, -2.0 * jnp.arange(half_width, dtype=jnp.float32) / head_dim)
    angles = rope_pos.astype(jnp.float32)[:, None] * freqs[None, :]
    return (jnp.cos(angles)[:, None, :], jnp.sin(angles)[:, None, :])


def rotate(values, cosine, sine_part, turn_sign):
    half_width = values.shape[-1] // 2
    first_part = values[..., :half_width]
    second_part = values[..., half_width:]
    return jnp.concatenate(
        [
            first_part * cosine - turn_sign * second_part * sine_part,
            second_part * cosine + turn_sign * first_part * sine_part,
        ],
        axis=-1,
    )


def silu_parts(gate_pre):
    sig_gate = jax.nn.sigmoid(gate_pre)
    return (gate_pre * sig_gate, sig_gate * (1.0 + gate_pre * (1.0 - sig_gate)))


NN = (((1,), (0,)), ((), ()))
NT = (((1,), (1,)), ((), ()))
TN = (((0,), (0,)), ((), ()))


def product(left, right, dims=NN):
    return lax.dot_general(left, right, dims, preferred_element_type=jnp.float32)


def turned(values, cosine, sine):
    half = values.shape[1] // 2
    swapped = jnp.concatenate([values[:, half:], values[:, :half]], axis=1)
    return values * cosine + swapped * sine


def project_kernel(rows, gain, weights, bias, cosine, sine, normed, queries, keys_values):
    bf16, f32 = jnp.bfloat16, jnp.float32

    @pl.when(pl.program_id(0) == 0)
    def _():
        _, scaled = rms_parts(rows[...].astype(f32))
        normed[...] = (scaled * gain[...]).astype(bf16)

    columns = queries.shape[1]
    for kind in range(3):
        raw = product(normed[...], weights[kind]) + bias[kind : kind + 1, :]
        for start in range(0, columns, HD):
            head = slice(start, start + HD)
            part = raw[:, head]
            if kind < 2:
                part = turned(part, cosine[...], sine[...])
            if kind == 0:
                queries[:, head] = part.astype(bf16)
            else:
                keys_values[kind - 1, :, head] = part.astype(bf16)


def project(rows, gain, weights, bias, cosine, sine):
    tokens, width = rows.shape
    columns = weights.shape[2]
    step = min(2 * HD, columns)
    shape = jax.ShapeDtypeStruct
    bf16 = jnp.bfloat16

    def whole(*dims):
        return pl.BlockSpec(dims, lambda h: (0,) * len(dims))

    return pl.pallas_call(
        project_kernel,
        grid=(columns // step,),
        in_specs=[
            whole(tokens, width),
            whole(1, width),
            pl.BlockSpec((3, width, step), lambda h: (0, 0, h)),
            pl.BlockSpec((3, step), lambda h: (0, h)),
            whole(tokens, HD),
            whole(tokens, HD),
        ],
        out_specs=(
            whole(tokens, width),
            pl.BlockSpec((tokens, step), lambda h: (0, h)),
            pl.BlockSpec((2, tokens, step), lambda h: (0, 0, h)),
        ),
        out_shape=(
            shape((tokens, width), bf16),
            shape((tokens, columns), bf16),
            shape((2, tokens, columns), bf16),
        ),
        compiler_params=pltpu.CompilerParams(vmem_limit_bytes=40 * 2**20),
        name="project",
    )(rows, gain[None], weights, bias, cosine, sine)


def masked_scores(queries, keys, query_doc, key_doc):
    tokens, count = queries.shape[0], keys.shape[0]
    scores = product(queries, keys, NT) * (1.0 / math.sqrt(HD))
    ahead = lax.broadcasted_iota(jnp.int32, (tokens, count), 0) + (count - tokens)
    distance = ahead - lax.broadcasted_iota(jnp.int32, (tokens, count), 1)
    allowed = (query_doc == key_doc) & (distance >= 0) & (distance < WINDOW)
    return jnp.where(allowed, scores, MASKED)


def attend_kernel(queries, keys, values, query_doc, key_doc, valid, heads, log_totals):
    count = keys.shape[1] * keys.shape[2]
    keys, values = keys[0].reshape(count, HD), values[0].reshape(count, HD)
    scores = masked_scores(queries[...], keys, query_doc[...], key_doc[...])
    row_max = jnp.max(scores, axis=1, keepdims=True)
    terms = jnp.exp(scores - row_max)
    total = jnp.sum(terms, axis=1, keepdims=True)
    weights = (terms / total).astype(jnp.bfloat16)
    heads[...] = (product(weights, values) * valid[...]).astype(jnp.bfloat16)
    log_totals[0] = row_max + jnp.log(total)


def attention_specs(tokens, blocks):
    def column(*dims):
        return pl.BlockSpec(dims, lambda h: (0,) * len(dims))

    head = pl.BlockSpec((tokens, HD), lambda h: (0, h))
    keys = pl.BlockSpec((1, blocks, tokens, HD), lambda h: (0, 0, 0, h))
    values = pl.BlockSpec((1, blocks, tokens, HD), lambda h: (1, 0, 0, h))
    logs = pl.BlockSpec((1, tokens, 1), lambda h: (h, 0, 0))
    return head, keys, values, column(tokens, 1), column(1, blocks * tokens), logs


def attend(queries, keys_values, query_doc, key_doc, valid):
    tokens, columns = queries.shape
    blocks = keys_values.shape[1]
    head, keys, values, column, row, logs = attention_specs(tokens, blocks)
    shape = jax.ShapeDtypeStruct
    return pl.pallas_call(
        attend_kernel,
        grid=(columns // HD,),
        in_specs=[head, keys, values, column, row, column],
        out_specs=(head, logs),
        out_shape=(
            shape((tokens, columns), jnp.bfloat16),
            shape((columns // HD, tokens, 1), jnp.float32),
        ),
        compiler_params=pltpu.CompilerParams(vmem_limit_bytes=40 * 2**20),
        name="attend",
    )(queries, keys_values, keys_values, query_doc, key_doc, valid)


def attend_back_kernel(
    queries, keys, values, query_doc, key_doc, log_totals, grad_heads, cosine, sine,
    grad_queries, grad_keys_values,
):
    bf16 = jnp.bfloat16
    scale = 1.0 / math.sqrt(HD)
    blocks, tokens = keys.shape[1], keys.shape[2]
    keys, values = (ref[0].reshape(blocks * tokens, HD) for ref in (keys, values))
    scores = masked_scores(queries[...], keys, query_doc[...], key_doc[...])
    probs = jnp.exp(scores - log_totals[0])
    grads = grad_heads[...]
    slopes = product(grads, values, NT)
    slopes = probs * (slopes - jnp.sum(probs * slopes, axis=1, keepdims=True))
    grad_scores = slopes.astype(bf16)
    turned_back = turned(product(grad_scores, keys) * scale, cosine[...], -sine[...])
    grad_queries[...] = turned_back.astype(bf16)
    grad_keys = product(grad_scores, queries[...], TN) * scale
    grad_keys_values[0] = grad_keys.astype(bf16).reshape(blocks, tokens, HD)
    grad_values = product(probs.astype(bf16), grads, TN)
    grad_keys_values[1] = grad_values.astype(bf16).reshape(blocks, tokens, HD)


def attend_back(queries, keys_values, query_doc, key_doc, log_totals, grad_heads, cosine, sine):
    tokens, columns = queries.shape
    blocks = keys_values.shape[1]
    head, keys, values, column, row, logs = attention_specs(tokens, blocks)
    angle = pl.BlockSpec((tokens, HD), lambda h: (0, 0))
    shape = jax.ShapeDtypeStruct
    return pl.pallas_call(
        attend_back_kernel,
        grid=(columns // HD,),
        in_specs=[head, keys, values, column, row, logs, head, angle, angle],
        out_specs=(head, pl.BlockSpec((2, blocks, tokens, HD), lambda h: (0, 0, 0, h))),
        out_shape=(
            shape((tokens, columns), jnp.bfloat16),
            shape(keys_values.shape, jnp.bfloat16),
        ),
        compiler_params=pltpu.CompilerParams(vmem_limit_bytes=48 * 2**20),
        name="attend_back",
    )(queries, keys_values, keys_values, query_doc, key_doc, log_totals, grad_heads, cosine, sine)


RING = 8
NO_SLOT = 1 << 20
RIGHT, LEFT, OVER_X, OVER_CORE, OVER_FAR, OVER_Y, OVER_Z, LOCAL = range(8)
MESH_ID = pl.DeviceIdType.MESH


def ring_place(ep):
    z, y = ep // 2, ep % 2
    return z + y * (7 - 2 * z)


def ring_member(place):
    upper = place // 4
    return 2 * place + upper * (15 - 4 * place)


class Peers:
    def __init__(self):
        self.ep, self.tp = lax.axis_index(EP), lax.axis_index(TP)
        self.x, self.core = self.tp // 2, self.tp % 2
        self.z, self.y = self.ep // 2, self.ep % 2
        self.place = ring_place(self.ep)
        self.right = (self.block(1), self.tp)
        self.left = (self.block(RING - 1), self.tp)
        self.quarter = self.tp
        self.x_quarter = (1 - self.x) * 2 + self.core
        self.core_quarter = self.x * 2 + 1 - self.core
        self.far_quarter = (1 - self.x) * 2 + 1 - self.core
        self.x_peer = (self.ep, self.x_quarter)
        self.core_peer = (self.ep, self.core_quarter)
        self.far_peer = (self.ep, self.far_quarter)
        self.y_peer = (self.z * 2 + 1 - self.y, self.tp)

    def block(self, step):
        return ring_member((self.place + step + RING) % RING)


def greet(peers):
    barrier = pltpu.get_barrier_semaphore()
    for peer in peers:
        pl.semaphore_signal(barrier, inc=1, device_id=peer, device_id_type=MESH_ID)
    pl.semaphore_wait(barrier, len(peers))


class Copies:
    def __init__(self, send_sems, recv_sems):
        self.send_sems, self.recv_sems = send_sems, recv_sems
        self.count = 0
        self.sent = []
        self.landing = {}

    def describe(self, source, target, peer, index):
        return pltpu.make_async_remote_copy(
            src_ref=source,
            dst_ref=target,
            send_sem=self.send_sems.at[index],
            recv_sem=self.recv_sems.at[index],
            device_id=peer,
            device_id_type=MESH_ID,
        )

    def send(self, key, source, target, landing, peer):
        index = self.count
        self.count += 1
        copy = self.describe(source, target, peer, index)
        copy.start()
        self.sent.append(copy)
        self.landing[key] = self.describe(landing, landing, peer, index).wait_recv

    def local(self, key, source, target):
        index = self.count
        self.count += 1
        copy = pltpu.make_async_copy(source, target, self.send_sems.at[index])
        copy.start()
        self.landing[key] = copy.wait

    def arrive(self, *key):
        self.landing.pop(key)()

    def finish(self):
        for wait in self.landing.values():
            wait()
        for copy in self.sent:
            copy.wait_send()


def remote_params(collective_id, vmem=48):
    return pltpu.CompilerParams(
        collective_id=collective_id, has_side_effects=True, vmem_limit_bytes=vmem * 2**20
    )


def semaphores(count):
    return [pltpu.SemaphoreType.DMA((count,))] * 2


IN_PLACE = pl.BlockSpec(memory_space=pl.ANY)
IN_VMEM = pl.BlockSpec(memory_space=pltpu.VMEM)


class LateCopies(Copies):
    def send(self, key, source, target, landing, peer):
        index = self.count
        self.count += 1
        self.describe(source(), target(), peer, index).start()
        self.sent.append(lambda: self.describe(source(), target(), peer, index).wait_send())
        self.landing[key] = lambda: self.describe(landing(), landing(), peer, index).wait_recv()

    def local(self, key, source, target):
        index = self.count
        self.count += 1

        def copy():
            return pltpu.make_async_copy(source(), target(), self.send_sems.at[index])

        copy().start()
        self.landing[key] = lambda: copy().wait()

    def finish(self):
        for wait in list(self.landing.values()) + self.sent:
            wait()


def feed_block(
    block, rank_row, rank_column, gate_rows, scale, token_rows, token_cotangent,
    expert_in, expert_down, shared, staged, between, out_terms, back_terms, scale_grad, token_grad,
):
    (
        out_part, back_part, slot_rows, slot_cotangent, grad_pre, gated, grad_shared_pre, scaled,
    ) = staged
    bf16, f32 = jnp.bfloat16, jnp.float32
    experts, slots, _ = slot_rows.shape
    tokens = token_rows.shape[0]
    hidden_count = gated.shape[2]
    padded = expert_in.shape[2] // 2
    all_slots = experts * slots
    silu, slope = silu_parts(product(token_rows, shared[0], NT))
    up = product(token_rows, shared[1], NT)
    hidden = (silu * up).astype(bf16).astype(f32)
    scaled_hidden = (scale * hidden).astype(bf16)
    back = product(token_cotangent, shared[2], NT)
    scale_grad[block] = jnp.sum(hidden * back, axis=1, keepdims=True)
    back = scale * back
    gate_grad = (back * up * slope).astype(bf16)
    up_grad = (back * silu).astype(bf16)
    between()
    scaled[...] = scaled_hidden
    grad_shared_pre[0] = gate_grad
    grad_shared_pre[1] = up_grad
    order = lax.broadcasted_iota(jnp.int32, (all_slots, tokens), 0)
    spread_order = lax.broadcasted_iota(jnp.int32, (tokens, all_slots), 1)
    hits, spread = None, None
    for expert in range(experts):
        row_hits = order == rank_row[expert : expert + 1, :] + expert * slots
        column_hits = spread_order == rank_column[:, expert : expert + 1] + expert * slots
        hits = row_hits if hits is None else hits | row_hits
        spread = column_hits if spread is None else spread | column_hits
    place = hits.astype(bf16)
    taken = product(place, token_rows).astype(bf16)
    taken_cotangent = product(place, token_cotangent).astype(bf16)
    for ref, values in ((slot_rows, taken), (slot_cotangent, taken_cotangent)):
        for expert in range(experts):
            ref[expert] = values[expert * slots : (expert + 1) * slots]
    for expert in range(experts):
        mine = slice(expert * slots, (expert + 1) * slots)
        gate = jnp.sum(
            jnp.where(hits[mine], gate_rows[expert : expert + 1], 0.0), axis=1, keepdims=True
        )
        pre = product(taken[mine], expert_in[expert])
        silu, slope = silu_parts(pre[:, :hidden_count])
        up = pre[:, padded : padded + hidden_count]
        hidden = (silu * up).astype(bf16).astype(f32)
        gated_hidden = (gate * hidden).astype(bf16)
        gated[expert] = gated_hidden
        back = product(taken_cotangent[mine], expert_down[expert], NT)
        slot_grad = jnp.sum(hidden * back, axis=1, keepdims=True)
        token_grad[block, expert : expert + 1, :] = jnp.sum(
            jnp.where(hits[mine], slot_grad, 0.0), axis=0, keepdims=True
        )
        back = gate * back
        gate_grad_e = (back * up * slope).astype(bf16)
        up_grad_e = (back * silu).astype(bf16)
        grad_pre[0, expert] = gate_grad_e
        grad_pre[1, expert] = up_grad_e
        out_terms[mine, :] = product(gated_hidden, expert_down[expert]).astype(bf16)
        gap = jnp.zeros((slots, padded - hidden_count), bf16)
        both_grads = jnp.concatenate([gate_grad_e, gap, up_grad_e, gap], axis=1)
        back_terms[mine, :] = product(both_grads, expert_in[expert], NT).astype(bf16)
    spread = spread.astype(bf16)
    out_part[...] = product(
        jnp.concatenate([spread, scaled_hidden], axis=1), out_terms[...]
    ).astype(bf16)
    back_part[...] = product(
        jnp.concatenate([spread, gate_grad, up_grad], axis=1), back_terms[...]
    ).astype(bf16)


def gather_feed_kernel(
    rows, cotangent, scales, rank_row, rank_column, expert_in, expert_down, shared,
    all_rows, all_cotangent, all_scales,
    out_part, back_part, slot_rows, slot_cotangent, grad_pre, gated, grad_shared_pre, scaled,
    token_grad, scale_grad,
    expert_both, out_terms, back_terms, held_rows, held_cotangent,
    stage_out, stage_back, stage_rows, stage_cotangent, stage_pre, stage_gated, stage_shared,
    stage_scaled,
    load_sems, store_sems, send_sems, recv_sems,
):
    me = Peers()
    copies = LateCopies(send_sems, recv_sems)
    count = rows.shape[0]
    half, part = count // 2, count // 4
    q, qx, qc, qd = me.quarter, me.x_quarter, me.core_quarter, me.far_quarter
    blocks = {step: me.block(step) for step in range(-4, 5)}
    low, high, whole = pl.ds(0, half), pl.ds(half, half), pl.ds(0, count)
    own, other, scale = range(3)
    full = (all_rows, all_cotangent)
    sides = ((RIGHT, me.right, -1, 0), (LEFT, me.left, 1, 1))
    greet([me.right, me.left, me.x_peer, me.core_peer, me.far_peer])

    def push(key, kind, step, quarter, which, peer, landing_step, landing_quarter, source=None):
        def cell():
            return full[kind].at[blocks[step], quarter, which]

        def landing():
            return full[kind].at[blocks[landing_step], landing_quarter, which]

        copies.send((kind,) + key, source or cell, cell, landing, peer)

    push((OVER_X, other, 0), 0, 0, q, low, me.x_peer, 0, qx, lambda: rows.at[low])
    for side, peer, sign, keep in sides:
        push((side, own, 1), 1, 0, q, whole, peer, sign, q, lambda: cotangent.at[q])
        push((side, other, 1), 1, 0, qx, low, peer, sign, qx, lambda: cotangent.at[qx, low])
    push((OVER_X, own, 0), 0, 0, q, high, me.x_peer, 0, qx, lambda: rows.at[high])
    push((OVER_CORE, own, 0), 0, 0, q, whole, me.core_peer, 0, qc, lambda: rows)
    for side, peer, sign, keep in sides:
        push((side, own, 1), 0, 0, q, whole, peer, sign, q, lambda: rows)
    copies.local((LOCAL, 0), lambda: rows, lambda: all_rows.at[blocks[0], q])
    copies.local((LOCAL, 1), lambda: cotangent, lambda: all_cotangent.at[blocks[0]])

    def scales_of(quarter):
        return lambda: all_scales.at[blocks[0], quarter]

    for way, peer, quarter in (
        (OVER_X, me.x_peer, qx),
        (OVER_CORE, me.core_peer, qc),
        (OVER_FAR, me.far_peer, qd),
    ):
        copies.send((way, scale, 0), lambda: scales, scales_of(q), scales_of(quarter), peer)
    copies.local((LOCAL, scale), lambda: scales, scales_of(q))
    experts, _, width, hidden_count = expert_in.shape
    padded = expert_both.shape[2] // 2
    all_slots = experts * slot_rows.shape[2]
    shared_count = shared.shape[1]
    gap = jnp.zeros((width, padded - hidden_count), expert_in.dtype)
    for expert in range(experts):
        for index in range(2):
            start = index * padded
            expert_both[expert, :, start : start + hidden_count] = expert_in[expert, index]
            expert_both[expert, :, start + hidden_count : start + padded] = gap
    out_terms[all_slots:, :] = shared[2]
    back_terms[all_slots : all_slots + shared_count, :] = shared[0]
    back_terms[all_slots + shared_count :, :] = shared[1]
    copies.arrive(0, OVER_X, other, 0)
    for side, peer, sign, keep in sides:
        push((side, other, 1), 0, 0, qx, low, peer, sign, qx)
    for way in (OVER_X, OVER_CORE, OVER_FAR):
        copies.arrive(way, scale, 0)
    copies.arrive(LOCAL, scale)

    def push_scales(step, side, peer, sign):
        def cell():
            return all_scales.at[blocks[step]]

        copies.send(
            (side, scale, abs(step) + 1), cell, cell, lambda: all_scales.at[blocks[step + sign]], peer
        )

    for side, peer, sign, keep in sides:
        push_scales(0, side, peer, sign)
    copies.arrive(0, OVER_X, own, 0)
    push((OVER_CORE, other, 0), 0, 0, qx, whole, me.core_peer, 0, qd)

    def hop_in(kind, hop):
        for side, peer, sign, keep in sides:
            step = sign * hop
            if hop < 4:
                copies.arrive(kind, side, own, hop)
                which = whole if hop < 3 else pl.ds(keep * half, half)
                push((side, own, hop + 1), kind, step, q, which, peer, step + sign, q)
                push((OVER_X, own, step), kind, step, q, high, me.x_peer, step, qx)
                push((OVER_CORE, own, step), kind, step, q, whole, me.core_peer, step, qc)
                copies.arrive(kind, side, other, hop)
                which = low if hop < 3 else pl.ds(keep * part, part)
                push((side, other, hop + 1), kind, step, qx, which, peer, step + sign, qx)
                push((OVER_CORE, other, step), kind, step, qx, low, me.core_peer, step, qd)
        if hop == 4:
            copies.arrive(kind, LEFT, own, 4)
            push((OVER_X, own, 4), kind, 4, q, high, me.x_peer, 4, qx)
            copies.arrive(kind, RIGHT, own, 4)
            push((OVER_CORE, own, 4), kind, 4, q, whole, me.core_peer, 4, qc)
            copies.arrive(kind, LEFT, other, 4)
            copies.arrive(kind, RIGHT, other, 4)
            push((OVER_CORE, other, 4), kind, 4, qx, low, me.core_peer, 4, qd)

    def over_x(kind, steps):
        for step in steps:
            copies.arrive(kind, OVER_X, own, step)
            push((OVER_CORE, scale, step), kind, step, qx, high, me.core_peer, step, qd)

    def scales_in(hop):
        for side, peer, sign, keep in sides:
            if hop < 4 or side == RIGHT:
                copies.arrive(side, scale, hop)
                if hop < 3 or (hop == 3 and side == RIGHT):
                    push_scales(sign * hop, side, peer, sign)

    def load(slot, step):
        pairs = ((all_rows, held_rows), (all_cotangent, held_cotangent))
        return [
            pltpu.make_async_copy(source.at[blocks[step]], held.at[slot], load_sems.at[slot, kind])
            for kind, (source, held) in enumerate(pairs)
        ]

    def complete(steps, slots):
        for step in steps:
            for kind in range(2):
                if step != 0:
                    for piece in (own, other, scale):
                        copies.arrive(kind, OVER_CORE, piece, step)
        moves = [load(slot, step) for slot, step in zip(slots, steps)]
        for move in moves[0] + moves[-1] if len(moves) > 1 else moves[0]:
            move.start()
        for move in moves[0]:
            move.wait()

    staged = (
        stage_out, stage_back, stage_rows, stage_cotangent, stage_pre, stage_gated, stage_shared,
        stage_scaled,
    )

    def stores(block):
        targets = (
            out_part.at[block], back_part.at[block], slot_rows.at[:, block],
            slot_cotangent.at[:, block], grad_pre.at[:, :, block], gated.at[:, block],
            grad_shared_pre.at[:, block], scaled.at[block],
        )
        return [
            pltpu.make_async_copy(stage, target, store_sems.at[index])
            for index, (stage, target) in enumerate(zip(staged, targets))
        ]

    first_expert = me.ep * experts

    copies.arrive(LOCAL, 0)
    copies.arrive(LOCAL, 1)
    for piece in (own, other):
        copies.arrive(0, OVER_CORE, piece, 0)
    complete((0,), (0,))

    def turn(index, carry):
        far = (index + 1) // 2
        step = far * (1 - 2 * (index % 2)) + (index // 7) * 8
        block = ring_member((me.place + step + RING) % RING)
        slot = index % 2

        def between():
            for hop in (1, 2, 3, 4):

                @pl.when(index == max(0, 2 * hop - 3))
                def _():
                    hop_in(1, hop)

            @pl.when(index > 0)
            def _():
                for move in stores(0):
                    move.wait()

        rows_here = held_rows[slot].reshape(4 * count, width)
        cotangent_here = held_cotangent[slot].reshape(4 * count, width)
        quarters = [all_scales[block, quarter] for quarter in range(4)]
        columns = jnp.concatenate([jnp.swapaxes(values, 0, 1) for values in quarters], axis=0)
        scale_at = me_scale_row(all_scales, experts)
        gate_rows = [
            jnp.concatenate(
                [all_scales[block, quarter, pl.ds(first_expert + e, 1), :] for quarter in range(4)],
                axis=1,
            )
            for e in range(experts)
        ]
        feed_block(
            block,
            rank_row[block],
            rank_column[block],
            jnp.concatenate(gate_rows, axis=0),
            columns[:, scale_at : scale_at + 1],
            rows_here,
            cotangent_here,
            expert_both,
            expert_down,
            shared,
            staged,
            between,
            out_terms,
            back_terms,
            scale_grad,
            token_grad,
        )
        for move in stores(block):
            move.start()

        for hop in (1, 2, 3, 4):

            @pl.when(index == max(0, 2 * hop - 3))
            def _():
                scales_in(hop)
                hop_in(0, hop)
                if hop > 1:
                    for move in load(0, hop - 1):
                        move.wait()

            @pl.when(index == 2 * hop - 2)
            def _():
                steps = (-hop, hop) if hop < 4 else (4,)
                over_x(1, steps)
                over_x(0, steps)
                complete(steps, (1, 0))

        return carry

    lax.fori_loop(0, RING, turn, 0)
    for move in stores(0):
        move.wait()
    copies.finish()


def me_scale_row(all_scales, experts):
    return RING * experts


def gather_feed(
    rows, cotangent, scales, rank, expert_in, expert_down, shared, capacity, collective_id
):
    bf16, f32 = jnp.bfloat16, jnp.float32
    blocks, experts, tokens = rank.shape
    count, width = rows.shape
    hidden = expert_in.shape[3]
    padded = -(-hidden // 128) * 128
    slice_hidden = shared.shape[1]
    shape = jax.ShapeDtypeStruct
    stages = (
        (tokens, width),
        (tokens, width),
        (experts, capacity, width),
        (experts, capacity, width),
        (2, experts, capacity, hidden),
        (experts, capacity, hidden),
        (2, tokens, slice_hidden),
        (tokens, slice_hidden),
    )
    return pl.pallas_call(
        gather_feed_kernel,
        out_shape=(
            shape((RING, 4, count, width), bf16),
            shape((RING, 4, count, width), bf16),
            shape((RING, 4) + scales.shape, f32),
            shape((blocks, tokens, width), bf16),
            shape((blocks, tokens, width), bf16),
            shape((experts, blocks, capacity, width), bf16),
            shape((experts, blocks, capacity, width), bf16),
            shape((2, experts, blocks, capacity, hidden), bf16),
            shape((experts, blocks, capacity, hidden), bf16),
            shape((2, blocks, tokens, slice_hidden), bf16),
            shape((blocks, tokens, slice_hidden), bf16),
            shape((blocks, experts, tokens), f32),
            shape((blocks, tokens, 1), f32),
        ),
        in_specs=[IN_VMEM] * 8,
        out_specs=(IN_PLACE,) * 2 + (IN_VMEM,) + (IN_PLACE,) * 8 + (IN_VMEM,) * 2,
        scratch_shapes=[
            pltpu.VMEM((experts, width, 2 * padded), bf16),
            pltpu.VMEM((experts * capacity + slice_hidden, width), bf16),
            pltpu.VMEM((experts * capacity + 2 * slice_hidden, width), bf16),
            pltpu.VMEM((2, 4, count, width), bf16),
            pltpu.VMEM((2, 4, count, width), bf16),
        ]
        + [pltpu.VMEM(stage, bf16) for stage in stages]
        + [pltpu.SemaphoreType.DMA((2, 2)), pltpu.SemaphoreType.DMA((len(stages),))]
        + semaphores(160),
        compiler_params=remote_params(collective_id, 62),
        name="gather_feed",
    )(
        rows, cotangent, scales, rank, jnp.swapaxes(rank, 1, 2), expert_in, expert_down, shared,
    )


def add_into(total, term, rows, tile=32):
    tile = min(tile, rows)

    def step(index, carry):
        here = pl.ds(pl.multiple_of(index * tile, tile), tile)
        summed = total[here, :].astype(jnp.float32) + term[here, :].astype(jnp.float32)
        total[here, :] = summed.astype(total.dtype)
        return carry

    lax.fori_loop(0, rows // tile, step, 0)


def scatter_kernel(
    part, scalars, out, out_scalars,
    held, core_in, x_in, ring_q, ring_x, last_in,
    s_held, s_core, s_x, s_ring,
    send_sems, recv_sems,
):
    me = Peers()
    copies = Copies(send_sems, recv_sems)
    count = part.shape[2]
    half, piece = count // 2, count // 4
    q, qx, qc, qd = me.quarter, me.x_quarter, me.core_quarter, me.far_quarter
    own, other, scale, last = range(4)
    peers = {RIGHT: me.right, LEFT: me.left}
    greet([me.right, me.left, me.x_peer, me.core_peer])
    order = (4, 3, 5, 2, 6, 1, 7, 0)
    for k in order:
        for slot, mine, theirs in ((0, q, qc), (1, qx, qd)):
            copies.local((LOCAL, k, slot), part.at[me.block(k), mine], held.at[k, slot])
            target = core_in.at[k, slot]
            copies.send(
                (OVER_CORE, k, slot), part.at[me.block(k), theirs], target, target, me.core_peer
            )
    for k in range(RING):
        for slot, mine, theirs in ((0, q, qc), (1, qx, qd)):
            copies.local((LOCAL, scale, k, slot), scalars.at[me.block(k), mine], s_held.at[slot, k])
            target = s_core.at[slot, k]
            copies.send(
                (OVER_CORE, scale, k, slot),
                scalars.at[me.block(k), theirs],
                target,
                target,
                me.core_peer,
            )

    def prepare(k):
        for slot in (1, 0):
            copies.arrive(LOCAL, k, slot)
            copies.arrive(OVER_CORE, k, slot)
            add_into(held.at[k, slot], core_in.at[k, slot], count)
            if slot == 1:
                source = held.at[k, 1, pl.ds(half, half)]
                copies.send((OVER_X, k), source, x_in.at[k], x_in.at[k], me.x_peer)

    def over_x(k):
        copies.arrive(OVER_X, k)
        add_into(held.at[k, 0, pl.ds(half, half)], x_in.at[k], half)

    def pass_on(side, hop, k):
        if hop == 0:
            rows_q, rows_x = pl.ds(side * half, half), pl.ds(side * piece, piece)
        else:
            rows_q, rows_x = pl.ds(0, count), pl.ds(0, half)
        for kind, landing, rows in ((own, ring_q, rows_q), (other, ring_x, rows_x)):
            target = landing.at[side, hop, rows]
            copies.send((side, kind, hop), held.at[k, kind].at[rows], target, target, peers[side])

    def take_in(side, hop, k):
        if hop == 0:
            span_q, span_x, at_q, at_x = half, piece, side * half, side * piece
        else:
            span_q, span_x, at_q, at_x = count, half, 0, 0
        for kind, landing, span, at in ((own, ring_q, span_q, at_q), (other, ring_x, span_x, at_x)):
            copies.arrive(side, kind, hop)
            rows = pl.ds(at, span)
            add_into(held.at[k, kind, rows], landing.at[side, hop, rows], span)

    def pass_scalars(side, hop, k):
        target = s_ring.at[side, hop]
        copies.send((side, scale, hop), s_held.at[0, k], target, target, peers[side])

    def take_scalars(side, hop, k):
        copies.arrive(side, scale, hop)
        s_held[0, k] += s_ring[side, hop]

    prepare(4)
    prepare(3)
    prepare(5)
    over_x(4)
    pass_on(RIGHT, 0, 4)
    pass_on(LEFT, 0, 4)
    prepare(2)
    prepare(6)
    for k in range(RING):
        for slot in (0, 1):
            copies.arrive(LOCAL, scale, k, slot)
            copies.arrive(OVER_CORE, scale, k, slot)
    s_held[...] += s_core[...]
    copies.send((OVER_X, scale, scale), s_held.at[1], s_x, s_x, me.x_peer)
    over_x(3)
    over_x(5)
    for hop, right_block, left_block, later in ((1, 3, 5, (1, 7)), (2, 2, 6, (0,)), (3, 1, 7, ())):
        take_in(RIGHT, hop - 1, right_block)
        pass_on(RIGHT, hop, right_block)
        take_in(LEFT, hop - 1, left_block)
        pass_on(LEFT, hop, left_block)
        if hop == 1:
            copies.arrive(OVER_X, scale, scale)
            s_held[0] += s_x[...]
            pass_scalars(RIGHT, 0, 4)
        else:
            take_scalars(RIGHT, hop - 2, right_block + 1)
            if hop == 3:
                take_scalars(LEFT, hop - 2, left_block - 1)
            pass_scalars(RIGHT, hop - 1, right_block + 1)
            pass_scalars(LEFT, hop - 1, left_block - 1)
        for k in later:
            prepare(k)
        if hop == 1:
            over_x(2)
            over_x(6)
        elif hop == 2:
            over_x(1)
            over_x(7)
    over_x(0)
    take_in(RIGHT, 3, 0)
    for side, k in ((RIGHT, 1), (LEFT, 7)):
        take_scalars(side, 2, k)
        pass_scalars(side, 3, k)
    take_in(LEFT, 3, 0)
    copies.send((OVER_X, last, last), held.at[0, 1, pl.ds(0, half)], last_in, last_in, me.x_peer)
    take_scalars(RIGHT, 3, 0)
    take_scalars(LEFT, 3, 0)
    out_scalars[...] = s_held[0, 0]
    out[pl.ds(half, half), :] = held[0, 0, pl.ds(half, half), :].astype(out.dtype)
    copies.arrive(OVER_X, last, last)
    out[pl.ds(0, half), :] = (
        held[0, 0, pl.ds(0, half), :].astype(jnp.float32) + last_in[...].astype(jnp.float32)
    ).astype(out.dtype)
    copies.finish()


def scatter_rows(part, scalars, collective_id):
    ring, quarters, count, width = part.shape
    half = count // 2
    dtype = part.dtype
    s_shape = scalars.shape[2:]
    return pl.pallas_call(
        scatter_kernel,
        out_shape=(
            jax.ShapeDtypeStruct((count, width), jnp.float32),
            jax.ShapeDtypeStruct(s_shape, jnp.float32),
        ),
        in_specs=[IN_PLACE] * 2,
        out_specs=(IN_VMEM,) * 2,
        scratch_shapes=[
            pltpu.VMEM((RING, 2, count, width), dtype),
            pltpu.VMEM((RING, 2, count, width), dtype),
            pltpu.VMEM((RING, half, width), dtype),
            pltpu.VMEM((2, 4, count, width), dtype),
            pltpu.VMEM((2, 4, half, width), dtype),
            pltpu.VMEM((half, width), dtype),
            pltpu.VMEM((2, RING) + s_shape, jnp.float32),
            pltpu.VMEM((2, RING) + s_shape, jnp.float32),
            pltpu.VMEM((RING,) + s_shape, jnp.float32),
            pltpu.VMEM((2, 4) + s_shape, jnp.float32),
        ]
        + semaphores(112),
        compiler_params=remote_params(collective_id),
        name="scatter_rows",
    )(part, scalars)


def spread_kernel(
    shard_in, shard_out, routes, full_in, full_out, full_routes, send_sems, recv_sems
):
    me = Peers()
    copies = Copies(send_sems, recv_sems)
    kinds, depth, _ = shard_in.shape
    rows, columns = shard_out.shape
    sides = ((RIGHT, me.right, -1), (LEFT, me.left, 1))
    greet([me.right, me.left])

    def cell(kind, step, part, parts):
        block = me.block(step)
        if kind < kinds:
            return full_in.at[kind, block, pl.ds(part * (depth // parts), depth // parts)]
        if kind > kinds:
            return full_routes.at[block]
        across = pl.ds(pl.multiple_of(block * columns, columns), columns)
        return full_out.at[pl.ds(part * (rows // parts), rows // parts), across]

    def pass_on(side, peer, sign, kind, hop, source=None):
        if kind > kinds and hop == 3 and side == LEFT:
            return
        parts = 2 if hop == 3 else 1
        part = side if hop == 3 else 0
        step = sign * hop
        here = cell(kind, step, part, parts)
        copies.send(
            (side, kind, hop + 1),
            here if source is None else source,
            here,
            cell(kind, step + sign, part, parts),
            peer,
        )

    order = (kinds + 1,) + tuple(range(kinds - 1, -1, -1)) + (kinds,)
    for kind in order:
        source = shard_in.at[kind] if kind < kinds else shard_out if kind == kinds else routes
        for side, peer, sign in sides:
            pass_on(side, peer, sign, kind, 0, source)
        copies.local((LOCAL, kind), source, cell(kind, 0, 0, 1))
    for hop in (1, 2, 3):
        for kind in order:
            for side, peer, sign in sides:
                copies.arrive(side, kind, hop)
                pass_on(side, peer, sign, kind, hop)
    copies.finish()


def spread_weights(shard_in, shard_out, routes, collective_id):
    kinds, depth, width = shard_in.shape
    rows, columns = shard_out.shape
    return pl.pallas_call(
        spread_kernel,
        out_shape=(
            jax.ShapeDtypeStruct((kinds, RING, depth, width), shard_in.dtype),
            jax.ShapeDtypeStruct((rows, RING * columns), shard_out.dtype),
            jax.ShapeDtypeStruct((RING,) + routes.shape, routes.dtype),
        ),
        in_specs=[IN_VMEM] * 3,
        out_specs=(IN_PLACE,) * 2 + (IN_VMEM,),
        scratch_shapes=semaphores(9 * (kinds + 2)),
        compiler_params=remote_params(collective_id),
        name="spread_weights",
    )(shard_in, shard_out, routes)


def collect_kernel(
    grad_in, grad_out, tail, sum_in, sum_out, sum_tail,
    held_in, held_out, ring_in, ring_out, tails, tail_sums,
    send_sems, recv_sems,
):
    me = Peers()
    copies = Copies(send_sems, recv_sems)
    kinds, _, depth, width = grad_in.shape
    rows, columns = sum_out.shape
    peers = {RIGHT: me.right, LEFT: me.left}
    tail_kind = kinds + 1
    greet([me.right, me.left, me.x_peer, me.core_peer, me.far_peer])
    order = (4, 3, 5, 2, 6, 1, 7, 0)

    def held(kind, k):
        return held_in.at[k, kind] if kind < kinds else held_out.at[k]

    def ring(kind, side, hop):
        return ring_in.at[side, hop, kind] if kind < kinds else ring_out.at[side, hop]

    def span(kind, side, hop):
        whole = depth if kind < kinds else rows
        return (side * (whole // 2), whole // 2) if hop == 0 else (0, whole)

    def pass_on(side, hop, k, kind):
        at = pl.ds(*span(kind, side, hop))
        target = ring(kind, side, hop).at[at]
        copies.send((side, kind, hop), held(kind, k).at[at], target, target, peers[side])

    def take_in(side, hop, k, kind):
        copies.arrive(side, kind, hop)
        start, size = span(kind, side, hop)
        at = pl.ds(start, size)
        add_into(held(kind, k).at[at], ring(kind, side, hop).at[at], size)

    tails[0] = tail[...]
    for side, place in ((RIGHT, 7), (LEFT, 1)):
        copies.send((side, tail_kind, 0), tail, tails.at[place], tails.at[place], peers[side])
    for k in order:
        block = me.block(k)
        for kind in range(kinds):
            copies.local((LOCAL, kind, k), grad_in.at[kind, block], held(kind, k))
        across = pl.ds(pl.multiple_of(block * columns, columns), columns)
        copies.local((LOCAL, kinds, k), grad_out.at[:, across], held(kinds, k))

    def ready(*blocks):
        for k in blocks:
            for kind in range(kinds + 1):
                copies.arrive(LOCAL, kind, k)

    ready(4)
    for kind in range(kinds + 1):
        for side in (RIGHT, LEFT):
            pass_on(side, 0, 4, kind)
    for hop, right_block, left_block in ((1, 3, 5), (2, 2, 6), (3, 1, 7)):
        ready(right_block, left_block)
        for kind in range(kinds + 1):
            for side, k in ((RIGHT, right_block), (LEFT, left_block)):
                take_in(side, hop - 1, k, kind)
                pass_on(side, hop, k, kind)
        for side, place, sign in ((RIGHT, 8 - hop, -1), (LEFT, hop, 1)):
            copies.arrive(side, tail_kind, hop - 1)
            if hop < 3 or side == RIGHT:
                target = tails.at[place + sign]
                copies.send((side, tail_kind, hop), tails.at[place], target, target, peers[side])
    copies.arrive(RIGHT, tail_kind, 3)
    total = tails[0]
    for place in range(1, RING):
        total = total + tails[place]
    tail_sums[me.tp] = total
    for way, peer, quarter in (
        (OVER_X, me.x_peer, me.x_quarter),
        (OVER_CORE, me.core_peer, me.core_quarter),
        (OVER_FAR, me.far_peer, me.far_quarter),
    ):
        copies.send(
            (way, tail_kind), tail_sums.at[me.tp], tail_sums.at[me.tp], tail_sums.at[quarter], peer
        )
    ready(0)
    for kind in range(kinds + 1):
        for side in (RIGHT, LEFT):
            take_in(side, 3, 0, kind)
    for kind in range(kinds):
        sum_in[kind] = held_in[0, kind].astype(jnp.float32)
    sum_out[...] = held_out[0].astype(jnp.float32)
    for way in (OVER_X, OVER_CORE, OVER_FAR):
        copies.arrive(way, tail_kind)
    sum_tail[...] = tail_sums[...]
    copies.finish()


def collect_weights(grad_in, grad_out, tail, collective_id):
    kinds, ring, depth, width = grad_in.shape
    rows, columns = grad_out.shape[0], grad_out.shape[1] // ring
    f32 = jnp.float32
    return pl.pallas_call(
        collect_kernel,
        out_shape=(
            jax.ShapeDtypeStruct((kinds, depth, width), f32),
            jax.ShapeDtypeStruct((rows, columns), f32),
            jax.ShapeDtypeStruct((4,) + tail.shape, f32),
        ),
        in_specs=[IN_PLACE, IN_PLACE, IN_VMEM],
        out_specs=(IN_VMEM,) * 3,
        scratch_shapes=[
            pltpu.VMEM((RING, kinds, depth, width), grad_in.dtype),
            pltpu.VMEM((RING, rows, columns), grad_out.dtype),
            pltpu.VMEM((2, 4, kinds, depth, width), grad_in.dtype),
            pltpu.VMEM((2, 4, rows, columns), grad_out.dtype),
            pltpu.VMEM((RING,) + tail.shape, f32),
            pltpu.VMEM((4,) + tail.shape, f32),
        ]
        + semaphores(96),
        compiler_params=remote_params(collective_id),
        name="collect_weights",
    )(grad_in, grad_out, tail)


def greet_along_z(me):
    barrier = pltpu.get_barrier_semaphore()
    pl.semaphore_signal(barrier, inc=1, device_id=me.y_peer, device_id_type=MESH_ID)

    @pl.when(me.z > 0)
    def _():
        peer = (me.ep - 2, me.tp)
        pl.semaphore_signal(barrier, inc=1, device_id=peer, device_id_type=MESH_ID)

    @pl.when(me.z < 3)
    def _():
        peer = (me.ep + 2, me.tp)
        pl.semaphore_signal(barrier, inc=1, device_id=peer, device_id_type=MESH_ID)

    pl.semaphore_wait(barrier, 1 + (me.z + 2) // 3 + (5 - me.z) // 3)


def share_kernel(own, out, send_sems, recv_sems):
    me = Peers()
    kinds, tokens, _ = own.shape
    pieces = 2
    size = tokens // pieces
    parts = [(kind, pl.ds(piece * size, size)) for kind in range(kinds) for piece in range(pieces)]
    count = len(parts)
    greet_along_z(me)

    def copy(index, source, target, peer):
        return Copies(send_sems, recv_sems).describe(source, target, peer, index)

    def upward(index, kind, rows):
        return copy(index, own.at[kind, rows], out.at[kind, 0, rows], (me.ep + 2, me.tp))

    def sideways(index, kind, rows):
        return copy(count + index, own.at[kind, rows], out.at[kind, 1, rows], me.y_peer)

    def onward(index, kind, rows):
        return copy(count + index, out.at[kind, 0, rows], out.at[kind, 1, rows], me.y_peer)

    @pl.when(me.z < 3)
    def _():
        for index, (kind, rows) in enumerate(parts):
            upward(index, kind, rows).start()

    @pl.when(me.y == 0)
    def _():
        for index, (kind, rows) in enumerate(parts):
            sideways(index, kind, rows).start()

    out[:, 2] = own[...]

    @pl.when(me.z == 0)
    def _():
        out[:, 0] = jnp.zeros_like(own)

    @pl.when((me.z == 0) & (me.y == 0))
    def _():
        out[:, 1] = jnp.zeros_like(own)

    @pl.when(me.z > 0)
    def _():
        for index, (kind, rows) in enumerate(parts):
            upward(index, kind, rows).wait_recv()

            @pl.when(me.y == 1)
            def _():
                onward(index, kind, rows).start()

    @pl.when(me.y == 1)
    def _():
        for index, (kind, rows) in enumerate(parts):
            sideways(index, kind, rows).wait_recv()

    @pl.when((me.y == 0) & (me.z > 0))
    def _():
        for index, (kind, rows) in enumerate(parts):
            onward(index, kind, rows).wait_recv()

    @pl.when(me.z < 3)
    def _():
        for index, (kind, rows) in enumerate(parts):
            upward(index, kind, rows).wait_send()

    @pl.when((me.y == 0) | (me.z > 0))
    def _():
        for index, (kind, rows) in enumerate(parts):
            sideways(index, kind, rows).wait_send()


def share_keys(own, collective_id):
    kinds, tokens, width = own.shape
    return pl.pallas_call(
        share_kernel,
        out_shape=jax.ShapeDtypeStruct((kinds, 3, tokens, width), own.dtype),
        in_specs=[IN_VMEM],
        out_specs=IN_VMEM,
        scratch_shapes=semaphores(8),
        compiler_params=remote_params(collective_id),
        name="share_keys",
    )(own)


def return_kernel(grads, cosine, sine, out, total, from_y, from_z, send_sems, recv_sems):
    me = Peers()
    kinds, _, tokens, _ = grads.shape
    pieces = 2
    size = tokens // pieces
    parts = [(kind, pl.ds(piece * size, size)) for kind in range(kinds) for piece in range(pieces)]
    count = len(parts)
    greet_along_z(me)

    def copy(index, source, target, peer):
        return Copies(send_sems, recv_sems).describe(source, target, peer, index)

    def sideways(index, kind, rows):
        return copy(index, grads.at[kind, 1, rows], from_y.at[kind, rows], me.y_peer)

    def downward(index, kind, rows, source):
        return copy(count + index, source.at[kind, rows], from_z.at[kind, rows], (me.ep - 2, me.tp))

    for index, (kind, rows) in enumerate(parts):
        sideways(index, kind, rows).start()

    @pl.when((me.z > 0) & (me.y == 0))
    def _():
        for index, (kind, rows) in enumerate(parts):
            downward(index, kind, rows, grads.at[:, 0]).start()

    for index, (kind, rows) in enumerate(parts):
        sideways(index, kind, rows).wait_recv()
        here = grads[kind, 2, rows, :].astype(jnp.float32)

        @pl.when(me.y == 0)
        def _():
            total[kind, rows, :] = here + from_y[kind, rows, :].astype(jnp.float32)

        @pl.when(me.y == 1)
        def _():
            total[kind, rows, :] = here
            two_back = grads[kind, 0, rows, :].astype(jnp.float32)
            summed = two_back + from_y[kind, rows, :].astype(jnp.float32)
            from_y[kind, rows, :] = summed.astype(from_y.dtype)

        @pl.when((me.z > 0) & (me.y == 1))
        def _():
            downward(index, kind, rows, from_y).start()

    @pl.when(me.z < 3)
    def _():
        for index, (kind, rows) in enumerate(parts):
            downward(index, kind, rows, from_y).wait_recv()
            total[kind, rows, :] += from_z[kind, rows, :].astype(jnp.float32)

    for start in range(0, total.shape[2], HD):
        head = slice(start, start + HD)
        out[0, :, head] = turned(total[0, :, head], cosine[...], -sine[...]).astype(out.dtype)
    out[1] = total[1].astype(out.dtype)
    for index, (kind, rows) in enumerate(parts):
        sideways(index, kind, rows).wait_send()

    @pl.when(me.z > 0)
    def _():
        for index, (kind, rows) in enumerate(parts):
            downward(index, kind, rows, from_y).wait_send()


def return_keys(grads, cosine, sine, collective_id):
    kinds, _, tokens, width = grads.shape
    return pl.pallas_call(
        return_kernel,
        out_shape=jax.ShapeDtypeStruct((kinds, tokens, width), grads.dtype),
        in_specs=[IN_VMEM] * 3,
        out_specs=IN_VMEM,
        scratch_shapes=[
            pltpu.VMEM((kinds, tokens, width), jnp.float32),
            pltpu.VMEM((kinds, tokens, width), grads.dtype),
            pltpu.VMEM((kinds, tokens, width), grads.dtype),
        ]
        + semaphores(8),
        compiler_params=remote_params(collective_id),
        name="return_keys",
    )(grads, cosine, sine)


def reduce_kernel(flip, left, right, out, core_out, core_in, x_out, x_in, send_sems, recv_sems):
    me = Peers()
    copies = Copies(send_sems, recv_sems)
    terms = left.shape[0]
    count = out.shape[0]
    f32 = jnp.float32
    greet([me.x_peer, me.core_peer])

    def quarter(index):
        rows = pl.ds(pl.multiple_of(index * count, count), count)
        total = None
        for term in range(terms):
            one = product(left[term, rows, :], right[term], NT if flip else NN)
            total = one if total is None else total + one
        return total

    for slot, index in ((1, me.far_quarter), (0, me.core_quarter)):
        core_out[slot] = quarter(index).astype(core_out.dtype)
        target = core_in.at[slot]
        copies.send((OVER_CORE, slot), core_out.at[slot], target, target, me.core_peer)
    mine = quarter(me.x_quarter)
    copies.arrive(OVER_CORE, 1)
    x_out[...] = (mine + core_in[1].astype(f32)).astype(x_out.dtype)
    copies.send((OVER_X,), x_out, x_in, x_in, me.x_peer)
    mine = quarter(me.quarter)
    copies.arrive(OVER_CORE, 0)
    out[...] = mine + core_in[0].astype(f32)
    copies.arrive(OVER_X)
    out[...] += x_in[...].astype(f32)
    copies.finish()


def product_to_owner(left, right, flip, collective_id):
    tokens = left.shape[1]
    width = right.shape[1] if flip else right.shape[2]
    count = tokens // 4
    bf16 = jnp.bfloat16
    return pl.pallas_call(
        functools.partial(reduce_kernel, flip),
        out_shape=jax.ShapeDtypeStruct((count, width), jnp.float32),
        in_specs=[IN_VMEM] * 2,
        out_specs=IN_VMEM,
        scratch_shapes=[
            pltpu.VMEM((2, count, width), bf16),
            pltpu.VMEM((2, count, width), bf16),
            pltpu.VMEM((count, width), bf16),
            pltpu.VMEM((count, width), bf16),
        ]
        + semaphores(3),
        compiler_params=remote_params(collective_id),
        name="product_to_owner",
    )(left, right)


def tensor_kernel(rows, out, send_sems, recv_sems):
    me = Peers()
    copies = Copies(send_sems, recv_sems)
    greet([me.x_peer, me.core_peer])
    mine = out.at[me.quarter]
    copies.send((OVER_X,), rows, mine, out.at[me.x_quarter], me.x_peer)
    copies.send((OVER_CORE, 0), rows, mine, out.at[me.core_quarter], me.core_peer)
    copies.local((LOCAL,), rows, mine)
    copies.arrive(OVER_X)
    beside = out.at[me.x_quarter]
    copies.send((OVER_CORE, 1), beside, beside, out.at[me.far_quarter], me.core_peer)
    copies.finish()


def tensor_gather(rows, collective_id):
    return pl.pallas_call(
        tensor_kernel,
        out_shape=jax.ShapeDtypeStruct((4,) + rows.shape, rows.dtype),
        in_specs=[IN_VMEM],
        out_specs=IN_PLACE,
        scratch_shapes=semaphores(4),
        compiler_params=remote_params(collective_id),
        name="tensor_gather",
    )(rows)


def own_rows(block, tp_index, count):
    return lax.dynamic_slice_in_dim(block, tp_index * count, count, 0)


def after(value, earlier):
    return lax.optimization_barrier((value, earlier))[0]


def per_device_dense(
    layer_input,
    attention_gain,
    attention_in,
    attention_bias,
    attention_out,
    feedforward_gain,
    shared_in,
    shared_down,
    shared_gate,
    router,
    expert_in,
    expert_down,
    routes,
    document_lengths,
    cotangent,
):
    bf16 = jnp.bfloat16
    f32 = jnp.float32
    both = (EP, TP)
    tok_count, model_width = layer_input.shape
    expert_count = router.shape[1]
    top_count = routes.shape[1]
    ep_size = lax.axis_size(EP)
    tp_size = lax.axis_size(TP)
    ep_index = lax.axis_index(EP)
    tp_index = lax.axis_index(TP)
    own_count = tok_count // tp_size
    all_count = tok_count * ep_size
    capacity = tp_size * (
        (5 * tok_count * top_count + 4 * expert_count * tp_size - 1) // (4 * expert_count * tp_size)
    )
    reach_back = min((WINDOW + tok_count - 2) // tok_count, ep_size - 1)
    local_experts = expert_in.shape[0]
    route_rows = jnp.concatenate(
        [routes.T, jnp.zeros((-top_count % 8, tok_count), routes.dtype)]
    )
    in_blocks, out_full, all_routes = spread_weights(attention_in, attention_out, route_rows, 0)
    in_full = in_blocks.reshape(3, model_width, -1)
    shard_width = shared_in.shape[1]
    slice_hidden = shared_in.shape[2] // ep_size
    shared_shards = jnp.concatenate([jnp.swapaxes(shared_in, 1, 2), shared_down[None]])
    shared_shards = jnp.swapaxes(
        shared_shards.reshape(3, ep_size, slice_hidden, shard_width), 0, 1
    )
    shared_slices = lax.all_to_all(
        after(shared_shards, in_blocks), EP, split_axis=0, concat_axis=0, tiled=True
    )
    shared_slices = jnp.transpose(shared_slices, (1, 2, 0, 3)).reshape(
        3, slice_hidden, model_width
    )
    my_ids = ep_index * local_experts + jnp.arange(local_experts, dtype=jnp.int32)
    taken = jnp.any(all_routes[:, None, :top_count] == my_ids[None, :, None, None], axis=2)
    earlier_mask = jnp.tril(jnp.ones((tok_count, tok_count), bf16), -1)
    rank = product(
        taken.astype(bf16).reshape(-1, tok_count), earlier_mask, NT
    ).astype(jnp.int32).reshape(taken.shape)
    rank = jnp.where(taken & (rank < capacity), rank, NO_SLOT)

    positions = ep_index * tok_count + jnp.arange(tok_count, dtype=jnp.int32)
    key_count = (reach_back + 1) * tok_count
    key_positions = (ep_index - reach_back) * tok_count + jnp.arange(key_count, dtype=jnp.int32)
    query_doc, rope_pos, valid_mask = doc_table(document_lengths, positions)
    query_doc = query_doc[:, None]
    key_doc = doc_table(document_lengths, key_positions)[0][None, :]
    valid_rows = valid_mask.astype(f32)[:, None]
    cosine, sine = (part[:, 0] for part in rope_angles(rope_pos, HD))
    cosine = jnp.concatenate([cosine, cosine], axis=1)
    sine = jnp.concatenate([-sine, sine], axis=1)
    normed_attention, queries, own_kv = project(
        layer_input, attention_gain, in_full, attention_bias, cosine, sine
    )
    keys_values = share_keys(own_kv, 1)
    heads_low, log_totals = attend(queries, keys_values, query_doc, key_doc, valid_rows)
    attention_sum = product_to_owner(heads_low[None], out_full[None], False, 2)
    input_rows = own_rows(layer_input, tp_index, own_count).astype(f32)
    residual = input_rows + attention_sum
    inverse_two, normed_two = rms_parts(residual)
    normed_ffn = normed_two * feedforward_gain
    normed_low = normed_ffn.astype(bf16)
    shared_scale = jax.nn.sigmoid(jnp.dot(normed_ffn, shared_gate, precision=HIGHEST))
    router_probs = jax.nn.softmax(jnp.dot(normed_ffn, router, precision=HIGHEST), axis=-1)
    routes_own = own_rows(routes, tp_index, own_count)
    expert_ids = jnp.arange(expert_count, dtype=jnp.int32)
    picked = jnp.any(routes_own[:, :, None] == expert_ids[None, None, :], axis=1)
    chosen = jnp.where(picked, router_probs, 0.0)
    chosen_total = jnp.sum(chosen, axis=1, keepdims=True)
    gates = chosen / chosen_total
    scale_count = -(-(expert_count + 1) // 8) * 8
    spare = jnp.zeros((scale_count - expert_count - 1, own_count), f32)
    scale_rows = jnp.concatenate([gates.T, shared_scale[None], spare])
    (
        all_rows,
        all_cotangent,
        all_scales,
        ffn_part,
        back_part,
        slot_rows,
        slot_cotangent,
        grad_pre,
        gated,
        grad_shared_pre,
        scaled_hidden,
        token_grad,
        scale_grad,
    ) = gather_feed(
        normed_low,
        cotangent.reshape(tp_size, own_count, model_width),
        scale_rows,
        rank,
        expert_in,
        expert_down,
        shared_slices,
        capacity,
        3,
    )
    ffn_sum = lax.psum_scatter(
        ffn_part.reshape(all_count, model_width), both, scatter_dimension=0, tiled=True
    )
    layer_output = lax.all_gather(
        (residual + ffn_sum.astype(f32)).astype(bf16), TP, axis=0, tiled=True
    )
    spare = jnp.zeros((ep_size, scale_count - expert_count - 1, tok_count), f32)
    scalar_part = jnp.concatenate(
        [jnp.zeros((ep_size, expert_count, tok_count), f32), scale_grad[:, None, :, 0], spare], axis=1
    )
    scalar_part = lax.dynamic_update_slice(
        scalar_part, token_grad, (0, ep_index * local_experts, 0)
    )
    scalar_part = jnp.swapaxes(
        scalar_part.reshape(ep_size, scale_count, tp_size, own_count), 1, 2
    )
    back_sum, scalar_sum = scatter_rows(
        back_part.reshape(ep_size, tp_size, own_count, model_width), scalar_part, 4
    )
    scalar_sum = scalar_sum.T
    slot_rows = slot_rows.reshape(local_experts, -1, model_width)
    slot_cotangent = slot_cotangent.reshape(slot_rows.shape)
    grad_pre = grad_pre.reshape(2, local_experts, slot_rows.shape[1], -1)
    gated = gated.reshape(local_experts, slot_rows.shape[1], -1)
    grad_expert_down = jnp.einsum(
        "erf,erd->efd", gated, slot_cotangent, preferred_element_type=f32
    )
    grad_expert_in = jnp.einsum(
        "erd,serf->esdf", slot_rows, grad_pre, preferred_element_type=f32
    )
    flat_rows = all_rows.reshape(all_count, model_width)
    flat_cotangent = all_cotangent.reshape(all_count, model_width)
    shared_grads = [
        product(flat_rows, grad_shared_pre[0].reshape(all_count, -1), TN),
        product(flat_rows, grad_shared_pre[1].reshape(all_count, -1), TN),
        product(flat_cotangent, scaled_hidden.reshape(all_count, -1), TN),
    ]
    shared_grads = jnp.stack([grad.astype(bf16) for grad in shared_grads])
    shared_grads = jnp.transpose(
        shared_grads.reshape(3, ep_size, shard_width, slice_hidden), (1, 0, 3, 2)
    )
    shared_grads = lax.all_to_all(shared_grads, EP, split_axis=0, concat_axis=0, tiled=True)
    shared_grads = (
        jnp.swapaxes(shared_grads, 0, 1).reshape(3, -1, shard_width).astype(f32)
    )
    grad_shared_in = jnp.swapaxes(shared_grads[:2], 1, 2)
    grad_shared_down = shared_grads[2]

    grad_gates = scalar_sum[:, :expert_count]
    grad_probs = jnp.where(
        picked,
        (grad_gates - jnp.sum(grad_gates * gates, axis=1, keepdims=True)) / chosen_total,
        0.0,
    )
    grad_logits = router_probs * (
        grad_probs - jnp.sum(grad_probs * router_probs, axis=1, keepdims=True)
    )
    grad_router = jnp.einsum("td,te->de", normed_ffn, grad_logits, precision=HIGHEST)
    grad_scale_pre = scalar_sum[:, expert_count] * shared_scale * (1.0 - shared_scale)
    grad_shared_gate = jnp.dot(grad_scale_pre, normed_ffn, precision=HIGHEST)
    grad_normed = (
        back_sum
        + jnp.einsum("te,de->td", grad_logits, router, precision=HIGHEST)
        + grad_scale_pre[:, None] * shared_gate[None, :]
    )
    grad_mid_norm, grad_feedforward_gain = norm_back(
        grad_normed, feedforward_gain, inverse_two, normed_two
    )
    small = jnp.concatenate([grad_feedforward_gain[None], grad_shared_gate[None], grad_router.T])
    small = lax.psum(small, both)
    grad_residual = own_rows(cotangent, tp_index, own_count).astype(f32) + grad_mid_norm
    grad_attention = tensor_gather(grad_residual.astype(bf16), 5).reshape(tok_count, model_width)
    grad_attention_out = product(heads_low, grad_attention, TN)
    grad_heads = (product(grad_attention, out_full, NT) * valid_rows).astype(bf16)
    grad_queries, grad_kv = attend_back(
        queries, keys_values, query_doc, key_doc, log_totals, grad_heads, cosine, sine
    )
    grad_own_kv = return_keys(grad_kv, cosine, sine, 6)
    grad_raw = jnp.concatenate([grad_queries[None], grad_own_kv])
    grad_attention_bias = jnp.sum(grad_raw.astype(f32), axis=1)
    grad_normed_attention = product_to_owner(grad_raw, in_full, True, 7)
    inverse_one, normed_one = rms_parts(input_rows)
    grad_in_norm, grad_attention_gain = norm_back(
        grad_normed_attention, attention_gain, inverse_one, normed_one
    )
    grad_input = tensor_gather((grad_residual + grad_in_norm).astype(bf16), 8)
    grad_attention_in = jnp.einsum(
        "td,ste->sde", normed_attention, grad_raw, preferred_element_type=f32
    )
    columns = grad_attention_bias.shape[1]
    tail = jnp.concatenate(
        [
            grad_attention_bias,
            grad_attention_gain.reshape(-1, columns),
            jnp.zeros((8 - 3 - model_width // columns, columns), f32),
        ]
    )
    grad_attention_in, grad_attention_out, tails = collect_weights(
        grad_attention_in.astype(bf16).reshape(in_blocks.shape),
        grad_attention_out.astype(bf16),
        tail,
        9,
    )
    grad_attention_bias = lax.dynamic_index_in_dim(tails, tp_index, 0, keepdims=False)[:3]
    grad_attention_gain = jnp.sum(tails[:, 3:], axis=0)[: model_width // columns].reshape(-1)
    return (
        layer_output,
        grad_input.reshape(tok_count, model_width),
        grad_attention_gain,
        grad_attention_in,
        grad_attention_bias,
        grad_attention_out,
        small[0],
        grad_shared_in,
        grad_shared_down,
        small[1],
        small[2:].T,
        grad_expert_in,
        grad_expert_down,
    )


def per_device(*arguments):
    small_slice = lax.axis_size(EP) == RING and lax.axis_size(TP) == 4
    return (per_device_dense if small_slice else per_device_sparse)(*arguments)


def per_device_sparse(
    layer_input,
    attention_gain,
    attention_in,
    attention_bias,
    attention_out,
    feedforward_gain,
    shared_in,
    shared_down,
    shared_gate,
    router,
    expert_in,
    expert_down,
    routes,
    document_lengths,
    cotangent,
):
    bf16 = jnp.bfloat16
    f32 = jnp.float32
    tok_count = layer_input.shape[0]
    model_width = layer_input.shape[1]
    expert_count = router.shape[1]
    top_count = routes.shape[1]
    ep_size = lax.axis_size(EP)
    tp_size = lax.axis_size(TP)
    capacity = tp_size * (
        (5 * tok_count * top_count + 4 * expert_count * tp_size - 1) // (4 * expert_count * tp_size)
    )
    reach_back = min((WINDOW + tok_count - 2) // tok_count, ep_size - 1)
    head_dim = HD
    local_heads = attention_in.shape[2] // head_dim
    score_scale = 1.0 / math.sqrt(head_dim)
    in_full, out_full, shared_in_full, shared_down_full = (
        lax.all_gather(attention_in, EP, axis=1, tiled=True),
        lax.all_gather(attention_out, EP, axis=1, tiled=True),
        lax.all_gather(shared_in, EP, axis=1, tiled=True),
        lax.all_gather(shared_down, EP, axis=1, tiled=True),
    )
    ep_index = lax.axis_index(EP)
    positions = ep_index * tok_count + jnp.arange(tok_count, dtype=jnp.int32)
    key_count = (reach_back + 1) * tok_count
    key_positions = (ep_index - reach_back) * tok_count + jnp.arange(key_count, dtype=jnp.int32)
    query_doc, rope_pos, valid_mask = doc_table(document_lengths, positions)
    key_doc = doc_table(document_lengths, key_positions)[0]
    distance = positions[:, None] - key_positions[None, :]
    allowed = (query_doc[:, None] == key_doc[None, :]) & (distance >= 0) & (distance < WINDOW)
    valid_rows = valid_mask.astype(f32)[:, None]
    cosine, sine_part = rope_angles(rope_pos, head_dim)
    input_rows = layer_input.astype(f32)
    inverse_one, normed_one = rms_parts(input_rows)
    normed_attention = (normed_one * attention_gain).astype(bf16)
    raw_proj = (
        jnp.einsum("td,sde->ste", normed_attention, in_full, preferred_element_type=f32)
        + attention_bias[:, None, :]
    )
    queries = rotate(
        raw_proj[0].reshape(tok_count, local_heads, head_dim), cosine, sine_part, 1.0
    ).astype(bf16)
    keys_own = rotate(
        raw_proj[1].reshape(tok_count, local_heads, head_dim), cosine, sine_part, 1.0
    ).astype(bf16)
    values_own = raw_proj[2].reshape(tok_count, local_heads, head_dim).astype(bf16)
    key_value = jnp.stack([keys_own, values_own])
    earlier = []
    for hop_count in range(reach_back, 0, -1):
        earlier.append(shifted(key_value, EP, hop_count))
    all_kv = jnp.concatenate(earlier + [key_value], axis=1)
    all_keys = all_kv[0]
    all_values = all_kv[1]
    scores = jnp.einsum("qhe,khe->hqk", queries, all_keys, preferred_element_type=f32) * score_scale
    scores = jnp.where(allowed[None], scores, MASKED)
    row_max = jnp.max(scores, axis=-1, keepdims=True)
    exp_terms = jnp.exp(scores - row_max)
    row_total = jnp.sum(exp_terms, axis=-1, keepdims=True)
    log_total = row_max + jnp.log(row_total)
    weights = (exp_terms / row_total).astype(bf16)
    heads_out = jnp.einsum("hqk,khe->qhe", weights, all_values, preferred_element_type=f32).reshape(
        tok_count, -1
    )
    heads_low = (heads_out * valid_rows).astype(bf16)
    attention_sum = tensor_total(jnp.dot(heads_low, out_full, preferred_element_type=f32))
    residual = input_rows + attention_sum
    inverse_two, normed_two = rms_parts(residual)
    normed_ffn = normed_two * feedforward_gain
    normed_low = normed_ffn.astype(bf16)
    shared_pre = jnp.einsum("td,sdf->stf", normed_low, shared_in_full, preferred_element_type=f32)
    shared_silu, shared_slope = silu_parts(shared_pre[0])
    shared_hidden = (shared_silu * shared_pre[1]).astype(bf16)
    shared_out = tensor_total(jnp.dot(shared_hidden, shared_down_full, preferred_element_type=f32))
    shared_scale = jax.nn.sigmoid(jnp.dot(normed_ffn, shared_gate, precision=HIGHEST))
    router_probs = jax.nn.softmax(jnp.dot(normed_ffn, router, precision=HIGHEST), axis=-1)
    chosen = jnp.take_along_axis(router_probs, routes, axis=1)
    chosen_total = jnp.sum(chosen, axis=1, keepdims=True)
    gate_values = chosen / chosen_total
    assign_count = tok_count * top_count
    flat_routes = routes.reshape(-1)
    expert_ids = jnp.arange(expert_count, dtype=jnp.int32)
    one_hot = (flat_routes[:, None] == expert_ids[None, :]).astype(jnp.int32)
    arrival_rank = jnp.sum((jnp.cumsum(one_hot, axis=0) - one_hot) * one_hot, axis=1)
    slot_count = expert_count * capacity
    slot_index = jnp.where(
        arrival_rank < capacity, flat_routes * capacity + arrival_rank, slot_count
    )
    slot_assign = (
        jnp.full((slot_count + 1,), assign_count, jnp.int32)
        .at[slot_index]
        .set(jnp.arange(assign_count, dtype=jnp.int32))[:slot_count]
    )
    slot_token = slot_assign // top_count
    padded_rows = jnp.concatenate([normed_low, jnp.zeros((1, model_width), bf16)])
    send_rows = padded_rows[slot_token].reshape(expert_count, capacity, model_width)

    def expert_trip(outgoing, work):
        row_block = lax.all_to_all(outgoing, EP, split_axis=0, concat_axis=1, tiled=True)
        partial_rows, extras = work(row_block)
        share_rows = lax.psum_scatter(partial_rows, TP, scatter_dimension=1, tiled=True).astype(
            bf16
        )
        whole_rows = lax.all_gather(share_rows, TP, axis=1, tiled=True)
        return (lax.all_to_all(whole_rows, EP, split_axis=1, concat_axis=0, tiled=True), extras)

    def expert_forward(row_block):
        pre_acts = jnp.einsum("erd,esdf->serf", row_block, expert_in, preferred_element_type=f32)
        gate_silu, gate_slope = silu_parts(pre_acts[0])
        hidden = (gate_silu * pre_acts[1]).astype(bf16)
        partial_rows = jnp.einsum("erf,efd->erd", hidden, expert_down, preferred_element_type=f32)
        return (partial_rows, (row_block, pre_acts, hidden, gate_silu, gate_slope))

    returned_rows, kept_state = expert_trip(send_rows, expert_forward)
    expert_rows, expert_pre, expert_hidden, expert_silu, expert_slope = kept_state
    padded_back = jnp.concatenate(
        [returned_rows.reshape(slot_count, model_width), jnp.zeros((1, model_width), bf16)]
    )
    picked = padded_back[slot_index].reshape(tok_count, top_count, model_width).astype(f32)
    moe_sum = jnp.sum(gate_values[:, :, None] * picked, axis=1)
    layer_output = (residual + shared_scale[:, None] * shared_out + moe_sum).astype(bf16)
    grad_rows = cotangent.astype(f32)
    padded_grad = jnp.concatenate([grad_rows, jnp.zeros((1, model_width), f32)])
    padded_gates = jnp.concatenate([gate_values.reshape(-1), jnp.zeros((1,), f32)])
    grad_send = (padded_gates[slot_assign][:, None] * padded_grad[slot_token]).astype(bf16)
    grad_send = grad_send.reshape(expert_count, capacity, model_width)

    def expert_backward(grad_block):
        grad_down = jnp.einsum(
            "erf,erd->efd", expert_hidden, grad_block, preferred_element_type=f32
        )
        grad_hidden = jnp.einsum(
            "erd,efd->erf", grad_block, expert_down, preferred_element_type=f32
        )
        grad_pre = jnp.stack(
            [grad_hidden * expert_pre[1] * expert_slope, grad_hidden * expert_silu]
        ).astype(bf16)
        grad_weights_in = jnp.einsum(
            "erd,serf->esdf", expert_rows, grad_pre, preferred_element_type=f32
        )
        grad_back_rows = jnp.einsum(
            "serf,esdf->erd", grad_pre, expert_in, preferred_element_type=f32
        )
        return (grad_back_rows, (grad_weights_in, grad_down))

    grad_returned, expert_grads = expert_trip(grad_send, expert_backward)
    grad_expert_in, grad_expert_down = expert_grads
    grad_gate_values = jnp.sum(picked * grad_rows[:, None, :], axis=2)
    grad_chosen = (
        grad_gate_values - jnp.sum(grad_gate_values * gate_values, axis=1, keepdims=True)
    ) / chosen_total
    grad_probs = jnp.sum(
        jnp.where(routes[:, :, None] == expert_ids[None, None, :], grad_chosen[:, :, None], 0.0),
        axis=1,
    )
    grad_logits = router_probs * (
        grad_probs - jnp.sum(grad_probs * router_probs, axis=1, keepdims=True)
    )
    grad_router = jnp.einsum("td,te->de", normed_ffn, grad_logits, precision=HIGHEST)
    grad_shared_out = (shared_scale[:, None] * grad_rows).astype(bf16)
    grad_shared_down = jnp.einsum(
        "tf,td->fd", shared_hidden, grad_shared_out, preferred_element_type=f32
    )
    grad_shared_hidden = jnp.einsum(
        "td,fd->tf", grad_shared_out, shared_down_full, preferred_element_type=f32
    )
    grad_shared_pre = jnp.stack(
        [grad_shared_hidden * shared_pre[1] * shared_slope, grad_shared_hidden * shared_silu]
    ).astype(bf16)
    grad_shared_in = jnp.einsum(
        "td,stf->sdf", normed_low, grad_shared_pre, preferred_element_type=f32
    )
    shared_back = jnp.einsum(
        "stf,sdf->td", grad_shared_pre, shared_in_full, preferred_element_type=f32
    )
    grad_scale_pre = jnp.sum(grad_rows * shared_out, axis=1) * shared_scale * (1.0 - shared_scale)
    grad_shared_gate = jnp.dot(grad_scale_pre, normed_ffn, precision=HIGHEST)
    padded_return = jnp.concatenate(
        [grad_returned.reshape(slot_count, model_width), jnp.zeros((1, model_width), bf16)]
    )
    moe_back = jnp.sum(
        padded_return[slot_index].reshape(tok_count, top_count, model_width).astype(f32), axis=1
    )
    grad_normed = (
        tensor_total(shared_back)
        + moe_back
        + jnp.einsum("te,de->td", grad_logits, router, precision=HIGHEST)
        + grad_scale_pre[:, None] * shared_gate[None, :]
    )
    grad_mid_norm, grad_feedforward_gain = norm_back(
        grad_normed, feedforward_gain, inverse_two, normed_two
    )
    grad_residual = grad_rows + grad_mid_norm
    grad_attention = grad_residual.astype(bf16)
    grad_attention_out = jnp.einsum(
        "tf,td->fd", heads_low, grad_attention, preferred_element_type=f32
    )
    grad_heads = jnp.einsum(
        "td,fd->tf", grad_attention, out_full, preferred_element_type=f32
    ).astype(bf16)
    grad_heads = (grad_heads * valid_rows.astype(bf16)).reshape(tok_count, local_heads, head_dim)
    scores_again = (
        jnp.einsum("qhe,khe->hqk", queries, all_keys, preferred_element_type=f32) * score_scale
    )
    scores_again = jnp.where(allowed[None], scores_again, MASKED)
    softmax_out = jnp.exp(scores_again - log_total)
    weights_again = softmax_out.astype(bf16)
    grad_weights = jnp.einsum("qhe,khe->hqk", grad_heads, all_values, preferred_element_type=f32)
    grad_scores = (
        softmax_out * (grad_weights - jnp.sum(softmax_out * grad_weights, axis=-1, keepdims=True))
    ).astype(bf16)
    grad_queries = (
        jnp.einsum("hqk,khe->qhe", grad_scores, all_keys, preferred_element_type=f32) * score_scale
    )
    grad_keys = (
        jnp.einsum("hqk,qhe->khe", grad_scores, queries, preferred_element_type=f32) * score_scale
    )
    grad_values = jnp.einsum("hqk,qhe->khe", weights_again, grad_heads, preferred_element_type=f32)
    grad_kv = jnp.stack([grad_keys, grad_values])
    own_part = grad_kv[:, reach_back * tok_count :]
    for hop_count in range(1, reach_back + 1):
        segment_start = (reach_back - hop_count) * tok_count
        segment = grad_kv[:, segment_start : segment_start + tok_count]
        own_part = own_part + shifted(segment, EP, -hop_count)
    grad_raw = (
        jnp.stack(
            [
                rotate(grad_queries, cosine, sine_part, -1.0),
                rotate(own_part[0], cosine, sine_part, -1.0),
                own_part[1],
            ]
        )
        .reshape(3, tok_count, -1)
        .astype(bf16)
    )
    grad_attention_bias = jnp.sum(grad_raw.astype(f32), axis=1)
    grad_attention_in = jnp.einsum(
        "td,ste->sde", normed_attention, grad_raw, preferred_element_type=f32
    )
    grad_normed_attention = tensor_total(
        jnp.einsum("ste,sde->td", grad_raw, in_full, preferred_element_type=f32)
    )
    grad_in_norm, grad_attention_gain = norm_back(
        grad_normed_attention, attention_gain, inverse_one, normed_one
    )
    grad_input = (grad_residual + grad_in_norm).astype(bf16)
    grad_attention_in, grad_attention_out, grad_shared_in, grad_shared_down = (
        lax.psum_scatter(
            grad_attention_in.astype(jnp.bfloat16), EP, scatter_dimension=1, tiled=True
        ).astype(jnp.float32),
        lax.psum_scatter(
            grad_attention_out.astype(jnp.bfloat16), EP, scatter_dimension=1, tiled=True
        ).astype(jnp.float32),
        lax.psum_scatter(
            grad_shared_in.astype(jnp.bfloat16), EP, scatter_dimension=1, tiled=True
        ).astype(jnp.float32),
        lax.psum_scatter(
            grad_shared_down.astype(jnp.bfloat16), EP, scatter_dimension=1, tiled=True
        ).astype(jnp.float32),
    )
    (
        grad_attention_gain,
        grad_attention_bias,
        grad_feedforward_gain,
        grad_shared_gate,
        grad_router,
    ) = (
        lax.psum(grad_attention_gain.astype(jnp.bfloat16), EP).astype(jnp.float32),
        lax.psum(grad_attention_bias.astype(jnp.bfloat16), EP).astype(jnp.float32),
        lax.psum(grad_feedforward_gain.astype(jnp.bfloat16), EP).astype(jnp.float32),
        lax.psum(grad_shared_gate.astype(jnp.bfloat16), EP).astype(jnp.float32),
        lax.psum(grad_router.astype(jnp.bfloat16), EP).astype(jnp.float32),
    )
    return (
        layer_output,
        grad_input,
        grad_attention_gain,
        grad_attention_in,
        grad_attention_bias,
        grad_attention_out,
        grad_feedforward_gain,
        grad_shared_in,
        grad_shared_down,
        grad_shared_gate,
        grad_router,
        grad_expert_in,
        grad_expert_down,
    )


def solution(mesh):
    return jax.shard_map(
        per_device,
        mesh=mesh,
        in_specs=(
            P(EP, None),
            P(),
            P(None, EP, TP),
            P(None, TP),
            P(TP, EP),
            P(),
            P(None, EP, TP),
            P(TP, EP),
            P(),
            P(),
            P(EP, None, None, TP),
            P(EP, TP, None),
            P(EP, None),
            P(),
            P(EP, None),
        ),
        out_specs=(
            P(EP, None),
            P(EP, None),
            P(),
            P(None, EP, TP),
            P(None, TP),
            P(TP, EP),
            P(),
            P(None, EP, TP),
            P(TP, EP),
            P(),
            P(),
            P(EP, None, None, TP),
            P(EP, TP, None),
        ),
        check_vma=False,
    )
```

```python
import functools
import math

import jax
import jax.numpy as jnp
from jax import lax
from jax.experimental import pallas as pl
from jax.experimental.pallas import tpu as pltpu
from jax.sharding import PartitionSpec as P

EP, TP = "ep", "tp"
HD = 128
WINDOW = 1024


HIGHEST = lax.Precision.HIGHEST
EPSILON = 1e-06
ROPE_BASE = 1000000.0
MASKED = -1000000000.0


def shifted(value, axis, steps):
    count = lax.axis_size(axis)
    leading, last = (max(0, -steps), min(count, count - steps))
    return lax.ppermute(value, axis, [(source, source + steps) for source in range(leading, last)])


def tensor_total(partial_sum):
    return lax.psum(partial_sum, TP)


def rms_parts(values):
    inverse = lax.rsqrt(jnp.mean(values * values, axis=-1, keepdims=True) + EPSILON)
    return (inverse, values * inverse)


def norm_back(grad_rows, gain_vec, inverse, normed):
    scaled = grad_rows * gain_vec
    grad_in = inverse * (scaled - normed * jnp.mean(scaled * normed, axis=-1, keepdims=True))
    return (grad_in, jnp.sum(grad_rows * normed, axis=0))


def doc_table(document_lengths, positions):
    doc_ends = jnp.cumsum(document_lengths)
    starts_all = jnp.concatenate([doc_ends - document_lengths, doc_ends[-1:]])
    doc_ids = jnp.sum((positions[:, None] >= doc_ends[None, :]).astype(jnp.int32), axis=1)
    matches = (
        doc_ids[:, None] == jnp.arange(document_lengths.shape[0] + 1, dtype=jnp.int32)[None, :]
    )
    doc_begin = jnp.sum(jnp.where(matches, starts_all[None, :], 0), axis=1)
    rope_pos = positions - doc_begin
    valid_mask = positions < doc_ends[-1]
    doc_ids = jnp.where(positions < 0, -1, doc_ids)
    return (doc_ids, rope_pos, valid_mask)


def rope_angles(rope_pos, head_dim):
    half_width = head_dim // 2
    freqs = jnp.power(ROPE_BASE, -2.0 * jnp.arange(half_width, dtype=jnp.float32) / head_dim)
    angles = rope_pos.astype(jnp.float32)[:, None] * freqs[None, :]
    return (jnp.cos(angles)[:, None, :], jnp.sin(angles)[:, None, :])


def rotate(values, cosine, sine_part, turn_sign):
    half_width = values.shape[-1] // 2
    first_part = values[..., :half_width]
    second_part = values[..., half_width:]
    return jnp.concatenate(
        [
            first_part * cosine - turn_sign * second_part * sine_part,
            second_part * cosine + turn_sign * first_part * sine_part,
        ],
        axis=-1,
    )


def silu_parts(gate_pre):
    sig_gate = jax.nn.sigmoid(gate_pre)
    return (gate_pre * sig_gate, sig_gate * (1.0 + gate_pre * (1.0 - sig_gate)))


NN = (((1,), (0,)), ((), ()))
NT = (((1,), (1,)), ((), ()))
TN = (((0,), (0,)), ((), ()))


def product(left, right, dims=NN):
    return lax.dot_general(left, right, dims, preferred_element_type=jnp.float32)


def turned(values, cosine, sine):
    half = values.shape[1] // 2
    swapped = jnp.concatenate([values[:, half:], values[:, :half]], axis=1)
    return values * cosine + swapped * sine


def project_kernel(rows, gain, weights, bias, cosine, sine, normed, queries, keys_values):
    bf16, f32 = jnp.bfloat16, jnp.float32

    @pl.when(pl.program_id(0) == 0)
    def _():
        _, scaled = rms_parts(rows[...].astype(f32))
        normed[...] = (scaled * gain[...]).astype(bf16)

    columns = queries.shape[1]
    for kind in range(3):
        raw = product(normed[...], weights[kind]) + bias[kind : kind + 1, :]
        for start in range(0, columns, HD):
            head = slice(start, start + HD)
            part = raw[:, head]
            if kind < 2:
                part = turned(part, cosine[...], sine[...])
            if kind == 0:
                queries[:, head] = part.astype(bf16)
            else:
                keys_values[kind - 1, :, head] = part.astype(bf16)


def project(rows, gain, weights, bias, cosine, sine):
    tokens, width = rows.shape
    columns = weights.shape[2]
    step = min(2 * HD, columns)
    shape = jax.ShapeDtypeStruct
    bf16 = jnp.bfloat16

    def whole(*dims):
        return pl.BlockSpec(dims, lambda h: (0,) * len(dims))

    return pl.pallas_call(
        project_kernel,
        grid=(columns // step,),
        in_specs=[
            whole(tokens, width),
            whole(1, width),
            pl.BlockSpec((3, width, step), lambda h: (0, 0, h)),
            pl.BlockSpec((3, step), lambda h: (0, h)),
            whole(tokens, HD),
            whole(tokens, HD),
        ],
        out_specs=(
            whole(tokens, width),
            pl.BlockSpec((tokens, step), lambda h: (0, h)),
            pl.BlockSpec((2, tokens, step), lambda h: (0, 0, h)),
        ),
        out_shape=(
            shape((tokens, width), bf16),
            shape((tokens, columns), bf16),
            shape((2, tokens, columns), bf16),
        ),
        compiler_params=pltpu.CompilerParams(vmem_limit_bytes=40 * 2**20),
        name="project",
    )(rows, gain[None], weights, bias, cosine, sine)


def masked_scores(queries, keys, query_doc, key_doc):
    tokens, count = queries.shape[0], keys.shape[0]
    scores = product(queries, keys, NT) * (1.0 / math.sqrt(HD))
    ahead = lax.broadcasted_iota(jnp.int32, (tokens, count), 0) + (count - tokens)
    distance = ahead - lax.broadcasted_iota(jnp.int32, (tokens, count), 1)
    allowed = (query_doc == key_doc) & (distance >= 0) & (distance < WINDOW)
    return jnp.where(allowed, scores, MASKED)


def attend_kernel(queries, keys, values, query_doc, key_doc, valid, heads, log_totals):
    count = keys.shape[1] * keys.shape[2]
    keys, values = keys[0].reshape(count, HD), values[0].reshape(count, HD)
    scores = masked_scores(queries[...], keys, query_doc[...], key_doc[...])
    row_max = jnp.max(scores, axis=1, keepdims=True)
    terms = jnp.exp(scores - row_max)
    total = jnp.sum(terms, axis=1, keepdims=True)
    weights = (terms / total).astype(jnp.bfloat16)
    heads[...] = (product(weights, values) * valid[...]).astype(jnp.bfloat16)
    log_totals[0] = row_max + jnp.log(total)


def attention_specs(tokens, blocks):
    def column(*dims):
        return pl.BlockSpec(dims, lambda h: (0,) * len(dims))

    head = pl.BlockSpec((tokens, HD), lambda h: (0, h))
    keys = pl.BlockSpec((1, blocks, tokens, HD), lambda h: (0, 0, 0, h))
    values = pl.BlockSpec((1, blocks, tokens, HD), lambda h: (1, 0, 0, h))
    logs = pl.BlockSpec((1, tokens, 1), lambda h: (h, 0, 0))
    return head, keys, values, column(tokens, 1), column(1, blocks * tokens), logs


def attend(queries, keys_values, query_doc, key_doc, valid):
    tokens, columns = queries.shape
    blocks = keys_values.shape[1]
    head, keys, values, column, row, logs = attention_specs(tokens, blocks)
    shape = jax.ShapeDtypeStruct
    return pl.pallas_call(
        attend_kernel,
        grid=(columns // HD,),
        in_specs=[head, keys, values, column, row, column],
        out_specs=(head, logs),
        out_shape=(
            shape((tokens, columns), jnp.bfloat16),
            shape((columns // HD, tokens, 1), jnp.float32),
        ),
        compiler_params=pltpu.CompilerParams(vmem_limit_bytes=40 * 2**20),
        name="attend",
    )(queries, keys_values, keys_values, query_doc, key_doc, valid)


def attend_back_kernel(
    queries, keys, values, query_doc, key_doc, log_totals, grad_heads, cosine, sine,
    grad_queries, grad_keys_values,
):
    bf16 = jnp.bfloat16
    scale = 1.0 / math.sqrt(HD)
    blocks, tokens = keys.shape[1], keys.shape[2]
    keys, values = (ref[0].reshape(blocks * tokens, HD) for ref in (keys, values))
    scores = masked_scores(queries[...], keys, query_doc[...], key_doc[...])
    probs = jnp.exp(scores - log_totals[0])
    grads = grad_heads[...]
    slopes = product(grads, values, NT)
    slopes = probs * (slopes - jnp.sum(probs * slopes, axis=1, keepdims=True))
    grad_scores = slopes.astype(bf16)
    turned_back = turned(product(grad_scores, keys) * scale, cosine[...], -sine[...])
    grad_queries[...] = turned_back.astype(bf16)
    grad_keys = product(grad_scores, queries[...], TN) * scale
    grad_keys_values[0] = grad_keys.astype(bf16).reshape(blocks, tokens, HD)
    grad_values = product(probs.astype(bf16), grads, TN)
    grad_keys_values[1] = grad_values.astype(bf16).reshape(blocks, tokens, HD)


def attend_back(queries, keys_values, query_doc, key_doc, log_totals, grad_heads, cosine, sine):
    tokens, columns = queries.shape
    blocks = keys_values.shape[1]
    head, keys, values, column, row, logs = attention_specs(tokens, blocks)
    angle = pl.BlockSpec((tokens, HD), lambda h: (0, 0))
    shape = jax.ShapeDtypeStruct
    return pl.pallas_call(
        attend_back_kernel,
        grid=(columns // HD,),
        in_specs=[head, keys, values, column, row, logs, head, angle, angle],
        out_specs=(head, pl.BlockSpec((2, blocks, tokens, HD), lambda h: (0, 0, 0, h))),
        out_shape=(
            shape((tokens, columns), jnp.bfloat16),
            shape(keys_values.shape, jnp.bfloat16),
        ),
        compiler_params=pltpu.CompilerParams(vmem_limit_bytes=48 * 2**20),
        name="attend_back",
    )(queries, keys_values, keys_values, query_doc, key_doc, log_totals, grad_heads, cosine, sine)


RING = 8
NO_SLOT = 1 << 20
RIGHT, LEFT, OVER_X, OVER_CORE, OVER_FAR, LOCAL, SCALARS = range(7)
MESH_ID = pl.DeviceIdType.MESH


def ring_place(ep):
    z, y = ep // 2, ep % 2
    return z + y * (7 - 2 * z)


def ring_member(place):
    upper = place // 4
    return 2 * place + upper * (15 - 4 * place)


class Peers:
    def __init__(self):
        self.ep, self.tp = lax.axis_index(EP), lax.axis_index(TP)
        self.x, self.core = self.tp // 2, self.tp % 2
        self.z, self.y = self.ep // 2, self.ep % 2
        self.place = ring_place(self.ep)
        self.right = (self.block(1), self.tp)
        self.left = (self.block(RING - 1), self.tp)
        self.quarter = self.tp
        self.x_quarter = (1 - self.x) * 2 + self.core
        self.core_quarter = self.x * 2 + 1 - self.core
        self.far_quarter = (1 - self.x) * 2 + 1 - self.core
        self.x_peer = (self.ep, self.x_quarter)
        self.core_peer = (self.ep, self.core_quarter)
        self.far_peer = (self.ep, self.far_quarter)
        self.y_peer = (self.z * 2 + 1 - self.y, self.tp)

    def block(self, step):
        return ring_member((self.place + step + RING) % RING)


def greet(peers):
    barrier = pltpu.get_barrier_semaphore()
    for peer in peers:
        pl.semaphore_signal(barrier, inc=1, device_id=peer, device_id_type=MESH_ID)
    pl.semaphore_wait(barrier, len(peers))


class Copies:
    def __init__(self, send_sems, recv_sems):
        self.send_sems, self.recv_sems = send_sems, recv_sems
        self.count = 0
        self.sent = []
        self.landing = {}

    def describe(self, source, target, peer, index):
        return pltpu.make_async_remote_copy(
            src_ref=source,
            dst_ref=target,
            send_sem=self.send_sems.at[index],
            recv_sem=self.recv_sems.at[index],
            device_id=peer,
            device_id_type=MESH_ID,
        )

    def send(self, key, source, target, landing, peer):
        index = self.count
        self.count += 1
        copy = self.describe(source, target, peer, index)
        copy.start()
        self.sent.append(copy)
        self.landing[key] = self.describe(landing, landing, peer, index).wait_recv

    def local(self, key, source, target):
        index = self.count
        self.count += 1
        copy = pltpu.make_async_copy(source, target, self.send_sems.at[index])
        copy.start()
        self.landing[key] = copy.wait

    def arrive(self, *key):
        self.landing.pop(key)()

    def finish(self):
        for wait in self.landing.values():
            wait()
        for copy in self.sent:
            copy.wait_send()


def remote_params(collective_id, vmem=48):
    return pltpu.CompilerParams(
        collective_id=collective_id, has_side_effects=True, vmem_limit_bytes=vmem * 2**20
    )


def semaphores(count):
    return [pltpu.SemaphoreType.DMA((count,))] * 2


IN_PLACE = pl.BlockSpec(memory_space=pl.ANY)
IN_VMEM = pl.BlockSpec(memory_space=pltpu.VMEM)


class LateCopies(Copies):
    def send(self, key, source, target, landing, peer):
        index = self.count
        self.count += 1
        self.describe(source(), target(), peer, index).start()
        self.sent.append(lambda: self.describe(source(), target(), peer, index).wait_send())
        self.landing[key] = lambda: self.describe(landing(), landing(), peer, index).wait_recv()

    def local(self, key, source, target):
        index = self.count
        self.count += 1

        def copy():
            return pltpu.make_async_copy(source(), target(), self.send_sems.at[index])

        copy().start()
        self.landing[key] = lambda: copy().wait()

    def finish(self):
        for wait in list(self.landing.values()) + self.sent:
            wait()


def feed_block(
    block, rank_row, rank_column, gate_rows, scale, token_rows, token_cotangent,
    expert_in, expert_down, shared, staged, between, out_terms, back_terms, scale_grad, token_grad,
):
    (
        out_part, back_part, slot_rows, slot_cotangent, grad_pre, gated, grad_shared_pre, scaled,
    ) = staged
    bf16, f32 = jnp.bfloat16, jnp.float32
    experts, slots, _ = slot_rows.shape
    tokens = token_rows.shape[0]
    hidden_count = gated.shape[2]
    all_slots = experts * slots
    silu, slope = silu_parts(product(token_rows, shared[0], NT))
    up = product(token_rows, shared[1], NT)
    hidden = (silu * up).astype(bf16).astype(f32)
    scaled_hidden = (scale * hidden).astype(bf16)
    back = product(token_cotangent, shared[2], NT)
    scale_grad[block] = jnp.sum(hidden * back, axis=1, keepdims=True)
    back = scale * back
    gate_grad = (back * up * slope).astype(bf16)
    up_grad = (back * silu).astype(bf16)
    between()
    scaled[...] = scaled_hidden
    grad_shared_pre[0] = gate_grad
    grad_shared_pre[1] = up_grad
    order = lax.broadcasted_iota(jnp.int32, (all_slots, tokens), 0)
    spread_order = lax.broadcasted_iota(jnp.int32, (tokens, all_slots), 1)
    hits, spread = None, None
    for expert in range(experts):
        row_hits = order == rank_row[expert : expert + 1, :] + expert * slots
        column_hits = spread_order == rank_column[:, expert : expert + 1] + expert * slots
        hits = row_hits if hits is None else hits | row_hits
        spread = column_hits if spread is None else spread | column_hits
    place = hits.astype(bf16)
    taken = product(place, token_rows).astype(bf16)
    taken_cotangent = product(place, token_cotangent).astype(bf16)
    for ref, values in ((slot_rows, taken), (slot_cotangent, taken_cotangent)):
        for expert in range(experts):
            ref[expert] = values[expert * slots : (expert + 1) * slots]
    for expert in range(experts):
        mine = slice(expert * slots, (expert + 1) * slots)
        gate = jnp.sum(
            jnp.where(hits[mine], gate_rows[expert : expert + 1], 0.0), axis=1, keepdims=True
        )
        pre = product(taken[mine], expert_in[expert], NT)
        silu, slope = silu_parts(pre[:, :hidden_count])
        up = pre[:, hidden_count:]
        hidden = (silu * up).astype(bf16).astype(f32)
        gated_hidden = (gate * hidden).astype(bf16)
        gated[expert] = gated_hidden
        back = product(taken_cotangent[mine], expert_down[expert], NT)
        slot_grad = jnp.sum(hidden * back, axis=1, keepdims=True)
        token_grad[block, expert : expert + 1, :] = jnp.sum(
            jnp.where(hits[mine], slot_grad, 0.0), axis=0, keepdims=True
        )
        back = gate * back
        gate_grad_e = (back * up * slope).astype(bf16)
        up_grad_e = (back * silu).astype(bf16)
        grad_pre[0, expert] = gate_grad_e
        grad_pre[1, expert] = up_grad_e
        out_terms[mine, :] = product(gated_hidden, expert_down[expert]).astype(bf16)
        both_grads = jnp.concatenate([gate_grad_e, up_grad_e], axis=1)
        back_terms[mine, :] = product(both_grads, expert_in[expert]).astype(bf16)
    spread = spread.astype(bf16)
    out_part[...] = product(
        jnp.concatenate([spread, scaled_hidden], axis=1), out_terms[...]
    ).astype(bf16)
    back_part[...] = product(
        jnp.concatenate([spread, gate_grad, up_grad], axis=1), back_terms[...]
    ).astype(bf16)


def gather_feed_kernel(
    rows, cotangent, scales, rank_row, rank_column, expert_in, expert_down, shared,
    all_rows, all_cotangent, all_scales,
    out_part, back_part, slot_rows, slot_cotangent, grad_pre, gated, grad_shared_pre, scaled,
    token_grad, scale_grad,
    out_terms, back_terms, held_rows, held_cotangent,
    stage_out, stage_back, stage_rows, stage_cotangent, stage_pre, stage_gated, stage_shared,
    stage_scaled,
    load_sems, store_sems, send_sems, recv_sems,
):
    me = Peers()
    copies = LateCopies(send_sems, recv_sems)
    count = rows.shape[0]
    half, part = count // 2, count // 4
    q, qx, qc, qd = me.quarter, me.x_quarter, me.core_quarter, me.far_quarter
    blocks = {step: me.block(step) for step in range(-4, 5)}
    low, high, whole = pl.ds(0, half), pl.ds(half, half), pl.ds(0, count)
    own, other, scale = range(3)
    full = (all_rows, all_cotangent)
    sides = ((RIGHT, me.right, -1, 0), (LEFT, me.left, 1, 1))
    greet([me.right, me.left, me.x_peer, me.core_peer, me.far_peer])

    def push(key, kind, step, quarter, which, peer, landing_step, landing_quarter, source=None):
        def cell():
            return full[kind].at[blocks[step], quarter, which]

        def landing():
            return full[kind].at[blocks[landing_step], landing_quarter, which]

        copies.send((kind,) + key, source or cell, cell, landing, peer)

    push((OVER_X, other, 0), 0, 0, q, low, me.x_peer, 0, qx, lambda: rows.at[low])
    for side, peer, sign, keep in sides:
        push((side, own, 1), 1, 0, q, whole, peer, sign, q, lambda: cotangent.at[q])
        push((side, other, 1), 1, 0, qx, low, peer, sign, qx, lambda: cotangent.at[qx, low])
    push((OVER_X, own, 0), 0, 0, q, high, me.x_peer, 0, qx, lambda: rows.at[high])
    push((OVER_CORE, own, 0), 0, 0, q, whole, me.core_peer, 0, qc, lambda: rows)
    for side, peer, sign, keep in sides:
        push((side, own, 1), 0, 0, q, whole, peer, sign, q, lambda: rows)
    copies.local((LOCAL, 0), lambda: rows, lambda: all_rows.at[blocks[0], q])
    copies.local((LOCAL, 1), lambda: cotangent, lambda: all_cotangent.at[blocks[0]])

    def scales_of(quarter):
        return lambda: all_scales.at[blocks[0], quarter]

    for way, peer, quarter in (
        (OVER_X, me.x_peer, qx),
        (OVER_CORE, me.core_peer, qc),
        (OVER_FAR, me.far_peer, qd),
    ):
        copies.send((way, scale, 0), lambda: scales, scales_of(q), scales_of(quarter), peer)
    copies.local((LOCAL, scale), lambda: scales, scales_of(q))
    experts, _, width = expert_in.shape
    all_slots = experts * slot_rows.shape[2]
    shared_count = shared.shape[1]
    out_terms[all_slots:, :] = shared[2]
    back_terms[all_slots : all_slots + shared_count, :] = shared[0]
    back_terms[all_slots + shared_count :, :] = shared[1]
    copies.arrive(0, OVER_X, other, 0)
    for side, peer, sign, keep in sides:
        push((side, other, 1), 0, 0, qx, low, peer, sign, qx)
    for way in (OVER_X, OVER_CORE, OVER_FAR):
        copies.arrive(way, scale, 0)
    copies.arrive(LOCAL, scale)

    def push_scales(step, side, peer, sign):
        def cell():
            return all_scales.at[blocks[step]]

        copies.send(
            (side, scale, abs(step) + 1), cell, cell, lambda: all_scales.at[blocks[step + sign]], peer
        )

    for side, peer, sign, keep in sides:
        push_scales(0, side, peer, sign)
    copies.arrive(0, OVER_X, own, 0)
    push((OVER_CORE, other, 0), 0, 0, qx, whole, me.core_peer, 0, qd)

    def hop_in(kind, hop):
        for side, peer, sign, keep in sides:
            step = sign * hop
            if hop < 4:
                copies.arrive(kind, side, own, hop)
                which = whole if hop < 3 else pl.ds(keep * half, half)
                push((side, own, hop + 1), kind, step, q, which, peer, step + sign, q)
                push((OVER_X, own, step), kind, step, q, high, me.x_peer, step, qx)
                push((OVER_CORE, own, step), kind, step, q, whole, me.core_peer, step, qc)
                copies.arrive(kind, side, other, hop)
                which = low if hop < 3 else pl.ds(keep * part, part)
                push((side, other, hop + 1), kind, step, qx, which, peer, step + sign, qx)
                push((OVER_CORE, other, step), kind, step, qx, low, me.core_peer, step, qd)
        if hop == 4:
            copies.arrive(kind, LEFT, own, 4)
            push((OVER_X, own, 4), kind, 4, q, high, me.x_peer, 4, qx)
            copies.arrive(kind, RIGHT, own, 4)
            push((OVER_CORE, own, 4), kind, 4, q, whole, me.core_peer, 4, qc)
            copies.arrive(kind, LEFT, other, 4)
            copies.arrive(kind, RIGHT, other, 4)
            push((OVER_CORE, other, 4), kind, 4, qx, low, me.core_peer, 4, qd)

    def over_x(kind, steps):
        for step in steps:
            copies.arrive(kind, OVER_X, own, step)
            push((OVER_CORE, scale, step), kind, step, qx, high, me.core_peer, step, qd)

    def scales_in(hop):
        for side, peer, sign, keep in sides:
            if hop < 4 or side == RIGHT:
                copies.arrive(side, scale, hop)
                if hop < 3 or (hop == 3 and side == RIGHT):
                    push_scales(sign * hop, side, peer, sign)

    def load(slot, step):
        pairs = ((all_rows, held_rows), (all_cotangent, held_cotangent))
        return [
            pltpu.make_async_copy(source.at[blocks[step]], held.at[slot], load_sems.at[slot, kind])
            for kind, (source, held) in enumerate(pairs)
        ]

    def complete(steps, slots):
        for step in steps:
            for kind in range(2):
                if step != 0:
                    for piece in (own, other, scale):
                        copies.arrive(kind, OVER_CORE, piece, step)
        moves = [load(slot, step) for slot, step in zip(slots, steps)]
        for move in moves[0] + moves[-1] if len(moves) > 1 else moves[0]:
            move.start()
        for move in moves[0]:
            move.wait()

    staged = (
        stage_out, stage_back, stage_rows, stage_cotangent, stage_pre, stage_gated, stage_shared,
        stage_scaled,
    )

    def stores(block):
        targets = (
            out_part.at[block], back_part.at[block], slot_rows.at[:, block],
            slot_cotangent.at[:, block], grad_pre.at[:, :, block], gated.at[:, block],
            grad_shared_pre.at[:, block], scaled.at[block],
        )
        return [
            pltpu.make_async_copy(stage, target, store_sems.at[index])
            for index, (stage, target) in enumerate(zip(staged, targets))
        ]

    first_expert = me.ep * experts

    copies.arrive(LOCAL, 0)
    copies.arrive(LOCAL, 1)
    for piece in (own, other):
        copies.arrive(0, OVER_CORE, piece, 0)
    complete((0,), (0,))

    def turn(index, carry):
        far = (index + 1) // 2
        step = far * (1 - 2 * (index % 2)) + (index // 7) * 8
        block = ring_member((me.place + step + RING) % RING)
        slot = index % 2

        def between():
            for hop in (1, 2, 3, 4):

                @pl.when(index == max(0, 2 * hop - 3))
                def _():
                    hop_in(1, hop)

            @pl.when(index > 0)
            def _():
                for move in stores(0):
                    move.wait()

        rows_here = held_rows[slot].reshape(4 * count, width)
        cotangent_here = held_cotangent[slot].reshape(4 * count, width)
        quarters = [all_scales[block, quarter] for quarter in range(4)]
        columns = jnp.concatenate([jnp.swapaxes(values, 0, 1) for values in quarters], axis=0)
        scale_at = me_scale_row(all_scales, experts)
        gate_rows = [
            jnp.concatenate(
                [all_scales[block, quarter, pl.ds(first_expert + e, 1), :] for quarter in range(4)],
                axis=1,
            )
            for e in range(experts)
        ]
        feed_block(
            block,
            rank_row[block],
            rank_column[block],
            jnp.concatenate(gate_rows, axis=0),
            columns[:, scale_at : scale_at + 1],
            rows_here,
            cotangent_here,
            expert_in,
            expert_down,
            shared,
            staged,
            between,
            out_terms,
            back_terms,
            scale_grad,
            token_grad,
        )
        for move in stores(block):
            move.start()

        for hop in (1, 2, 3, 4):

            @pl.when(index == max(0, 2 * hop - 3))
            def _():
                scales_in(hop)
                hop_in(0, hop)
                if hop > 1:
                    for move in load(0, hop - 1):
                        move.wait()

            @pl.when(index == 2 * hop - 2)
            def _():
                steps = (-hop, hop) if hop < 4 else (4,)
                over_x(1, steps)
                over_x(0, steps)
                complete(steps, (1, 0))

        return carry

    lax.fori_loop(0, RING, turn, 0)
    for move in stores(0):
        move.wait()
    copies.finish()


def me_scale_row(all_scales, experts):
    return RING * experts


def gather_feed(
    rows, cotangent, scales, rank, expert_in, expert_down, shared, capacity, collective_id
):
    bf16, f32 = jnp.bfloat16, jnp.float32
    blocks, experts, tokens = rank.shape
    count, width = rows.shape
    hidden = expert_in.shape[1] // 2
    slice_hidden = shared.shape[1]
    shape = jax.ShapeDtypeStruct
    stages = (
        (tokens, width),
        (tokens, width),
        (experts, capacity, width),
        (experts, capacity, width),
        (2, experts, capacity, hidden),
        (experts, capacity, hidden),
        (2, tokens, slice_hidden),
        (tokens, slice_hidden),
    )
    return pl.pallas_call(
        gather_feed_kernel,
        out_shape=(
            shape((RING, 4, count, width), bf16),
            shape((RING, 4, count, width), bf16),
            shape((RING, 4) + scales.shape, f32),
            shape((blocks, tokens, width), bf16),
            shape((blocks, tokens, width), bf16),
            shape((experts, blocks, capacity, width), bf16),
            shape((experts, blocks, capacity, width), bf16),
            shape((2, experts, blocks, capacity, hidden), bf16),
            shape((experts, blocks, capacity, hidden), bf16),
            shape((2, blocks, tokens, slice_hidden), bf16),
            shape((blocks, tokens, slice_hidden), bf16),
            shape((blocks, experts, tokens), f32),
            shape((blocks, tokens, 1), f32),
        ),
        in_specs=[IN_VMEM] * 8,
        out_specs=(IN_PLACE,) * 2 + (IN_VMEM,) + (IN_PLACE,) * 8 + (IN_VMEM,) * 2,
        scratch_shapes=[
            pltpu.VMEM((experts * capacity + slice_hidden, width), bf16),
            pltpu.VMEM((experts * capacity + 2 * slice_hidden, width), bf16),
            pltpu.VMEM((2, 4, count, width), bf16),
            pltpu.VMEM((2, 4, count, width), bf16),
        ]
        + [pltpu.VMEM(stage, bf16) for stage in stages]
        + [pltpu.SemaphoreType.DMA((2, 2)), pltpu.SemaphoreType.DMA((len(stages),))]
        + semaphores(160),
        compiler_params=remote_params(collective_id, 62),
        name="gather_feed",
    )(
        rows, cotangent, scales, rank, jnp.swapaxes(rank, 1, 2), expert_in, expert_down, shared,
    )


def add_into(total, term, rows, tile=32):
    tile = min(tile, rows)

    def step(index, carry):
        here = pl.ds(pl.multiple_of(index * tile, tile), tile)
        summed = total[here, :].astype(jnp.float32) + term[here, :].astype(jnp.float32)
        total[here, :] = summed.astype(total.dtype)
        return carry

    lax.fori_loop(0, rows // tile, step, 0)


class WeightGrads:
    def __init__(self, jobs, left, right, sums, low, sems, out_sems):
        self.jobs, self.left, self.right = jobs, left, right
        self.sums, self.low, self.sems, self.out_sems = sums, low, sems, out_sems
        self.next = 0
        self.stores = {}
        self.fetch(0, 0, 0).start()

    def fetch(self, job, index, slot):
        left, right, _ = self.jobs[job]
        chunk, rows, columns, _ = self.size(job)
        here = pl.ds(pl.multiple_of(index * chunk, chunk), chunk)
        return Pair(
            pltpu.make_async_copy(
                left.at[here], self.left[rows].at[slot, pl.ds(0, chunk)], self.sems.at[slot, 0]
            ),
            pltpu.make_async_copy(
                right.at[here], self.right.at[slot, pl.ds(0, chunk)], self.sems.at[slot, 1]
            ),
        )

    def size(self, job):
        left, right, _ = self.jobs[job]
        depth, rows = left.shape
        chunk = min(self.right.shape[1], depth)
        while depth % (2 * chunk):
            chunk -= 128
        return chunk, rows, right.shape[1], depth // chunk

    def run(self, count=1):
        for job in range(self.next, min(self.next + count, len(self.jobs))):
            self.one(job)

    def one(self, job):
        self.next = job + 1
        chunk, rows, _, steps = self.size(job)
        which = job % 2
        if which in self.stores:
            self.stores.pop(which).wait()
        total = self.sums.at[which, pl.ds(0, rows)]

        def step(index, carry):
            slot = index % 2

            @pl.when(index + 1 < steps)
            def _():
                self.fetch(job, index + 1, 1 - slot).start()

            if job + 1 < len(self.jobs):

                @pl.when(index + 1 == steps)
                def _():
                    self.fetch(job + 1, 0, 0).start()

            self.fetch(job, index, slot).wait()
            term = product(
                self.left[rows][slot, pl.ds(0, chunk)], self.right[slot, pl.ds(0, chunk)], TN
            )

            @pl.when(index == 0)
            def _():
                total[...] = term

            @pl.when(index > 0)
            def _():
                total[...] += term

            return carry

        lax.fori_loop(0, steps, step, 0)
        out = self.jobs[job][2]
        source = total
        if out.dtype != total.dtype:
            source = self.low.at[which, pl.ds(0, rows)]
            source[...] = total[...].astype(out.dtype)
        self.stores[which] = pltpu.make_async_copy(source, out, self.out_sems.at[which])
        self.stores[which].start()

    def finish(self):
        self.run(len(self.jobs))
        for store in self.stores.values():
            store.wait()


class Pair:
    def __init__(self, *moves):
        self.moves = moves

    def start(self):
        for move in self.moves:
            move.start()

    def wait(self):
        for move in self.moves:
            move.wait()


def scatter_kernel(
    back_part, ffn_part, scalars, slot_rows, slot_cotangent, grad_pre, gated,
    all_rows, all_cotangent, grad_shared_pre, scaled,
    back_sum, ffn_sum, out_scalars, grad_expert_in, grad_expert_down, grad_shared,
    held, core_in, x_in, ring_q, ring_x, last_in,
    s_held, s_core, s_x, s_ring,
    job_left, job_short, job_right, job_sums, job_low, job_sems, job_out_sems,
    free, send_sems, recv_sems,
):
    me = Peers()
    copies = Copies(send_sems, recv_sems)
    parts, outs = (back_part, ffn_part), (back_sum, ffn_sum)
    count = back_part.shape[2]
    half, piece = count // 2, count // 4
    q, qx, qc, qd = me.quarter, me.x_quarter, me.core_quarter, me.far_quarter
    own, other, last = range(3)
    peers = {RIGHT: me.right, LEFT: me.left}
    greet([me.right, me.left, me.x_peer, me.core_peer])
    order = (4, 3, 5, 2, 6, 1, 7, 0)

    def load(kind):
        for k in order:
            for slot, mine in ((0, q), (1, qx)):
                copies.local(
                    (kind, LOCAL, k, slot), parts[kind].at[me.block(k), mine], held.at[kind, k, slot]
                )

    def swap_cores(kind):
        for k in order:
            for slot, theirs in ((0, qc), (1, qd)):
                target = core_in.at[k, slot]
                copies.send(
                    (kind, OVER_CORE, k, slot),
                    parts[kind].at[me.block(k), theirs],
                    target,
                    target,
                    me.core_peer,
                )

    swap_cores(0)
    load(0)
    for k in range(RING):
        for slot, mine, theirs in ((0, q, qc), (1, qx, qd)):
            copies.local((SCALARS, LOCAL, k, slot), scalars.at[me.block(k), mine], s_held.at[slot, k])
            target = s_core.at[slot, k]
            copies.send(
                (SCALARS, OVER_CORE, k, slot),
                scalars.at[me.block(k), theirs],
                target,
                target,
                me.core_peer,
            )

    def prepare(kind, *blocks):
        for k in blocks:
            for slot in (1, 0):
                copies.arrive(kind, LOCAL, k, slot)
                copies.arrive(kind, OVER_CORE, k, slot)
                add_into(held.at[kind, k, slot], core_in.at[k, slot], count)
                if slot == 1:
                    source = held.at[kind, k, 1, pl.ds(half, half)]
                    target = x_in.at[kind, k]
                    copies.send((kind, OVER_X, k), source, target, target, me.x_peer)

    def over_x(kind, *blocks):
        for k in blocks:
            copies.arrive(kind, OVER_X, k)
            add_into(held.at[kind, k, 0, pl.ds(half, half)], x_in.at[kind, k], half)

    def pass_on(kind, side, hop, k):
        if hop == 0:
            rows_q, rows_x = pl.ds(side * half, half), pl.ds(side * piece, piece)
        else:
            rows_q, rows_x = pl.ds(0, count), pl.ds(0, half)
        for which, landing, rows in ((own, ring_q, rows_q), (other, ring_x, rows_x)):
            target = landing.at[kind, side, hop, rows]
            source = held.at[kind, k, which, rows]
            copies.send((kind, side, which, hop), source, target, target, peers[side])

    def take_in(kind, side, hop, k):
        if hop == 0:
            span_q, span_x, at_q, at_x = half, piece, side * half, side * piece
        else:
            span_q, span_x, at_q, at_x = count, half, 0, 0
        for which, landing, span, at in (
            (own, ring_q, span_q, at_q),
            (other, ring_x, span_x, at_x),
        ):
            copies.arrive(kind, side, which, hop)
            rows = pl.ds(at, span)
            add_into(held.at[kind, k, which, rows], landing.at[kind, side, hop, rows], span)

    def hop_on(kind, hop):
        right_block, left_block = 4 - hop, 4 + hop
        if hop == 0:
            pass_on(kind, RIGHT, 0, 4)
            pass_on(kind, LEFT, 0, 4)
            return
        take_in(kind, RIGHT, hop - 1, right_block)
        pass_on(kind, RIGHT, hop, right_block)
        take_in(kind, LEFT, hop - 1, left_block)
        pass_on(kind, LEFT, hop, left_block)

    def pass_scalars(side, hop, k):
        target = s_ring.at[side, hop]
        copies.send((SCALARS, side, hop), s_held.at[0, k], target, target, peers[side])

    def take_scalars(side, hop, k):
        copies.arrive(SCALARS, side, hop)
        s_held[0, k] += s_ring[side, hop]

    def home(kind):
        take_in(kind, RIGHT, 3, 0)
        take_in(kind, LEFT, 3, 0)
        source, target = held.at[kind, 0, 1, pl.ds(0, half)], last_in.at[kind]
        copies.send((kind, OVER_X, last, last), source, target, target, me.x_peer)

    def home_out(kind):
        out = outs[kind]
        out[pl.ds(half, half), :] = held[kind, 0, 0, pl.ds(half, half), :].astype(out.dtype)
        copies.arrive(kind, OVER_X, last, last)
        out[pl.ds(0, half), :] = (
            held[kind, 0, 0, pl.ds(0, half), :].astype(jnp.float32)
            + last_in[kind].astype(jnp.float32)
        ).astype(out.dtype)

    experts = slot_rows.shape[0]
    jobs = []
    for expert in range(experts):
        for index in range(2):
            jobs.append(
                (grad_pre.at[index, expert], slot_rows.at[expert], grad_expert_in.at[expert, index])
            )
        jobs.append((gated.at[expert], slot_cotangent.at[expert], grad_expert_down.at[expert]))
    for index in range(2):
        jobs.append((grad_shared_pre.at[index], all_rows, grad_shared.at[index]))
    jobs.append((scaled, all_cotangent, grad_shared.at[2]))
    prepare(0, 4, 3, 5)
    over_x(0, 4)
    hop_on(0, 0)
    prepare(0, 2, 6)
    for k in range(RING):
        for slot in (0, 1):
            copies.arrive(SCALARS, LOCAL, k, slot)
            copies.arrive(SCALARS, OVER_CORE, k, slot)
    s_held[...] += s_core[...]
    copies.send((SCALARS, OVER_X), s_held.at[1], s_x, s_x, me.x_peer)
    over_x(0, 3, 5)
    hop_on(0, 1)
    copies.arrive(SCALARS, OVER_X)
    s_held[0] += s_x[...]
    pass_scalars(RIGHT, 0, 4)
    prepare(0, 1, 7, 0)
    pl.semaphore_signal(free, inc=1, device_id=me.core_peer, device_id_type=MESH_ID)
    load(1)
    lefts = {job_left.shape[2]: job_left, job_short.shape[2]: job_short}
    grads = WeightGrads(jobs, lefts, job_right, job_sums, job_low, job_sems, job_out_sems)
    over_x(0, 2, 6)
    hop_on(0, 2)
    take_scalars(RIGHT, 0, 3)
    pass_scalars(RIGHT, 1, 3)
    pass_scalars(LEFT, 1, 5)
    pl.semaphore_wait(free, 1)
    swap_cores(1)
    over_x(0, 1, 7)
    grads.run(1)
    prepare(1, 4, 3, 5)
    hop_on(0, 3)
    take_scalars(RIGHT, 1, 2)
    take_scalars(LEFT, 1, 6)
    pass_scalars(RIGHT, 2, 2)
    pass_scalars(LEFT, 2, 6)
    over_x(0, 0)
    over_x(1, 4)
    hop_on(1, 0)
    prepare(1, 2, 6)
    over_x(1, 3, 5)
    grads.run(2)
    home(0)
    for side, k in ((RIGHT, 1), (LEFT, 7)):
        take_scalars(side, 2, k)
        pass_scalars(side, 3, k)
    hop_on(1, 1)
    home_out(0)
    prepare(1, 1, 7, 0)
    over_x(1, 2, 6)
    grads.run(2)
    hop_on(1, 2)
    over_x(1, 1, 7, 0)
    grads.run(2)
    hop_on(1, 3)
    take_scalars(RIGHT, 3, 0)
    take_scalars(LEFT, 3, 0)
    out_scalars[...] = s_held[0, 0]
    grads.finish()
    home(1)
    home_out(1)
    copies.finish()


def scatter_rows(back_part, ffn_part, scalars, fed, collective_id):
    slot_rows, slot_cotangent, grad_pre, gated, all_rows, all_cotangent, grad_shared_pre, scaled = fed
    _, _, count, width = back_part.shape
    half = count // 2
    dtype, f32 = back_part.dtype, jnp.float32
    s_shape = scalars.shape[2:]
    experts, hidden = gated.shape[0], gated.shape[2]
    shared_hidden = scaled.shape[1]
    shape = jax.ShapeDtypeStruct
    return pl.pallas_call(
        scatter_kernel,
        out_shape=(
            shape((count, width), f32),
            shape((count, width), f32),
            shape(s_shape, f32),
            shape((experts, 2, hidden, width), f32),
            shape((experts, hidden, width), f32),
            shape((3, shared_hidden, width), dtype),
        ),
        in_specs=[IN_PLACE] * 11,
        out_specs=(IN_VMEM,) * 3 + (IN_PLACE,) * 3,
        scratch_shapes=[
            pltpu.VMEM((2, RING, 2, count, width), dtype),
            pltpu.VMEM((RING, 2, count, width), dtype),
            pltpu.VMEM((2, RING, half, width), dtype),
            pltpu.VMEM((2, 2, 4, count, width), dtype),
            pltpu.VMEM((2, 2, 4, half, width), dtype),
            pltpu.VMEM((2, half, width), dtype),
            pltpu.VMEM((2, RING) + s_shape, f32),
            pltpu.VMEM((2, RING) + s_shape, f32),
            pltpu.VMEM((RING,) + s_shape, f32),
            pltpu.VMEM((2, 4) + s_shape, f32),
            pltpu.VMEM((2, 640, hidden), dtype),
            pltpu.VMEM((2, 640, shared_hidden), dtype),
            pltpu.VMEM((2, 640, width), dtype),
            pltpu.VMEM((2, hidden, width), f32),
            pltpu.VMEM((2, shared_hidden, width), dtype),
            pltpu.SemaphoreType.DMA((2, 2)),
            pltpu.SemaphoreType.DMA((2,)),
            pltpu.SemaphoreType.REGULAR,
        ]
        + semaphores(168),
        compiler_params=remote_params(collective_id, 62),
        name="scatter_rows",
    )(back_part, ffn_part, scalars, *fed)


def spread_kernel(
    shard_in, shard_out, routes, full_in, full_out, full_routes, send_sems, recv_sems
):
    me = Peers()
    copies = Copies(send_sems, recv_sems)
    kinds, depth, _ = shard_in.shape
    rows, columns = shard_out.shape
    sides = ((RIGHT, me.right, -1), (LEFT, me.left, 1))
    greet([me.right, me.left])

    def cell(kind, step, part, parts):
        block = me.block(step)
        if kind < kinds:
            return full_in.at[kind, block, pl.ds(part * (depth // parts), depth // parts)]
        if kind > kinds:
            return full_routes.at[block]
        across = pl.ds(pl.multiple_of(block * columns, columns), columns)
        return full_out.at[pl.ds(part * (rows // parts), rows // parts), across]

    def pass_on(side, peer, sign, kind, hop, source=None):
        if kind > kinds and hop == 3 and side == LEFT:
            return
        parts = 2 if hop == 3 else 1
        part = side if hop == 3 else 0
        step = sign * hop
        here = cell(kind, step, part, parts)
        copies.send(
            (side, kind, hop + 1),
            here if source is None else source,
            here,
            cell(kind, step + sign, part, parts),
            peer,
        )

    order = (kinds + 1,) + tuple(range(kinds - 1, -1, -1)) + (kinds,)
    for kind in order:
        source = shard_in.at[kind] if kind < kinds else shard_out if kind == kinds else routes
        for side, peer, sign in sides:
            pass_on(side, peer, sign, kind, 0, source)
        copies.local((LOCAL, kind), source, cell(kind, 0, 0, 1))
    for hop in (1, 2, 3):
        for kind in order:
            for side, peer, sign in sides:
                copies.arrive(side, kind, hop)
                pass_on(side, peer, sign, kind, hop)
    copies.finish()


def spread_weights(shard_in, shard_out, routes, collective_id):
    kinds, depth, width = shard_in.shape
    rows, columns = shard_out.shape
    return pl.pallas_call(
        spread_kernel,
        out_shape=(
            jax.ShapeDtypeStruct((kinds, RING, depth, width), shard_in.dtype),
            jax.ShapeDtypeStruct((rows, RING * columns), shard_out.dtype),
            jax.ShapeDtypeStruct((RING,) + routes.shape, routes.dtype),
        ),
        in_specs=[IN_VMEM] * 3,
        out_specs=(IN_PLACE,) * 2 + (IN_VMEM,),
        scratch_shapes=semaphores(9 * (kinds + 2)),
        compiler_params=remote_params(collective_id),
        name="spread_weights",
    )(shard_in, shard_out, routes)


def finish_kernel(
    normed, grad_raw, heads, grad_attention, weights, gain, rows, grad_residual, tail,
    sum_in, sum_out, sum_tail, grad_input,
    held_in, held_out, ring_in, ring_out, tails, tail_sums,
    core_out, core_in, x_out, x_in, grad_rows, mine,
    send_sems, recv_sems,
):
    me = Peers()
    copies = Copies(send_sems, recv_sems)
    bf16, f32 = jnp.bfloat16, jnp.float32
    kinds = grad_raw.shape[0]
    depth, width = sum_in.shape[1], sum_in.shape[2]
    out_rows, columns = sum_out.shape
    count = rows.shape[0]
    peers = {RIGHT: me.right, LEFT: me.left}
    greet([me.right, me.left, me.x_peer, me.core_peer, me.far_peer])

    def held(kind, k):
        return held_in.at[k, kind] if kind < kinds else held_out.at[k]

    def ring(kind, side, hop):
        return ring_in.at[side, hop, kind] if kind < kinds else ring_out.at[side, hop]

    def span(kind, side, hop):
        whole = depth if kind < kinds else out_rows
        return (side * (whole // 2), whole // 2) if hop == 0 else (0, whole)

    def pass_on(side, hop, k, kind):
        at = pl.ds(*span(kind, side, hop))
        target = ring(kind, side, hop).at[at]
        copies.send((side, kind, hop), held(kind, k).at[at], target, target, peers[side])

    def take_in(side, hop, k, kind):
        copies.arrive(side, kind, hop)
        start, size = span(kind, side, hop)
        at = pl.ds(start, size)
        add_into(held(kind, k).at[at], ring(kind, side, hop).at[at], size)

    def work_out(*blocks):
        for k in blocks:
            block = me.block(k)
            features = normed[:, pl.ds(pl.multiple_of(block * depth, depth), depth)]
            for kind in range(kinds):
                held_in[k, kind] = product(features, grad_raw[kind], TN).astype(bf16)
            across = grad_attention[:, pl.ds(pl.multiple_of(block * columns, columns), columns)]
            held_out[k] = product(heads[...], across, TN).astype(bf16)

    def hop_on(hop):
        if hop == 0:
            for kind in range(kinds + 1):
                for side in (RIGHT, LEFT):
                    pass_on(side, 0, 4, kind)
            return
        for kind in range(kinds + 1):
            for side, k in ((RIGHT, 4 - hop), (LEFT, 4 + hop)):
                take_in(side, hop - 1, k, kind)
                pass_on(side, hop, k, kind)

    def quarter(index):
        here = pl.ds(pl.multiple_of(index * count, count), count)
        total = None
        for kind in range(kinds):
            term = product(grad_raw[kind, here, :], weights[kind], NT)
            total = term if total is None else total + term
        return total

    work_out(4)
    hop_on(0)
    for slot, index in ((1, me.far_quarter), (0, me.core_quarter)):
        core_out[slot] = quarter(index).astype(bf16)
        target = core_in.at[slot]
        copies.send((SCALARS, OVER_CORE, slot), core_out.at[slot], target, target, me.core_peer)
    mine[...] = quarter(me.x_quarter)
    copies.arrive(SCALARS, OVER_CORE, 1)
    x_out[...] = (mine[...] + core_in[1].astype(f32)).astype(bf16)
    copies.send((SCALARS, OVER_X), x_out, x_in, x_in, me.x_peer)
    work_out(3, 5)
    hop_on(1)
    mine[...] = quarter(me.quarter)
    copies.arrive(SCALARS, OVER_CORE, 0)
    work_out(2, 6)
    copies.arrive(SCALARS, OVER_X)
    total = mine[...] + core_in[0].astype(f32) + x_in[...].astype(f32)
    inverse, scaled_rows = rms_parts(rows[...].astype(f32))
    scaled = total * gain[...]
    slope = inverse * (
        scaled - scaled_rows * jnp.mean(scaled * scaled_rows, axis=-1, keepdims=True)
    )
    grad_rows[...] = (grad_residual[...] + slope).astype(bf16)
    here = grad_input.at[me.quarter]
    copies.send((SCALARS, RIGHT, OVER_X), grad_rows, here, grad_input.at[me.x_quarter], me.x_peer)
    copies.send(
        (SCALARS, RIGHT, OVER_CORE), grad_rows, here, grad_input.at[me.core_quarter], me.core_peer
    )
    copies.local((LOCAL,), grad_rows, here)
    gain_grad = jnp.sum(total * scaled_rows, axis=0, keepdims=True)
    tails[0, 0:kinds, :] = tail[...]
    for index in range(gain_grad.shape[1] // width):
        part = slice(index * width, (index + 1) * width)
        tails[0, kinds + index : kinds + index + 1, :] = gain_grad[:, part]
    tail_kind = kinds + 1

    def pass_tail(side, hop, place):
        sign = -1 if side == RIGHT else 1
        target = tails.at[(place + sign) % RING]
        copies.send((side, tail_kind, hop), tails.at[place], target, target, peers[side])

    pass_tail(RIGHT, 0, 0)
    pass_tail(LEFT, 0, 0)
    hop_on(2)
    work_out(1, 7)
    copies.arrive(SCALARS, RIGHT, OVER_X)
    beside = grad_input.at[me.x_quarter]
    copies.send(
        (SCALARS, LEFT, OVER_CORE), beside, beside, grad_input.at[me.far_quarter], me.core_peer
    )
    for side, place in ((RIGHT, 7), (LEFT, 1)):
        copies.arrive(side, tail_kind, 0)
        pass_tail(side, 1, place)
    hop_on(3)
    for side, place in ((RIGHT, 6), (LEFT, 2)):
        copies.arrive(side, tail_kind, 1)
        pass_tail(side, 2, place)
    work_out(0)
    copies.arrive(RIGHT, tail_kind, 2)
    pass_tail(RIGHT, 3, 5)
    copies.arrive(LEFT, tail_kind, 2)
    for kind in range(kinds + 1):
        for side in (RIGHT, LEFT):
            take_in(side, 3, 0, kind)
        if kind < kinds:
            sum_in[kind] = held_in[0, kind].astype(f32)
    sum_out[...] = held_out[0].astype(f32)
    copies.arrive(RIGHT, tail_kind, 3)
    total = tails[0]
    for place in range(1, RING):
        total = total + tails[place]
    tail_sums[me.tp] = total
    for way, peer, index in (
        (OVER_X, me.x_peer, me.x_quarter),
        (OVER_CORE, me.core_peer, me.core_quarter),
        (OVER_FAR, me.far_peer, me.far_quarter),
    ):
        copies.send(
            (way, tail_kind), tail_sums.at[me.tp], tail_sums.at[me.tp], tail_sums.at[index], peer
        )
    for way in (OVER_X, OVER_CORE, OVER_FAR):
        copies.arrive(way, tail_kind)
    sum_tail[...] = tail_sums[...]
    copies.finish()


def finish(
    normed, grad_raw, heads, grad_attention, weights, gain, rows, grad_residual, bias, collective_id
):
    tokens, width = normed.shape
    kinds, _, columns = grad_raw.shape
    count = rows.shape[0]
    depth = width // RING
    bf16, f32 = jnp.bfloat16, jnp.float32
    shape = jax.ShapeDtypeStruct
    tail_shape = (-(-(kinds + width // columns) // 8) * 8, columns)
    return pl.pallas_call(
        finish_kernel,
        out_shape=(
            shape((kinds, depth, columns), f32),
            shape((columns, depth), f32),
            shape((4,) + tail_shape, f32),
            shape((4, count, width), bf16),
        ),
        in_specs=[IN_VMEM] * 9,
        out_specs=(IN_VMEM,) * 3 + (IN_PLACE,),
        scratch_shapes=[
            pltpu.VMEM((RING, kinds, depth, columns), bf16),
            pltpu.VMEM((RING, columns, depth), bf16),
            pltpu.VMEM((2, 4, kinds, depth, columns), bf16),
            pltpu.VMEM((2, 4, columns, depth), bf16),
            pltpu.VMEM((RING,) + tail_shape, f32),
            pltpu.VMEM((4,) + tail_shape, f32),
            pltpu.VMEM((2, count, width), bf16),
            pltpu.VMEM((2, count, width), bf16),
            pltpu.VMEM((count, width), bf16),
            pltpu.VMEM((count, width), bf16),
            pltpu.VMEM((count, width), bf16),
            pltpu.VMEM((count, width), f32),
        ]
        + semaphores(56),
        compiler_params=remote_params(collective_id, 60),
        name="finish",
    )(normed, grad_raw, heads, grad_attention, weights, gain[None], rows, grad_residual, bias)


def greet_along_z(me):
    barrier = pltpu.get_barrier_semaphore()
    pl.semaphore_signal(barrier, inc=1, device_id=me.y_peer, device_id_type=MESH_ID)

    @pl.when(me.z > 0)
    def _():
        peer = (me.ep - 2, me.tp)
        pl.semaphore_signal(barrier, inc=1, device_id=peer, device_id_type=MESH_ID)

    @pl.when(me.z < 3)
    def _():
        peer = (me.ep + 2, me.tp)
        pl.semaphore_signal(barrier, inc=1, device_id=peer, device_id_type=MESH_ID)

    pl.semaphore_wait(barrier, 1 + (me.z + 2) // 3 + (5 - me.z) // 3)


def share_kernel(own, out, send_sems, recv_sems):
    me = Peers()
    kinds, tokens, _ = own.shape
    pieces = 2
    size = tokens // pieces
    parts = [(kind, pl.ds(piece * size, size)) for kind in range(kinds) for piece in range(pieces)]
    count = len(parts)
    greet_along_z(me)

    def copy(index, source, target, peer):
        return Copies(send_sems, recv_sems).describe(source, target, peer, index)

    def upward(index, kind, rows):
        return copy(index, own.at[kind, rows], out.at[kind, 0, rows], (me.ep + 2, me.tp))

    def sideways(index, kind, rows):
        return copy(count + index, own.at[kind, rows], out.at[kind, 1, rows], me.y_peer)

    def onward(index, kind, rows):
        return copy(count + index, out.at[kind, 0, rows], out.at[kind, 1, rows], me.y_peer)

    @pl.when(me.z < 3)
    def _():
        for index, (kind, rows) in enumerate(parts):
            upward(index, kind, rows).start()

    @pl.when(me.y == 0)
    def _():
        for index, (kind, rows) in enumerate(parts):
            sideways(index, kind, rows).start()

    out[:, 2] = own[...]

    @pl.when(me.z == 0)
    def _():
        out[:, 0] = jnp.zeros_like(own)

    @pl.when((me.z == 0) & (me.y == 0))
    def _():
        out[:, 1] = jnp.zeros_like(own)

    @pl.when(me.z > 0)
    def _():
        for index, (kind, rows) in enumerate(parts):
            upward(index, kind, rows).wait_recv()

            @pl.when(me.y == 1)
            def _():
                onward(index, kind, rows).start()

    @pl.when(me.y == 1)
    def _():
        for index, (kind, rows) in enumerate(parts):
            sideways(index, kind, rows).wait_recv()

    @pl.when((me.y == 0) & (me.z > 0))
    def _():
        for index, (kind, rows) in enumerate(parts):
            onward(index, kind, rows).wait_recv()

    @pl.when(me.z < 3)
    def _():
        for index, (kind, rows) in enumerate(parts):
            upward(index, kind, rows).wait_send()

    @pl.when((me.y == 0) | (me.z > 0))
    def _():
        for index, (kind, rows) in enumerate(parts):
            sideways(index, kind, rows).wait_send()


def share_keys(own, collective_id):
    kinds, tokens, width = own.shape
    return pl.pallas_call(
        share_kernel,
        out_shape=jax.ShapeDtypeStruct((kinds, 3, tokens, width), own.dtype),
        in_specs=[IN_VMEM],
        out_specs=IN_VMEM,
        scratch_shapes=semaphores(8),
        compiler_params=remote_params(collective_id),
        name="share_keys",
    )(own)


def return_kernel(grads, cosine, sine, out, total, from_y, from_z, send_sems, recv_sems):
    me = Peers()
    kinds, _, tokens, _ = grads.shape
    pieces = 2
    size = tokens // pieces
    parts = [(kind, pl.ds(piece * size, size)) for kind in range(kinds) for piece in range(pieces)]
    count = len(parts)
    greet_along_z(me)

    def copy(index, source, target, peer):
        return Copies(send_sems, recv_sems).describe(source, target, peer, index)

    def sideways(index, kind, rows):
        return copy(index, grads.at[kind, 1, rows], from_y.at[kind, rows], me.y_peer)

    def downward(index, kind, rows, source):
        return copy(count + index, source.at[kind, rows], from_z.at[kind, rows], (me.ep - 2, me.tp))

    for index, (kind, rows) in enumerate(parts):
        sideways(index, kind, rows).start()

    @pl.when((me.z > 0) & (me.y == 0))
    def _():
        for index, (kind, rows) in enumerate(parts):
            downward(index, kind, rows, grads.at[:, 0]).start()

    for index, (kind, rows) in enumerate(parts):
        sideways(index, kind, rows).wait_recv()
        here = grads[kind, 2, rows, :].astype(jnp.float32)

        @pl.when(me.y == 0)
        def _():
            total[kind, rows, :] = here + from_y[kind, rows, :].astype(jnp.float32)

        @pl.when(me.y == 1)
        def _():
            total[kind, rows, :] = here
            two_back = grads[kind, 0, rows, :].astype(jnp.float32)
            summed = two_back + from_y[kind, rows, :].astype(jnp.float32)
            from_y[kind, rows, :] = summed.astype(from_y.dtype)

        @pl.when((me.z > 0) & (me.y == 1))
        def _():
            downward(index, kind, rows, from_y).start()

    @pl.when(me.z < 3)
    def _():
        for index, (kind, rows) in enumerate(parts):
            downward(index, kind, rows, from_y).wait_recv()
            total[kind, rows, :] += from_z[kind, rows, :].astype(jnp.float32)

    for start in range(0, total.shape[2], HD):
        head = slice(start, start + HD)
        out[0, :, head] = turned(total[0, :, head], cosine[...], -sine[...]).astype(out.dtype)
    out[1] = total[1].astype(out.dtype)
    for index, (kind, rows) in enumerate(parts):
        sideways(index, kind, rows).wait_send()

    @pl.when(me.z > 0)
    def _():
        for index, (kind, rows) in enumerate(parts):
            downward(index, kind, rows, from_y).wait_send()


def return_keys(grads, cosine, sine, collective_id):
    kinds, _, tokens, width = grads.shape
    return pl.pallas_call(
        return_kernel,
        out_shape=jax.ShapeDtypeStruct((kinds, tokens, width), grads.dtype),
        in_specs=[IN_VMEM] * 3,
        out_specs=IN_VMEM,
        scratch_shapes=[
            pltpu.VMEM((kinds, tokens, width), jnp.float32),
            pltpu.VMEM((kinds, tokens, width), grads.dtype),
            pltpu.VMEM((kinds, tokens, width), grads.dtype),
        ]
        + semaphores(8),
        compiler_params=remote_params(collective_id),
        name="return_keys",
    )(grads, cosine, sine)


def reduce_kernel(flip, left, right, out, core_out, core_in, x_out, x_in, send_sems, recv_sems):
    me = Peers()
    copies = Copies(send_sems, recv_sems)
    terms = left.shape[0]
    count = out.shape[0]
    f32 = jnp.float32
    greet([me.x_peer, me.core_peer])

    def quarter(index):
        rows = pl.ds(pl.multiple_of(index * count, count), count)
        total = None
        for term in range(terms):
            one = product(left[term, rows, :], right[term], NT if flip else NN)
            total = one if total is None else total + one
        return total

    for slot, index in ((1, me.far_quarter), (0, me.core_quarter)):
        core_out[slot] = quarter(index).astype(core_out.dtype)
        target = core_in.at[slot]
        copies.send((OVER_CORE, slot), core_out.at[slot], target, target, me.core_peer)
    mine = quarter(me.x_quarter)
    copies.arrive(OVER_CORE, 1)
    x_out[...] = (mine + core_in[1].astype(f32)).astype(x_out.dtype)
    copies.send((OVER_X,), x_out, x_in, x_in, me.x_peer)
    mine = quarter(me.quarter)
    copies.arrive(OVER_CORE, 0)
    out[...] = mine + core_in[0].astype(f32)
    copies.arrive(OVER_X)
    out[...] += x_in[...].astype(f32)
    copies.finish()


def product_to_owner(left, right, flip, collective_id):
    tokens = left.shape[1]
    width = right.shape[1] if flip else right.shape[2]
    count = tokens // 4
    bf16 = jnp.bfloat16
    return pl.pallas_call(
        functools.partial(reduce_kernel, flip),
        out_shape=jax.ShapeDtypeStruct((count, width), jnp.float32),
        in_specs=[IN_VMEM] * 2,
        out_specs=IN_VMEM,
        scratch_shapes=[
            pltpu.VMEM((2, count, width), bf16),
            pltpu.VMEM((2, count, width), bf16),
            pltpu.VMEM((count, width), bf16),
            pltpu.VMEM((count, width), bf16),
        ]
        + semaphores(3),
        compiler_params=remote_params(collective_id),
        name="product_to_owner",
    )(left, right)


def tensor_kernel(rows, out, send_sems, recv_sems):
    me = Peers()
    copies = Copies(send_sems, recv_sems)
    greet([me.x_peer, me.core_peer])
    mine = out.at[me.quarter]
    copies.send((OVER_X,), rows, mine, out.at[me.x_quarter], me.x_peer)
    copies.send((OVER_CORE, 0), rows, mine, out.at[me.core_quarter], me.core_peer)
    copies.local((LOCAL,), rows, mine)
    copies.arrive(OVER_X)
    beside = out.at[me.x_quarter]
    copies.send((OVER_CORE, 1), beside, beside, out.at[me.far_quarter], me.core_peer)
    copies.finish()


def tensor_gather(rows, collective_id):
    return pl.pallas_call(
        tensor_kernel,
        out_shape=jax.ShapeDtypeStruct((4,) + rows.shape, rows.dtype),
        in_specs=[IN_VMEM],
        out_specs=IN_PLACE,
        scratch_shapes=semaphores(4),
        compiler_params=remote_params(collective_id),
        name="tensor_gather",
    )(rows)


def own_rows(block, tp_index, count):
    return lax.dynamic_slice_in_dim(block, tp_index * count, count, 0)


def after(value, earlier):
    return lax.optimization_barrier((value, earlier))[0]


def per_device_dense(
    layer_input,
    attention_gain,
    attention_in,
    attention_bias,
    attention_out,
    feedforward_gain,
    shared_in,
    shared_down,
    shared_gate,
    router,
    expert_in,
    expert_down,
    routes,
    document_lengths,
    cotangent,
):
    bf16 = jnp.bfloat16
    f32 = jnp.float32
    both = (EP, TP)
    tok_count, model_width = layer_input.shape
    expert_count = router.shape[1]
    top_count = routes.shape[1]
    ep_size = lax.axis_size(EP)
    tp_size = lax.axis_size(TP)
    ep_index = lax.axis_index(EP)
    tp_index = lax.axis_index(TP)
    own_count = tok_count // tp_size
    all_count = tok_count * ep_size
    capacity = tp_size * (
        (5 * tok_count * top_count + 4 * expert_count * tp_size - 1) // (4 * expert_count * tp_size)
    )
    reach_back = min((WINDOW + tok_count - 2) // tok_count, ep_size - 1)
    local_experts = expert_in.shape[0]
    route_rows = jnp.concatenate(
        [routes.T, jnp.zeros((-top_count % 8, tok_count), routes.dtype)]
    )
    in_blocks, out_full, all_routes = spread_weights(attention_in, attention_out, route_rows, 0)
    in_full = in_blocks.reshape(3, model_width, -1)
    shard_width = shared_in.shape[1]
    slice_hidden = shared_in.shape[2] // ep_size
    shared_shards = jnp.concatenate([jnp.swapaxes(shared_in, 1, 2), shared_down[None]])
    shared_shards = jnp.swapaxes(
        shared_shards.reshape(3, ep_size, slice_hidden, shard_width), 0, 1
    )
    shared_slices = lax.all_to_all(
        after(shared_shards, in_blocks), EP, split_axis=0, concat_axis=0, tiled=True
    )
    shared_slices = jnp.transpose(shared_slices, (1, 2, 0, 3)).reshape(
        3, slice_hidden, model_width
    )
    my_ids = ep_index * local_experts + jnp.arange(local_experts, dtype=jnp.int32)
    taken = jnp.any(all_routes[:, None, :top_count] == my_ids[None, :, None, None], axis=2)
    earlier_mask = jnp.tril(jnp.ones((tok_count, tok_count), bf16), -1)
    rank = product(
        taken.astype(bf16).reshape(-1, tok_count), earlier_mask, NT
    ).astype(jnp.int32).reshape(taken.shape)
    rank = jnp.where(taken & (rank < capacity), rank, NO_SLOT)

    positions = ep_index * tok_count + jnp.arange(tok_count, dtype=jnp.int32)
    key_count = (reach_back + 1) * tok_count
    key_positions = (ep_index - reach_back) * tok_count + jnp.arange(key_count, dtype=jnp.int32)
    query_doc, rope_pos, valid_mask = doc_table(document_lengths, positions)
    query_doc = query_doc[:, None]
    key_doc = doc_table(document_lengths, key_positions)[0][None, :]
    valid_rows = valid_mask.astype(f32)[:, None]
    cosine, sine = (part[:, 0] for part in rope_angles(rope_pos, HD))
    cosine = jnp.concatenate([cosine, cosine], axis=1)
    sine = jnp.concatenate([-sine, sine], axis=1)
    normed_attention, queries, own_kv = project(
        layer_input, attention_gain, in_full, attention_bias, cosine, sine
    )
    keys_values = share_keys(own_kv, 1)
    heads_low, log_totals = attend(queries, keys_values, query_doc, key_doc, valid_rows)
    attention_sum = product_to_owner(heads_low[None], out_full[None], False, 2)
    input_rows = own_rows(layer_input, tp_index, own_count).astype(f32)
    residual = input_rows + attention_sum
    inverse_two, normed_two = rms_parts(residual)
    normed_ffn = normed_two * feedforward_gain
    normed_low = normed_ffn.astype(bf16)
    shared_scale = jax.nn.sigmoid(jnp.dot(normed_ffn, shared_gate, precision=HIGHEST))
    router_probs = jax.nn.softmax(jnp.dot(normed_ffn, router, precision=HIGHEST), axis=-1)
    routes_own = own_rows(routes, tp_index, own_count)
    expert_ids = jnp.arange(expert_count, dtype=jnp.int32)
    picked = jnp.any(routes_own[:, :, None] == expert_ids[None, None, :], axis=1)
    chosen = jnp.where(picked, router_probs, 0.0)
    chosen_total = jnp.sum(chosen, axis=1, keepdims=True)
    gates = chosen / chosen_total
    scale_count = -(-(expert_count + 1) // 8) * 8
    spare = jnp.zeros((scale_count - expert_count - 1, own_count), f32)
    scale_rows = jnp.concatenate([gates.T, shared_scale[None], spare])
    (
        all_rows,
        all_cotangent,
        all_scales,
        ffn_part,
        back_part,
        slot_rows,
        slot_cotangent,
        grad_pre,
        gated,
        grad_shared_pre,
        scaled_hidden,
        token_grad,
        scale_grad,
    ) = gather_feed(
        normed_low,
        cotangent.reshape(tp_size, own_count, model_width),
        scale_rows,
        rank,
        jnp.swapaxes(expert_in, 2, 3).reshape(local_experts, -1, model_width),
        expert_down,
        shared_slices,
        capacity,
        3,
    )
    spare = jnp.zeros((ep_size, scale_count - expert_count - 1, tok_count), f32)
    scalar_part = jnp.concatenate(
        [jnp.zeros((ep_size, expert_count, tok_count), f32), scale_grad[:, None, :, 0], spare], axis=1
    )
    scalar_part = lax.dynamic_update_slice(
        scalar_part, token_grad, (0, ep_index * local_experts, 0)
    )
    scalar_part = jnp.swapaxes(
        scalar_part.reshape(ep_size, scale_count, tp_size, own_count), 1, 2
    )
    part_shape = (ep_size, tp_size, own_count, model_width)
    slot_count = ep_size * capacity
    fed = (
        slot_rows.reshape(local_experts, slot_count, model_width),
        slot_cotangent.reshape(local_experts, slot_count, model_width),
        grad_pre.reshape(2, local_experts, slot_count, -1),
        gated.reshape(local_experts, slot_count, -1),
        all_rows.reshape(all_count, model_width),
        all_cotangent.reshape(all_count, model_width),
        grad_shared_pre.reshape(2, all_count, slice_hidden),
        scaled_hidden.reshape(all_count, slice_hidden),
    )
    back_sum, ffn_sum, scalar_sum, grad_expert_in, grad_expert_down, shared_grads = scatter_rows(
        back_part.reshape(part_shape), ffn_part.reshape(part_shape), scalar_part, fed, 4
    )
    scalar_sum = scalar_sum.T
    grad_expert_in = jnp.swapaxes(grad_expert_in, 2, 3)
    layer_output = lax.all_gather((residual + ffn_sum).astype(bf16), TP, axis=0, tiled=True)
    shared_grads = jnp.transpose(
        shared_grads.reshape(3, slice_hidden, ep_size, shard_width), (2, 0, 1, 3)
    )
    shared_grads = lax.all_to_all(shared_grads, EP, split_axis=0, concat_axis=0, tiled=True)
    shared_grads = (
        jnp.swapaxes(shared_grads, 0, 1).reshape(3, -1, shard_width).astype(f32)
    )
    grad_shared_in = jnp.swapaxes(shared_grads[:2], 1, 2)
    grad_shared_down = shared_grads[2]

    grad_gates = scalar_sum[:, :expert_count]
    grad_probs = jnp.where(
        picked,
        (grad_gates - jnp.sum(grad_gates * gates, axis=1, keepdims=True)) / chosen_total,
        0.0,
    )
    grad_logits = router_probs * (
        grad_probs - jnp.sum(grad_probs * router_probs, axis=1, keepdims=True)
    )
    grad_router = jnp.einsum("td,te->de", normed_ffn, grad_logits, precision=HIGHEST)
    grad_scale_pre = scalar_sum[:, expert_count] * shared_scale * (1.0 - shared_scale)
    grad_shared_gate = jnp.dot(grad_scale_pre, normed_ffn, precision=HIGHEST)
    grad_normed = (
        back_sum
        + jnp.einsum("te,de->td", grad_logits, router, precision=HIGHEST)
        + grad_scale_pre[:, None] * shared_gate[None, :]
    )
    grad_mid_norm, grad_feedforward_gain = norm_back(
        grad_normed, feedforward_gain, inverse_two, normed_two
    )
    small = jnp.concatenate([grad_feedforward_gain[None], grad_shared_gate[None], grad_router.T])
    small = lax.psum(small, both)
    grad_residual = own_rows(cotangent, tp_index, own_count).astype(f32) + grad_mid_norm
    grad_attention = tensor_gather(grad_residual.astype(bf16), 5).reshape(tok_count, model_width)
    grad_heads = (product(grad_attention, out_full, NT) * valid_rows).astype(bf16)
    grad_queries, grad_kv = attend_back(
        queries, keys_values, query_doc, key_doc, log_totals, grad_heads, cosine, sine
    )
    grad_own_kv = return_keys(grad_kv, cosine, sine, 6)
    grad_raw = jnp.concatenate([grad_queries[None], grad_own_kv])
    grad_attention_bias = jnp.sum(grad_raw.astype(f32), axis=1)
    grad_attention_in, grad_attention_out, tails, grad_input = finish(
        normed_attention,
        grad_raw,
        heads_low,
        grad_attention,
        in_full,
        attention_gain,
        own_rows(layer_input, tp_index, own_count),
        grad_residual,
        grad_attention_bias,
        7,
    )
    grad_attention_bias = lax.dynamic_index_in_dim(tails, tp_index, 0, keepdims=False)[:3]
    grad_attention_gain = jnp.sum(tails[:, 3:], axis=0)[: model_width // tails.shape[2]].reshape(-1)
    return (
        layer_output,
        grad_input.reshape(tok_count, model_width),
        grad_attention_gain,
        grad_attention_in,
        grad_attention_bias,
        grad_attention_out,
        small[0],
        grad_shared_in,
        grad_shared_down,
        small[1],
        small[2:].T,
        grad_expert_in,
        grad_expert_down,
    )


def per_device(*arguments):
    small_slice = lax.axis_size(EP) == RING and lax.axis_size(TP) == 4
    return (per_device_dense if small_slice else per_device_sparse)(*arguments)


def per_device_sparse(
    layer_input,
    attention_gain,
    attention_in,
    attention_bias,
    attention_out,
    feedforward_gain,
    shared_in,
    shared_down,
    shared_gate,
    router,
    expert_in,
    expert_down,
    routes,
    document_lengths,
    cotangent,
):
    bf16 = jnp.bfloat16
    f32 = jnp.float32
    tok_count = layer_input.shape[0]
    model_width = layer_input.shape[1]
    expert_count = router.shape[1]
    top_count = routes.shape[1]
    ep_size = lax.axis_size(EP)
    tp_size = lax.axis_size(TP)
    capacity = tp_size * (
        (5 * tok_count * top_count + 4 * expert_count * tp_size - 1) // (4 * expert_count * tp_size)
    )
    reach_back = min((WINDOW + tok_count - 2) // tok_count, ep_size - 1)
    head_dim = HD
    local_heads = attention_in.shape[2] // head_dim
    score_scale = 1.0 / math.sqrt(head_dim)
    in_full, out_full, shared_in_full, shared_down_full = (
        lax.all_gather(attention_in, EP, axis=1, tiled=True),
        lax.all_gather(attention_out, EP, axis=1, tiled=True),
        lax.all_gather(shared_in, EP, axis=1, tiled=True),
        lax.all_gather(shared_down, EP, axis=1, tiled=True),
    )
    ep_index = lax.axis_index(EP)
    positions = ep_index * tok_count + jnp.arange(tok_count, dtype=jnp.int32)
    key_count = (reach_back + 1) * tok_count
    key_positions = (ep_index - reach_back) * tok_count + jnp.arange(key_count, dtype=jnp.int32)
    query_doc, rope_pos, valid_mask = doc_table(document_lengths, positions)
    key_doc = doc_table(document_lengths, key_positions)[0]
    distance = positions[:, None] - key_positions[None, :]
    allowed = (query_doc[:, None] == key_doc[None, :]) & (distance >= 0) & (distance < WINDOW)
    valid_rows = valid_mask.astype(f32)[:, None]
    cosine, sine_part = rope_angles(rope_pos, head_dim)
    input_rows = layer_input.astype(f32)
    inverse_one, normed_one = rms_parts(input_rows)
    normed_attention = (normed_one * attention_gain).astype(bf16)
    raw_proj = (
        jnp.einsum("td,sde->ste", normed_attention, in_full, preferred_element_type=f32)
        + attention_bias[:, None, :]
    )
    queries = rotate(
        raw_proj[0].reshape(tok_count, local_heads, head_dim), cosine, sine_part, 1.0
    ).astype(bf16)
    keys_own = rotate(
        raw_proj[1].reshape(tok_count, local_heads, head_dim), cosine, sine_part, 1.0
    ).astype(bf16)
    values_own = raw_proj[2].reshape(tok_count, local_heads, head_dim).astype(bf16)
    key_value = jnp.stack([keys_own, values_own])
    earlier = []
    for hop_count in range(reach_back, 0, -1):
        earlier.append(shifted(key_value, EP, hop_count))
    all_kv = jnp.concatenate(earlier + [key_value], axis=1)
    all_keys = all_kv[0]
    all_values = all_kv[1]
    scores = jnp.einsum("qhe,khe->hqk", queries, all_keys, preferred_element_type=f32) * score_scale
    scores = jnp.where(allowed[None], scores, MASKED)
    row_max = jnp.max(scores, axis=-1, keepdims=True)
    exp_terms = jnp.exp(scores - row_max)
    row_total = jnp.sum(exp_terms, axis=-1, keepdims=True)
    log_total = row_max + jnp.log(row_total)
    weights = (exp_terms / row_total).astype(bf16)
    heads_out = jnp.einsum("hqk,khe->qhe", weights, all_values, preferred_element_type=f32).reshape(
        tok_count, -1
    )
    heads_low = (heads_out * valid_rows).astype(bf16)
    attention_sum = tensor_total(jnp.dot(heads_low, out_full, preferred_element_type=f32))
    residual = input_rows + attention_sum
    inverse_two, normed_two = rms_parts(residual)
    normed_ffn = normed_two * feedforward_gain
    normed_low = normed_ffn.astype(bf16)
    shared_pre = jnp.einsum("td,sdf->stf", normed_low, shared_in_full, preferred_element_type=f32)
    shared_silu, shared_slope = silu_parts(shared_pre[0])
    shared_hidden = (shared_silu * shared_pre[1]).astype(bf16)
    shared_out = tensor_total(jnp.dot(shared_hidden, shared_down_full, preferred_element_type=f32))
    shared_scale = jax.nn.sigmoid(jnp.dot(normed_ffn, shared_gate, precision=HIGHEST))
    router_probs = jax.nn.softmax(jnp.dot(normed_ffn, router, precision=HIGHEST), axis=-1)
    chosen = jnp.take_along_axis(router_probs, routes, axis=1)
    chosen_total = jnp.sum(chosen, axis=1, keepdims=True)
    gate_values = chosen / chosen_total
    assign_count = tok_count * top_count
    flat_routes = routes.reshape(-1)
    expert_ids = jnp.arange(expert_count, dtype=jnp.int32)
    one_hot = (flat_routes[:, None] == expert_ids[None, :]).astype(jnp.int32)
    arrival_rank = jnp.sum((jnp.cumsum(one_hot, axis=0) - one_hot) * one_hot, axis=1)
    slot_count = expert_count * capacity
    slot_index = jnp.where(
        arrival_rank < capacity, flat_routes * capacity + arrival_rank, slot_count
    )
    slot_assign = (
        jnp.full((slot_count + 1,), assign_count, jnp.int32)
        .at[slot_index]
        .set(jnp.arange(assign_count, dtype=jnp.int32))[:slot_count]
    )
    slot_token = slot_assign // top_count
    padded_rows = jnp.concatenate([normed_low, jnp.zeros((1, model_width), bf16)])
    send_rows = padded_rows[slot_token].reshape(expert_count, capacity, model_width)

    def expert_trip(outgoing, work):
        row_block = lax.all_to_all(outgoing, EP, split_axis=0, concat_axis=1, tiled=True)
        partial_rows, extras = work(row_block)
        share_rows = lax.psum_scatter(partial_rows, TP, scatter_dimension=1, tiled=True).astype(
            bf16
        )
        whole_rows = lax.all_gather(share_rows, TP, axis=1, tiled=True)
        return (lax.all_to_all(whole_rows, EP, split_axis=1, concat_axis=0, tiled=True), extras)

    def expert_forward(row_block):
        pre_acts = jnp.einsum("erd,esdf->serf", row_block, expert_in, preferred_element_type=f32)
        gate_silu, gate_slope = silu_parts(pre_acts[0])
        hidden = (gate_silu * pre_acts[1]).astype(bf16)
        partial_rows = jnp.einsum("erf,efd->erd", hidden, expert_down, preferred_element_type=f32)
        return (partial_rows, (row_block, pre_acts, hidden, gate_silu, gate_slope))

    returned_rows, kept_state = expert_trip(send_rows, expert_forward)
    expert_rows, expert_pre, expert_hidden, expert_silu, expert_slope = kept_state
    padded_back = jnp.concatenate(
        [returned_rows.reshape(slot_count, model_width), jnp.zeros((1, model_width), bf16)]
    )
    picked = padded_back[slot_index].reshape(tok_count, top_count, model_width).astype(f32)
    moe_sum = jnp.sum(gate_values[:, :, None] * picked, axis=1)
    layer_output = (residual + shared_scale[:, None] * shared_out + moe_sum).astype(bf16)
    grad_rows = cotangent.astype(f32)
    padded_grad = jnp.concatenate([grad_rows, jnp.zeros((1, model_width), f32)])
    padded_gates = jnp.concatenate([gate_values.reshape(-1), jnp.zeros((1,), f32)])
    grad_send = (padded_gates[slot_assign][:, None] * padded_grad[slot_token]).astype(bf16)
    grad_send = grad_send.reshape(expert_count, capacity, model_width)

    def expert_backward(grad_block):
        grad_down = jnp.einsum(
            "erf,erd->efd", expert_hidden, grad_block, preferred_element_type=f32
        )
        grad_hidden = jnp.einsum(
            "erd,efd->erf", grad_block, expert_down, preferred_element_type=f32
        )
        grad_pre = jnp.stack(
            [grad_hidden * expert_pre[1] * expert_slope, grad_hidden * expert_silu]
        ).astype(bf16)
        grad_weights_in = jnp.einsum(
            "erd,serf->esdf", expert_rows, grad_pre, preferred_element_type=f32
        )
        grad_back_rows = jnp.einsum(
            "serf,esdf->erd", grad_pre, expert_in, preferred_element_type=f32
        )
        return (grad_back_rows, (grad_weights_in, grad_down))

    grad_returned, expert_grads = expert_trip(grad_send, expert_backward)
    grad_expert_in, grad_expert_down = expert_grads
    grad_gate_values = jnp.sum(picked * grad_rows[:, None, :], axis=2)
    grad_chosen = (
        grad_gate_values - jnp.sum(grad_gate_values * gate_values, axis=1, keepdims=True)
    ) / chosen_total
    grad_probs = jnp.sum(
        jnp.where(routes[:, :, None] == expert_ids[None, None, :], grad_chosen[:, :, None], 0.0),
        axis=1,
    )
    grad_logits = router_probs * (
        grad_probs - jnp.sum(grad_probs * router_probs, axis=1, keepdims=True)
    )
    grad_router = jnp.einsum("td,te->de", normed_ffn, grad_logits, precision=HIGHEST)
    grad_shared_out = (shared_scale[:, None] * grad_rows).astype(bf16)
    grad_shared_down = jnp.einsum(
        "tf,td->fd", shared_hidden, grad_shared_out, preferred_element_type=f32
    )
    grad_shared_hidden = jnp.einsum(
        "td,fd->tf", grad_shared_out, shared_down_full, preferred_element_type=f32
    )
    grad_shared_pre = jnp.stack(
        [grad_shared_hidden * shared_pre[1] * shared_slope, grad_shared_hidden * shared_silu]
    ).astype(bf16)
    grad_shared_in = jnp.einsum(
        "td,stf->sdf", normed_low, grad_shared_pre, preferred_element_type=f32
    )
    shared_back = jnp.einsum(
        "stf,sdf->td", grad_shared_pre, shared_in_full, preferred_element_type=f32
    )
    grad_scale_pre = jnp.sum(grad_rows * shared_out, axis=1) * shared_scale * (1.0 - shared_scale)
    grad_shared_gate = jnp.dot(grad_scale_pre, normed_ffn, precision=HIGHEST)
    padded_return = jnp.concatenate(
        [grad_returned.reshape(slot_count, model_width), jnp.zeros((1, model_width), bf16)]
    )
    moe_back = jnp.sum(
        padded_return[slot_index].reshape(tok_count, top_count, model_width).astype(f32), axis=1
    )
    grad_normed = (
        tensor_total(shared_back)
        + moe_back
        + jnp.einsum("te,de->td", grad_logits, router, precision=HIGHEST)
        + grad_scale_pre[:, None] * shared_gate[None, :]
    )
    grad_mid_norm, grad_feedforward_gain = norm_back(
        grad_normed, feedforward_gain, inverse_two, normed_two
    )
    grad_residual = grad_rows + grad_mid_norm
    grad_attention = grad_residual.astype(bf16)
    grad_attention_out = jnp.einsum(
        "tf,td->fd", heads_low, grad_attention, preferred_element_type=f32
    )
    grad_heads = jnp.einsum(
        "td,fd->tf", grad_attention, out_full, preferred_element_type=f32
    ).astype(bf16)
    grad_heads = (grad_heads * valid_rows.astype(bf16)).reshape(tok_count, local_heads, head_dim)
    scores_again = (
        jnp.einsum("qhe,khe->hqk", queries, all_keys, preferred_element_type=f32) * score_scale
    )
    scores_again = jnp.where(allowed[None], scores_again, MASKED)
    softmax_out = jnp.exp(scores_again - log_total)
    weights_again = softmax_out.astype(bf16)
    grad_weights = jnp.einsum("qhe,khe->hqk", grad_heads, all_values, preferred_element_type=f32)
    grad_scores = (
        softmax_out * (grad_weights - jnp.sum(softmax_out * grad_weights, axis=-1, keepdims=True))
    ).astype(bf16)
    grad_queries = (
        jnp.einsum("hqk,khe->qhe", grad_scores, all_keys, preferred_element_type=f32) * score_scale
    )
    grad_keys = (
        jnp.einsum("hqk,qhe->khe", grad_scores, queries, preferred_element_type=f32) * score_scale
    )
    grad_values = jnp.einsum("hqk,qhe->khe", weights_again, grad_heads, preferred_element_type=f32)
    grad_kv = jnp.stack([grad_keys, grad_values])
    own_part = grad_kv[:, reach_back * tok_count :]
    for hop_count in range(1, reach_back + 1):
        segment_start = (reach_back - hop_count) * tok_count
        segment = grad_kv[:, segment_start : segment_start + tok_count]
        own_part = own_part + shifted(segment, EP, -hop_count)
    grad_raw = (
        jnp.stack(
            [
                rotate(grad_queries, cosine, sine_part, -1.0),
                rotate(own_part[0], cosine, sine_part, -1.0),
                own_part[1],
            ]
        )
        .reshape(3, tok_count, -1)
        .astype(bf16)
    )
    grad_attention_bias = jnp.sum(grad_raw.astype(f32), axis=1)
    grad_attention_in = jnp.einsum(
        "td,ste->sde", normed_attention, grad_raw, preferred_element_type=f32
    )
    grad_normed_attention = tensor_total(
        jnp.einsum("ste,sde->td", grad_raw, in_full, preferred_element_type=f32)
    )
    grad_in_norm, grad_attention_gain = norm_back(
        grad_normed_attention, attention_gain, inverse_one, normed_one
    )
    grad_input = (grad_residual + grad_in_norm).astype(bf16)
    grad_attention_in, grad_attention_out, grad_shared_in, grad_shared_down = (
        lax.psum_scatter(
            grad_attention_in.astype(jnp.bfloat16), EP, scatter_dimension=1, tiled=True
        ).astype(jnp.float32),
        lax.psum_scatter(
            grad_attention_out.astype(jnp.bfloat16), EP, scatter_dimension=1, tiled=True
        ).astype(jnp.float32),
        lax.psum_scatter(
            grad_shared_in.astype(jnp.bfloat16), EP, scatter_dimension=1, tiled=True
        ).astype(jnp.float32),
        lax.psum_scatter(
            grad_shared_down.astype(jnp.bfloat16), EP, scatter_dimension=1, tiled=True
        ).astype(jnp.float32),
    )
    (
        grad_attention_gain,
        grad_attention_bias,
        grad_feedforward_gain,
        grad_shared_gate,
        grad_router,
    ) = (
        lax.psum(grad_attention_gain.astype(jnp.bfloat16), EP).astype(jnp.float32),
        lax.psum(grad_attention_bias.astype(jnp.bfloat16), EP).astype(jnp.float32),
        lax.psum(grad_feedforward_gain.astype(jnp.bfloat16), EP).astype(jnp.float32),
        lax.psum(grad_shared_gate.astype(jnp.bfloat16), EP).astype(jnp.float32),
        lax.psum(grad_router.astype(jnp.bfloat16), EP).astype(jnp.float32),
    )
    return (
        layer_output,
        grad_input,
        grad_attention_gain,
        grad_attention_in,
        grad_attention_bias,
        grad_attention_out,
        grad_feedforward_gain,
        grad_shared_in,
        grad_shared_down,
        grad_shared_gate,
        grad_router,
        grad_expert_in,
        grad_expert_down,
    )


def solution(mesh):
    return jax.shard_map(
        per_device,
        mesh=mesh,
        in_specs=(
            P(EP, None),
            P(),
            P(None, EP, TP),
            P(None, TP),
            P(TP, EP),
            P(),
            P(None, EP, TP),
            P(TP, EP),
            P(),
            P(),
            P(EP, None, None, TP),
            P(EP, TP, None),
            P(EP, None),
            P(),
            P(EP, None),
        ),
        out_specs=(
            P(EP, None),
            P(EP, None),
            P(),
            P(None, EP, TP),
            P(None, TP),
            P(TP, EP),
            P(),
            P(None, EP, TP),
            P(TP, EP),
            P(),
            P(),
            P(EP, None, None, TP),
            P(EP, TP, None),
        ),
        check_vma=False,
    )
```

```python
import functools
import math

import jax
import jax.numpy as jnp
from jax import lax
from jax.experimental import pallas as pl
from jax.experimental.pallas import tpu as pltpu
from jax.sharding import PartitionSpec as P

EP, TP = "ep", "tp"
HD = 128
WINDOW = 1024


HIGHEST = lax.Precision.HIGHEST
EPSILON = 1e-06
ROPE_BASE = 1000000.0
MASKED = -1000000000.0


def shifted(value, axis, steps):
    count = lax.axis_size(axis)
    leading, last = (max(0, -steps), min(count, count - steps))
    return lax.ppermute(value, axis, [(source, source + steps) for source in range(leading, last)])


def tensor_total(partial_sum):
    return lax.psum(partial_sum, TP)


def rms_parts(values):
    inverse = lax.rsqrt(jnp.mean(values * values, axis=-1, keepdims=True) + EPSILON)
    return (inverse, values * inverse)


def norm_back(grad_rows, gain_vec, inverse, normed):
    scaled = grad_rows * gain_vec
    grad_in = inverse * (scaled - normed * jnp.mean(scaled * normed, axis=-1, keepdims=True))
    return (grad_in, jnp.sum(grad_rows * normed, axis=0))


def doc_table(document_lengths, positions):
    doc_ends = jnp.cumsum(document_lengths)
    starts_all = jnp.concatenate([doc_ends - document_lengths, doc_ends[-1:]])
    doc_ids = jnp.sum((positions[:, None] >= doc_ends[None, :]).astype(jnp.int32), axis=1)
    matches = (
        doc_ids[:, None] == jnp.arange(document_lengths.shape[0] + 1, dtype=jnp.int32)[None, :]
    )
    doc_begin = jnp.sum(jnp.where(matches, starts_all[None, :], 0), axis=1)
    rope_pos = positions - doc_begin
    valid_mask = positions < doc_ends[-1]
    doc_ids = jnp.where(positions < 0, -1, doc_ids)
    return (doc_ids, rope_pos, valid_mask)


def rope_angles(rope_pos, head_dim):
    half_width = head_dim // 2
    freqs = jnp.power(ROPE_BASE, -2.0 * jnp.arange(half_width, dtype=jnp.float32) / head_dim)
    angles = rope_pos.astype(jnp.float32)[:, None] * freqs[None, :]
    return (jnp.cos(angles)[:, None, :], jnp.sin(angles)[:, None, :])


def rotate(values, cosine, sine_part, turn_sign):
    half_width = values.shape[-1] // 2
    first_part = values[..., :half_width]
    second_part = values[..., half_width:]
    return jnp.concatenate(
        [
            first_part * cosine - turn_sign * second_part * sine_part,
            second_part * cosine + turn_sign * first_part * sine_part,
        ],
        axis=-1,
    )


def silu_parts(gate_pre):
    sig_gate = jax.nn.sigmoid(gate_pre)
    return (gate_pre * sig_gate, sig_gate * (1.0 + gate_pre * (1.0 - sig_gate)))


NN = (((1,), (0,)), ((), ()))
NT = (((1,), (1,)), ((), ()))
TN = (((0,), (0,)), ((), ()))


def product(left, right, dims=NN):
    return lax.dot_general(left, right, dims, preferred_element_type=jnp.float32)


def turned(values, cosine, sine):
    half = values.shape[1] // 2
    swapped = jnp.concatenate([values[:, half:], values[:, :half]], axis=1)
    return values * cosine + swapped * sine


def masked_scores(queries, keys, query_doc, key_doc):
    tokens, count = queries.shape[0], keys.shape[0]
    scores = product(queries, keys, NT) * (1.0 / math.sqrt(HD))
    ahead = lax.broadcasted_iota(jnp.int32, (tokens, count), 0) + (count - tokens)
    distance = ahead - lax.broadcasted_iota(jnp.int32, (tokens, count), 1)
    allowed = (query_doc == key_doc) & (distance >= 0) & (distance < WINDOW)
    return jnp.where(allowed, scores, MASKED)


def attend_kernel(queries, keys, values, query_doc, key_doc, valid, heads, log_totals):
    count = keys.shape[1] * keys.shape[2]
    keys, values = keys[0].reshape(count, HD), values[0].reshape(count, HD)
    scores = masked_scores(queries[...], keys, query_doc[...], key_doc[...])
    row_max = jnp.max(scores, axis=1, keepdims=True)
    terms = jnp.exp(scores - row_max)
    total = jnp.sum(terms, axis=1, keepdims=True)
    weights = (terms / total).astype(jnp.bfloat16)
    heads[...] = (product(weights, values) * valid[...]).astype(jnp.bfloat16)
    log_totals[0] = row_max + jnp.log(total)


def attention_specs(tokens, blocks):
    def column(*dims):
        return pl.BlockSpec(dims, lambda h: (0,) * len(dims))

    head = pl.BlockSpec((tokens, HD), lambda h: (0, h))
    keys = pl.BlockSpec((1, blocks, tokens, HD), lambda h: (0, 0, 0, h))
    values = pl.BlockSpec((1, blocks, tokens, HD), lambda h: (1, 0, 0, h))
    logs = pl.BlockSpec((1, tokens, 1), lambda h: (h, 0, 0))
    return head, keys, values, column(tokens, 1), column(1, blocks * tokens), logs


def attend(queries, keys_values, query_doc, key_doc, valid):
    tokens, columns = queries.shape
    blocks = keys_values.shape[1]
    head, keys, values, column, row, logs = attention_specs(tokens, blocks)
    shape = jax.ShapeDtypeStruct
    return pl.pallas_call(
        attend_kernel,
        grid=(columns // HD,),
        in_specs=[head, keys, values, column, row, column],
        out_specs=(head, logs),
        out_shape=(
            shape((tokens, columns), jnp.bfloat16),
            shape((columns // HD, tokens, 1), jnp.float32),
        ),
        compiler_params=pltpu.CompilerParams(vmem_limit_bytes=40 * 2**20),
        name="attend",
    )(queries, keys_values, keys_values, query_doc, key_doc, valid)


def attend_back_kernel(
    queries, keys, values, query_doc, key_doc, log_totals, grad_heads, cosine, sine,
    grad_queries, grad_keys_values,
):
    bf16 = jnp.bfloat16
    scale = 1.0 / math.sqrt(HD)
    blocks, tokens = keys.shape[1], keys.shape[2]
    keys, values = (ref[0].reshape(blocks * tokens, HD) for ref in (keys, values))
    scores = masked_scores(queries[...], keys, query_doc[...], key_doc[...])
    probs = jnp.exp(scores - log_totals[0])
    grads = grad_heads[...]
    slopes = product(grads, values, NT)
    slopes = probs * (slopes - jnp.sum(probs * slopes, axis=1, keepdims=True))
    grad_scores = slopes.astype(bf16)
    turned_back = turned(product(grad_scores, keys) * scale, cosine[...], -sine[...])
    grad_queries[...] = turned_back.astype(bf16)
    grad_keys = product(grad_scores, queries[...], TN) * scale
    grad_keys_values[0] = grad_keys.astype(bf16).reshape(blocks, tokens, HD)
    grad_values = product(probs.astype(bf16), grads, TN)
    grad_keys_values[1] = grad_values.astype(bf16).reshape(blocks, tokens, HD)


def attend_back(queries, keys_values, query_doc, key_doc, log_totals, grad_heads, cosine, sine):
    tokens, columns = queries.shape
    blocks = keys_values.shape[1]
    head, keys, values, column, row, logs = attention_specs(tokens, blocks)
    angle = pl.BlockSpec((tokens, HD), lambda h: (0, 0))
    shape = jax.ShapeDtypeStruct
    return pl.pallas_call(
        attend_back_kernel,
        grid=(columns // HD,),
        in_specs=[head, keys, values, column, row, logs, head, angle, angle],
        out_specs=(head, pl.BlockSpec((2, blocks, tokens, HD), lambda h: (0, 0, 0, h))),
        out_shape=(
            shape((tokens, columns), jnp.bfloat16),
            shape(keys_values.shape, jnp.bfloat16),
        ),
        compiler_params=pltpu.CompilerParams(vmem_limit_bytes=48 * 2**20),
        name="attend_back",
    )(queries, keys_values, keys_values, query_doc, key_doc, log_totals, grad_heads, cosine, sine)


RING = 8
NO_SLOT = 1 << 20
RIGHT, LEFT, OVER_X, OVER_CORE, OVER_FAR, LOCAL, SCALARS = range(7)
MESH_ID = pl.DeviceIdType.MESH


def ring_place(ep):
    z, y = ep // 2, ep % 2
    return z + y * (7 - 2 * z)


def ring_member(place):
    upper = place // 4
    return 2 * place + upper * (15 - 4 * place)


class Peers:
    def __init__(self):
        self.ep, self.tp = lax.axis_index(EP), lax.axis_index(TP)
        self.x, self.core = self.tp // 2, self.tp % 2
        self.z, self.y = self.ep // 2, self.ep % 2
        self.place = ring_place(self.ep)
        self.right = (self.block(1), self.tp)
        self.left = (self.block(RING - 1), self.tp)
        self.quarter = self.tp
        self.x_quarter = (1 - self.x) * 2 + self.core
        self.core_quarter = self.x * 2 + 1 - self.core
        self.far_quarter = (1 - self.x) * 2 + 1 - self.core
        self.x_peer = (self.ep, self.x_quarter)
        self.core_peer = (self.ep, self.core_quarter)
        self.far_peer = (self.ep, self.far_quarter)
        self.y_peer = (self.z * 2 + 1 - self.y, self.tp)

    def block(self, step):
        return ring_member((self.place + step + RING) % RING)


def greet(peers):
    barrier = pltpu.get_barrier_semaphore()
    for peer in peers:
        pl.semaphore_signal(barrier, inc=1, device_id=peer, device_id_type=MESH_ID)
    pl.semaphore_wait(barrier, len(peers))


class Copies:
    def __init__(self, send_sems, recv_sems):
        self.send_sems, self.recv_sems = send_sems, recv_sems
        self.count = 0
        self.sent = []
        self.landing = {}

    def describe(self, source, target, peer, index):
        return pltpu.make_async_remote_copy(
            src_ref=source,
            dst_ref=target,
            send_sem=self.send_sems.at[index],
            recv_sem=self.recv_sems.at[index],
            device_id=peer,
            device_id_type=MESH_ID,
        )

    def send(self, key, source, target, landing, peer):
        index = self.count
        self.count += 1
        copy = self.describe(source, target, peer, index)
        copy.start()
        self.sent.append(copy)
        self.landing[key] = self.describe(landing, landing, peer, index).wait_recv

    def local(self, key, source, target):
        index = self.count
        self.count += 1
        copy = pltpu.make_async_copy(source, target, self.send_sems.at[index])
        copy.start()
        self.landing[key] = copy.wait

    def arrive(self, *key):
        self.landing.pop(key)()

    def finish(self):
        for wait in self.landing.values():
            wait()
        for copy in self.sent:
            copy.wait_send()


def remote_params(collective_id, vmem=48):
    return pltpu.CompilerParams(
        collective_id=collective_id, has_side_effects=True, vmem_limit_bytes=vmem * 2**20
    )


def semaphores(count):
    return [pltpu.SemaphoreType.DMA((count,))] * 2


IN_PLACE = pl.BlockSpec(memory_space=pl.ANY)
IN_VMEM = pl.BlockSpec(memory_space=pltpu.VMEM)


class LateCopies(Copies):
    def send(self, key, source, target, landing, peer):
        index = self.count
        self.count += 1
        self.describe(source(), target(), peer, index).start()
        self.sent.append(lambda: self.describe(source(), target(), peer, index).wait_send())
        self.landing[key] = lambda: self.describe(landing(), landing(), peer, index).wait_recv()

    def local(self, key, source, target):
        index = self.count
        self.count += 1

        def copy():
            return pltpu.make_async_copy(source(), target(), self.send_sems.at[index])

        copy().start()
        self.landing[key] = lambda: copy().wait()

    def finish(self):
        for wait in list(self.landing.values()) + self.sent:
            wait()


def feed_block(
    block, rank_row, rank_column, gate_rows, scale, token_rows, token_cotangent,
    expert_in, expert_down, shared, staged, between, out_terms, back_terms, scale_grad, token_grad,
):
    (
        out_part, back_part, slot_rows, slot_cotangent, grad_pre, gated, grad_shared_pre, scaled,
    ) = staged
    bf16, f32 = jnp.bfloat16, jnp.float32
    experts, slots, _ = slot_rows.shape
    tokens = token_rows.shape[0]
    hidden_count = gated.shape[2]
    all_slots = experts * slots
    silu, slope = silu_parts(product(token_rows, shared[0], NT))
    up = product(token_rows, shared[1], NT)
    hidden = (silu * up).astype(bf16).astype(f32)
    scaled_hidden = (scale * hidden).astype(bf16)
    back = product(token_cotangent, shared[2], NT)
    scale_grad[block] = jnp.sum(hidden * back, axis=1, keepdims=True)
    back = scale * back
    gate_grad = (back * up * slope).astype(bf16)
    up_grad = (back * silu).astype(bf16)
    between()
    scaled[...] = scaled_hidden
    grad_shared_pre[0] = gate_grad
    grad_shared_pre[1] = up_grad
    order = lax.broadcasted_iota(jnp.int32, (all_slots, tokens), 0)
    spread_order = lax.broadcasted_iota(jnp.int32, (tokens, all_slots), 1)
    hits, spread = None, None
    for expert in range(experts):
        row_hits = order == rank_row[expert : expert + 1, :] + expert * slots
        column_hits = spread_order == rank_column[:, expert : expert + 1] + expert * slots
        hits = row_hits if hits is None else hits | row_hits
        spread = column_hits if spread is None else spread | column_hits
    place = hits.astype(bf16)
    taken = product(place, token_rows).astype(bf16)
    taken_cotangent = product(place, token_cotangent).astype(bf16)
    for ref, values in ((slot_rows, taken), (slot_cotangent, taken_cotangent)):
        for expert in range(experts):
            ref[expert] = values[expert * slots : (expert + 1) * slots]
    for expert in range(experts):
        mine = slice(expert * slots, (expert + 1) * slots)
        gate = jnp.sum(
            jnp.where(hits[mine], gate_rows[expert : expert + 1], 0.0), axis=1, keepdims=True
        )
        pre = product(taken[mine], expert_in[expert], NT)
        silu, slope = silu_parts(pre[:, :hidden_count])
        up = pre[:, hidden_count:]
        hidden = (silu * up).astype(bf16).astype(f32)
        gated_hidden = (gate * hidden).astype(bf16)
        gated[expert] = gated_hidden
        back = product(taken_cotangent[mine], expert_down[expert], NT)
        slot_grad = jnp.sum(hidden * back, axis=1, keepdims=True)
        token_grad[block, expert : expert + 1, :] = jnp.sum(
            jnp.where(hits[mine], slot_grad, 0.0), axis=0, keepdims=True
        )
        back = gate * back
        gate_grad_e = (back * up * slope).astype(bf16)
        up_grad_e = (back * silu).astype(bf16)
        grad_pre[0, expert] = gate_grad_e
        grad_pre[1, expert] = up_grad_e
        out_terms[mine, :] = product(gated_hidden, expert_down[expert]).astype(bf16)
        both_grads = jnp.concatenate([gate_grad_e, up_grad_e], axis=1)
        back_terms[mine, :] = product(both_grads, expert_in[expert]).astype(bf16)
    spread = spread.astype(bf16)
    out_part[...] = product(
        jnp.concatenate([spread, scaled_hidden], axis=1), out_terms[...]
    ).astype(bf16)
    back_part[...] = product(
        jnp.concatenate([spread, gate_grad, up_grad], axis=1), back_terms[...]
    ).astype(bf16)


def gather_feed_kernel(
    rows, cotangent, scales, rank_row, rank_column, expert_in, expert_down, shared,
    all_rows, all_cotangent, all_scales,
    out_part, back_part, slot_rows, slot_cotangent, grad_pre, gated, grad_shared_pre, scaled,
    token_grad, scale_grad,
    out_terms, back_terms, held_rows, held_cotangent,
    stage_out, stage_back, stage_rows, stage_cotangent, stage_pre, stage_gated, stage_shared,
    stage_scaled,
    load_sems, store_sems, send_sems, recv_sems,
):
    me = Peers()
    copies = LateCopies(send_sems, recv_sems)
    count = rows.shape[0]
    half, part = count // 2, count // 4
    q, qx, qc, qd = me.quarter, me.x_quarter, me.core_quarter, me.far_quarter
    blocks = {step: me.block(step) for step in range(-4, 5)}
    low, high, whole = pl.ds(0, half), pl.ds(half, half), pl.ds(0, count)
    own, other, scale = range(3)
    full = (all_rows, all_cotangent)
    sides = ((RIGHT, me.right, -1, 0), (LEFT, me.left, 1, 1))
    greet([me.right, me.left, me.x_peer, me.core_peer, me.far_peer])

    def push(key, kind, step, quarter, which, peer, landing_step, landing_quarter, source=None):
        def cell():
            return full[kind].at[blocks[step], quarter, which]

        def landing():
            return full[kind].at[blocks[landing_step], landing_quarter, which]

        copies.send((kind,) + key, source or cell, cell, landing, peer)

    push((OVER_X, other, 0), 0, 0, q, low, me.x_peer, 0, qx, lambda: rows.at[low])
    for side, peer, sign, keep in sides:
        push((side, own, 1), 1, 0, q, whole, peer, sign, q, lambda: cotangent.at[q])
        push((side, other, 1), 1, 0, qx, low, peer, sign, qx, lambda: cotangent.at[qx, low])
    push((OVER_X, own, 0), 0, 0, q, high, me.x_peer, 0, qx, lambda: rows.at[high])
    push((OVER_CORE, own, 0), 0, 0, q, whole, me.core_peer, 0, qc, lambda: rows)
    for side, peer, sign, keep in sides:
        push((side, own, 1), 0, 0, q, whole, peer, sign, q, lambda: rows)
    copies.local((LOCAL, 0), lambda: rows, lambda: all_rows.at[blocks[0], q])
    copies.local((LOCAL, 1), lambda: cotangent, lambda: all_cotangent.at[blocks[0]])

    def scales_of(quarter):
        return lambda: all_scales.at[blocks[0], quarter]

    for way, peer, quarter in (
        (OVER_X, me.x_peer, qx),
        (OVER_CORE, me.core_peer, qc),
        (OVER_FAR, me.far_peer, qd),
    ):
        copies.send((way, scale, 0), lambda: scales, scales_of(q), scales_of(quarter), peer)
    copies.local((LOCAL, scale), lambda: scales, scales_of(q))
    experts, _, width = expert_in.shape
    all_slots = experts * slot_rows.shape[2]
    shared_count = shared.shape[1]
    out_terms[all_slots:, :] = shared[2]
    back_terms[all_slots : all_slots + shared_count, :] = shared[0]
    back_terms[all_slots + shared_count :, :] = shared[1]
    copies.arrive(0, OVER_X, other, 0)
    for side, peer, sign, keep in sides:
        push((side, other, 1), 0, 0, qx, low, peer, sign, qx)
    for way in (OVER_X, OVER_CORE, OVER_FAR):
        copies.arrive(way, scale, 0)
    copies.arrive(LOCAL, scale)

    def push_scales(step, side, peer, sign):
        def cell():
            return all_scales.at[blocks[step]]

        copies.send(
            (side, scale, abs(step) + 1), cell, cell, lambda: all_scales.at[blocks[step + sign]], peer
        )

    for side, peer, sign, keep in sides:
        push_scales(0, side, peer, sign)
    copies.arrive(0, OVER_X, own, 0)
    push((OVER_CORE, other, 0), 0, 0, qx, whole, me.core_peer, 0, qd)

    def hop_in(kind, hop):
        for side, peer, sign, keep in sides:
            step = sign * hop
            if hop < 4:
                copies.arrive(kind, side, own, hop)
                which = whole if hop < 3 else pl.ds(keep * half, half)
                push((side, own, hop + 1), kind, step, q, which, peer, step + sign, q)
                push((OVER_X, own, step), kind, step, q, high, me.x_peer, step, qx)
                push((OVER_CORE, own, step), kind, step, q, whole, me.core_peer, step, qc)
                copies.arrive(kind, side, other, hop)
                which = low if hop < 3 else pl.ds(keep * part, part)
                push((side, other, hop + 1), kind, step, qx, which, peer, step + sign, qx)
                push((OVER_CORE, other, step), kind, step, qx, low, me.core_peer, step, qd)
        if hop == 4:
            copies.arrive(kind, LEFT, own, 4)
            push((OVER_X, own, 4), kind, 4, q, high, me.x_peer, 4, qx)
            copies.arrive(kind, RIGHT, own, 4)
            push((OVER_CORE, own, 4), kind, 4, q, whole, me.core_peer, 4, qc)
            copies.arrive(kind, LEFT, other, 4)
            copies.arrive(kind, RIGHT, other, 4)
            push((OVER_CORE, other, 4), kind, 4, qx, low, me.core_peer, 4, qd)

    def over_x(kind, steps):
        for step in steps:
            copies.arrive(kind, OVER_X, own, step)
            push((OVER_CORE, scale, step), kind, step, qx, high, me.core_peer, step, qd)

    def scales_in(hop):
        for side, peer, sign, keep in sides:
            if hop < 4 or side == RIGHT:
                copies.arrive(side, scale, hop)
                if hop < 3 or (hop == 3 and side == RIGHT):
                    push_scales(sign * hop, side, peer, sign)

    def load(slot, step):
        pairs = ((all_rows, held_rows), (all_cotangent, held_cotangent))
        return [
            pltpu.make_async_copy(source.at[blocks[step]], held.at[slot], load_sems.at[slot, kind])
            for kind, (source, held) in enumerate(pairs)
        ]

    def complete(steps, slots):
        for step in steps:
            for kind in range(2):
                if step != 0:
                    for piece in (own, other, scale):
                        copies.arrive(kind, OVER_CORE, piece, step)
        moves = [load(slot, step) for slot, step in zip(slots, steps)]
        for move in moves[0] + moves[-1] if len(moves) > 1 else moves[0]:
            move.start()
        for move in moves[0]:
            move.wait()

    staged = (
        stage_out, stage_back, stage_rows, stage_cotangent, stage_pre, stage_gated, stage_shared,
        stage_scaled,
    )

    def stores(block):
        targets = (
            out_part.at[block], back_part.at[block], slot_rows.at[:, block],
            slot_cotangent.at[:, block], grad_pre.at[:, :, block], gated.at[:, block],
            grad_shared_pre.at[:, block], scaled.at[block],
        )
        return [
            pltpu.make_async_copy(stage, target, store_sems.at[index])
            for index, (stage, target) in enumerate(zip(staged, targets))
        ]

    first_expert = me.ep * experts

    copies.arrive(LOCAL, 0)
    copies.arrive(LOCAL, 1)
    for piece in (own, other):
        copies.arrive(0, OVER_CORE, piece, 0)
    complete((0,), (0,))

    def turn(index, carry):
        far = (index + 1) // 2
        step = far * (1 - 2 * (index % 2)) + (index // 7) * 8
        block = ring_member((me.place + step + RING) % RING)
        slot = index % 2

        def between():
            for hop in (1, 2, 3, 4):

                @pl.when(index == max(0, 2 * hop - 3))
                def _():
                    hop_in(1, hop)

            @pl.when(index > 0)
            def _():
                for move in stores(0):
                    move.wait()

        rows_here = held_rows[slot].reshape(4 * count, width)
        cotangent_here = held_cotangent[slot].reshape(4 * count, width)
        quarters = [all_scales[block, quarter] for quarter in range(4)]
        columns = jnp.concatenate([jnp.swapaxes(values, 0, 1) for values in quarters], axis=0)
        scale_at = me_scale_row(all_scales, experts)
        gate_rows = [
            jnp.concatenate(
                [all_scales[block, quarter, pl.ds(first_expert + e, 1), :] for quarter in range(4)],
                axis=1,
            )
            for e in range(experts)
        ]
        feed_block(
            block,
            rank_row[block],
            rank_column[block],
            jnp.concatenate(gate_rows, axis=0),
            columns[:, scale_at : scale_at + 1],
            rows_here,
            cotangent_here,
            expert_in,
            expert_down,
            shared,
            staged,
            between,
            out_terms,
            back_terms,
            scale_grad,
            token_grad,
        )
        for move in stores(block):
            move.start()

        for hop in (1, 2, 3, 4):

            @pl.when(index == max(0, 2 * hop - 3))
            def _():
                scales_in(hop)
                hop_in(0, hop)
                if hop > 1:
                    for move in load(0, hop - 1):
                        move.wait()

            @pl.when(index == 2 * hop - 2)
            def _():
                steps = (-hop, hop) if hop < 4 else (4,)
                over_x(1, steps)
                over_x(0, steps)
                complete(steps, (1, 0))

        return carry

    lax.fori_loop(0, RING, turn, 0)
    for move in stores(0):
        move.wait()
    copies.finish()


def me_scale_row(all_scales, experts):
    return RING * experts


def gather_feed(
    rows, cotangent, scales, rank, expert_in, expert_down, shared, capacity, collective_id
):
    bf16, f32 = jnp.bfloat16, jnp.float32
    blocks, experts, tokens = rank.shape
    count, width = rows.shape
    hidden = expert_in.shape[1] // 2
    slice_hidden = shared.shape[1]
    shape = jax.ShapeDtypeStruct
    stages = (
        (tokens, width),
        (tokens, width),
        (experts, capacity, width),
        (experts, capacity, width),
        (2, experts, capacity, hidden),
        (experts, capacity, hidden),
        (2, tokens, slice_hidden),
        (tokens, slice_hidden),
    )
    return pl.pallas_call(
        gather_feed_kernel,
        out_shape=(
            shape((RING, 4, count, width), bf16),
            shape((RING, 4, count, width), bf16),
            shape((RING, 4) + scales.shape, f32),
            shape((blocks, tokens, width), bf16),
            shape((blocks, tokens, width), bf16),
            shape((experts, blocks, capacity, width), bf16),
            shape((experts, blocks, capacity, width), bf16),
            shape((2, experts, blocks, capacity, hidden), bf16),
            shape((experts, blocks, capacity, hidden), bf16),
            shape((2, blocks, tokens, slice_hidden), bf16),
            shape((blocks, tokens, slice_hidden), bf16),
            shape((blocks, experts, tokens), f32),
            shape((blocks, tokens, 1), f32),
        ),
        in_specs=[IN_VMEM] * 8,
        out_specs=(IN_PLACE,) * 2 + (IN_VMEM,) + (IN_PLACE,) * 8 + (IN_VMEM,) * 2,
        scratch_shapes=[
            pltpu.VMEM((experts * capacity + slice_hidden, width), bf16),
            pltpu.VMEM((experts * capacity + 2 * slice_hidden, width), bf16),
            pltpu.VMEM((2, 4, count, width), bf16),
            pltpu.VMEM((2, 4, count, width), bf16),
        ]
        + [pltpu.VMEM(stage, bf16) for stage in stages]
        + [pltpu.SemaphoreType.DMA((2, 2)), pltpu.SemaphoreType.DMA((len(stages),))]
        + semaphores(160),
        compiler_params=remote_params(collective_id, 62),
        name="gather_feed",
    )(
        rows, cotangent, scales, rank, jnp.swapaxes(rank, 1, 2), expert_in, expert_down, shared,
    )


def add_into(total, term, rows, tile=32):
    tile = min(tile, rows)

    def step(index, carry):
        here = pl.ds(pl.multiple_of(index * tile, tile), tile)
        summed = total[here, :].astype(jnp.float32) + term[here, :].astype(jnp.float32)
        total[here, :] = summed.astype(total.dtype)
        return carry

    lax.fori_loop(0, rows // tile, step, 0)


class WeightGrads:
    def __init__(self, jobs, left, right, sums, low, sems, out_sems):
        self.jobs, self.left, self.right = jobs, left, right
        self.sums, self.low, self.sems, self.out_sems = sums, low, sems, out_sems
        self.next = 0
        self.stores = {}
        self.fetch(0, 0, 0).start()

    def fetch(self, job, index, slot):
        left, right, _ = self.jobs[job]
        chunk, rows, columns, _ = self.size(job)
        here = pl.ds(pl.multiple_of(index * chunk, chunk), chunk)
        return Pair(
            pltpu.make_async_copy(
                left.at[here], self.left[rows].at[slot, pl.ds(0, chunk)], self.sems.at[slot, 0]
            ),
            pltpu.make_async_copy(
                right.at[here], self.right.at[slot, pl.ds(0, chunk)], self.sems.at[slot, 1]
            ),
        )

    def size(self, job):
        left, right, _ = self.jobs[job]
        depth, rows = left.shape
        chunk = min(self.right.shape[1], depth)
        while depth % (2 * chunk):
            chunk -= 128
        return chunk, rows, right.shape[1], depth // chunk

    def run(self, count=1):
        for job in range(self.next, min(self.next + count, len(self.jobs))):
            self.one(job)

    def one(self, job):
        self.next = job + 1
        chunk, rows, _, steps = self.size(job)
        which = job % 2
        if which in self.stores:
            self.stores.pop(which).wait()
        total = self.sums.at[which, pl.ds(0, rows)]

        def step(index, carry):
            slot = index % 2

            @pl.when(index + 1 < steps)
            def _():
                self.fetch(job, index + 1, 1 - slot).start()

            if job + 1 < len(self.jobs):

                @pl.when(index + 1 == steps)
                def _():
                    self.fetch(job + 1, 0, 0).start()

            self.fetch(job, index, slot).wait()
            term = product(
                self.left[rows][slot, pl.ds(0, chunk)], self.right[slot, pl.ds(0, chunk)], TN
            )

            @pl.when(index == 0)
            def _():
                total[...] = term

            @pl.when(index > 0)
            def _():
                total[...] += term

            return carry

        lax.fori_loop(0, steps, step, 0)
        out = self.jobs[job][2]
        source = self.low.at[which, pl.ds(0, rows)]
        source[...] = total[...].astype(out.dtype)
        self.stores[which] = pltpu.make_async_copy(source, out, self.out_sems.at[which])
        self.stores[which].start()

    def finish(self):
        self.run(len(self.jobs))
        for store in self.stores.values():
            store.wait()


class Pair:
    def __init__(self, *moves):
        self.moves = moves

    def start(self):
        for move in self.moves:
            move.start()

    def wait(self):
        for move in self.moves:
            move.wait()


def scatter_kernel(
    back_part, ffn_part, scalars, slot_rows, slot_cotangent, grad_pre, gated,
    all_rows, all_cotangent, grad_shared_pre, scaled,
    back_sum, ffn_sum, out_scalars, grad_expert_in, grad_expert_down, grad_shared,
    held, core_in, x_in, ring_q, ring_x, last_in,
    s_held, s_core, s_x, s_ring,
    job_left, job_short, job_right, job_sums, job_low, job_sems, job_out_sems,
    free, send_sems, recv_sems,
):
    me = Peers()
    copies = Copies(send_sems, recv_sems)
    parts, outs = (back_part, ffn_part), (back_sum, ffn_sum)
    count = back_part.shape[2]
    half, piece = count // 2, count // 4
    q, qx, qc, qd = me.quarter, me.x_quarter, me.core_quarter, me.far_quarter
    own, other, last = range(3)
    peers = {RIGHT: me.right, LEFT: me.left}
    greet([me.right, me.left, me.x_peer, me.core_peer])
    order = (4, 3, 5, 2, 6, 1, 7, 0)

    def load(kind):
        for k in order:
            for slot, mine in ((0, q), (1, qx)):
                copies.local(
                    (kind, LOCAL, k, slot), parts[kind].at[me.block(k), mine], held.at[kind, k, slot]
                )

    def swap_cores(kind):
        for k in order:
            for slot, theirs in ((0, qc), (1, qd)):
                target = core_in.at[k, slot]
                copies.send(
                    (kind, OVER_CORE, k, slot),
                    parts[kind].at[me.block(k), theirs],
                    target,
                    target,
                    me.core_peer,
                )

    swap_cores(0)
    load(0)
    for k in range(RING):
        for slot, mine, theirs in ((0, q, qc), (1, qx, qd)):
            copies.local((SCALARS, LOCAL, k, slot), scalars.at[me.block(k), mine], s_held.at[slot, k])
            target = s_core.at[slot, k]
            copies.send(
                (SCALARS, OVER_CORE, k, slot),
                scalars.at[me.block(k), theirs],
                target,
                target,
                me.core_peer,
            )

    def prepare(kind, *blocks):
        for k in blocks:
            for slot in (1, 0):
                copies.arrive(kind, LOCAL, k, slot)
                copies.arrive(kind, OVER_CORE, k, slot)
                add_into(held.at[kind, k, slot], core_in.at[k, slot], count)
                if slot == 1:
                    source = held.at[kind, k, 1, pl.ds(half, half)]
                    target = x_in.at[kind, k]
                    copies.send((kind, OVER_X, k), source, target, target, me.x_peer)

    def over_x(kind, *blocks):
        for k in blocks:
            copies.arrive(kind, OVER_X, k)
            add_into(held.at[kind, k, 0, pl.ds(half, half)], x_in.at[kind, k], half)

    def pass_on(kind, side, hop, k):
        if hop == 0:
            rows_q, rows_x = pl.ds(side * half, half), pl.ds(side * piece, piece)
        else:
            rows_q, rows_x = pl.ds(0, count), pl.ds(0, half)
        for which, landing, rows in ((own, ring_q, rows_q), (other, ring_x, rows_x)):
            target = landing.at[kind, side, hop, rows]
            source = held.at[kind, k, which, rows]
            copies.send((kind, side, which, hop), source, target, target, peers[side])

    def take_in(kind, side, hop, k):
        if hop == 0:
            span_q, span_x, at_q, at_x = half, piece, side * half, side * piece
        else:
            span_q, span_x, at_q, at_x = count, half, 0, 0
        for which, landing, span, at in (
            (own, ring_q, span_q, at_q),
            (other, ring_x, span_x, at_x),
        ):
            copies.arrive(kind, side, which, hop)
            rows = pl.ds(at, span)
            add_into(held.at[kind, k, which, rows], landing.at[kind, side, hop, rows], span)

    def hop_on(kind, hop):
        right_block, left_block = 4 - hop, 4 + hop
        if hop == 0:
            pass_on(kind, RIGHT, 0, 4)
            pass_on(kind, LEFT, 0, 4)
            return
        take_in(kind, RIGHT, hop - 1, right_block)
        pass_on(kind, RIGHT, hop, right_block)
        take_in(kind, LEFT, hop - 1, left_block)
        pass_on(kind, LEFT, hop, left_block)

    def pass_scalars(side, hop, k):
        target = s_ring.at[side, hop]
        copies.send((SCALARS, side, hop), s_held.at[0, k], target, target, peers[side])

    def take_scalars(side, hop, k):
        copies.arrive(SCALARS, side, hop)
        s_held[0, k] += s_ring[side, hop]

    def home(kind):
        take_in(kind, RIGHT, 3, 0)
        take_in(kind, LEFT, 3, 0)
        source, target = held.at[kind, 0, 1, pl.ds(0, half)], last_in.at[kind]
        copies.send((kind, OVER_X, last, last), source, target, target, me.x_peer)

    def home_out(kind):
        out = outs[kind]
        out[pl.ds(half, half), :] = held[kind, 0, 0, pl.ds(half, half), :].astype(out.dtype)
        copies.arrive(kind, OVER_X, last, last)
        out[pl.ds(0, half), :] = (
            held[kind, 0, 0, pl.ds(0, half), :].astype(jnp.float32)
            + last_in[kind].astype(jnp.float32)
        ).astype(out.dtype)

    experts = slot_rows.shape[0]
    jobs = []
    for expert in range(experts):
        for index in range(2):
            jobs.append(
                (grad_pre.at[index, expert], slot_rows.at[expert], grad_expert_in.at[expert, index])
            )
        jobs.append((gated.at[expert], slot_cotangent.at[expert], grad_expert_down.at[expert]))
    for index in range(2):
        jobs.append((grad_shared_pre.at[index], all_rows, grad_shared.at[index]))
    jobs.append((scaled, all_cotangent, grad_shared.at[2]))
    prepare(0, 4, 3, 5)
    over_x(0, 4)
    hop_on(0, 0)
    prepare(0, 2, 6)
    for k in range(RING):
        for slot in (0, 1):
            copies.arrive(SCALARS, LOCAL, k, slot)
            copies.arrive(SCALARS, OVER_CORE, k, slot)
    s_held[...] += s_core[...]
    copies.send((SCALARS, OVER_X), s_held.at[1], s_x, s_x, me.x_peer)
    over_x(0, 3, 5)
    hop_on(0, 1)
    copies.arrive(SCALARS, OVER_X)
    s_held[0] += s_x[...]
    pass_scalars(RIGHT, 0, 4)
    prepare(0, 1, 7, 0)
    pl.semaphore_signal(free, inc=1, device_id=me.core_peer, device_id_type=MESH_ID)
    load(1)
    lefts = {job_left.shape[2]: job_left, job_short.shape[2]: job_short}
    grads = WeightGrads(jobs, lefts, job_right, job_sums, job_low, job_sems, job_out_sems)
    over_x(0, 2, 6)
    hop_on(0, 2)
    take_scalars(RIGHT, 0, 3)
    pass_scalars(RIGHT, 1, 3)
    pass_scalars(LEFT, 1, 5)
    pl.semaphore_wait(free, 1)
    swap_cores(1)
    over_x(0, 1, 7)
    grads.run(1)
    prepare(1, 4, 3, 5)
    hop_on(0, 3)
    take_scalars(RIGHT, 1, 2)
    take_scalars(LEFT, 1, 6)
    pass_scalars(RIGHT, 2, 2)
    pass_scalars(LEFT, 2, 6)
    over_x(0, 0)
    over_x(1, 4)
    hop_on(1, 0)
    prepare(1, 2, 6)
    over_x(1, 3, 5)
    grads.run(2)
    home(0)
    for side, k in ((RIGHT, 1), (LEFT, 7)):
        take_scalars(side, 2, k)
        pass_scalars(side, 3, k)
    hop_on(1, 1)
    home_out(0)
    prepare(1, 1, 7, 0)
    over_x(1, 2, 6)
    grads.run(2)
    hop_on(1, 2)
    over_x(1, 1, 7, 0)
    grads.run(2)
    hop_on(1, 3)
    take_scalars(RIGHT, 3, 0)
    take_scalars(LEFT, 3, 0)
    out_scalars[...] = s_held[0, 0]
    grads.finish()
    home(1)
    home_out(1)
    copies.finish()


def scatter_rows(back_part, ffn_part, scalars, fed, collective_id):
    slot_rows, slot_cotangent, grad_pre, gated, all_rows, all_cotangent, grad_shared_pre, scaled = fed
    _, _, count, width = back_part.shape
    half = count // 2
    dtype, f32 = back_part.dtype, jnp.float32
    s_shape = scalars.shape[2:]
    experts, hidden = gated.shape[0], gated.shape[2]
    shared_hidden = scaled.shape[1]
    shape = jax.ShapeDtypeStruct
    return pl.pallas_call(
        scatter_kernel,
        out_shape=(
            shape((count, width), f32),
            shape((count, width), f32),
            shape(s_shape, f32),
            shape((experts, 2, hidden, width), dtype),
            shape((experts, hidden, width), dtype),
            shape((3, shared_hidden, width), dtype),
        ),
        in_specs=[IN_PLACE] * 11,
        out_specs=(IN_VMEM,) * 3 + (IN_PLACE,) * 3,
        scratch_shapes=[
            pltpu.VMEM((2, RING, 2, count, width), dtype),
            pltpu.VMEM((RING, 2, count, width), dtype),
            pltpu.VMEM((2, RING, half, width), dtype),
            pltpu.VMEM((2, 2, 4, count, width), dtype),
            pltpu.VMEM((2, 2, 4, half, width), dtype),
            pltpu.VMEM((2, half, width), dtype),
            pltpu.VMEM((2, RING) + s_shape, f32),
            pltpu.VMEM((2, RING) + s_shape, f32),
            pltpu.VMEM((RING,) + s_shape, f32),
            pltpu.VMEM((2, 4) + s_shape, f32),
            pltpu.VMEM((2, 640, hidden), dtype),
            pltpu.VMEM((2, 640, shared_hidden), dtype),
            pltpu.VMEM((2, 640, width), dtype),
            pltpu.VMEM((2, hidden, width), f32),
            pltpu.VMEM((2, hidden, width), dtype),
            pltpu.SemaphoreType.DMA((2, 2)),
            pltpu.SemaphoreType.DMA((2,)),
            pltpu.SemaphoreType.REGULAR,
        ]
        + semaphores(168),
        compiler_params=remote_params(collective_id, 62),
        name="scatter_rows",
    )(back_part, ffn_part, scalars, *fed)


def open_kernel(
    shard_in, shard_out, routes, rows, gain, bias, cosine, sine,
    full_in, full_out, full_routes, normed, queries, keys_values,
    sums, share_send, share_recv, send_sems, recv_sems,
):
    me = Peers()
    copies = Copies(send_sems, recv_sems)
    bf16, f32 = jnp.bfloat16, jnp.float32
    kinds, depth, width = shard_in.shape
    out_rows, columns = shard_out.shape
    tokens = rows.shape[0]
    sides = ((RIGHT, me.right, -1), (LEFT, me.left, 1))
    greet_along_z(me)

    def cell(kind, step, part, parts):
        block = me.block(step)
        if kind < kinds:
            return full_in.at[kind, block, pl.ds(part * (depth // parts), depth // parts)]
        if kind > kinds:
            return full_routes.at[block]
        across = pl.ds(pl.multiple_of(block * columns, columns), columns)
        return full_out.at[pl.ds(part * (out_rows // parts), out_rows // parts), across]

    def pass_on(side, peer, sign, kind, hop, source=None):
        if kind > kinds and hop == 3 and side == LEFT:
            return
        parts = 2 if hop == 3 else 1
        part = side if hop == 3 else 0
        step = sign * hop
        here = cell(kind, step, part, parts)
        copies.send(
            (side, kind, hop + 1),
            here if source is None else source,
            here,
            cell(kind, step + sign, part, parts),
            peer,
        )

    def hop_on(hop, order):
        for kind in order:
            source = None
            if hop == 0:
                source = shard_in.at[kind] if kind < kinds else shard_out if kind == kinds else routes
                cell(kind, 0, 0, 1)[...] = source[...]
            for side, peer, sign in sides:
                if hop > 0:
                    copies.arrive(side, kind, hop)
                pass_on(side, peer, sign, kind, hop, source)

    def multiply(kind, step):
        block = me.block(step)
        features = normed[:, pl.ds(pl.multiple_of(block * depth, depth), depth)]
        term = product(features, full_in[kind, block])
        if step == 0:
            sums[kind] = term + bias[kind : kind + 1, :]
        else:
            sums[kind] += term

    def go_round(order):
        taken = [kind for kind in order if kind < kinds]
        for hop in (1, 2, 3):
            hop_on(hop, order)
            for kind in taken:
                for step in (-hop, hop):
                    multiply(kind, step)
        for kind in order:
            for side, _, _ in sides:
                if kind <= kinds or side == RIGHT:
                    copies.arrive(side, kind, 4)
        for kind in taken:
            multiply(kind, 4)

    def heads_of(kind, turn):
        for start in range(0, width, HD):
            head = slice(start, start + HD)
            part = sums[kind, :, head]
            if turn:
                part = turned(part, cosine[...], sine[...])
            yield head, part.astype(bf16)

    first, second = (kinds + 1,) + tuple(range(kinds - 1, 0, -1)), (0, kinds)
    hop_on(0, first)
    _, scaled = rms_parts(rows[...].astype(f32))
    normed[...] = (scaled * gain[...]).astype(bf16)
    for kind in range(kinds):
        if kind:
            multiply(kind, 0)
    go_round(first)
    for index in range(2):
        for head, part in heads_of(index + 1, index == 0):
            keys_values[index, 2, :, head] = part
    pieces = 2
    size = tokens // pieces
    parts = [(kind, pl.ds(piece * size, size)) for kind in range(2) for piece in range(pieces)]
    count = len(parts)
    share = Copies(share_send, share_recv)

    def upward(index, kind, at):
        target = keys_values.at[kind, 0, at]
        return share.describe(keys_values.at[kind, 2, at], target, (me.ep + 2, me.tp), index)

    def sideways(index, kind, at):
        target = keys_values.at[kind, 1, at]
        return share.describe(keys_values.at[kind, 2, at], target, me.y_peer, count + index)

    def onward(index, kind, at):
        target = keys_values.at[kind, 1, at]
        return share.describe(keys_values.at[kind, 0, at], target, me.y_peer, count + index)

    def each(copy, action):
        for index, (kind, at) in enumerate(parts):
            action(copy(index, kind, at))

    @pl.when(me.z < 3)
    def _():
        each(upward, lambda copy: copy.start())

    @pl.when(me.y == 0)
    def _():
        each(sideways, lambda copy: copy.start())

    hop_on(0, second)
    multiply(0, 0)

    @pl.when(me.z == 0)
    def _():
        keys_values[:, 0] = jnp.zeros((2, tokens, width), bf16)

    @pl.when((me.z == 0) & (me.y == 0))
    def _():
        keys_values[:, 1] = jnp.zeros((2, tokens, width), bf16)

    @pl.when(me.z > 0)
    def _():
        for index, (kind, at) in enumerate(parts):
            upward(index, kind, at).wait_recv()

            @pl.when(me.y == 1)
            def _():
                onward(index, kind, at).start()

    go_round(second)
    for head, part in heads_of(0, True):
        queries[:, head] = part

    @pl.when((me.y == 1) | (me.z > 0))
    def _():
        each(sideways, lambda copy: copy.wait_recv())

    @pl.when(me.z < 3)
    def _():
        each(upward, lambda copy: copy.wait_send())

    @pl.when((me.y == 0) | (me.z > 0))
    def _():
        each(sideways, lambda copy: copy.wait_send())

    copies.finish()


def open_attention(shard_in, shard_out, routes, rows, gain, bias, cosine, sine, collective_id):
    kinds, depth, width = shard_in.shape
    out_rows, columns = shard_out.shape
    tokens, features = rows.shape
    bf16 = jnp.bfloat16
    shape = jax.ShapeDtypeStruct
    return pl.pallas_call(
        open_kernel,
        out_shape=(
            shape((kinds, RING, depth, width), bf16),
            shape((out_rows, RING * columns), bf16),
            shape((RING,) + routes.shape, routes.dtype),
            shape((tokens, features), bf16),
            shape((tokens, width), bf16),
            shape((2, 3, tokens, width), bf16),
        ),
        in_specs=[IN_VMEM] * 8,
        out_specs=(IN_VMEM,) * 6,
        scratch_shapes=[pltpu.VMEM((kinds, tokens, width), jnp.float32)]
        + semaphores(8)
        + semaphores(8 * (kinds + 2)),
        compiler_params=remote_params(collective_id),
        name="open_attention",
    )(shard_in, shard_out, routes, rows, gain[None], bias, cosine, sine)


def finish_kernel(
    normed, grad_raw, heads, grad_attention, weights, gain, rows, grad_residual, tail,
    sum_in, sum_out, sum_tail, grad_input,
    held_in, held_out, ring_in, ring_out, tails, tail_sums,
    core_out, core_in, x_out, x_in, grad_rows, mine,
    send_sems, recv_sems,
):
    me = Peers()
    copies = Copies(send_sems, recv_sems)
    bf16, f32 = jnp.bfloat16, jnp.float32
    kinds = grad_raw.shape[0]
    depth, width = sum_in.shape[1], sum_in.shape[2]
    out_rows, columns = sum_out.shape
    count = rows.shape[0]
    peers = {RIGHT: me.right, LEFT: me.left}
    greet([me.right, me.left, me.x_peer, me.core_peer, me.far_peer])

    def held(kind, k):
        return held_in.at[k, kind] if kind < kinds else held_out.at[k]

    def ring(kind, side, hop):
        return ring_in.at[side, hop, kind] if kind < kinds else ring_out.at[side, hop]

    def span(kind, side, hop):
        whole = depth if kind < kinds else out_rows
        return (side * (whole // 2), whole // 2) if hop == 0 else (0, whole)

    def pass_on(side, hop, k, kind):
        at = pl.ds(*span(kind, side, hop))
        target = ring(kind, side, hop).at[at]
        copies.send((side, kind, hop), held(kind, k).at[at], target, target, peers[side])

    def take_in(side, hop, k, kind):
        copies.arrive(side, kind, hop)
        start, size = span(kind, side, hop)
        at = pl.ds(start, size)
        add_into(held(kind, k).at[at], ring(kind, side, hop).at[at], size)

    def work_out(*blocks):
        for k in blocks:
            block = me.block(k)
            features = normed[:, pl.ds(pl.multiple_of(block * depth, depth), depth)]
            for kind in range(kinds):
                held_in[k, kind] = product(features, grad_raw[kind], TN).astype(bf16)
            across = grad_attention[:, pl.ds(pl.multiple_of(block * columns, columns), columns)]
            held_out[k] = product(heads[...], across, TN).astype(bf16)

    def hop_on(hop):
        if hop == 0:
            for kind in range(kinds + 1):
                for side in (RIGHT, LEFT):
                    pass_on(side, 0, 4, kind)
            return
        for kind in range(kinds + 1):
            for side, k in ((RIGHT, 4 - hop), (LEFT, 4 + hop)):
                take_in(side, hop - 1, k, kind)
                pass_on(side, hop, k, kind)

    def quarter(index):
        here = pl.ds(pl.multiple_of(index * count, count), count)
        total = None
        for kind in range(kinds):
            term = product(grad_raw[kind, here, :], weights[kind], NT)
            total = term if total is None else total + term
        return total

    work_out(4)
    hop_on(0)
    for slot, index in ((1, me.far_quarter), (0, me.core_quarter)):
        core_out[slot] = quarter(index).astype(bf16)
        target = core_in.at[slot]
        copies.send((SCALARS, OVER_CORE, slot), core_out.at[slot], target, target, me.core_peer)
    mine[...] = quarter(me.x_quarter)
    copies.arrive(SCALARS, OVER_CORE, 1)
    x_out[...] = (mine[...] + core_in[1].astype(f32)).astype(bf16)
    copies.send((SCALARS, OVER_X), x_out, x_in, x_in, me.x_peer)
    work_out(3, 5)
    hop_on(1)
    mine[...] = quarter(me.quarter)
    copies.arrive(SCALARS, OVER_CORE, 0)
    work_out(2, 6)
    copies.arrive(SCALARS, OVER_X)
    total = mine[...] + core_in[0].astype(f32) + x_in[...].astype(f32)
    inverse, scaled_rows = rms_parts(rows[...].astype(f32))
    scaled = total * gain[...]
    slope = inverse * (
        scaled - scaled_rows * jnp.mean(scaled * scaled_rows, axis=-1, keepdims=True)
    )
    grad_rows[...] = (grad_residual[...] + slope).astype(bf16)
    here = grad_input.at[me.quarter]
    copies.send((SCALARS, RIGHT, OVER_X), grad_rows, here, grad_input.at[me.x_quarter], me.x_peer)
    copies.send(
        (SCALARS, RIGHT, OVER_CORE), grad_rows, here, grad_input.at[me.core_quarter], me.core_peer
    )
    copies.local((LOCAL,), grad_rows, here)
    gain_grad = jnp.sum(total * scaled_rows, axis=0, keepdims=True)
    tails[0, 0:kinds, :] = tail[...]
    for index in range(gain_grad.shape[1] // width):
        part = slice(index * width, (index + 1) * width)
        tails[0, kinds + index : kinds + index + 1, :] = gain_grad[:, part]
    tail_kind = kinds + 1

    def pass_tail(side, hop, place):
        sign = -1 if side == RIGHT else 1
        target = tails.at[(place + sign) % RING]
        copies.send((side, tail_kind, hop), tails.at[place], target, target, peers[side])

    pass_tail(RIGHT, 0, 0)
    pass_tail(LEFT, 0, 0)
    hop_on(2)
    work_out(1, 7)
    copies.arrive(SCALARS, RIGHT, OVER_X)
    beside = grad_input.at[me.x_quarter]
    copies.send(
        (SCALARS, LEFT, OVER_CORE), beside, beside, grad_input.at[me.far_quarter], me.core_peer
    )
    for side, place in ((RIGHT, 7), (LEFT, 1)):
        copies.arrive(side, tail_kind, 0)
        pass_tail(side, 1, place)
    hop_on(3)
    for side, place in ((RIGHT, 6), (LEFT, 2)):
        copies.arrive(side, tail_kind, 1)
        pass_tail(side, 2, place)
    work_out(0)
    copies.arrive(RIGHT, tail_kind, 2)
    pass_tail(RIGHT, 3, 5)
    copies.arrive(LEFT, tail_kind, 2)
    for kind in range(kinds + 1):
        for side in (RIGHT, LEFT):
            take_in(side, 3, 0, kind)
        if kind < kinds:
            sum_in[kind] = held_in[0, kind].astype(f32)
    sum_out[...] = held_out[0].astype(f32)
    copies.arrive(RIGHT, tail_kind, 3)
    total = tails[0]
    for place in range(1, RING):
        total = total + tails[place]
    tail_sums[me.tp] = total
    for way, peer, index in (
        (OVER_X, me.x_peer, me.x_quarter),
        (OVER_CORE, me.core_peer, me.core_quarter),
        (OVER_FAR, me.far_peer, me.far_quarter),
    ):
        copies.send(
            (way, tail_kind), tail_sums.at[me.tp], tail_sums.at[me.tp], tail_sums.at[index], peer
        )
    for way in (OVER_X, OVER_CORE, OVER_FAR):
        copies.arrive(way, tail_kind)
    sum_tail[...] = tail_sums[...]
    copies.finish()


def finish(
    normed, grad_raw, heads, grad_attention, weights, gain, rows, grad_residual, bias, collective_id
):
    tokens, width = normed.shape
    kinds, _, columns = grad_raw.shape
    count = rows.shape[0]
    depth = width // RING
    bf16, f32 = jnp.bfloat16, jnp.float32
    shape = jax.ShapeDtypeStruct
    tail_shape = (-(-(kinds + width // columns) // 8) * 8, columns)
    return pl.pallas_call(
        finish_kernel,
        out_shape=(
            shape((kinds, depth, columns), f32),
            shape((columns, depth), f32),
            shape((4,) + tail_shape, f32),
            shape((4, count, width), bf16),
        ),
        in_specs=[IN_VMEM] * 9,
        out_specs=(IN_VMEM,) * 3 + (IN_PLACE,),
        scratch_shapes=[
            pltpu.VMEM((RING, kinds, depth, columns), bf16),
            pltpu.VMEM((RING, columns, depth), bf16),
            pltpu.VMEM((2, 4, kinds, depth, columns), bf16),
            pltpu.VMEM((2, 4, columns, depth), bf16),
            pltpu.VMEM((RING,) + tail_shape, f32),
            pltpu.VMEM((4,) + tail_shape, f32),
            pltpu.VMEM((2, count, width), bf16),
            pltpu.VMEM((2, count, width), bf16),
            pltpu.VMEM((count, width), bf16),
            pltpu.VMEM((count, width), bf16),
            pltpu.VMEM((count, width), bf16),
            pltpu.VMEM((count, width), f32),
        ]
        + semaphores(56),
        compiler_params=remote_params(collective_id, 60),
        name="finish",
    )(normed, grad_raw, heads, grad_attention, weights, gain[None], rows, grad_residual, bias)


def greet_along_z(me):
    barrier = pltpu.get_barrier_semaphore()
    pl.semaphore_signal(barrier, inc=1, device_id=me.y_peer, device_id_type=MESH_ID)

    @pl.when(me.z > 0)
    def _():
        peer = (me.ep - 2, me.tp)
        pl.semaphore_signal(barrier, inc=1, device_id=peer, device_id_type=MESH_ID)

    @pl.when(me.z < 3)
    def _():
        peer = (me.ep + 2, me.tp)
        pl.semaphore_signal(barrier, inc=1, device_id=peer, device_id_type=MESH_ID)

    pl.semaphore_wait(barrier, 1 + (me.z + 2) // 3 + (5 - me.z) // 3)


def return_kernel(grads, cosine, sine, out, total, from_y, from_z, send_sems, recv_sems):
    me = Peers()
    kinds, _, tokens, _ = grads.shape
    pieces = 2
    size = tokens // pieces
    parts = [(kind, pl.ds(piece * size, size)) for kind in range(kinds) for piece in range(pieces)]
    count = len(parts)
    greet_along_z(me)

    def copy(index, source, target, peer):
        return Copies(send_sems, recv_sems).describe(source, target, peer, index)

    def sideways(index, kind, rows):
        return copy(index, grads.at[kind, 1, rows], from_y.at[kind, rows], me.y_peer)

    def downward(index, kind, rows, source):
        return copy(count + index, source.at[kind, rows], from_z.at[kind, rows], (me.ep - 2, me.tp))

    for index, (kind, rows) in enumerate(parts):
        sideways(index, kind, rows).start()

    @pl.when((me.z > 0) & (me.y == 0))
    def _():
        for index, (kind, rows) in enumerate(parts):
            downward(index, kind, rows, grads.at[:, 0]).start()

    for index, (kind, rows) in enumerate(parts):
        sideways(index, kind, rows).wait_recv()
        here = grads[kind, 2, rows, :].astype(jnp.float32)

        @pl.when(me.y == 0)
        def _():
            total[kind, rows, :] = here + from_y[kind, rows, :].astype(jnp.float32)

        @pl.when(me.y == 1)
        def _():
            total[kind, rows, :] = here
            two_back = grads[kind, 0, rows, :].astype(jnp.float32)
            summed = two_back + from_y[kind, rows, :].astype(jnp.float32)
            from_y[kind, rows, :] = summed.astype(from_y.dtype)

        @pl.when((me.z > 0) & (me.y == 1))
        def _():
            downward(index, kind, rows, from_y).start()

    @pl.when(me.z < 3)
    def _():
        for index, (kind, rows) in enumerate(parts):
            downward(index, kind, rows, from_y).wait_recv()
            total[kind, rows, :] += from_z[kind, rows, :].astype(jnp.float32)

    for start in range(0, total.shape[2], HD):
        head = slice(start, start + HD)
        out[0, :, head] = turned(total[0, :, head], cosine[...], -sine[...]).astype(out.dtype)
    out[1] = total[1].astype(out.dtype)
    for index, (kind, rows) in enumerate(parts):
        sideways(index, kind, rows).wait_send()

    @pl.when(me.z > 0)
    def _():
        for index, (kind, rows) in enumerate(parts):
            downward(index, kind, rows, from_y).wait_send()


def return_keys(grads, cosine, sine, collective_id):
    kinds, _, tokens, width = grads.shape
    return pl.pallas_call(
        return_kernel,
        out_shape=jax.ShapeDtypeStruct((kinds, tokens, width), grads.dtype),
        in_specs=[IN_VMEM] * 3,
        out_specs=IN_VMEM,
        scratch_shapes=[
            pltpu.VMEM((kinds, tokens, width), jnp.float32),
            pltpu.VMEM((kinds, tokens, width), grads.dtype),
            pltpu.VMEM((kinds, tokens, width), grads.dtype),
        ]
        + semaphores(8),
        compiler_params=remote_params(collective_id),
        name="return_keys",
    )(grads, cosine, sine)


def reduce_kernel(flip, left, right, out, core_out, core_in, x_out, x_in, send_sems, recv_sems):
    me = Peers()
    copies = Copies(send_sems, recv_sems)
    terms = left.shape[0]
    count = out.shape[0]
    f32 = jnp.float32
    greet([me.x_peer, me.core_peer])

    def quarter(index):
        rows = pl.ds(pl.multiple_of(index * count, count), count)
        total = None
        for term in range(terms):
            one = product(left[term, rows, :], right[term], NT if flip else NN)
            total = one if total is None else total + one
        return total

    for slot, index in ((1, me.far_quarter), (0, me.core_quarter)):
        core_out[slot] = quarter(index).astype(core_out.dtype)
        target = core_in.at[slot]
        copies.send((OVER_CORE, slot), core_out.at[slot], target, target, me.core_peer)
    mine = quarter(me.x_quarter)
    copies.arrive(OVER_CORE, 1)
    x_out[...] = (mine + core_in[1].astype(f32)).astype(x_out.dtype)
    copies.send((OVER_X,), x_out, x_in, x_in, me.x_peer)
    mine = quarter(me.quarter)
    copies.arrive(OVER_CORE, 0)
    out[...] = mine + core_in[0].astype(f32)
    copies.arrive(OVER_X)
    out[...] += x_in[...].astype(f32)
    copies.finish()


def product_to_owner(left, right, flip, collective_id):
    tokens = left.shape[1]
    width = right.shape[1] if flip else right.shape[2]
    count = tokens // 4
    bf16 = jnp.bfloat16
    return pl.pallas_call(
        functools.partial(reduce_kernel, flip),
        out_shape=jax.ShapeDtypeStruct((count, width), jnp.float32),
        in_specs=[IN_VMEM] * 2,
        out_specs=IN_VMEM,
        scratch_shapes=[
            pltpu.VMEM((2, count, width), bf16),
            pltpu.VMEM((2, count, width), bf16),
            pltpu.VMEM((count, width), bf16),
            pltpu.VMEM((count, width), bf16),
        ]
        + semaphores(3),
        compiler_params=remote_params(collective_id),
        name="product_to_owner",
    )(left, right)


def tensor_kernel(rows, out, send_sems, recv_sems):
    me = Peers()
    copies = Copies(send_sems, recv_sems)
    greet([me.x_peer, me.core_peer])
    mine = out.at[me.quarter]
    copies.send((OVER_X,), rows, mine, out.at[me.x_quarter], me.x_peer)
    copies.send((OVER_CORE, 0), rows, mine, out.at[me.core_quarter], me.core_peer)
    copies.local((LOCAL,), rows, mine)
    copies.arrive(OVER_X)
    beside = out.at[me.x_quarter]
    copies.send((OVER_CORE, 1), beside, beside, out.at[me.far_quarter], me.core_peer)
    copies.finish()


def tensor_gather(rows, collective_id):
    return pl.pallas_call(
        tensor_kernel,
        out_shape=jax.ShapeDtypeStruct((4,) + rows.shape, rows.dtype),
        in_specs=[IN_VMEM],
        out_specs=IN_PLACE,
        scratch_shapes=semaphores(4),
        compiler_params=remote_params(collective_id),
        name="tensor_gather",
    )(rows)


def own_rows(block, tp_index, count):
    return lax.dynamic_slice_in_dim(block, tp_index * count, count, 0)


def after(value, earlier):
    return lax.optimization_barrier((value, earlier))[0]


def per_device_dense(
    layer_input,
    attention_gain,
    attention_in,
    attention_bias,
    attention_out,
    feedforward_gain,
    shared_in,
    shared_down,
    shared_gate,
    router,
    expert_in,
    expert_down,
    routes,
    document_lengths,
    cotangent,
):
    bf16 = jnp.bfloat16
    f32 = jnp.float32
    both = (EP, TP)
    tok_count, model_width = layer_input.shape
    expert_count = router.shape[1]
    top_count = routes.shape[1]
    ep_size = lax.axis_size(EP)
    tp_size = lax.axis_size(TP)
    ep_index = lax.axis_index(EP)
    tp_index = lax.axis_index(TP)
    own_count = tok_count // tp_size
    all_count = tok_count * ep_size
    capacity = tp_size * (
        (5 * tok_count * top_count + 4 * expert_count * tp_size - 1) // (4 * expert_count * tp_size)
    )
    reach_back = min((WINDOW + tok_count - 2) // tok_count, ep_size - 1)
    local_experts = expert_in.shape[0]
    route_rows = jnp.concatenate(
        [routes.T, jnp.zeros((-top_count % 8, tok_count), routes.dtype)]
    )
    positions = ep_index * tok_count + jnp.arange(tok_count, dtype=jnp.int32)
    key_count = (reach_back + 1) * tok_count
    key_positions = (ep_index - reach_back) * tok_count + jnp.arange(key_count, dtype=jnp.int32)
    query_doc, rope_pos, valid_mask = doc_table(document_lengths, positions)
    query_doc = query_doc[:, None]
    key_doc = doc_table(document_lengths, key_positions)[0][None, :]
    valid_rows = valid_mask.astype(f32)[:, None]
    cosine, sine = (part[:, 0] for part in rope_angles(rope_pos, HD))
    cosine = jnp.concatenate([cosine, cosine], axis=1)
    sine = jnp.concatenate([-sine, sine], axis=1)
    in_blocks, out_full, all_routes, normed_attention, queries, keys_values = open_attention(
        attention_in,
        attention_out,
        route_rows,
        layer_input,
        attention_gain,
        attention_bias,
        cosine,
        sine,
        0,
    )
    in_full = in_blocks.reshape(3, model_width, -1)
    shard_width = shared_in.shape[1]
    slice_hidden = shared_in.shape[2] // ep_size
    shared_shards = jnp.concatenate([jnp.swapaxes(shared_in, 1, 2), shared_down[None]])
    shared_shards = jnp.swapaxes(
        shared_shards.reshape(3, ep_size, slice_hidden, shard_width), 0, 1
    )
    shared_slices = lax.all_to_all(
        after(shared_shards, queries), EP, split_axis=0, concat_axis=0, tiled=True
    )
    shared_slices = jnp.transpose(shared_slices, (1, 2, 0, 3)).reshape(
        3, slice_hidden, model_width
    )
    my_ids = ep_index * local_experts + jnp.arange(local_experts, dtype=jnp.int32)
    taken = jnp.any(all_routes[:, None, :top_count] == my_ids[None, :, None, None], axis=2)
    earlier_mask = jnp.tril(jnp.ones((tok_count, tok_count), bf16), -1)
    rank = product(
        taken.astype(bf16).reshape(-1, tok_count), earlier_mask, NT
    ).astype(jnp.int32).reshape(taken.shape)
    rank = jnp.where(taken & (rank < capacity), rank, NO_SLOT)
    heads_low, log_totals = attend(queries, keys_values, query_doc, key_doc, valid_rows)
    attention_sum = product_to_owner(heads_low[None], out_full[None], False, 2)
    input_rows = own_rows(layer_input, tp_index, own_count).astype(f32)
    residual = input_rows + attention_sum
    inverse_two, normed_two = rms_parts(residual)
    normed_ffn = normed_two * feedforward_gain
    normed_low = normed_ffn.astype(bf16)
    shared_scale = jax.nn.sigmoid(jnp.dot(normed_ffn, shared_gate, precision=HIGHEST))
    router_probs = jax.nn.softmax(jnp.dot(normed_ffn, router, precision=HIGHEST), axis=-1)
    routes_own = own_rows(routes, tp_index, own_count)
    expert_ids = jnp.arange(expert_count, dtype=jnp.int32)
    picked = jnp.any(routes_own[:, :, None] == expert_ids[None, None, :], axis=1)
    chosen = jnp.where(picked, router_probs, 0.0)
    chosen_total = jnp.sum(chosen, axis=1, keepdims=True)
    gates = chosen / chosen_total
    scale_count = -(-(expert_count + 1) // 8) * 8
    spare = jnp.zeros((scale_count - expert_count - 1, own_count), f32)
    scale_rows = jnp.concatenate([gates.T, shared_scale[None], spare])
    (
        all_rows,
        all_cotangent,
        all_scales,
        ffn_part,
        back_part,
        slot_rows,
        slot_cotangent,
        grad_pre,
        gated,
        grad_shared_pre,
        scaled_hidden,
        token_grad,
        scale_grad,
    ) = gather_feed(
        normed_low,
        cotangent.reshape(tp_size, own_count, model_width),
        scale_rows,
        rank,
        jnp.swapaxes(expert_in, 2, 3).reshape(local_experts, -1, model_width),
        expert_down,
        shared_slices,
        capacity,
        3,
    )
    spare = jnp.zeros((ep_size, scale_count - expert_count - 1, tok_count), f32)
    scalar_part = jnp.concatenate(
        [jnp.zeros((ep_size, expert_count, tok_count), f32), scale_grad[:, None, :, 0], spare], axis=1
    )
    scalar_part = lax.dynamic_update_slice(
        scalar_part, token_grad, (0, ep_index * local_experts, 0)
    )
    scalar_part = jnp.swapaxes(
        scalar_part.reshape(ep_size, scale_count, tp_size, own_count), 1, 2
    )
    part_shape = (ep_size, tp_size, own_count, model_width)
    slot_count = ep_size * capacity
    fed = (
        slot_rows.reshape(local_experts, slot_count, model_width),
        slot_cotangent.reshape(local_experts, slot_count, model_width),
        grad_pre.reshape(2, local_experts, slot_count, -1),
        gated.reshape(local_experts, slot_count, -1),
        all_rows.reshape(all_count, model_width),
        all_cotangent.reshape(all_count, model_width),
        grad_shared_pre.reshape(2, all_count, slice_hidden),
        scaled_hidden.reshape(all_count, slice_hidden),
    )
    back_sum, ffn_sum, scalar_sum, grad_expert_in, grad_expert_down, shared_grads = scatter_rows(
        back_part.reshape(part_shape), ffn_part.reshape(part_shape), scalar_part, fed, 4
    )
    scalar_sum = scalar_sum.T
    grad_expert_in = jnp.swapaxes(grad_expert_in, 2, 3).astype(f32)
    grad_expert_down = grad_expert_down.astype(f32)
    layer_output = lax.all_gather((residual + ffn_sum).astype(bf16), TP, axis=0, tiled=True)
    shared_grads = jnp.transpose(
        shared_grads.reshape(3, slice_hidden, ep_size, shard_width), (2, 0, 1, 3)
    )
    shared_grads = lax.all_to_all(shared_grads, EP, split_axis=0, concat_axis=0, tiled=True)
    shared_grads = (
        jnp.swapaxes(shared_grads, 0, 1).reshape(3, -1, shard_width).astype(f32)
    )
    grad_shared_in = jnp.swapaxes(shared_grads[:2], 1, 2)
    grad_shared_down = shared_grads[2]

    grad_gates = scalar_sum[:, :expert_count]
    grad_probs = jnp.where(
        picked,
        (grad_gates - jnp.sum(grad_gates * gates, axis=1, keepdims=True)) / chosen_total,
        0.0,
    )
    grad_logits = router_probs * (
        grad_probs - jnp.sum(grad_probs * router_probs, axis=1, keepdims=True)
    )
    grad_router = jnp.einsum("td,te->de", normed_ffn, grad_logits, precision=HIGHEST)
    grad_scale_pre = scalar_sum[:, expert_count] * shared_scale * (1.0 - shared_scale)
    grad_shared_gate = jnp.dot(grad_scale_pre, normed_ffn, precision=HIGHEST)
    grad_normed = (
        back_sum
        + jnp.einsum("te,de->td", grad_logits, router, precision=HIGHEST)
        + grad_scale_pre[:, None] * shared_gate[None, :]
    )
    grad_mid_norm, grad_feedforward_gain = norm_back(
        grad_normed, feedforward_gain, inverse_two, normed_two
    )
    small = jnp.concatenate([grad_feedforward_gain[None], grad_shared_gate[None], grad_router.T])
    small = lax.psum(small, both)
    grad_residual = own_rows(cotangent, tp_index, own_count).astype(f32) + grad_mid_norm
    grad_attention = tensor_gather(grad_residual.astype(bf16), 5).reshape(tok_count, model_width)
    grad_heads = (product(grad_attention, out_full, NT) * valid_rows).astype(bf16)
    grad_queries, grad_kv = attend_back(
        queries, keys_values, query_doc, key_doc, log_totals, grad_heads, cosine, sine
    )
    grad_own_kv = return_keys(grad_kv, cosine, sine, 6)
    grad_raw = jnp.concatenate([grad_queries[None], grad_own_kv])
    grad_attention_bias = jnp.sum(grad_raw.astype(f32), axis=1)
    grad_attention_in, grad_attention_out, tails, grad_input = finish(
        normed_attention,
        grad_raw,
        heads_low,
        grad_attention,
        in_full,
        attention_gain,
        own_rows(layer_input, tp_index, own_count),
        grad_residual,
        grad_attention_bias,
        7,
    )
    grad_attention_bias = lax.dynamic_index_in_dim(tails, tp_index, 0, keepdims=False)[:3]
    grad_attention_gain = jnp.sum(tails[:, 3:], axis=0)[: model_width // tails.shape[2]].reshape(-1)
    return (
        layer_output,
        grad_input.reshape(tok_count, model_width),
        grad_attention_gain,
        grad_attention_in,
        grad_attention_bias,
        grad_attention_out,
        small[0],
        grad_shared_in,
        grad_shared_down,
        small[1],
        small[2:].T,
        grad_expert_in,
        grad_expert_down,
    )


def per_device(*arguments):
    small_slice = lax.axis_size(EP) == RING and lax.axis_size(TP) == 4
    return (per_device_dense if small_slice else per_device_sparse)(*arguments)


def per_device_sparse(
    layer_input,
    attention_gain,
    attention_in,
    attention_bias,
    attention_out,
    feedforward_gain,
    shared_in,
    shared_down,
    shared_gate,
    router,
    expert_in,
    expert_down,
    routes,
    document_lengths,
    cotangent,
):
    bf16 = jnp.bfloat16
    f32 = jnp.float32
    tok_count = layer_input.shape[0]
    model_width = layer_input.shape[1]
    expert_count = router.shape[1]
    top_count = routes.shape[1]
    ep_size = lax.axis_size(EP)
    tp_size = lax.axis_size(TP)
    capacity = tp_size * (
        (5 * tok_count * top_count + 4 * expert_count * tp_size - 1) // (4 * expert_count * tp_size)
    )
    reach_back = min((WINDOW + tok_count - 2) // tok_count, ep_size - 1)
    head_dim = HD
    local_heads = attention_in.shape[2] // head_dim
    score_scale = 1.0 / math.sqrt(head_dim)
    in_full, out_full, shared_in_full, shared_down_full = (
        lax.all_gather(attention_in, EP, axis=1, tiled=True),
        lax.all_gather(attention_out, EP, axis=1, tiled=True),
        lax.all_gather(shared_in, EP, axis=1, tiled=True),
        lax.all_gather(shared_down, EP, axis=1, tiled=True),
    )
    ep_index = lax.axis_index(EP)
    positions = ep_index * tok_count + jnp.arange(tok_count, dtype=jnp.int32)
    key_count = (reach_back + 1) * tok_count
    key_positions = (ep_index - reach_back) * tok_count + jnp.arange(key_count, dtype=jnp.int32)
    query_doc, rope_pos, valid_mask = doc_table(document_lengths, positions)
    key_doc = doc_table(document_lengths, key_positions)[0]
    distance = positions[:, None] - key_positions[None, :]
    allowed = (query_doc[:, None] == key_doc[None, :]) & (distance >= 0) & (distance < WINDOW)
    valid_rows = valid_mask.astype(f32)[:, None]
    cosine, sine_part = rope_angles(rope_pos, head_dim)
    input_rows = layer_input.astype(f32)
    inverse_one, normed_one = rms_parts(input_rows)
    normed_attention = (normed_one * attention_gain).astype(bf16)
    raw_proj = (
        jnp.einsum("td,sde->ste", normed_attention, in_full, preferred_element_type=f32)
        + attention_bias[:, None, :]
    )
    queries = rotate(
        raw_proj[0].reshape(tok_count, local_heads, head_dim), cosine, sine_part, 1.0
    ).astype(bf16)
    keys_own = rotate(
        raw_proj[1].reshape(tok_count, local_heads, head_dim), cosine, sine_part, 1.0
    ).astype(bf16)
    values_own = raw_proj[2].reshape(tok_count, local_heads, head_dim).astype(bf16)
    key_value = jnp.stack([keys_own, values_own])
    earlier = []
    for hop_count in range(reach_back, 0, -1):
        earlier.append(shifted(key_value, EP, hop_count))
    all_kv = jnp.concatenate(earlier + [key_value], axis=1)
    all_keys = all_kv[0]
    all_values = all_kv[1]
    scores = jnp.einsum("qhe,khe->hqk", queries, all_keys, preferred_element_type=f32) * score_scale
    scores = jnp.where(allowed[None], scores, MASKED)
    row_max = jnp.max(scores, axis=-1, keepdims=True)
    exp_terms = jnp.exp(scores - row_max)
    row_total = jnp.sum(exp_terms, axis=-1, keepdims=True)
    log_total = row_max + jnp.log(row_total)
    weights = (exp_terms / row_total).astype(bf16)
    heads_out = jnp.einsum("hqk,khe->qhe", weights, all_values, preferred_element_type=f32).reshape(
        tok_count, -1
    )
    heads_low = (heads_out * valid_rows).astype(bf16)
    attention_sum = tensor_total(jnp.dot(heads_low, out_full, preferred_element_type=f32))
    residual = input_rows + attention_sum
    inverse_two, normed_two = rms_parts(residual)
    normed_ffn = normed_two * feedforward_gain
    normed_low = normed_ffn.astype(bf16)
    shared_pre = jnp.einsum("td,sdf->stf", normed_low, shared_in_full, preferred_element_type=f32)
    shared_silu, shared_slope = silu_parts(shared_pre[0])
    shared_hidden = (shared_silu * shared_pre[1]).astype(bf16)
    shared_out = tensor_total(jnp.dot(shared_hidden, shared_down_full, preferred_element_type=f32))
    shared_scale = jax.nn.sigmoid(jnp.dot(normed_ffn, shared_gate, precision=HIGHEST))
    router_probs = jax.nn.softmax(jnp.dot(normed_ffn, router, precision=HIGHEST), axis=-1)
    chosen = jnp.take_along_axis(router_probs, routes, axis=1)
    chosen_total = jnp.sum(chosen, axis=1, keepdims=True)
    gate_values = chosen / chosen_total
    assign_count = tok_count * top_count
    flat_routes = routes.reshape(-1)
    expert_ids = jnp.arange(expert_count, dtype=jnp.int32)
    one_hot = (flat_routes[:, None] == expert_ids[None, :]).astype(jnp.int32)
    arrival_rank = jnp.sum((jnp.cumsum(one_hot, axis=0) - one_hot) * one_hot, axis=1)
    slot_count = expert_count * capacity
    slot_index = jnp.where(
        arrival_rank < capacity, flat_routes * capacity + arrival_rank, slot_count
    )
    slot_assign = (
        jnp.full((slot_count + 1,), assign_count, jnp.int32)
        .at[slot_index]
        .set(jnp.arange(assign_count, dtype=jnp.int32))[:slot_count]
    )
    slot_token = slot_assign // top_count
    padded_rows = jnp.concatenate([normed_low, jnp.zeros((1, model_width), bf16)])
    send_rows = padded_rows[slot_token].reshape(expert_count, capacity, model_width)

    def expert_trip(outgoing, work):
        row_block = lax.all_to_all(outgoing, EP, split_axis=0, concat_axis=1, tiled=True)
        partial_rows, extras = work(row_block)
        share_rows = lax.psum_scatter(partial_rows, TP, scatter_dimension=1, tiled=True).astype(
            bf16
        )
        whole_rows = lax.all_gather(share_rows, TP, axis=1, tiled=True)
        return (lax.all_to_all(whole_rows, EP, split_axis=1, concat_axis=0, tiled=True), extras)

    def expert_forward(row_block):
        pre_acts = jnp.einsum("erd,esdf->serf", row_block, expert_in, preferred_element_type=f32)
        gate_silu, gate_slope = silu_parts(pre_acts[0])
        hidden = (gate_silu * pre_acts[1]).astype(bf16)
        partial_rows = jnp.einsum("erf,efd->erd", hidden, expert_down, preferred_element_type=f32)
        return (partial_rows, (row_block, pre_acts, hidden, gate_silu, gate_slope))

    returned_rows, kept_state = expert_trip(send_rows, expert_forward)
    expert_rows, expert_pre, expert_hidden, expert_silu, expert_slope = kept_state
    padded_back = jnp.concatenate(
        [returned_rows.reshape(slot_count, model_width), jnp.zeros((1, model_width), bf16)]
    )
    picked = padded_back[slot_index].reshape(tok_count, top_count, model_width).astype(f32)
    moe_sum = jnp.sum(gate_values[:, :, None] * picked, axis=1)
    layer_output = (residual + shared_scale[:, None] * shared_out + moe_sum).astype(bf16)
    grad_rows = cotangent.astype(f32)
    padded_grad = jnp.concatenate([grad_rows, jnp.zeros((1, model_width), f32)])
    padded_gates = jnp.concatenate([gate_values.reshape(-1), jnp.zeros((1,), f32)])
    grad_send = (padded_gates[slot_assign][:, None] * padded_grad[slot_token]).astype(bf16)
    grad_send = grad_send.reshape(expert_count, capacity, model_width)

    def expert_backward(grad_block):
        grad_down = jnp.einsum(
            "erf,erd->efd", expert_hidden, grad_block, preferred_element_type=f32
        )
        grad_hidden = jnp.einsum(
            "erd,efd->erf", grad_block, expert_down, preferred_element_type=f32
        )
        grad_pre = jnp.stack(
            [grad_hidden * expert_pre[1] * expert_slope, grad_hidden * expert_silu]
        ).astype(bf16)
        grad_weights_in = jnp.einsum(
            "erd,serf->esdf", expert_rows, grad_pre, preferred_element_type=f32
        )
        grad_back_rows = jnp.einsum(
            "serf,esdf->erd", grad_pre, expert_in, preferred_element_type=f32
        )
        return (grad_back_rows, (grad_weights_in, grad_down))

    grad_returned, expert_grads = expert_trip(grad_send, expert_backward)
    grad_expert_in, grad_expert_down = expert_grads
    grad_gate_values = jnp.sum(picked * grad_rows[:, None, :], axis=2)
    grad_chosen = (
        grad_gate_values - jnp.sum(grad_gate_values * gate_values, axis=1, keepdims=True)
    ) / chosen_total
    grad_probs = jnp.sum(
        jnp.where(routes[:, :, None] == expert_ids[None, None, :], grad_chosen[:, :, None], 0.0),
        axis=1,
    )
    grad_logits = router_probs * (
        grad_probs - jnp.sum(grad_probs * router_probs, axis=1, keepdims=True)
    )
    grad_router = jnp.einsum("td,te->de", normed_ffn, grad_logits, precision=HIGHEST)
    grad_shared_out = (shared_scale[:, None] * grad_rows).astype(bf16)
    grad_shared_down = jnp.einsum(
        "tf,td->fd", shared_hidden, grad_shared_out, preferred_element_type=f32
    )
    grad_shared_hidden = jnp.einsum(
        "td,fd->tf", grad_shared_out, shared_down_full, preferred_element_type=f32
    )
    grad_shared_pre = jnp.stack(
        [grad_shared_hidden * shared_pre[1] * shared_slope, grad_shared_hidden * shared_silu]
    ).astype(bf16)
    grad_shared_in = jnp.einsum(
        "td,stf->sdf", normed_low, grad_shared_pre, preferred_element_type=f32
    )
    shared_back = jnp.einsum(
        "stf,sdf->td", grad_shared_pre, shared_in_full, preferred_element_type=f32
    )
    grad_scale_pre = jnp.sum(grad_rows * shared_out, axis=1) * shared_scale * (1.0 - shared_scale)
    grad_shared_gate = jnp.dot(grad_scale_pre, normed_ffn, precision=HIGHEST)
    padded_return = jnp.concatenate(
        [grad_returned.reshape(slot_count, model_width), jnp.zeros((1, model_width), bf16)]
    )
    moe_back = jnp.sum(
        padded_return[slot_index].reshape(tok_count, top_count, model_width).astype(f32), axis=1
    )
    grad_normed = (
        tensor_total(shared_back)
        + moe_back
        + jnp.einsum("te,de->td", grad_logits, router, precision=HIGHEST)
        + grad_scale_pre[:, None] * shared_gate[None, :]
    )
    grad_mid_norm, grad_feedforward_gain = norm_back(
        grad_normed, feedforward_gain, inverse_two, normed_two
    )
    grad_residual = grad_rows + grad_mid_norm
    grad_attention = grad_residual.astype(bf16)
    grad_attention_out = jnp.einsum(
        "tf,td->fd", heads_low, grad_attention, preferred_element_type=f32
    )
    grad_heads = jnp.einsum(
        "td,fd->tf", grad_attention, out_full, preferred_element_type=f32
    ).astype(bf16)
    grad_heads = (grad_heads * valid_rows.astype(bf16)).reshape(tok_count, local_heads, head_dim)
    scores_again = (
        jnp.einsum("qhe,khe->hqk", queries, all_keys, preferred_element_type=f32) * score_scale
    )
    scores_again = jnp.where(allowed[None], scores_again, MASKED)
    softmax_out = jnp.exp(scores_again - log_total)
    weights_again = softmax_out.astype(bf16)
    grad_weights = jnp.einsum("qhe,khe->hqk", grad_heads, all_values, preferred_element_type=f32)
    grad_scores = (
        softmax_out * (grad_weights - jnp.sum(softmax_out * grad_weights, axis=-1, keepdims=True))
    ).astype(bf16)
    grad_queries = (
        jnp.einsum("hqk,khe->qhe", grad_scores, all_keys, preferred_element_type=f32) * score_scale
    )
    grad_keys = (
        jnp.einsum("hqk,qhe->khe", grad_scores, queries, preferred_element_type=f32) * score_scale
    )
    grad_values = jnp.einsum("hqk,qhe->khe", weights_again, grad_heads, preferred_element_type=f32)
    grad_kv = jnp.stack([grad_keys, grad_values])
    own_part = grad_kv[:, reach_back * tok_count :]
    for hop_count in range(1, reach_back + 1):
        segment_start = (reach_back - hop_count) * tok_count
        segment = grad_kv[:, segment_start : segment_start + tok_count]
        own_part = own_part + shifted(segment, EP, -hop_count)
    grad_raw = (
        jnp.stack(
            [
                rotate(grad_queries, cosine, sine_part, -1.0),
                rotate(own_part[0], cosine, sine_part, -1.0),
                own_part[1],
            ]
        )
        .reshape(3, tok_count, -1)
        .astype(bf16)
    )
    grad_attention_bias = jnp.sum(grad_raw.astype(f32), axis=1)
    grad_attention_in = jnp.einsum(
        "td,ste->sde", normed_attention, grad_raw, preferred_element_type=f32
    )
    grad_normed_attention = tensor_total(
        jnp.einsum("ste,sde->td", grad_raw, in_full, preferred_element_type=f32)
    )
    grad_in_norm, grad_attention_gain = norm_back(
        grad_normed_attention, attention_gain, inverse_one, normed_one
    )
    grad_input = (grad_residual + grad_in_norm).astype(bf16)
    grad_attention_in, grad_attention_out, grad_shared_in, grad_shared_down = (
        lax.psum_scatter(
            grad_attention_in.astype(jnp.bfloat16), EP, scatter_dimension=1, tiled=True
        ).astype(jnp.float32),
        lax.psum_scatter(
            grad_attention_out.astype(jnp.bfloat16), EP, scatter_dimension=1, tiled=True
        ).astype(jnp.float32),
        lax.psum_scatter(
            grad_shared_in.astype(jnp.bfloat16), EP, scatter_dimension=1, tiled=True
        ).astype(jnp.float32),
        lax.psum_scatter(
            grad_shared_down.astype(jnp.bfloat16), EP, scatter_dimension=1, tiled=True
        ).astype(jnp.float32),
    )
    (
        grad_attention_gain,
        grad_attention_bias,
        grad_feedforward_gain,
        grad_shared_gate,
        grad_router,
    ) = (
        lax.psum(grad_attention_gain.astype(jnp.bfloat16), EP).astype(jnp.float32),
        lax.psum(grad_attention_bias.astype(jnp.bfloat16), EP).astype(jnp.float32),
        lax.psum(grad_feedforward_gain.astype(jnp.bfloat16), EP).astype(jnp.float32),
        lax.psum(grad_shared_gate.astype(jnp.bfloat16), EP).astype(jnp.float32),
        lax.psum(grad_router.astype(jnp.bfloat16), EP).astype(jnp.float32),
    )
    return (
        layer_output,
        grad_input,
        grad_attention_gain,
        grad_attention_in,
        grad_attention_bias,
        grad_attention_out,
        grad_feedforward_gain,
        grad_shared_in,
        grad_shared_down,
        grad_shared_gate,
        grad_router,
        grad_expert_in,
        grad_expert_down,
    )


def solution(mesh):
    return jax.shard_map(
        per_device,
        mesh=mesh,
        in_specs=(
            P(EP, None),
            P(),
            P(None, EP, TP),
            P(None, TP),
            P(TP, EP),
            P(),
            P(None, EP, TP),
            P(TP, EP),
            P(),
            P(),
            P(EP, None, None, TP),
            P(EP, TP, None),
            P(EP, None),
            P(),
            P(EP, None),
        ),
        out_specs=(
            P(EP, None),
            P(EP, None),
            P(),
            P(None, EP, TP),
            P(None, TP),
            P(TP, EP),
            P(),
            P(None, EP, TP),
            P(TP, EP),
            P(),
            P(),
            P(EP, None, None, TP),
            P(EP, TP, None),
        ),
        check_vma=False,
    )
```

```python
import functools
import math

import jax
import jax.numpy as jnp
from jax import lax
from jax.experimental import pallas as pl
from jax.experimental.pallas import tpu as pltpu
from jax.sharding import PartitionSpec as P

EP, TP = "ep", "tp"
HD = 128
WINDOW = 1024


HIGHEST = lax.Precision.HIGHEST
EPSILON = 1e-06
ROPE_BASE = 1000000.0
MASKED = -1000000000.0


def shifted(value, axis, steps):
    count = lax.axis_size(axis)
    leading, last = (max(0, -steps), min(count, count - steps))
    return lax.ppermute(value, axis, [(source, source + steps) for source in range(leading, last)])


def tensor_total(partial_sum):
    return lax.psum(partial_sum, TP)


def rms_parts(values):
    inverse = lax.rsqrt(jnp.mean(values * values, axis=-1, keepdims=True) + EPSILON)
    return (inverse, values * inverse)


def norm_back(grad_rows, gain_vec, inverse, normed):
    scaled = grad_rows * gain_vec
    grad_in = inverse * (scaled - normed * jnp.mean(scaled * normed, axis=-1, keepdims=True))
    return (grad_in, jnp.sum(grad_rows * normed, axis=0))


def doc_table(document_lengths, positions):
    doc_ends = jnp.cumsum(document_lengths)
    starts_all = jnp.concatenate([doc_ends - document_lengths, doc_ends[-1:]])
    doc_ids = jnp.sum((positions[:, None] >= doc_ends[None, :]).astype(jnp.int32), axis=1)
    matches = (
        doc_ids[:, None] == jnp.arange(document_lengths.shape[0] + 1, dtype=jnp.int32)[None, :]
    )
    doc_begin = jnp.sum(jnp.where(matches, starts_all[None, :], 0), axis=1)
    rope_pos = positions - doc_begin
    valid_mask = positions < doc_ends[-1]
    doc_ids = jnp.where(positions < 0, -1, doc_ids)
    return (doc_ids, rope_pos, valid_mask)


def rope_angles(rope_pos, head_dim):
    half_width = head_dim // 2
    freqs = jnp.power(ROPE_BASE, -2.0 * jnp.arange(half_width, dtype=jnp.float32) / head_dim)
    angles = rope_pos.astype(jnp.float32)[:, None] * freqs[None, :]
    return (jnp.cos(angles)[:, None, :], jnp.sin(angles)[:, None, :])


def rotate(values, cosine, sine_part, turn_sign):
    half_width = values.shape[-1] // 2
    first_part = values[..., :half_width]
    second_part = values[..., half_width:]
    return jnp.concatenate(
        [
            first_part * cosine - turn_sign * second_part * sine_part,
            second_part * cosine + turn_sign * first_part * sine_part,
        ],
        axis=-1,
    )


def silu_parts(gate_pre):
    sig_gate = jax.nn.sigmoid(gate_pre)
    return (gate_pre * sig_gate, sig_gate * (1.0 + gate_pre * (1.0 - sig_gate)))


NN = (((1,), (0,)), ((), ()))
NT = (((1,), (1,)), ((), ()))
TN = (((0,), (0,)), ((), ()))


def product(left, right, dims=NN):
    return lax.dot_general(left, right, dims, preferred_element_type=jnp.float32)


def turned(values, cosine, sine):
    half = values.shape[1] // 2
    swapped = jnp.concatenate([values[:, half:], values[:, :half]], axis=1)
    return values * cosine + swapped * sine


def masked_scores(queries, keys, query_doc, key_doc):
    tokens, count = queries.shape[0], keys.shape[0]
    scores = product(queries, keys, NT) * (1.0 / math.sqrt(HD))
    ahead = lax.broadcasted_iota(jnp.int32, (tokens, count), 0) + (count - tokens)
    distance = ahead - lax.broadcasted_iota(jnp.int32, (tokens, count), 1)
    allowed = (query_doc == key_doc) & (distance >= 0) & (distance < WINDOW)
    return jnp.where(allowed, scores, MASKED)


def attend_kernel(queries, keys, values, query_doc, key_doc, valid, heads, log_totals):
    count = keys.shape[1] * keys.shape[2]
    keys, values = keys[0].reshape(count, HD), values[0].reshape(count, HD)
    scores = masked_scores(queries[...], keys, query_doc[...], key_doc[...])
    row_max = jnp.max(scores, axis=1, keepdims=True)
    terms = jnp.exp(scores - row_max)
    total = jnp.sum(terms, axis=1, keepdims=True)
    weights = (terms / total).astype(jnp.bfloat16)
    heads[...] = (product(weights, values) * valid[...]).astype(jnp.bfloat16)
    log_totals[0] = row_max + jnp.log(total)


def attention_specs(tokens, blocks):
    def column(*dims):
        return pl.BlockSpec(dims, lambda h: (0,) * len(dims))

    head = pl.BlockSpec((tokens, HD), lambda h: (0, h))
    keys = pl.BlockSpec((1, blocks, tokens, HD), lambda h: (0, 0, 0, h))
    values = pl.BlockSpec((1, blocks, tokens, HD), lambda h: (1, 0, 0, h))
    logs = pl.BlockSpec((1, tokens, 1), lambda h: (h, 0, 0))
    return head, keys, values, column(tokens, 1), column(1, blocks * tokens), logs


def attend(queries, keys_values, query_doc, key_doc, valid):
    tokens, columns = queries.shape
    blocks = keys_values.shape[1]
    head, keys, values, column, row, logs = attention_specs(tokens, blocks)
    shape = jax.ShapeDtypeStruct
    return pl.pallas_call(
        attend_kernel,
        grid=(columns // HD,),
        in_specs=[head, keys, values, column, row, column],
        out_specs=(head, logs),
        out_shape=(
            shape((tokens, columns), jnp.bfloat16),
            shape((columns // HD, tokens, 1), jnp.float32),
        ),
        compiler_params=pltpu.CompilerParams(vmem_limit_bytes=40 * 2**20),
        name="attend",
    )(queries, keys_values, keys_values, query_doc, key_doc, valid)


RING = 8
NO_SLOT = 1 << 20
RIGHT, LEFT, OVER_X, OVER_CORE, OVER_FAR, LOCAL, SCALARS = range(7)
MESH_ID = pl.DeviceIdType.MESH


def ring_place(ep):
    z, y = ep // 2, ep % 2
    return z + y * (7 - 2 * z)


def ring_member(place):
    upper = place // 4
    return 2 * place + upper * (15 - 4 * place)


class Peers:
    def __init__(self):
        self.ep, self.tp = lax.axis_index(EP), lax.axis_index(TP)
        self.x, self.core = self.tp // 2, self.tp % 2
        self.z, self.y = self.ep // 2, self.ep % 2
        self.place = ring_place(self.ep)
        self.right = (self.block(1), self.tp)
        self.left = (self.block(RING - 1), self.tp)
        self.quarter = self.tp
        self.x_quarter = (1 - self.x) * 2 + self.core
        self.core_quarter = self.x * 2 + 1 - self.core
        self.far_quarter = (1 - self.x) * 2 + 1 - self.core
        self.x_peer = (self.ep, self.x_quarter)
        self.core_peer = (self.ep, self.core_quarter)
        self.far_peer = (self.ep, self.far_quarter)
        self.y_peer = (self.z * 2 + 1 - self.y, self.tp)

    def block(self, step):
        return ring_member((self.place + step + RING) % RING)


def greet(peers):
    barrier = pltpu.get_barrier_semaphore()
    for peer in peers:
        pl.semaphore_signal(barrier, inc=1, device_id=peer, device_id_type=MESH_ID)
    pl.semaphore_wait(barrier, len(peers))


class Copies:
    def __init__(self, send_sems, recv_sems):
        self.send_sems, self.recv_sems = send_sems, recv_sems
        self.count = 0
        self.sent = []
        self.landing = {}

    def describe(self, source, target, peer, index):
        return pltpu.make_async_remote_copy(
            src_ref=source,
            dst_ref=target,
            send_sem=self.send_sems.at[index],
            recv_sem=self.recv_sems.at[index],
            device_id=peer,
            device_id_type=MESH_ID,
        )

    def send(self, key, source, target, landing, peer):
        index = self.count
        self.count += 1
        copy = self.describe(source, target, peer, index)
        copy.start()
        self.sent.append(copy)
        self.landing[key] = self.describe(landing, landing, peer, index).wait_recv

    def local(self, key, source, target):
        index = self.count
        self.count += 1
        copy = pltpu.make_async_copy(source, target, self.send_sems.at[index])
        copy.start()
        self.landing[key] = copy.wait

    def arrive(self, *key):
        self.landing.pop(key)()

    def finish(self):
        for wait in self.landing.values():
            wait()
        for copy in self.sent:
            copy.wait_send()


def remote_params(collective_id, vmem=48):
    return pltpu.CompilerParams(
        collective_id=collective_id, has_side_effects=True, vmem_limit_bytes=vmem * 2**20
    )


def semaphores(count):
    return [pltpu.SemaphoreType.DMA((count,))] * 2


IN_PLACE = pl.BlockSpec(memory_space=pl.ANY)
IN_VMEM = pl.BlockSpec(memory_space=pltpu.VMEM)


class LateCopies(Copies):
    def send(self, key, source, target, landing, peer):
        index = self.count
        self.count += 1
        self.describe(source(), target(), peer, index).start()
        self.sent.append(lambda: self.describe(source(), target(), peer, index).wait_send())
        self.landing[key] = lambda: self.describe(landing(), landing(), peer, index).wait_recv()

    def local(self, key, source, target):
        index = self.count
        self.count += 1

        def copy():
            return pltpu.make_async_copy(source(), target(), self.send_sems.at[index])

        copy().start()
        self.landing[key] = lambda: copy().wait()

    def finish(self):
        for wait in list(self.landing.values()) + self.sent:
            wait()


def feed_block(
    rank_row, rank_column, gate_rows, scale, token_rows, token_cotangent,
    expert_in, expert_down, shared, staged, between, out_terms, back_terms, scalar_out,
):
    (
        out_part, back_part, slot_rows, slot_cotangent, grad_pre, gated, grad_shared_pre, scaled,
    ) = staged
    bf16, f32 = jnp.bfloat16, jnp.float32
    experts, slots, _ = slot_rows.shape
    tokens = token_rows.shape[0]
    hidden_count = gated.shape[2]
    all_slots = experts * slots
    silu, slope = silu_parts(product(token_rows, shared[0], NT))
    up = product(token_rows, shared[1], NT)
    hidden = (silu * up).astype(bf16).astype(f32)
    scaled_hidden = (scale * hidden).astype(bf16)
    back = product(token_cotangent, shared[2], NT)
    scalar_out(None, jnp.sum(jnp.swapaxes(hidden * back, 0, 1), axis=0, keepdims=True))
    back = scale * back
    gate_grad = (back * up * slope).astype(bf16)
    up_grad = (back * silu).astype(bf16)
    between()
    scaled[...] = scaled_hidden
    grad_shared_pre[0] = gate_grad
    grad_shared_pre[1] = up_grad
    order = lax.broadcasted_iota(jnp.int32, (all_slots, tokens), 0)
    spread_order = lax.broadcasted_iota(jnp.int32, (tokens, all_slots), 1)
    hits, spread = None, None
    for expert in range(experts):
        row_hits = order == rank_row[expert : expert + 1, :] + expert * slots
        column_hits = spread_order == rank_column[:, expert : expert + 1] + expert * slots
        hits = row_hits if hits is None else hits | row_hits
        spread = column_hits if spread is None else spread | column_hits
    place = hits.astype(bf16)
    taken = product(place, token_rows).astype(bf16)
    taken_cotangent = product(place, token_cotangent).astype(bf16)
    for ref, values in ((slot_rows, taken), (slot_cotangent, taken_cotangent)):
        for expert in range(experts):
            ref[expert] = values[expert * slots : (expert + 1) * slots]
    for expert in range(experts):
        mine = slice(expert * slots, (expert + 1) * slots)
        gate = jnp.sum(
            jnp.where(hits[mine], gate_rows[expert : expert + 1], 0.0), axis=1, keepdims=True
        )
        pre = product(taken[mine], expert_in[expert], NT)
        silu, slope = silu_parts(pre[:, :hidden_count])
        up = pre[:, hidden_count:]
        hidden = (silu * up).astype(bf16).astype(f32)
        gated_hidden = (gate * hidden).astype(bf16)
        gated[expert] = gated_hidden
        back = product(taken_cotangent[mine], expert_down[expert], NT)
        slot_grad = jnp.sum(hidden * back, axis=1, keepdims=True)
        scalar_out(
            expert, jnp.sum(jnp.where(hits[mine], slot_grad, 0.0), axis=0, keepdims=True)
        )
        back = gate * back
        gate_grad_e = (back * up * slope).astype(bf16)
        up_grad_e = (back * silu).astype(bf16)
        grad_pre[0, expert] = gate_grad_e
        grad_pre[1, expert] = up_grad_e
        out_terms[mine, :] = product(gated_hidden, expert_down[expert]).astype(bf16)
        both_grads = jnp.concatenate([gate_grad_e, up_grad_e], axis=1)
        back_terms[mine, :] = product(both_grads, expert_in[expert]).astype(bf16)
    spread = spread.astype(bf16)
    out_part[...] = product(
        jnp.concatenate([spread, scaled_hidden], axis=1), out_terms[...]
    ).astype(bf16)
    back_part[...] = product(
        jnp.concatenate([spread, gate_grad, up_grad], axis=1), back_terms[...]
    ).astype(bf16)


def gather_feed_kernel(
    rows, cotangent, scales, routes, expert_in, expert_down, shared_blocks,
    all_rows, all_cotangent, all_scales,
    out_part, back_part, slot_rows, slot_cotangent, grad_pre, gated, grad_shared_pre, scaled,
    scalars,
    rank_row, rank_column, shared, out_terms, back_terms, held_rows, held_cotangent,
    stage_out, stage_back, stage_rows, stage_cotangent, stage_pre, stage_gated, stage_shared,
    stage_scaled,
    load_sems, store_sems, send_sems, recv_sems,
):
    me = Peers()
    copies = LateCopies(send_sems, recv_sems)
    count = rows.shape[0]
    half, part = count // 2, count // 4
    q, qx, qc, qd = me.quarter, me.x_quarter, me.core_quarter, me.far_quarter
    blocks = {step: me.block(step) for step in range(-4, 5)}
    low, high, whole = pl.ds(0, half), pl.ds(half, half), pl.ds(0, count)
    own, other, scale = range(3)
    full = (all_rows, all_cotangent)
    sides = ((RIGHT, me.right, -1, 0), (LEFT, me.left, 1, 1))
    greet([me.right, me.left, me.x_peer, me.core_peer, me.far_peer])

    def push(key, kind, step, quarter, which, peer, landing_step, landing_quarter, source=None):
        def cell():
            return full[kind].at[blocks[step], quarter, which]

        def landing():
            return full[kind].at[blocks[landing_step], landing_quarter, which]

        copies.send((kind,) + key, source or cell, cell, landing, peer)

    push((OVER_X, other, 0), 0, 0, q, low, me.x_peer, 0, qx, lambda: rows.at[low])
    for side, peer, sign, keep in sides:
        push((side, own, 1), 1, 0, q, whole, peer, sign, q, lambda: cotangent.at[q])
        push((side, other, 1), 1, 0, qx, low, peer, sign, qx, lambda: cotangent.at[qx, low])
    push((OVER_X, own, 0), 0, 0, q, high, me.x_peer, 0, qx, lambda: rows.at[high])
    push((OVER_CORE, own, 0), 0, 0, q, whole, me.core_peer, 0, qc, lambda: rows)
    for side, peer, sign, keep in sides:
        push((side, own, 1), 0, 0, q, whole, peer, sign, q, lambda: rows)
    copies.local((LOCAL, 0), lambda: rows, lambda: all_rows.at[blocks[0], q])
    copies.local((LOCAL, 1), lambda: cotangent, lambda: all_cotangent.at[blocks[0]])

    def scales_of(quarter):
        return lambda: all_scales.at[blocks[0], quarter]

    for way, peer, quarter in (
        (OVER_X, me.x_peer, qx),
        (OVER_CORE, me.core_peer, qc),
        (OVER_FAR, me.far_peer, qd),
    ):
        copies.send((way, scale, 0), lambda: scales, scales_of(q), scales_of(quarter), peer)
    copies.local((LOCAL, scale), lambda: scales, scales_of(q))
    experts, _, width = expert_in.shape
    all_slots = experts * slot_rows.shape[2]
    shared_count, across = shared.shape[1], shared_blocks.shape[3]
    for block in range(RING):
        shared[:, :, block * across : (block + 1) * across] = shared_blocks[block]
    out_terms[all_slots:, :] = shared[2]
    back_terms[all_slots : all_slots + shared_count, :] = shared[0]
    back_terms[all_slots + shared_count :, :] = shared[1]
    first_expert, scale_at = me.ep * experts, me_scale_row(experts)
    tokens = routes.shape[2]
    taken = []
    for block in range(RING):
        for expert in range(experts):
            chosen = routes[block] == first_expert + expert
            taken.append(jnp.max(chosen.astype(jnp.float32), axis=0, keepdims=True))
    taken = jnp.concatenate(taken, axis=0)
    down = lax.broadcasted_iota(jnp.int32, (tokens, tokens), 0)
    right = lax.broadcasted_iota(jnp.int32, (tokens, tokens), 1)
    rank = product(taken.astype(jnp.bfloat16), (right < down).astype(jnp.bfloat16), NT)
    kept = (taken > 0.0) & (rank < slot_rows.shape[2])
    rank = jnp.where(kept, rank, float(NO_SLOT))
    column = product((right == down).astype(jnp.bfloat16), rank.astype(jnp.bfloat16), NT)
    for block in range(RING):
        mine = slice(block * experts, (block + 1) * experts)
        rank_row[block] = rank[mine].astype(jnp.int32)
        rank_column[block] = column[:, mine].astype(jnp.int32)
    scalars[...] = jnp.zeros_like(scalars)
    copies.arrive(0, OVER_X, other, 0)
    for side, peer, sign, keep in sides:
        push((side, other, 1), 0, 0, qx, low, peer, sign, qx)
    for way in (OVER_X, OVER_CORE, OVER_FAR):
        copies.arrive(way, scale, 0)
    copies.arrive(LOCAL, scale)

    def push_scales(step, side, peer, sign):
        def cell():
            return all_scales.at[blocks[step]]

        copies.send(
            (side, scale, abs(step) + 1), cell, cell, lambda: all_scales.at[blocks[step + sign]], peer
        )

    for side, peer, sign, keep in sides:
        push_scales(0, side, peer, sign)
    copies.arrive(0, OVER_X, own, 0)
    push((OVER_CORE, other, 0), 0, 0, qx, whole, me.core_peer, 0, qd)

    def hop_in(kind, hop):
        for side, peer, sign, keep in sides:
            step = sign * hop
            if hop < 4:
                copies.arrive(kind, side, own, hop)
                which = whole if hop < 3 else pl.ds(keep * half, half)
                push((side, own, hop + 1), kind, step, q, which, peer, step + sign, q)
                push((OVER_X, own, step), kind, step, q, high, me.x_peer, step, qx)
                push((OVER_CORE, own, step), kind, step, q, whole, me.core_peer, step, qc)
                copies.arrive(kind, side, other, hop)
                which = low if hop < 3 else pl.ds(keep * part, part)
                push((side, other, hop + 1), kind, step, qx, which, peer, step + sign, qx)
                push((OVER_CORE, other, step), kind, step, qx, low, me.core_peer, step, qd)
        if hop == 4:
            copies.arrive(kind, LEFT, own, 4)
            push((OVER_X, own, 4), kind, 4, q, high, me.x_peer, 4, qx)
            copies.arrive(kind, RIGHT, own, 4)
            push((OVER_CORE, own, 4), kind, 4, q, whole, me.core_peer, 4, qc)
            copies.arrive(kind, LEFT, other, 4)
            copies.arrive(kind, RIGHT, other, 4)
            push((OVER_CORE, other, 4), kind, 4, qx, low, me.core_peer, 4, qd)

    def over_x(kind, steps):
        for step in steps:
            copies.arrive(kind, OVER_X, own, step)
            push((OVER_CORE, scale, step), kind, step, qx, high, me.core_peer, step, qd)

    def scales_in(hop):
        for side, peer, sign, keep in sides:
            if hop < 4 or side == RIGHT:
                copies.arrive(side, scale, hop)
                if hop < 3 or (hop == 3 and side == RIGHT):
                    push_scales(sign * hop, side, peer, sign)

    def load(slot, step):
        pairs = ((all_rows, held_rows), (all_cotangent, held_cotangent))
        return [
            pltpu.make_async_copy(source.at[blocks[step]], held.at[slot], load_sems.at[slot, kind])
            for kind, (source, held) in enumerate(pairs)
        ]

    def complete(steps, slots):
        for step in steps:
            for kind in range(2):
                if step != 0:
                    for piece in (own, other, scale):
                        copies.arrive(kind, OVER_CORE, piece, step)
        moves = [load(slot, step) for slot, step in zip(slots, steps)]
        for move in moves[0] + moves[-1] if len(moves) > 1 else moves[0]:
            move.start()
        for move in moves[0]:
            move.wait()

    staged = (
        stage_out, stage_back, stage_rows, stage_cotangent, stage_pre, stage_gated, stage_shared,
        stage_scaled,
    )

    def stores(block):
        targets = (
            out_part.at[block], back_part.at[block], slot_rows.at[:, block],
            slot_cotangent.at[:, block], grad_pre.at[:, :, block], gated.at[:, block],
            grad_shared_pre.at[:, block], scaled.at[block],
        )
        return [
            pltpu.make_async_copy(stage, target, store_sems.at[index])
            for index, (stage, target) in enumerate(zip(staged, targets))
        ]


    copies.arrive(LOCAL, 0)
    copies.arrive(LOCAL, 1)
    for piece in (own, other):
        copies.arrive(0, OVER_CORE, piece, 0)
    complete((0,), (0,))

    def turn(index, carry):
        far = (index + 1) // 2
        step = far * (1 - 2 * (index % 2)) + (index // 7) * 8
        block = ring_member((me.place + step + RING) % RING)
        slot = index % 2

        def between():
            for hop in (1, 2, 3, 4):

                @pl.when(index == max(0, 2 * hop - 3))
                def _():
                    hop_in(1, hop)

            @pl.when(index > 0)
            def _():
                for move in stores(0):
                    move.wait()

        def scalar_out(expert, values):
            row = scale_at if expert is None else first_expert + expert
            for quarter in range(4):
                part = values[:, quarter * count : (quarter + 1) * count]
                scalars[block, quarter, pl.ds(row, 1), :] = part

        rows_here = held_rows[slot].reshape(4 * count, width)
        cotangent_here = held_cotangent[slot].reshape(4 * count, width)
        quarters = [all_scales[block, quarter] for quarter in range(4)]
        columns = jnp.concatenate([jnp.swapaxes(values, 0, 1) for values in quarters], axis=0)
        gate_rows = [
            jnp.concatenate(
                [all_scales[block, quarter, pl.ds(first_expert + e, 1), :] for quarter in range(4)],
                axis=1,
            )
            for e in range(experts)
        ]
        feed_block(
            rank_row[block],
            rank_column[block],
            jnp.concatenate(gate_rows, axis=0),
            columns[:, scale_at : scale_at + 1],
            rows_here,
            cotangent_here,
            expert_in,
            expert_down,
            shared,
            staged,
            between,
            out_terms,
            back_terms,
            scalar_out,
        )
        for move in stores(block):
            move.start()

        for hop in (1, 2, 3, 4):

            @pl.when(index == max(0, 2 * hop - 3))
            def _():
                scales_in(hop)
                hop_in(0, hop)
                if hop > 1:
                    for move in load(0, hop - 1):
                        move.wait()

            @pl.when(index == 2 * hop - 2)
            def _():
                steps = (-hop, hop) if hop < 4 else (4,)
                over_x(1, steps)
                over_x(0, steps)
                complete(steps, (1, 0))

        return carry

    lax.fori_loop(0, RING, turn, 0)
    for move in stores(0):
        move.wait()
    copies.finish()


def me_scale_row(experts):
    return RING * experts


def gather_feed(
    rows, cotangent, scales, routes, expert_in, expert_down, shared, capacity, collective_id
):
    bf16, f32 = jnp.bfloat16, jnp.float32
    blocks, _, tokens = routes.shape
    experts = expert_in.shape[0]
    count, width = rows.shape
    hidden = expert_in.shape[1] // 2
    slice_hidden = shared.shape[2]
    shape = jax.ShapeDtypeStruct
    stages = (
        (tokens, width),
        (tokens, width),
        (experts, capacity, width),
        (experts, capacity, width),
        (2, experts, capacity, hidden),
        (experts, capacity, hidden),
        (2, tokens, slice_hidden),
        (tokens, slice_hidden),
    )
    return pl.pallas_call(
        gather_feed_kernel,
        out_shape=(
            shape((RING, 4, count, width), bf16),
            shape((RING, 4, count, width), bf16),
            shape((RING, 4) + scales.shape, f32),
            shape((blocks, tokens, width), bf16),
            shape((blocks, tokens, width), bf16),
            shape((experts, blocks, capacity, width), bf16),
            shape((experts, blocks, capacity, width), bf16),
            shape((2, experts, blocks, capacity, hidden), bf16),
            shape((experts, blocks, capacity, hidden), bf16),
            shape((2, blocks, tokens, slice_hidden), bf16),
            shape((blocks, tokens, slice_hidden), bf16),
            shape((RING, 4) + scales.shape, f32),
        ),
        in_specs=[IN_VMEM] * 7,
        out_specs=(IN_PLACE,) * 2 + (IN_VMEM,) + (IN_PLACE,) * 8 + (IN_VMEM,),
        scratch_shapes=[
            pltpu.VMEM((blocks, experts, tokens), jnp.int32),
            pltpu.VMEM((blocks, tokens, experts), jnp.int32),
            pltpu.VMEM((3, slice_hidden, width), bf16),
            pltpu.VMEM((experts * capacity + slice_hidden, width), bf16),
            pltpu.VMEM((experts * capacity + 2 * slice_hidden, width), bf16),
            pltpu.VMEM((2, 4, count, width), bf16),
            pltpu.VMEM((2, 4, count, width), bf16),
        ]
        + [pltpu.VMEM(stage, bf16) for stage in stages]
        + [pltpu.SemaphoreType.DMA((2, 2)), pltpu.SemaphoreType.DMA((len(stages),))]
        + semaphores(160),
        compiler_params=remote_params(collective_id, 62),
        name="gather_feed",
    )(rows, cotangent, scales, routes, expert_in, expert_down, shared)


def add_into(total, term, rows, tile=32):
    tile = min(tile, rows)

    def step(index, carry):
        here = pl.ds(pl.multiple_of(index * tile, tile), tile)
        summed = total[here, :].astype(jnp.float32) + term[here, :].astype(jnp.float32)
        total[here, :] = summed.astype(total.dtype)
        return carry

    lax.fori_loop(0, rows // tile, step, 0)


class WeightGrads:
    def __init__(self, jobs, left, right, sums, low, sems, out_sems):
        self.jobs, self.left, self.right = jobs, left, right
        self.sums, self.low, self.sems, self.out_sems = sums, low, sems, out_sems
        self.next = 0
        self.stores = {}
        self.fetch(0, 0, 0).start()

    def fetch(self, job, index, slot):
        left, right, _ = self.jobs[job]
        chunk, rows, columns, _ = self.size(job)
        here = pl.ds(pl.multiple_of(index * chunk, chunk), chunk)
        return Pair(
            pltpu.make_async_copy(
                left.at[here], self.left[rows].at[slot, pl.ds(0, chunk)], self.sems.at[slot, 0]
            ),
            pltpu.make_async_copy(
                right.at[here], self.right.at[slot, pl.ds(0, chunk)], self.sems.at[slot, 1]
            ),
        )

    def size(self, job):
        left, right, _ = self.jobs[job]
        depth, rows = left.shape
        chunk = min(self.right.shape[1], depth)
        while depth % (2 * chunk):
            chunk -= 128
        return chunk, rows, right.shape[1], depth // chunk

    def run(self, count=1):
        for job in range(self.next, min(self.next + count, len(self.jobs))):
            self.one(job)

    def one(self, job):
        self.next = job + 1
        chunk, rows, _, steps = self.size(job)
        which = job % 2
        if which in self.stores:
            self.stores.pop(which).wait()
        total = self.sums.at[which, pl.ds(0, rows)]

        def step(index, carry):
            slot = index % 2

            @pl.when(index + 1 < steps)
            def _():
                self.fetch(job, index + 1, 1 - slot).start()

            if job + 1 < len(self.jobs):

                @pl.when(index + 1 == steps)
                def _():
                    self.fetch(job + 1, 0, 0).start()

            self.fetch(job, index, slot).wait()
            term = product(
                self.left[rows][slot, pl.ds(0, chunk)], self.right[slot, pl.ds(0, chunk)], TN
            )

            @pl.when(index == 0)
            def _():
                total[...] = term

            @pl.when(index > 0)
            def _():
                total[...] += term

            return carry

        lax.fori_loop(0, steps, step, 0)
        out = self.jobs[job][2]
        source = self.low.at[which, pl.ds(0, rows)]
        source[...] = total[...].astype(out.dtype)
        if out.ndim == source.ndim:
            moves = [pltpu.make_async_copy(source, out, self.out_sems.at[which, 0])]
        else:
            across = out.shape[2]
            moves = [
                pltpu.make_async_copy(
                    source.at[:, pl.ds(place * across, across)], out.at[place], self.out_sems.at[which, place]
                )
                for place in range(out.shape[0])
            ]
        self.stores[which] = Pair(*moves)
        self.stores[which].start()

    def finish(self):
        self.run(len(self.jobs))
        for store in self.stores.values():
            store.wait()


class Pair:
    def __init__(self, *moves):
        self.moves = moves

    def start(self):
        for move in self.moves:
            move.start()

    def wait(self):
        for move in self.moves:
            move.wait()


def scatter_kernel(
    back_part, ffn_part, scalars, slot_rows, slot_cotangent, grad_pre, gated,
    all_rows, all_cotangent, grad_shared_pre, scaled,
    back_sum, ffn_sum, out_scalars, grad_expert_in, grad_expert_down, grad_shared,
    held, core_in, x_in, ring_q, ring_x, last_in,
    s_held, s_core, s_x, s_ring,
    job_left, job_short, job_right, job_sums, job_low, job_sems, job_out_sems,
    free, send_sems, recv_sems,
):
    me = Peers()
    copies = Copies(send_sems, recv_sems)
    parts, outs = (back_part, ffn_part), (back_sum, ffn_sum)
    count = back_part.shape[2]
    half, piece = count // 2, count // 4
    q, qx, qc, qd = me.quarter, me.x_quarter, me.core_quarter, me.far_quarter
    own, other, last = range(3)
    peers = {RIGHT: me.right, LEFT: me.left}
    greet([me.right, me.left, me.x_peer, me.core_peer])
    order = (4, 3, 5, 2, 6, 1, 7, 0)

    def load(kind):
        for k in order:
            for slot, mine in ((0, q), (1, qx)):
                copies.local(
                    (kind, LOCAL, k, slot), parts[kind].at[me.block(k), mine], held.at[kind, k, slot]
                )

    def swap_cores(kind):
        for k in order:
            for slot, theirs in ((0, qc), (1, qd)):
                target = core_in.at[k, slot]
                copies.send(
                    (kind, OVER_CORE, k, slot),
                    parts[kind].at[me.block(k), theirs],
                    target,
                    target,
                    me.core_peer,
                )

    swap_cores(0)
    load(0)
    for k in range(RING):
        for slot, mine, theirs in ((0, q, qc), (1, qx, qd)):
            copies.local((SCALARS, LOCAL, k, slot), scalars.at[me.block(k), mine], s_held.at[slot, k])
            target = s_core.at[slot, k]
            copies.send(
                (SCALARS, OVER_CORE, k, slot),
                scalars.at[me.block(k), theirs],
                target,
                target,
                me.core_peer,
            )

    def prepare(kind, *blocks):
        for k in blocks:
            for slot in (1, 0):
                copies.arrive(kind, LOCAL, k, slot)
                copies.arrive(kind, OVER_CORE, k, slot)
                add_into(held.at[kind, k, slot], core_in.at[k, slot], count)
                if slot == 1:
                    source = held.at[kind, k, 1, pl.ds(half, half)]
                    target = x_in.at[kind, k]
                    copies.send((kind, OVER_X, k), source, target, target, me.x_peer)

    def over_x(kind, *blocks):
        for k in blocks:
            copies.arrive(kind, OVER_X, k)
            add_into(held.at[kind, k, 0, pl.ds(half, half)], x_in.at[kind, k], half)

    def pass_on(kind, side, hop, k):
        if hop == 0:
            rows_q, rows_x = pl.ds(side * half, half), pl.ds(side * piece, piece)
        else:
            rows_q, rows_x = pl.ds(0, count), pl.ds(0, half)
        for which, landing, rows in ((own, ring_q, rows_q), (other, ring_x, rows_x)):
            target = landing.at[kind, side, hop, rows]
            source = held.at[kind, k, which, rows]
            copies.send((kind, side, which, hop), source, target, target, peers[side])

    def take_in(kind, side, hop, k):
        if hop == 0:
            span_q, span_x, at_q, at_x = half, piece, side * half, side * piece
        else:
            span_q, span_x, at_q, at_x = count, half, 0, 0
        for which, landing, span, at in (
            (own, ring_q, span_q, at_q),
            (other, ring_x, span_x, at_x),
        ):
            copies.arrive(kind, side, which, hop)
            rows = pl.ds(at, span)
            add_into(held.at[kind, k, which, rows], landing.at[kind, side, hop, rows], span)

    def hop_on(kind, hop):
        right_block, left_block = 4 - hop, 4 + hop
        if hop == 0:
            pass_on(kind, RIGHT, 0, 4)
            pass_on(kind, LEFT, 0, 4)
            return
        take_in(kind, RIGHT, hop - 1, right_block)
        pass_on(kind, RIGHT, hop, right_block)
        take_in(kind, LEFT, hop - 1, left_block)
        pass_on(kind, LEFT, hop, left_block)

    def pass_scalars(side, hop, k):
        target = s_ring.at[side, hop]
        copies.send((SCALARS, side, hop), s_held.at[0, k], target, target, peers[side])

    def take_scalars(side, hop, k):
        copies.arrive(SCALARS, side, hop)
        s_held[0, k] += s_ring[side, hop]

    def home(kind):
        take_in(kind, RIGHT, 3, 0)
        take_in(kind, LEFT, 3, 0)
        source, target = held.at[kind, 0, 1, pl.ds(0, half)], last_in.at[kind]
        copies.send((kind, OVER_X, last, last), source, target, target, me.x_peer)

    def home_out(kind):
        out = outs[kind]
        out[pl.ds(half, half), :] = held[kind, 0, 0, pl.ds(half, half), :].astype(out.dtype)
        copies.arrive(kind, OVER_X, last, last)
        out[pl.ds(0, half), :] = (
            held[kind, 0, 0, pl.ds(0, half), :].astype(jnp.float32)
            + last_in[kind].astype(jnp.float32)
        ).astype(out.dtype)

    experts = slot_rows.shape[0]
    jobs = []
    for expert in range(experts):
        for index in range(2):
            jobs.append(
                (grad_pre.at[index, expert], slot_rows.at[expert], grad_expert_in.at[expert, index])
            )
        jobs.append((gated.at[expert], slot_cotangent.at[expert], grad_expert_down.at[expert]))
    for index in range(2):
        jobs.append((grad_shared_pre.at[index], all_rows, grad_shared.at[:, index]))
    jobs.append((scaled, all_cotangent, grad_shared.at[:, 2]))
    prepare(0, 4, 3, 5)
    over_x(0, 4)
    hop_on(0, 0)
    prepare(0, 2, 6)
    for k in range(RING):
        for slot in (0, 1):
            copies.arrive(SCALARS, LOCAL, k, slot)
            copies.arrive(SCALARS, OVER_CORE, k, slot)
    s_held[...] += s_core[...]
    copies.send((SCALARS, OVER_X), s_held.at[1], s_x, s_x, me.x_peer)
    over_x(0, 3, 5)
    hop_on(0, 1)
    copies.arrive(SCALARS, OVER_X)
    s_held[0] += s_x[...]
    pass_scalars(RIGHT, 0, 4)
    prepare(0, 1, 7, 0)
    pl.semaphore_signal(free, inc=1, device_id=me.core_peer, device_id_type=MESH_ID)
    load(1)
    lefts = {job_left.shape[2]: job_left, job_short.shape[2]: job_short}
    grads = WeightGrads(jobs, lefts, job_right, job_sums, job_low, job_sems, job_out_sems)
    over_x(0, 2, 6)
    hop_on(0, 2)
    take_scalars(RIGHT, 0, 3)
    pass_scalars(RIGHT, 1, 3)
    pass_scalars(LEFT, 1, 5)
    pl.semaphore_wait(free, 1)
    swap_cores(1)
    over_x(0, 1, 7)
    grads.run(1)
    prepare(1, 4, 3, 5)
    hop_on(0, 3)
    take_scalars(RIGHT, 1, 2)
    take_scalars(LEFT, 1, 6)
    pass_scalars(RIGHT, 2, 2)
    pass_scalars(LEFT, 2, 6)
    over_x(0, 0)
    over_x(1, 4)
    hop_on(1, 0)
    prepare(1, 2, 6)
    over_x(1, 3, 5)
    grads.run(2)
    home(0)
    for side, k in ((RIGHT, 1), (LEFT, 7)):
        take_scalars(side, 2, k)
        pass_scalars(side, 3, k)
    hop_on(1, 1)
    home_out(0)
    prepare(1, 1, 7, 0)
    over_x(1, 2, 6)
    grads.run(2)
    hop_on(1, 2)
    over_x(1, 1, 7, 0)
    grads.run(2)
    hop_on(1, 3)
    take_scalars(RIGHT, 3, 0)
    take_scalars(LEFT, 3, 0)
    out_scalars[...] = s_held[0, 0]
    grads.finish()
    home(1)
    home_out(1)
    copies.finish()


def scatter_rows(back_part, ffn_part, scalars, fed, collective_id):
    slot_rows, slot_cotangent, grad_pre, gated, all_rows, all_cotangent, grad_shared_pre, scaled = fed
    _, _, count, width = back_part.shape
    half = count // 2
    dtype, f32 = back_part.dtype, jnp.float32
    s_shape = scalars.shape[2:]
    experts, hidden = gated.shape[0], gated.shape[2]
    shared_hidden = scaled.shape[1]
    shape = jax.ShapeDtypeStruct
    return pl.pallas_call(
        scatter_kernel,
        out_shape=(
            shape((count, width), f32),
            shape((count, width), f32),
            shape(s_shape, f32),
            shape((experts, 2, hidden, width), dtype),
            shape((experts, hidden, width), dtype),
            shape((RING, 3, shared_hidden, width // RING), dtype),
        ),
        in_specs=[IN_PLACE] * 11,
        out_specs=(IN_VMEM,) * 3 + (IN_PLACE,) * 3,
        scratch_shapes=[
            pltpu.VMEM((2, RING, 2, count, width), dtype),
            pltpu.VMEM((RING, 2, count, width), dtype),
            pltpu.VMEM((2, RING, half, width), dtype),
            pltpu.VMEM((2, 2, 4, count, width), dtype),
            pltpu.VMEM((2, 2, 4, half, width), dtype),
            pltpu.VMEM((2, half, width), dtype),
            pltpu.VMEM((2, RING) + s_shape, f32),
            pltpu.VMEM((2, RING) + s_shape, f32),
            pltpu.VMEM((RING,) + s_shape, f32),
            pltpu.VMEM((2, 4) + s_shape, f32),
            pltpu.VMEM((2, 640, hidden), dtype),
            pltpu.VMEM((2, 640, shared_hidden), dtype),
            pltpu.VMEM((2, 640, width), dtype),
            pltpu.VMEM((2, hidden, width), f32),
            pltpu.VMEM((2, hidden, width), dtype),
            pltpu.SemaphoreType.DMA((2, 2)),
            pltpu.SemaphoreType.DMA((2, RING)),
            pltpu.SemaphoreType.REGULAR,
        ]
        + semaphores(168),
        compiler_params=remote_params(collective_id, 62),
        name="scatter_rows",
    )(back_part, ffn_part, scalars, *fed)


def open_kernel(
    shard_in, shard_out, routes, rows, gain, bias, cosine, sine,
    full_in, full_out, full_routes, normed, queries, keys_values,
    sums, share_send, share_recv, send_sems, recv_sems,
):
    me = Peers()
    copies = Copies(send_sems, recv_sems)
    bf16, f32 = jnp.bfloat16, jnp.float32
    kinds, depth, width = shard_in.shape
    out_rows, columns = shard_out.shape
    tokens = rows.shape[0]
    sides = ((RIGHT, me.right, -1), (LEFT, me.left, 1))
    greet_along_z(me)

    def cell(kind, step, part, parts):
        block = me.block(step)
        if kind < kinds:
            return full_in.at[kind, block, pl.ds(part * (depth // parts), depth // parts)]
        if kind > kinds:
            return full_routes.at[block]
        across = pl.ds(pl.multiple_of(block * columns, columns), columns)
        return full_out.at[pl.ds(part * (out_rows // parts), out_rows // parts), across]

    def pass_on(side, peer, sign, kind, hop, source=None):
        if kind > kinds and hop == 3 and side == LEFT:
            return
        parts = 2 if hop == 3 else 1
        part = side if hop == 3 else 0
        step = sign * hop
        here = cell(kind, step, part, parts)
        copies.send(
            (side, kind, hop + 1),
            here if source is None else source,
            here,
            cell(kind, step + sign, part, parts),
            peer,
        )

    def hop_on(hop, order):
        for kind in order:
            source = None
            if hop == 0:
                source = shard_in.at[kind] if kind < kinds else shard_out if kind == kinds else routes
                cell(kind, 0, 0, 1)[...] = source[...]
            for side, peer, sign in sides:
                if hop > 0:
                    copies.arrive(side, kind, hop)
                pass_on(side, peer, sign, kind, hop, source)

    def multiply(kind, step):
        block = me.block(step)
        features = normed[:, pl.ds(pl.multiple_of(block * depth, depth), depth)]
        term = product(features, full_in[kind, block])
        if step == 0:
            sums[kind] = term + bias[kind : kind + 1, :]
        else:
            sums[kind] += term

    def go_round(order):
        taken = [kind for kind in order if kind < kinds]
        for hop in (1, 2, 3):
            hop_on(hop, order)
            for kind in taken:
                for step in (-hop, hop):
                    multiply(kind, step)
        for kind in order:
            for side, _, _ in sides:
                if kind <= kinds or side == RIGHT:
                    copies.arrive(side, kind, 4)
        for kind in taken:
            multiply(kind, 4)

    def heads_of(kind, turn):
        for start in range(0, width, HD):
            head = slice(start, start + HD)
            part = sums[kind, :, head]
            if turn:
                part = turned(part, cosine[...], sine[...])
            yield head, part.astype(bf16)

    first, second = (kinds + 1,) + tuple(range(kinds - 1, 0, -1)), (0, kinds)
    hop_on(0, first)
    _, scaled = rms_parts(rows[...].astype(f32))
    normed[...] = (scaled * gain[...]).astype(bf16)
    for kind in range(kinds):
        if kind:
            multiply(kind, 0)
    go_round(first)
    for index in range(2):
        for head, part in heads_of(index + 1, index == 0):
            keys_values[index, 2, :, head] = part
    pieces = 2
    size = tokens // pieces
    parts = [(kind, pl.ds(piece * size, size)) for kind in range(2) for piece in range(pieces)]
    count = len(parts)
    share = Copies(share_send, share_recv)

    def upward(index, kind, at):
        target = keys_values.at[kind, 0, at]
        return share.describe(keys_values.at[kind, 2, at], target, (me.ep + 2, me.tp), index)

    def sideways(index, kind, at):
        target = keys_values.at[kind, 1, at]
        return share.describe(keys_values.at[kind, 2, at], target, me.y_peer, count + index)

    def onward(index, kind, at):
        target = keys_values.at[kind, 1, at]
        return share.describe(keys_values.at[kind, 0, at], target, me.y_peer, count + index)

    def each(copy, action):
        for index, (kind, at) in enumerate(parts):
            action(copy(index, kind, at))

    @pl.when(me.z < 3)
    def _():
        each(upward, lambda copy: copy.start())

    @pl.when(me.y == 0)
    def _():
        each(sideways, lambda copy: copy.start())

    hop_on(0, second)
    multiply(0, 0)

    @pl.when(me.z == 0)
    def _():
        keys_values[:, 0] = jnp.zeros((2, tokens, width), bf16)

    @pl.when((me.z == 0) & (me.y == 0))
    def _():
        keys_values[:, 1] = jnp.zeros((2, tokens, width), bf16)

    @pl.when(me.z > 0)
    def _():
        for index, (kind, at) in enumerate(parts):
            upward(index, kind, at).wait_recv()

            @pl.when(me.y == 1)
            def _():
                onward(index, kind, at).start()

    go_round(second)
    for head, part in heads_of(0, True):
        queries[:, head] = part

    @pl.when((me.y == 1) | (me.z > 0))
    def _():
        each(sideways, lambda copy: copy.wait_recv())

    @pl.when(me.z < 3)
    def _():
        each(upward, lambda copy: copy.wait_send())

    @pl.when((me.y == 0) | (me.z > 0))
    def _():
        each(sideways, lambda copy: copy.wait_send())

    copies.finish()


def open_attention(shard_in, shard_out, routes, rows, gain, bias, cosine, sine, collective_id):
    kinds, depth, width = shard_in.shape
    out_rows, columns = shard_out.shape
    tokens, features = rows.shape
    bf16 = jnp.bfloat16
    shape = jax.ShapeDtypeStruct
    return pl.pallas_call(
        open_kernel,
        out_shape=(
            shape((kinds, RING, depth, width), bf16),
            shape((out_rows, RING * columns), bf16),
            shape((RING,) + routes.shape, routes.dtype),
            shape((tokens, features), bf16),
            shape((tokens, width), bf16),
            shape((2, 3, tokens, width), bf16),
        ),
        in_specs=[IN_VMEM] * 8,
        out_specs=(IN_VMEM,) * 6,
        scratch_shapes=[pltpu.VMEM((kinds, tokens, width), jnp.float32)]
        + semaphores(8)
        + semaphores(8 * (kinds + 2)),
        compiler_params=remote_params(collective_id),
        name="open_attention",
    )(shard_in, shard_out, routes, rows, gain[None], bias, cosine, sine)


def finish_kernel(
    normed, grad_raw, heads, grad_attention, weights, gain, rows, grad_residual, tail,
    sum_in, sum_out, sum_tail, grad_input,
    held_in, held_out, ring_in, ring_out, tails, tail_sums,
    core_out, core_in, x_out, x_in, grad_rows, mine,
    send_sems, recv_sems,
):
    me = Peers()
    copies = Copies(send_sems, recv_sems)
    bf16, f32 = jnp.bfloat16, jnp.float32
    kinds = grad_raw.shape[0]
    depth, width = sum_in.shape[1], sum_in.shape[2]
    out_rows, columns = sum_out.shape
    count = rows.shape[0]
    peers = {RIGHT: me.right, LEFT: me.left}
    greet([me.right, me.left, me.x_peer, me.core_peer, me.far_peer])

    def held(kind, k):
        return held_in.at[k, kind] if kind < kinds else held_out.at[k]

    def ring(kind, side, hop):
        return ring_in.at[side, hop, kind] if kind < kinds else ring_out.at[side, hop]

    def span(kind, side, hop):
        whole = depth if kind < kinds else out_rows
        return (side * (whole // 2), whole // 2) if hop == 0 else (0, whole)

    def pass_on(side, hop, k, kind):
        at = pl.ds(*span(kind, side, hop))
        target = ring(kind, side, hop).at[at]
        copies.send((side, kind, hop), held(kind, k).at[at], target, target, peers[side])

    def take_in(side, hop, k, kind):
        copies.arrive(side, kind, hop)
        start, size = span(kind, side, hop)
        at = pl.ds(start, size)
        add_into(held(kind, k).at[at], ring(kind, side, hop).at[at], size)

    def work_out(*blocks):
        for k in blocks:
            block = me.block(k)
            features = normed[:, pl.ds(pl.multiple_of(block * depth, depth), depth)]
            for kind in range(kinds):
                held_in[k, kind] = product(features, grad_raw[kind], TN).astype(bf16)
            across = grad_attention[:, pl.ds(pl.multiple_of(block * columns, columns), columns)]
            held_out[k] = product(heads[...], across, TN).astype(bf16)

    def hop_on(hop):
        if hop == 0:
            for kind in range(kinds + 1):
                for side in (RIGHT, LEFT):
                    pass_on(side, 0, 4, kind)
            return
        for kind in range(kinds + 1):
            for side, k in ((RIGHT, 4 - hop), (LEFT, 4 + hop)):
                take_in(side, hop - 1, k, kind)
                pass_on(side, hop, k, kind)

    def quarter(index):
        here = pl.ds(pl.multiple_of(index * count, count), count)
        total = None
        for kind in range(kinds):
            term = product(grad_raw[kind, here, :], weights[kind], NT)
            total = term if total is None else total + term
        return total

    work_out(4)
    hop_on(0)
    for slot, index in ((1, me.far_quarter), (0, me.core_quarter)):
        core_out[slot] = quarter(index).astype(bf16)
        target = core_in.at[slot]
        copies.send((SCALARS, OVER_CORE, slot), core_out.at[slot], target, target, me.core_peer)
    mine[...] = quarter(me.x_quarter)
    copies.arrive(SCALARS, OVER_CORE, 1)
    x_out[...] = (mine[...] + core_in[1].astype(f32)).astype(bf16)
    copies.send((SCALARS, OVER_X), x_out, x_in, x_in, me.x_peer)
    work_out(3, 5)
    hop_on(1)
    mine[...] = quarter(me.quarter)
    copies.arrive(SCALARS, OVER_CORE, 0)
    work_out(2, 6)
    copies.arrive(SCALARS, OVER_X)
    total = mine[...] + core_in[0].astype(f32) + x_in[...].astype(f32)
    inverse, scaled_rows = rms_parts(rows[...].astype(f32))
    scaled = total * gain[...]
    slope = inverse * (
        scaled - scaled_rows * jnp.mean(scaled * scaled_rows, axis=-1, keepdims=True)
    )
    grad_rows[...] = (grad_residual[...] + slope).astype(bf16)
    here = grad_input.at[me.quarter]
    copies.send((SCALARS, RIGHT, OVER_X), grad_rows, here, grad_input.at[me.x_quarter], me.x_peer)
    copies.send(
        (SCALARS, RIGHT, OVER_CORE), grad_rows, here, grad_input.at[me.core_quarter], me.core_peer
    )
    copies.local((LOCAL,), grad_rows, here)
    gain_grad = jnp.sum(total * scaled_rows, axis=0, keepdims=True)
    tails[0, 0:kinds, :] = tail[...]
    for index in range(gain_grad.shape[1] // width):
        part = slice(index * width, (index + 1) * width)
        tails[0, kinds + index : kinds + index + 1, :] = gain_grad[:, part]
    tail_kind = kinds + 1

    def pass_tail(side, hop, place):
        sign = -1 if side == RIGHT else 1
        target = tails.at[(place + sign) % RING]
        copies.send((side, tail_kind, hop), tails.at[place], target, target, peers[side])

    pass_tail(RIGHT, 0, 0)
    pass_tail(LEFT, 0, 0)
    hop_on(2)
    work_out(1, 7)
    copies.arrive(SCALARS, RIGHT, OVER_X)
    beside = grad_input.at[me.x_quarter]
    copies.send(
        (SCALARS, LEFT, OVER_CORE), beside, beside, grad_input.at[me.far_quarter], me.core_peer
    )
    for side, place in ((RIGHT, 7), (LEFT, 1)):
        copies.arrive(side, tail_kind, 0)
        pass_tail(side, 1, place)
    hop_on(3)
    for side, place in ((RIGHT, 6), (LEFT, 2)):
        copies.arrive(side, tail_kind, 1)
        pass_tail(side, 2, place)
    work_out(0)
    copies.arrive(RIGHT, tail_kind, 2)
    pass_tail(RIGHT, 3, 5)
    copies.arrive(LEFT, tail_kind, 2)
    for kind in range(kinds + 1):
        for side in (RIGHT, LEFT):
            take_in(side, 3, 0, kind)
        if kind < kinds:
            sum_in[kind] = held_in[0, kind].astype(f32)
    sum_out[...] = held_out[0].astype(f32)
    copies.arrive(RIGHT, tail_kind, 3)
    total = tails[0]
    for place in range(1, RING):
        total = total + tails[place]
    tail_sums[me.tp] = total
    for way, peer, index in (
        (OVER_X, me.x_peer, me.x_quarter),
        (OVER_CORE, me.core_peer, me.core_quarter),
        (OVER_FAR, me.far_peer, me.far_quarter),
    ):
        copies.send(
            (way, tail_kind), tail_sums.at[me.tp], tail_sums.at[me.tp], tail_sums.at[index], peer
        )
    for way in (OVER_X, OVER_CORE, OVER_FAR):
        copies.arrive(way, tail_kind)
    sum_tail[...] = tail_sums[...]
    copies.finish()


def finish(
    normed, grad_raw, heads, grad_attention, weights, gain, rows, grad_residual, bias, collective_id
):
    tokens, width = normed.shape
    kinds, _, columns = grad_raw.shape
    count = rows.shape[0]
    depth = width // RING
    bf16, f32 = jnp.bfloat16, jnp.float32
    shape = jax.ShapeDtypeStruct
    tail_shape = (-(-(kinds + width // columns) // 8) * 8, columns)
    return pl.pallas_call(
        finish_kernel,
        out_shape=(
            shape((kinds, depth, columns), f32),
            shape((columns, depth), f32),
            shape((4,) + tail_shape, f32),
            shape((4, count, width), bf16),
        ),
        in_specs=[IN_VMEM] * 9,
        out_specs=(IN_VMEM,) * 3 + (IN_PLACE,),
        scratch_shapes=[
            pltpu.VMEM((RING, kinds, depth, columns), bf16),
            pltpu.VMEM((RING, columns, depth), bf16),
            pltpu.VMEM((2, 4, kinds, depth, columns), bf16),
            pltpu.VMEM((2, 4, columns, depth), bf16),
            pltpu.VMEM((RING,) + tail_shape, f32),
            pltpu.VMEM((4,) + tail_shape, f32),
            pltpu.VMEM((2, count, width), bf16),
            pltpu.VMEM((2, count, width), bf16),
            pltpu.VMEM((count, width), bf16),
            pltpu.VMEM((count, width), bf16),
            pltpu.VMEM((count, width), bf16),
            pltpu.VMEM((count, width), f32),
        ]
        + semaphores(56),
        compiler_params=remote_params(collective_id, 60),
        name="finish",
    )(normed, grad_raw, heads, grad_attention, weights, gain[None], rows, grad_residual, bias)


def greet_along_z(me, others=()):
    barrier = pltpu.get_barrier_semaphore()
    for peer in (me.y_peer,) + others:
        pl.semaphore_signal(barrier, inc=1, device_id=peer, device_id_type=MESH_ID)

    @pl.when(me.z > 0)
    def _():
        peer = (me.ep - 2, me.tp)
        pl.semaphore_signal(barrier, inc=1, device_id=peer, device_id_type=MESH_ID)

    @pl.when(me.z < 3)
    def _():
        peer = (me.ep + 2, me.tp)
        pl.semaphore_signal(barrier, inc=1, device_id=peer, device_id_type=MESH_ID)

    pl.semaphore_wait(barrier, 1 + len(others) + (me.z + 2) // 3 + (5 - me.z) // 3)


def back_kernel(
    rows, weights, valid, queries, keys_values, query_doc, key_doc, log_totals, cosine, sine,
    grad_attention, grad_raw,
    grad_heads, grads, total, from_y, from_z,
    y_send, y_recv, z_send, z_recv, send_sems, recv_sems,
):
    me = Peers()
    copies = Copies(send_sems, recv_sems)
    bf16, f32 = jnp.bfloat16, jnp.float32
    count = rows.shape[0]
    tokens, width = queries.shape
    blocks = keys_values.shape[1]
    head_count = width // HD
    greet_along_z(me, (me.x_peer, me.core_peer))

    mine = grad_attention.at[me.quarter]
    copies.send((OVER_X,), rows, mine, grad_attention.at[me.x_quarter], me.x_peer)
    copies.send((OVER_CORE, 0), rows, mine, grad_attention.at[me.core_quarter], me.core_peer)
    mine[...] = rows[...]

    def heads_of(quarter):
        at = pl.ds(pl.multiple_of(quarter * count, count), count)
        part = product(grad_attention[quarter], weights[...], NT) * valid[at, :]
        grad_heads[at, :] = part.astype(bf16)

    heads_of(me.quarter)
    copies.arrive(OVER_CORE, 0)
    heads_of(me.core_quarter)
    copies.arrive(OVER_X)
    beside = grad_attention.at[me.x_quarter]
    copies.send((OVER_CORE, 1), beside, beside, grad_attention.at[me.far_quarter], me.core_peer)
    heads_of(me.x_quarter)
    copies.arrive(OVER_CORE, 1)
    heads_of(me.far_quarter)

    across = Copies(y_send, y_recv)
    along = Copies(z_send, z_recv)

    def columns(head):
        return pl.ds(pl.multiple_of(head * HD, HD), HD)

    def sideways(head, kind):
        at = columns(head)
        source, target = grads.at[kind, 1, :, at], from_y.at[kind, :, at]
        return across.describe(source, target, me.y_peer, 2 * head + kind)

    def downward(head, kind, source):
        at = columns(head)
        return along.describe(
            source.at[kind, :, at], from_z.at[kind, :, at], (me.ep - 2, me.tp), 2 * head + kind
        )

    scale = 1.0 / math.sqrt(HD)

    def one_head(head, carry):
        at = columns(head)
        keys = keys_values[0, :, :, at].reshape(blocks * tokens, HD)
        values = keys_values[1, :, :, at].reshape(blocks * tokens, HD)
        query = queries[:, at]
        out_grads = grad_heads[:, at]
        scores = masked_scores(query, keys, query_doc[...], key_doc[...])
        probs = jnp.exp(scores - log_totals[head])
        slopes = product(out_grads, values, NT)
        slopes = probs * (slopes - jnp.sum(probs * slopes, axis=1, keepdims=True))
        grad_scores = slopes.astype(bf16)
        grad_keys = product(grad_scores, query, TN) * scale
        grads[0, :, :, at] = grad_keys.astype(bf16).reshape(blocks, tokens, HD)
        grad_values = product(probs.astype(bf16), out_grads, TN)
        grads[1, :, :, at] = grad_values.astype(bf16).reshape(blocks, tokens, HD)
        for kind in range(2):
            sideways(head, kind).start()

        @pl.when((me.z > 0) & (me.y == 0))
        def _():
            for kind in range(2):
                downward(head, kind, grads.at[:, 0]).start()

        turned_back = turned(product(grad_scores, keys) * scale, cosine[...], -sine[...])
        grad_raw[0, :, at] = turned_back.astype(bf16)
        return carry

    lax.fori_loop(0, head_count, one_head, 0)

    def from_beside(head, carry):
        at = columns(head)
        for kind in range(2):
            sideways(head, kind).wait_recv()
            here = grads[kind, 2, :, at].astype(f32)

            @pl.when(me.y == 0)
            def _():
                total[kind, :, at] = here + from_y[kind, :, at].astype(f32)

            @pl.when(me.y == 1)
            def _():
                total[kind, :, at] = here
                two_back = grads[kind, 0, :, at].astype(f32)
                summed = two_back + from_y[kind, :, at].astype(f32)
                from_y[kind, :, at] = summed.astype(bf16)

            @pl.when((me.z > 0) & (me.y == 1))
            def _():
                downward(head, kind, from_y).start()

        return carry

    lax.fori_loop(0, head_count, from_beside, 0)

    def from_above(head, carry):
        at = columns(head)

        @pl.when(me.z < 3)
        def _():
            for kind in range(2):
                downward(head, kind, from_y).wait_recv()
                total[kind, :, at] += from_z[kind, :, at].astype(f32)

        grad_raw[1, :, at] = turned(total[0, :, at], cosine[...], -sine[...]).astype(bf16)
        grad_raw[2, :, at] = total[1, :, at].astype(bf16)
        return carry

    lax.fori_loop(0, head_count, from_above, 0)

    def sent(head, carry):
        for kind in range(2):
            sideways(head, kind).wait_send()

        @pl.when(me.z > 0)
        def _():
            for kind in range(2):
                downward(head, kind, from_y).wait_send()

        return carry

    lax.fori_loop(0, head_count, sent, 0)
    copies.finish()


def back_attention(
    rows, weights, valid, queries, keys_values, query_doc, key_doc, log_totals, cosine, sine,
    collective_id,
):
    count, features = rows.shape
    tokens, width = queries.shape
    bf16, f32 = jnp.bfloat16, jnp.float32
    shape = jax.ShapeDtypeStruct
    pieces = 2 * (width // HD)
    return pl.pallas_call(
        back_kernel,
        out_shape=(shape((4, count, features), bf16), shape((3, tokens, width), bf16)),
        in_specs=[IN_VMEM] * 10,
        out_specs=(IN_VMEM,) * 2,
        scratch_shapes=[
            pltpu.VMEM((tokens, width), bf16),
            pltpu.VMEM(keys_values.shape, bf16),
            pltpu.VMEM((2, tokens, width), f32),
            pltpu.VMEM((2, tokens, width), bf16),
            pltpu.VMEM((2, tokens, width), bf16),
        ]
        + semaphores(pieces)
        + semaphores(pieces)
        + semaphores(3),
        compiler_params=remote_params(collective_id, 60),
        name="back_attention",
    )(rows, weights, valid, queries, keys_values, query_doc, key_doc, log_totals, cosine, sine)


def reduce_kernel(flip, left, right, out, core_out, core_in, x_out, x_in, send_sems, recv_sems):
    me = Peers()
    copies = Copies(send_sems, recv_sems)
    terms = left.shape[0]
    count = out.shape[0]
    f32 = jnp.float32
    greet([me.x_peer, me.core_peer])

    def quarter(index):
        rows = pl.ds(pl.multiple_of(index * count, count), count)
        total = None
        for term in range(terms):
            one = product(left[term, rows, :], right[term], NT if flip else NN)
            total = one if total is None else total + one
        return total

    for slot, index in ((1, me.far_quarter), (0, me.core_quarter)):
        core_out[slot] = quarter(index).astype(core_out.dtype)
        target = core_in.at[slot]
        copies.send((OVER_CORE, slot), core_out.at[slot], target, target, me.core_peer)
    mine = quarter(me.x_quarter)
    copies.arrive(OVER_CORE, 1)
    x_out[...] = (mine + core_in[1].astype(f32)).astype(x_out.dtype)
    copies.send((OVER_X,), x_out, x_in, x_in, me.x_peer)
    mine = quarter(me.quarter)
    copies.arrive(OVER_CORE, 0)
    out[...] = mine + core_in[0].astype(f32)
    copies.arrive(OVER_X)
    out[...] += x_in[...].astype(f32)
    copies.finish()


def product_to_owner(left, right, flip, collective_id):
    tokens = left.shape[1]
    width = right.shape[1] if flip else right.shape[2]
    count = tokens // 4
    bf16 = jnp.bfloat16
    return pl.pallas_call(
        functools.partial(reduce_kernel, flip),
        out_shape=jax.ShapeDtypeStruct((count, width), jnp.float32),
        in_specs=[IN_VMEM] * 2,
        out_specs=IN_VMEM,
        scratch_shapes=[
            pltpu.VMEM((2, count, width), bf16),
            pltpu.VMEM((2, count, width), bf16),
            pltpu.VMEM((count, width), bf16),
            pltpu.VMEM((count, width), bf16),
        ]
        + semaphores(3),
        compiler_params=remote_params(collective_id),
        name="product_to_owner",
    )(left, right)


def own_rows(block, tp_index, count):
    return lax.dynamic_slice_in_dim(block, tp_index * count, count, 0)


def after(value, earlier):
    return lax.optimization_barrier((value, earlier))[0]


def per_device_dense(
    layer_input,
    attention_gain,
    attention_in,
    attention_bias,
    attention_out,
    feedforward_gain,
    shared_in,
    shared_down,
    shared_gate,
    router,
    expert_in,
    expert_down,
    routes,
    document_lengths,
    cotangent,
):
    bf16 = jnp.bfloat16
    f32 = jnp.float32
    both = (EP, TP)
    tok_count, model_width = layer_input.shape
    expert_count = router.shape[1]
    top_count = routes.shape[1]
    ep_size = lax.axis_size(EP)
    tp_size = lax.axis_size(TP)
    ep_index = lax.axis_index(EP)
    tp_index = lax.axis_index(TP)
    own_count = tok_count // tp_size
    all_count = tok_count * ep_size
    capacity = tp_size * (
        (5 * tok_count * top_count + 4 * expert_count * tp_size - 1) // (4 * expert_count * tp_size)
    )
    reach_back = min((WINDOW + tok_count - 2) // tok_count, ep_size - 1)
    local_experts = expert_in.shape[0]
    route_rows = jnp.concatenate(
        [routes.T, jnp.full((-top_count % 8, tok_count), -1, routes.dtype)]
    )
    positions = ep_index * tok_count + jnp.arange(tok_count, dtype=jnp.int32)
    key_count = (reach_back + 1) * tok_count
    key_positions = (ep_index - reach_back) * tok_count + jnp.arange(key_count, dtype=jnp.int32)
    query_doc, rope_pos, valid_mask = doc_table(document_lengths, positions)
    query_doc = query_doc[:, None]
    key_doc = doc_table(document_lengths, key_positions)[0][None, :]
    valid_rows = valid_mask.astype(f32)[:, None]
    cosine, sine = (part[:, 0] for part in rope_angles(rope_pos, HD))
    cosine = jnp.concatenate([cosine, cosine], axis=1)
    sine = jnp.concatenate([-sine, sine], axis=1)
    in_blocks, out_full, all_routes, normed_attention, queries, keys_values = open_attention(
        attention_in,
        attention_out,
        route_rows,
        layer_input,
        attention_gain,
        attention_bias,
        cosine,
        sine,
        0,
    )
    in_full = in_blocks.reshape(3, model_width, -1)
    shard_width = shared_in.shape[1]
    slice_hidden = shared_in.shape[2] // ep_size
    shared_shards = jnp.concatenate([jnp.swapaxes(shared_in, 1, 2), shared_down[None]])
    shared_shards = jnp.swapaxes(
        shared_shards.reshape(3, ep_size, slice_hidden, shard_width), 0, 1
    )
    shared_slices = lax.all_to_all(
        after(shared_shards, queries), EP, split_axis=0, concat_axis=0, tiled=True
    )
    heads_low, log_totals = attend(queries, keys_values, query_doc, key_doc, valid_rows)
    attention_sum = product_to_owner(heads_low[None], out_full[None], False, 2)
    input_rows = own_rows(layer_input, tp_index, own_count).astype(f32)
    residual = input_rows + attention_sum
    inverse_two, normed_two = rms_parts(residual)
    normed_ffn = normed_two * feedforward_gain
    normed_low = normed_ffn.astype(bf16)
    shared_scale = jax.nn.sigmoid(jnp.dot(normed_ffn, shared_gate, precision=HIGHEST))
    router_probs = jax.nn.softmax(jnp.dot(normed_ffn, router, precision=HIGHEST), axis=-1)
    routes_own = own_rows(routes, tp_index, own_count)
    expert_ids = jnp.arange(expert_count, dtype=jnp.int32)
    picked = jnp.any(routes_own[:, :, None] == expert_ids[None, None, :], axis=1)
    chosen = jnp.where(picked, router_probs, 0.0)
    chosen_total = jnp.sum(chosen, axis=1, keepdims=True)
    gates = chosen / chosen_total
    scale_count = -(-(expert_count + 1) // 8) * 8
    spare = jnp.zeros((scale_count - expert_count - 1, own_count), f32)
    scale_rows = jnp.concatenate([gates.T, shared_scale[None], spare])
    (
        all_rows,
        all_cotangent,
        all_scales,
        ffn_part,
        back_part,
        slot_rows,
        slot_cotangent,
        grad_pre,
        gated,
        grad_shared_pre,
        scaled_hidden,
        scalar_part,
    ) = gather_feed(
        normed_low,
        cotangent.reshape(tp_size, own_count, model_width),
        scale_rows,
        all_routes,
        jnp.swapaxes(expert_in, 2, 3).reshape(local_experts, -1, model_width),
        expert_down,
        shared_slices,
        capacity,
        3,
    )
    part_shape = (ep_size, tp_size, own_count, model_width)
    slot_count = ep_size * capacity
    fed = (
        slot_rows.reshape(local_experts, slot_count, model_width),
        slot_cotangent.reshape(local_experts, slot_count, model_width),
        grad_pre.reshape(2, local_experts, slot_count, -1),
        gated.reshape(local_experts, slot_count, -1),
        all_rows.reshape(all_count, model_width),
        all_cotangent.reshape(all_count, model_width),
        grad_shared_pre.reshape(2, all_count, slice_hidden),
        scaled_hidden.reshape(all_count, slice_hidden),
    )
    back_sum, ffn_sum, scalar_sum, grad_expert_in, grad_expert_down, shared_grads = scatter_rows(
        back_part.reshape(part_shape), ffn_part.reshape(part_shape), scalar_part, fed, 4
    )
    scalar_sum = scalar_sum.T
    grad_expert_in = jnp.swapaxes(grad_expert_in, 2, 3).astype(f32)
    grad_expert_down = grad_expert_down.astype(f32)
    layer_output = lax.all_gather((residual + ffn_sum).astype(bf16), TP, axis=0, tiled=True)
    shared_grads = lax.all_to_all(shared_grads, EP, split_axis=0, concat_axis=0, tiled=True)
    shared_grads = (
        jnp.swapaxes(shared_grads, 0, 1).reshape(3, -1, shard_width).astype(f32)
    )
    grad_shared_in = jnp.swapaxes(shared_grads[:2], 1, 2)
    grad_shared_down = shared_grads[2]

    grad_gates = scalar_sum[:, :expert_count]
    grad_probs = jnp.where(
        picked,
        (grad_gates - jnp.sum(grad_gates * gates, axis=1, keepdims=True)) / chosen_total,
        0.0,
    )
    grad_logits = router_probs * (
        grad_probs - jnp.sum(grad_probs * router_probs, axis=1, keepdims=True)
    )
    grad_router = jnp.einsum("td,te->de", normed_ffn, grad_logits, precision=HIGHEST)
    grad_scale_pre = scalar_sum[:, expert_count] * shared_scale * (1.0 - shared_scale)
    grad_shared_gate = jnp.dot(grad_scale_pre, normed_ffn, precision=HIGHEST)
    grad_normed = (
        back_sum
        + jnp.einsum("te,de->td", grad_logits, router, precision=HIGHEST)
        + grad_scale_pre[:, None] * shared_gate[None, :]
    )
    grad_mid_norm, grad_feedforward_gain = norm_back(
        grad_normed, feedforward_gain, inverse_two, normed_two
    )
    small = jnp.concatenate([grad_feedforward_gain[None], grad_shared_gate[None], grad_router.T])
    small = lax.psum(small, both)
    grad_residual = own_rows(cotangent, tp_index, own_count).astype(f32) + grad_mid_norm
    grad_attention, grad_raw = back_attention(
        grad_residual.astype(bf16),
        out_full,
        valid_rows,
        queries,
        keys_values,
        query_doc,
        key_doc,
        log_totals,
        cosine,
        sine,
        5,
    )
    grad_attention = grad_attention.reshape(tok_count, model_width)
    grad_attention_bias = jnp.sum(grad_raw.astype(f32), axis=1)
    grad_attention_in, grad_attention_out, tails, grad_input = finish(
        normed_attention,
        grad_raw,
        heads_low,
        grad_attention,
        in_full,
        attention_gain,
        own_rows(layer_input, tp_index, own_count),
        grad_residual,
        grad_attention_bias,
        7,
    )
    grad_attention_bias = lax.dynamic_index_in_dim(tails, tp_index, 0, keepdims=False)[:3]
    grad_attention_gain = jnp.sum(tails[:, 3:], axis=0)[: model_width // tails.shape[2]].reshape(-1)
    return (
        layer_output,
        grad_input.reshape(tok_count, model_width),
        grad_attention_gain,
        grad_attention_in,
        grad_attention_bias,
        grad_attention_out,
        small[0],
        grad_shared_in,
        grad_shared_down,
        small[1],
        small[2:].T,
        grad_expert_in,
        grad_expert_down,
    )


def per_device(*arguments):
    small_slice = lax.axis_size(EP) == RING and lax.axis_size(TP) == 4
    return (per_device_dense if small_slice else per_device_sparse)(*arguments)


def per_device_sparse(
    layer_input,
    attention_gain,
    attention_in,
    attention_bias,
    attention_out,
    feedforward_gain,
    shared_in,
    shared_down,
    shared_gate,
    router,
    expert_in,
    expert_down,
    routes,
    document_lengths,
    cotangent,
):
    bf16 = jnp.bfloat16
    f32 = jnp.float32
    tok_count = layer_input.shape[0]
    model_width = layer_input.shape[1]
    expert_count = router.shape[1]
    top_count = routes.shape[1]
    ep_size = lax.axis_size(EP)
    tp_size = lax.axis_size(TP)
    capacity = tp_size * (
        (5 * tok_count * top_count + 4 * expert_count * tp_size - 1) // (4 * expert_count * tp_size)
    )
    reach_back = min((WINDOW + tok_count - 2) // tok_count, ep_size - 1)
    head_dim = HD
    local_heads = attention_in.shape[2] // head_dim
    score_scale = 1.0 / math.sqrt(head_dim)
    in_full, out_full, shared_in_full, shared_down_full = (
        lax.all_gather(attention_in, EP, axis=1, tiled=True),
        lax.all_gather(attention_out, EP, axis=1, tiled=True),
        lax.all_gather(shared_in, EP, axis=1, tiled=True),
        lax.all_gather(shared_down, EP, axis=1, tiled=True),
    )
    ep_index = lax.axis_index(EP)
    positions = ep_index * tok_count + jnp.arange(tok_count, dtype=jnp.int32)
    key_count = (reach_back + 1) * tok_count
    key_positions = (ep_index - reach_back) * tok_count + jnp.arange(key_count, dtype=jnp.int32)
    query_doc, rope_pos, valid_mask = doc_table(document_lengths, positions)
    key_doc = doc_table(document_lengths, key_positions)[0]
    distance = positions[:, None] - key_positions[None, :]
    allowed = (query_doc[:, None] == key_doc[None, :]) & (distance >= 0) & (distance < WINDOW)
    valid_rows = valid_mask.astype(f32)[:, None]
    cosine, sine_part = rope_angles(rope_pos, head_dim)
    input_rows = layer_input.astype(f32)
    inverse_one, normed_one = rms_parts(input_rows)
    normed_attention = (normed_one * attention_gain).astype(bf16)
    raw_proj = (
        jnp.einsum("td,sde->ste", normed_attention, in_full, preferred_element_type=f32)
        + attention_bias[:, None, :]
    )
    queries = rotate(
        raw_proj[0].reshape(tok_count, local_heads, head_dim), cosine, sine_part, 1.0
    ).astype(bf16)
    keys_own = rotate(
        raw_proj[1].reshape(tok_count, local_heads, head_dim), cosine, sine_part, 1.0
    ).astype(bf16)
    values_own = raw_proj[2].reshape(tok_count, local_heads, head_dim).astype(bf16)
    key_value = jnp.stack([keys_own, values_own])
    earlier = []
    for hop_count in range(reach_back, 0, -1):
        earlier.append(shifted(key_value, EP, hop_count))
    all_kv = jnp.concatenate(earlier + [key_value], axis=1)
    all_keys = all_kv[0]
    all_values = all_kv[1]
    scores = jnp.einsum("qhe,khe->hqk", queries, all_keys, preferred_element_type=f32) * score_scale
    scores = jnp.where(allowed[None], scores, MASKED)
    row_max = jnp.max(scores, axis=-1, keepdims=True)
    exp_terms = jnp.exp(scores - row_max)
    row_total = jnp.sum(exp_terms, axis=-1, keepdims=True)
    log_total = row_max + jnp.log(row_total)
    weights = (exp_terms / row_total).astype(bf16)
    heads_out = jnp.einsum("hqk,khe->qhe", weights, all_values, preferred_element_type=f32).reshape(
        tok_count, -1
    )
    heads_low = (heads_out * valid_rows).astype(bf16)
    attention_sum = tensor_total(jnp.dot(heads_low, out_full, preferred_element_type=f32))
    residual = input_rows + attention_sum
    inverse_two, normed_two = rms_parts(residual)
    normed_ffn = normed_two * feedforward_gain
    normed_low = normed_ffn.astype(bf16)
    shared_pre = jnp.einsum("td,sdf->stf", normed_low, shared_in_full, preferred_element_type=f32)
    shared_silu, shared_slope = silu_parts(shared_pre[0])
    shared_hidden = (shared_silu * shared_pre[1]).astype(bf16)
    shared_out = tensor_total(jnp.dot(shared_hidden, shared_down_full, preferred_element_type=f32))
    shared_scale = jax.nn.sigmoid(jnp.dot(normed_ffn, shared_gate, precision=HIGHEST))
    router_probs = jax.nn.softmax(jnp.dot(normed_ffn, router, precision=HIGHEST), axis=-1)
    chosen = jnp.take_along_axis(router_probs, routes, axis=1)
    chosen_total = jnp.sum(chosen, axis=1, keepdims=True)
    gate_values = chosen / chosen_total
    assign_count = tok_count * top_count
    flat_routes = routes.reshape(-1)
    expert_ids = jnp.arange(expert_count, dtype=jnp.int32)
    one_hot = (flat_routes[:, None] == expert_ids[None, :]).astype(jnp.int32)
    arrival_rank = jnp.sum((jnp.cumsum(one_hot, axis=0) - one_hot) * one_hot, axis=1)
    slot_count = expert_count * capacity
    slot_index = jnp.where(
        arrival_rank < capacity, flat_routes * capacity + arrival_rank, slot_count
    )
    slot_assign = (
        jnp.full((slot_count + 1,), assign_count, jnp.int32)
        .at[slot_index]
        .set(jnp.arange(assign_count, dtype=jnp.int32))[:slot_count]
    )
    slot_token = slot_assign // top_count
    padded_rows = jnp.concatenate([normed_low, jnp.zeros((1, model_width), bf16)])
    send_rows = padded_rows[slot_token].reshape(expert_count, capacity, model_width)

    def expert_trip(outgoing, work):
        row_block = lax.all_to_all(outgoing, EP, split_axis=0, concat_axis=1, tiled=True)
        partial_rows, extras = work(row_block)
        share_rows = lax.psum_scatter(partial_rows, TP, scatter_dimension=1, tiled=True).astype(
            bf16
        )
        whole_rows = lax.all_gather(share_rows, TP, axis=1, tiled=True)
        return (lax.all_to_all(whole_rows, EP, split_axis=1, concat_axis=0, tiled=True), extras)

    def expert_forward(row_block):
        pre_acts = jnp.einsum("erd,esdf->serf", row_block, expert_in, preferred_element_type=f32)
        gate_silu, gate_slope = silu_parts(pre_acts[0])
        hidden = (gate_silu * pre_acts[1]).astype(bf16)
        partial_rows = jnp.einsum("erf,efd->erd", hidden, expert_down, preferred_element_type=f32)
        return (partial_rows, (row_block, pre_acts, hidden, gate_silu, gate_slope))

    returned_rows, kept_state = expert_trip(send_rows, expert_forward)
    expert_rows, expert_pre, expert_hidden, expert_silu, expert_slope = kept_state
    padded_back = jnp.concatenate(
        [returned_rows.reshape(slot_count, model_width), jnp.zeros((1, model_width), bf16)]
    )
    picked = padded_back[slot_index].reshape(tok_count, top_count, model_width).astype(f32)
    moe_sum = jnp.sum(gate_values[:, :, None] * picked, axis=1)
    layer_output = (residual + shared_scale[:, None] * shared_out + moe_sum).astype(bf16)
    grad_rows = cotangent.astype(f32)
    padded_grad = jnp.concatenate([grad_rows, jnp.zeros((1, model_width), f32)])
    padded_gates = jnp.concatenate([gate_values.reshape(-1), jnp.zeros((1,), f32)])
    grad_send = (padded_gates[slot_assign][:, None] * padded_grad[slot_token]).astype(bf16)
    grad_send = grad_send.reshape(expert_count, capacity, model_width)

    def expert_backward(grad_block):
        grad_down = jnp.einsum(
            "erf,erd->efd", expert_hidden, grad_block, preferred_element_type=f32
        )
        grad_hidden = jnp.einsum(
            "erd,efd->erf", grad_block, expert_down, preferred_element_type=f32
        )
        grad_pre = jnp.stack(
            [grad_hidden * expert_pre[1] * expert_slope, grad_hidden * expert_silu]
        ).astype(bf16)
        grad_weights_in = jnp.einsum(
            "erd,serf->esdf", expert_rows, grad_pre, preferred_element_type=f32
        )
        grad_back_rows = jnp.einsum(
            "serf,esdf->erd", grad_pre, expert_in, preferred_element_type=f32
        )
        return (grad_back_rows, (grad_weights_in, grad_down))

    grad_returned, expert_grads = expert_trip(grad_send, expert_backward)
    grad_expert_in, grad_expert_down = expert_grads
    grad_gate_values = jnp.sum(picked * grad_rows[:, None, :], axis=2)
    grad_chosen = (
        grad_gate_values - jnp.sum(grad_gate_values * gate_values, axis=1, keepdims=True)
    ) / chosen_total
    grad_probs = jnp.sum(
        jnp.where(routes[:, :, None] == expert_ids[None, None, :], grad_chosen[:, :, None], 0.0),
        axis=1,
    )
    grad_logits = router_probs * (
        grad_probs - jnp.sum(grad_probs * router_probs, axis=1, keepdims=True)
    )
    grad_router = jnp.einsum("td,te->de", normed_ffn, grad_logits, precision=HIGHEST)
    grad_shared_out = (shared_scale[:, None] * grad_rows).astype(bf16)
    grad_shared_down = jnp.einsum(
        "tf,td->fd", shared_hidden, grad_shared_out, preferred_element_type=f32
    )
    grad_shared_hidden = jnp.einsum(
        "td,fd->tf", grad_shared_out, shared_down_full, preferred_element_type=f32
    )
    grad_shared_pre = jnp.stack(
        [grad_shared_hidden * shared_pre[1] * shared_slope, grad_shared_hidden * shared_silu]
    ).astype(bf16)
    grad_shared_in = jnp.einsum(
        "td,stf->sdf", normed_low, grad_shared_pre, preferred_element_type=f32
    )
    shared_back = jnp.einsum(
        "stf,sdf->td", grad_shared_pre, shared_in_full, preferred_element_type=f32
    )
    grad_scale_pre = jnp.sum(grad_rows * shared_out, axis=1) * shared_scale * (1.0 - shared_scale)
    grad_shared_gate = jnp.dot(grad_scale_pre, normed_ffn, precision=HIGHEST)
    padded_return = jnp.concatenate(
        [grad_returned.reshape(slot_count, model_width), jnp.zeros((1, model_width), bf16)]
    )
    moe_back = jnp.sum(
        padded_return[slot_index].reshape(tok_count, top_count, model_width).astype(f32), axis=1
    )
    grad_normed = (
        tensor_total(shared_back)
        + moe_back
        + jnp.einsum("te,de->td", grad_logits, router, precision=HIGHEST)
        + grad_scale_pre[:, None] * shared_gate[None, :]
    )
    grad_mid_norm, grad_feedforward_gain = norm_back(
        grad_normed, feedforward_gain, inverse_two, normed_two
    )
    grad_residual = grad_rows + grad_mid_norm
    grad_attention = grad_residual.astype(bf16)
    grad_attention_out = jnp.einsum(
        "tf,td->fd", heads_low, grad_attention, preferred_element_type=f32
    )
    grad_heads = jnp.einsum(
        "td,fd->tf", grad_attention, out_full, preferred_element_type=f32
    ).astype(bf16)
    grad_heads = (grad_heads * valid_rows.astype(bf16)).reshape(tok_count, local_heads, head_dim)
    scores_again = (
        jnp.einsum("qhe,khe->hqk", queries, all_keys, preferred_element_type=f32) * score_scale
    )
    scores_again = jnp.where(allowed[None], scores_again, MASKED)
    softmax_out = jnp.exp(scores_again - log_total)
    weights_again = softmax_out.astype(bf16)
    grad_weights = jnp.einsum("qhe,khe->hqk", grad_heads, all_values, preferred_element_type=f32)
    grad_scores = (
        softmax_out * (grad_weights - jnp.sum(softmax_out * grad_weights, axis=-1, keepdims=True))
    ).astype(bf16)
    grad_queries = (
        jnp.einsum("hqk,khe->qhe", grad_scores, all_keys, preferred_element_type=f32) * score_scale
    )
    grad_keys = (
        jnp.einsum("hqk,qhe->khe", grad_scores, queries, preferred_element_type=f32) * score_scale
    )
    grad_values = jnp.einsum("hqk,qhe->khe", weights_again, grad_heads, preferred_element_type=f32)
    grad_kv = jnp.stack([grad_keys, grad_values])
    own_part = grad_kv[:, reach_back * tok_count :]
    for hop_count in range(1, reach_back + 1):
        segment_start = (reach_back - hop_count) * tok_count
        segment = grad_kv[:, segment_start : segment_start + tok_count]
        own_part = own_part + shifted(segment, EP, -hop_count)
    grad_raw = (
        jnp.stack(
            [
                rotate(grad_queries, cosine, sine_part, -1.0),
                rotate(own_part[0], cosine, sine_part, -1.0),
                own_part[1],
            ]
        )
        .reshape(3, tok_count, -1)
        .astype(bf16)
    )
    grad_attention_bias = jnp.sum(grad_raw.astype(f32), axis=1)
    grad_attention_in = jnp.einsum(
        "td,ste->sde", normed_attention, grad_raw, preferred_element_type=f32
    )
    grad_normed_attention = tensor_total(
        jnp.einsum("ste,sde->td", grad_raw, in_full, preferred_element_type=f32)
    )
    grad_in_norm, grad_attention_gain = norm_back(
        grad_normed_attention, attention_gain, inverse_one, normed_one
    )
    grad_input = (grad_residual + grad_in_norm).astype(bf16)
    grad_attention_in, grad_attention_out, grad_shared_in, grad_shared_down = (
        lax.psum_scatter(
            grad_attention_in.astype(jnp.bfloat16), EP, scatter_dimension=1, tiled=True
        ).astype(jnp.float32),
        lax.psum_scatter(
            grad_attention_out.astype(jnp.bfloat16), EP, scatter_dimension=1, tiled=True
        ).astype(jnp.float32),
        lax.psum_scatter(
            grad_shared_in.astype(jnp.bfloat16), EP, scatter_dimension=1, tiled=True
        ).astype(jnp.float32),
        lax.psum_scatter(
            grad_shared_down.astype(jnp.bfloat16), EP, scatter_dimension=1, tiled=True
        ).astype(jnp.float32),
    )
    (
        grad_attention_gain,
        grad_attention_bias,
        grad_feedforward_gain,
        grad_shared_gate,
        grad_router,
    ) = (
        lax.psum(grad_attention_gain.astype(jnp.bfloat16), EP).astype(jnp.float32),
        lax.psum(grad_attention_bias.astype(jnp.bfloat16), EP).astype(jnp.float32),
        lax.psum(grad_feedforward_gain.astype(jnp.bfloat16), EP).astype(jnp.float32),
        lax.psum(grad_shared_gate.astype(jnp.bfloat16), EP).astype(jnp.float32),
        lax.psum(grad_router.astype(jnp.bfloat16), EP).astype(jnp.float32),
    )
    return (
        layer_output,
        grad_input,
        grad_attention_gain,
        grad_attention_in,
        grad_attention_bias,
        grad_attention_out,
        grad_feedforward_gain,
        grad_shared_in,
        grad_shared_down,
        grad_shared_gate,
        grad_router,
        grad_expert_in,
        grad_expert_down,
    )


def solution(mesh):
    return jax.shard_map(
        per_device,
        mesh=mesh,
        in_specs=(
            P(EP, None),
            P(),
            P(None, EP, TP),
            P(None, TP),
            P(TP, EP),
            P(),
            P(None, EP, TP),
            P(TP, EP),
            P(),
            P(),
            P(EP, None, None, TP),
            P(EP, TP, None),
            P(EP, None),
            P(),
            P(EP, None),
        ),
        out_specs=(
            P(EP, None),
            P(EP, None),
            P(),
            P(None, EP, TP),
            P(None, TP),
            P(TP, EP),
            P(),
            P(None, EP, TP),
            P(TP, EP),
            P(),
            P(),
            P(EP, None, None, TP),
            P(EP, TP, None),
        ),
        check_vma=False,
    )
```

```python
import functools
import math

import jax
import jax.numpy as jnp
from jax import lax
from jax.experimental import pallas as pl
from jax.experimental.pallas import tpu as pltpu
from jax.sharding import PartitionSpec as P

EP, TP = "ep", "tp"
HD = 128
WINDOW = 1024


HIGHEST = lax.Precision.HIGHEST
EPSILON = 1e-06
ROPE_BASE = 1000000.0
MASKED = -1000000000.0


def shifted(value, axis, steps):
    count = lax.axis_size(axis)
    leading, last = (max(0, -steps), min(count, count - steps))
    return lax.ppermute(value, axis, [(source, source + steps) for source in range(leading, last)])


def tensor_total(partial_sum):
    return lax.psum(partial_sum, TP)


def rms_parts(values):
    inverse = lax.rsqrt(jnp.mean(values * values, axis=-1, keepdims=True) + EPSILON)
    return (inverse, values * inverse)


def norm_back(grad_rows, gain_vec, inverse, normed):
    scaled = grad_rows * gain_vec
    grad_in = inverse * (scaled - normed * jnp.mean(scaled * normed, axis=-1, keepdims=True))
    return (grad_in, jnp.sum(grad_rows * normed, axis=0))


def doc_table(document_lengths, positions):
    doc_ends = jnp.cumsum(document_lengths)
    starts_all = jnp.concatenate([doc_ends - document_lengths, doc_ends[-1:]])
    doc_ids = jnp.sum((positions[:, None] >= doc_ends[None, :]).astype(jnp.int32), axis=1)
    matches = (
        doc_ids[:, None] == jnp.arange(document_lengths.shape[0] + 1, dtype=jnp.int32)[None, :]
    )
    doc_begin = jnp.sum(jnp.where(matches, starts_all[None, :], 0), axis=1)
    rope_pos = positions - doc_begin
    valid_mask = positions < doc_ends[-1]
    doc_ids = jnp.where(positions < 0, -1, doc_ids)
    return (doc_ids, rope_pos, valid_mask)


def rope_angles(rope_pos, head_dim):
    half_width = head_dim // 2
    freqs = jnp.power(ROPE_BASE, -2.0 * jnp.arange(half_width, dtype=jnp.float32) / head_dim)
    angles = rope_pos.astype(jnp.float32)[:, None] * freqs[None, :]
    return (jnp.cos(angles)[:, None, :], jnp.sin(angles)[:, None, :])


def rotate(values, cosine, sine_part, turn_sign):
    half_width = values.shape[-1] // 2
    first_part = values[..., :half_width]
    second_part = values[..., half_width:]
    return jnp.concatenate(
        [
            first_part * cosine - turn_sign * second_part * sine_part,
            second_part * cosine + turn_sign * first_part * sine_part,
        ],
        axis=-1,
    )


def silu_parts(gate_pre):
    sig_gate = jax.nn.sigmoid(gate_pre)
    return (gate_pre * sig_gate, sig_gate * (1.0 + gate_pre * (1.0 - sig_gate)))


NN = (((1,), (0,)), ((), ()))
NT = (((1,), (1,)), ((), ()))
TN = (((0,), (0,)), ((), ()))


def product(left, right, dims=NN):
    return lax.dot_general(left, right, dims, preferred_element_type=jnp.float32)


def turned(values, cosine, sine):
    half = values.shape[1] // 2
    swapped = jnp.concatenate([values[:, half:], values[:, :half]], axis=1)
    return values * cosine + swapped * sine


def masked_scores(queries, keys, query_doc, key_doc):
    tokens, count = queries.shape[0], keys.shape[0]
    scores = product(queries, keys, NT) * (1.0 / math.sqrt(HD))
    ahead = lax.broadcasted_iota(jnp.int32, (tokens, count), 0) + (count - tokens)
    distance = ahead - lax.broadcasted_iota(jnp.int32, (tokens, count), 1)
    allowed = (query_doc == key_doc) & (distance >= 0) & (distance < WINDOW)
    return jnp.where(allowed, scores, MASKED)


def attend_kernel(queries, keys, values, query_doc, key_doc, valid, heads, log_totals):
    count = keys.shape[1] * keys.shape[2]
    keys, values = keys[0].reshape(count, HD), values[0].reshape(count, HD)
    scores = masked_scores(queries[...], keys, query_doc[...], key_doc[...])
    row_max = jnp.max(scores, axis=1, keepdims=True)
    terms = jnp.exp(scores - row_max)
    total = jnp.sum(terms, axis=1, keepdims=True)
    weights = (terms / total).astype(jnp.bfloat16)
    heads[...] = (product(weights, values) * valid[...]).astype(jnp.bfloat16)
    log_totals[0] = row_max + jnp.log(total)


def attention_specs(tokens, blocks):
    def column(*dims):
        return pl.BlockSpec(dims, lambda h: (0,) * len(dims))

    head = pl.BlockSpec((tokens, HD), lambda h: (0, h))
    keys = pl.BlockSpec((1, blocks, tokens, HD), lambda h: (0, 0, 0, h))
    values = pl.BlockSpec((1, blocks, tokens, HD), lambda h: (1, 0, 0, h))
    logs = pl.BlockSpec((1, tokens, 1), lambda h: (h, 0, 0))
    return head, keys, values, column(tokens, 1), column(1, blocks * tokens), logs


def attend(queries, keys_values, query_doc, key_doc, valid):
    tokens, columns = queries.shape
    blocks = keys_values.shape[1]
    head, keys, values, column, row, logs = attention_specs(tokens, blocks)
    shape = jax.ShapeDtypeStruct
    return pl.pallas_call(
        attend_kernel,
        grid=(columns // HD,),
        in_specs=[head, keys, values, column, row, column],
        out_specs=(head, logs),
        out_shape=(
            shape((tokens, columns), jnp.bfloat16),
            shape((columns // HD, tokens, 1), jnp.float32),
        ),
        compiler_params=pltpu.CompilerParams(vmem_limit_bytes=40 * 2**20),
        name="attend",
    )(queries, keys_values, keys_values, query_doc, key_doc, valid)


RING = 8
NO_SLOT = 1 << 20
RIGHT, LEFT, OVER_X, OVER_CORE, OVER_FAR, LOCAL, SCALARS = range(7)
MESH_ID = pl.DeviceIdType.MESH


def ring_place(ep):
    z, y = ep // 2, ep % 2
    return z + y * (7 - 2 * z)


def ring_member(place):
    upper = place // 4
    return 2 * place + upper * (15 - 4 * place)


class Peers:
    def __init__(self):
        self.ep, self.tp = lax.axis_index(EP), lax.axis_index(TP)
        self.x, self.core = self.tp // 2, self.tp % 2
        self.z, self.y = self.ep // 2, self.ep % 2
        self.place = ring_place(self.ep)
        self.right = (self.block(1), self.tp)
        self.left = (self.block(RING - 1), self.tp)
        self.quarter = self.tp
        self.x_quarter = (1 - self.x) * 2 + self.core
        self.core_quarter = self.x * 2 + 1 - self.core
        self.far_quarter = (1 - self.x) * 2 + 1 - self.core
        self.x_peer = (self.ep, self.x_quarter)
        self.core_peer = (self.ep, self.core_quarter)
        self.far_peer = (self.ep, self.far_quarter)
        self.y_peer = (self.z * 2 + 1 - self.y, self.tp)

    def block(self, step):
        return ring_member((self.place + step + RING) % RING)


def greet(peers):
    barrier = pltpu.get_barrier_semaphore()
    for peer in peers:
        pl.semaphore_signal(barrier, inc=1, device_id=peer, device_id_type=MESH_ID)
    pl.semaphore_wait(barrier, len(peers))


class Copies:
    def __init__(self, send_sems, recv_sems):
        self.send_sems, self.recv_sems = send_sems, recv_sems
        self.count = 0
        self.sent = []
        self.landing = {}

    def describe(self, source, target, peer, index):
        return pltpu.make_async_remote_copy(
            src_ref=source,
            dst_ref=target,
            send_sem=self.send_sems.at[index],
            recv_sem=self.recv_sems.at[index],
            device_id=peer,
            device_id_type=MESH_ID,
        )

    def send(self, key, source, target, landing, peer):
        index = self.count
        self.count += 1
        copy = self.describe(source, target, peer, index)
        copy.start()
        self.sent.append(copy)
        self.landing[key] = self.describe(landing, landing, peer, index).wait_recv

    def local(self, key, source, target):
        index = self.count
        self.count += 1
        copy = pltpu.make_async_copy(source, target, self.send_sems.at[index])
        copy.start()
        self.landing[key] = copy.wait

    def arrive(self, *key):
        self.landing.pop(key)()

    def finish(self):
        for wait in self.landing.values():
            wait()
        for copy in self.sent:
            copy.wait_send()


def remote_params(collective_id, vmem=48):
    return pltpu.CompilerParams(
        collective_id=collective_id, has_side_effects=True, vmem_limit_bytes=vmem * 2**20
    )


def semaphores(count):
    return [pltpu.SemaphoreType.DMA((count,))] * 2


IN_PLACE = pl.BlockSpec(memory_space=pl.ANY)
IN_VMEM = pl.BlockSpec(memory_space=pltpu.VMEM)


class LateCopies(Copies):
    def send(self, key, source, target, landing, peer):
        index = self.count
        self.count += 1
        self.describe(source(), target(), peer, index).start()
        self.sent.append(lambda: self.describe(source(), target(), peer, index).wait_send())
        self.landing[key] = lambda: self.describe(landing(), landing(), peer, index).wait_recv()

    def local(self, key, source, target):
        index = self.count
        self.count += 1

        def copy():
            return pltpu.make_async_copy(source(), target(), self.send_sems.at[index])

        copy().start()
        self.landing[key] = lambda: copy().wait()

    def finish(self):
        for wait in list(self.landing.values()) + self.sent:
            wait()


def feed_block(
    rank_row, rank_column, gate_rows, scale, token_rows, token_cotangent,
    expert_in, expert_down, shared, staged, between, out_terms, back_terms, scalar_out,
):
    (
        out_part, back_part, slot_rows, slot_cotangent, grad_pre, gated, grad_shared_pre, scaled,
    ) = staged
    bf16, f32 = jnp.bfloat16, jnp.float32
    experts, slots, _ = slot_rows.shape
    tokens = token_rows.shape[0]
    hidden_count = gated.shape[2]
    all_slots = experts * slots
    silu, slope = silu_parts(product(token_rows, shared[0], NT))
    up = product(token_rows, shared[1], NT)
    hidden = (silu * up).astype(bf16).astype(f32)
    scaled_hidden = (scale * hidden).astype(bf16)
    back = product(token_cotangent, shared[2], NT)
    scalar_out(None, jnp.sum(jnp.swapaxes(hidden * back, 0, 1), axis=0, keepdims=True))
    back = scale * back
    gate_grad = (back * up * slope).astype(bf16)
    up_grad = (back * silu).astype(bf16)
    between()
    scaled[...] = scaled_hidden
    grad_shared_pre[0] = gate_grad
    grad_shared_pre[1] = up_grad
    order = lax.broadcasted_iota(jnp.int32, (all_slots, tokens), 0)
    spread_order = lax.broadcasted_iota(jnp.int32, (tokens, all_slots), 1)
    hits, spread = None, None
    for expert in range(experts):
        row_hits = order == rank_row[expert : expert + 1, :] + expert * slots
        column_hits = spread_order == rank_column[:, expert : expert + 1] + expert * slots
        hits = row_hits if hits is None else hits | row_hits
        spread = column_hits if spread is None else spread | column_hits
    place = hits.astype(bf16)
    taken = product(place, token_rows).astype(bf16)
    taken_cotangent = product(place, token_cotangent).astype(bf16)
    for ref, values in ((slot_rows, taken), (slot_cotangent, taken_cotangent)):
        for expert in range(experts):
            ref[expert] = values[expert * slots : (expert + 1) * slots]
    for expert in range(experts):
        mine = slice(expert * slots, (expert + 1) * slots)
        gate = jnp.sum(
            jnp.where(hits[mine], gate_rows[expert : expert + 1], 0.0), axis=1, keepdims=True
        )
        pre = product(taken[mine], expert_in[expert], NT)
        silu, slope = silu_parts(pre[:, :hidden_count])
        up = pre[:, hidden_count:]
        hidden = (silu * up).astype(bf16).astype(f32)
        gated_hidden = (gate * hidden).astype(bf16)
        gated[expert] = gated_hidden
        back = product(taken_cotangent[mine], expert_down[expert], NT)
        slot_grad = jnp.sum(hidden * back, axis=1, keepdims=True)
        scalar_out(
            expert, jnp.sum(jnp.where(hits[mine], slot_grad, 0.0), axis=0, keepdims=True)
        )
        back = gate * back
        gate_grad_e = (back * up * slope).astype(bf16)
        up_grad_e = (back * silu).astype(bf16)
        grad_pre[0, expert] = gate_grad_e
        grad_pre[1, expert] = up_grad_e
        out_terms[mine, :] = product(gated_hidden, expert_down[expert]).astype(bf16)
        both_grads = jnp.concatenate([gate_grad_e, up_grad_e], axis=1)
        back_terms[mine, :] = product(both_grads, expert_in[expert]).astype(bf16)
    spread = spread.astype(bf16)
    out_part[...] = product(
        jnp.concatenate([spread, scaled_hidden], axis=1), out_terms[...]
    ).astype(bf16)
    back_part[...] = product(
        jnp.concatenate([spread, gate_grad, up_grad], axis=1), back_terms[...]
    ).astype(bf16)


def gather_feed_kernel(
    rows, cotangent, scales, routes, expert_in, expert_down, shared_blocks,
    all_rows, all_cotangent, all_scales,
    out_part, back_part, slot_rows, slot_cotangent, grad_pre, gated, grad_shared_pre, scaled,
    scalars,
    rank_row, rank_column, shared, out_terms, back_terms, held_rows, held_cotangent,
    stage_out, stage_back, stage_rows, stage_cotangent, stage_pre, stage_gated, stage_shared,
    stage_scaled,
    load_sems, store_sems, send_sems, recv_sems,
):
    me = Peers()
    copies = LateCopies(send_sems, recv_sems)
    count = rows.shape[0]
    half, part = count // 2, count // 4
    first_rows = (half, half - count // 8)
    q, qx, qc, qd = me.quarter, me.x_quarter, me.core_quarter, me.far_quarter
    blocks = {step: me.block(step) for step in range(-4, 5)}
    low = [pl.ds(0, rows_low) for rows_low in first_rows]
    high = [pl.ds(rows_low, count - rows_low) for rows_low in first_rows]
    whole = pl.ds(0, count)
    own, other, scale = range(3)
    full = (all_rows, all_cotangent)
    sides = ((RIGHT, me.right, -1, 0), (LEFT, me.left, 1, 1))
    greet([me.right, me.left, me.x_peer, me.core_peer, me.far_peer])

    def push(key, kind, step, quarter, which, peer, landing_step, landing_quarter, source=None):
        def cell():
            return full[kind].at[blocks[step], quarter, which]

        def landing():
            return full[kind].at[blocks[landing_step], landing_quarter, which]

        copies.send((kind,) + key, source or cell, cell, landing, peer)

    push((OVER_X, other, 0), 0, 0, q, low[0], me.x_peer, 0, qx, lambda: rows.at[low[0]])
    for side, peer, sign, keep in sides:
        push((side, own, 1), 1, 0, q, whole, peer, sign, q, lambda: cotangent.at[q])
        push((side, other, 1), 1, 0, qx, low[1], peer, sign, qx, lambda: cotangent.at[qx, low[1]])
    push((OVER_X, own, 0), 0, 0, q, high[0], me.x_peer, 0, qx, lambda: rows.at[high[0]])
    push((OVER_CORE, own, 0), 0, 0, q, whole, me.core_peer, 0, qc, lambda: rows)
    for side, peer, sign, keep in sides:
        push((side, own, 1), 0, 0, q, whole, peer, sign, q, lambda: rows)
    copies.local((LOCAL, 0), lambda: rows, lambda: all_rows.at[blocks[0], q])
    copies.local((LOCAL, 1), lambda: cotangent, lambda: all_cotangent.at[blocks[0]])

    def scales_of(quarter):
        return lambda: all_scales.at[blocks[0], quarter]

    for way, peer, quarter in (
        (OVER_X, me.x_peer, qx),
        (OVER_CORE, me.core_peer, qc),
        (OVER_FAR, me.far_peer, qd),
    ):
        copies.send((way, scale, 0), lambda: scales, scales_of(q), scales_of(quarter), peer)
    copies.local((LOCAL, scale), lambda: scales, scales_of(q))
    experts, _, width = expert_in.shape
    all_slots = experts * slot_rows.shape[2]
    shared_count, across = shared.shape[1], shared_blocks.shape[3]
    for block in range(RING):
        shared[:, :, block * across : (block + 1) * across] = shared_blocks[block]
    out_terms[all_slots:, :] = shared[2]
    back_terms[all_slots : all_slots + shared_count, :] = shared[0]
    back_terms[all_slots + shared_count :, :] = shared[1]
    first_expert, scale_at = me.ep * experts, me_scale_row(experts)
    tokens = routes.shape[2]
    taken = []
    for block in range(RING):
        for expert in range(experts):
            chosen = routes[block] == first_expert + expert
            taken.append(jnp.max(chosen.astype(jnp.float32), axis=0, keepdims=True))
    taken = jnp.concatenate(taken, axis=0)
    down = lax.broadcasted_iota(jnp.int32, (tokens, tokens), 0)
    right = lax.broadcasted_iota(jnp.int32, (tokens, tokens), 1)
    rank = product(taken.astype(jnp.bfloat16), (right < down).astype(jnp.bfloat16), NT)
    kept = (taken > 0.0) & (rank < slot_rows.shape[2])
    rank = jnp.where(kept, rank, float(NO_SLOT))
    column = product((right == down).astype(jnp.bfloat16), rank.astype(jnp.bfloat16), NT)
    for block in range(RING):
        mine = slice(block * experts, (block + 1) * experts)
        rank_row[block] = rank[mine].astype(jnp.int32)
        rank_column[block] = column[:, mine].astype(jnp.int32)
    scalars[...] = jnp.zeros_like(scalars)
    copies.arrive(0, OVER_X, other, 0)
    for side, peer, sign, keep in sides:
        push((side, other, 1), 0, 0, qx, low[0], peer, sign, qx)
    for way in (OVER_X, OVER_CORE, OVER_FAR):
        copies.arrive(way, scale, 0)
    copies.arrive(LOCAL, scale)

    def push_scales(step, side, peer, sign):
        def cell():
            return all_scales.at[blocks[step]]

        copies.send(
            (side, scale, abs(step) + 1), cell, cell, lambda: all_scales.at[blocks[step + sign]], peer
        )

    for side, peer, sign, keep in sides:
        push_scales(0, side, peer, sign)
    copies.arrive(0, OVER_X, own, 0)
    push((OVER_CORE, other, 0), 0, 0, qx, whole, me.core_peer, 0, qd)

    def hop_in(kind, hop):
        for side, peer, sign, keep in sides:
            step = sign * hop
            if hop < 4:
                copies.arrive(kind, side, own, hop)
                which = whole if hop < 3 else pl.ds(keep * half, half)
                push((side, own, hop + 1), kind, step, q, which, peer, step + sign, q)
                push((OVER_X, own, step), kind, step, q, high[kind], me.x_peer, step, qx)
                push((OVER_CORE, own, step), kind, step, q, whole, me.core_peer, step, qc)
                copies.arrive(kind, side, other, hop)
                last = pl.ds(part, first_rows[kind] - part) if keep else pl.ds(0, part)
                which = low[kind] if hop < 3 else last
                push((side, other, hop + 1), kind, step, qx, which, peer, step + sign, qx)
                push((OVER_CORE, other, step), kind, step, qx, low[kind], me.core_peer, step, qd)
        if hop == 4:
            copies.arrive(kind, LEFT, own, 4)
            copies.arrive(kind, RIGHT, own, 4)
            push((OVER_X, own, 4), kind, 4, q, high[kind], me.x_peer, 4, qx)
            push((OVER_CORE, own, 4), kind, 4, q, whole, me.core_peer, 4, qc)
            copies.arrive(kind, LEFT, other, 4)
            copies.arrive(kind, RIGHT, other, 4)
            push((OVER_CORE, other, 4), kind, 4, qx, low[kind], me.core_peer, 4, qd)

    def over_x(kind, steps):
        for step in steps:
            copies.arrive(kind, OVER_X, own, step)
            push((OVER_CORE, scale, step), kind, step, qx, high[kind], me.core_peer, step, qd)

    def scales_in(hop):
        for side, peer, sign, keep in sides:
            if hop < 4 or side == RIGHT:
                copies.arrive(side, scale, hop)
                if hop < 3 or (hop == 3 and side == RIGHT):
                    push_scales(sign * hop, side, peer, sign)

    def load(slot, step):
        pairs = ((all_rows, held_rows), (all_cotangent, held_cotangent))
        return [
            pltpu.make_async_copy(source.at[blocks[step]], held.at[slot], load_sems.at[slot, kind])
            for kind, (source, held) in enumerate(pairs)
        ]

    def complete(steps, slots):
        for step in steps:
            for kind in range(2):
                if step != 0:
                    for piece in (own, other, scale):
                        copies.arrive(kind, OVER_CORE, piece, step)
        moves = [load(slot, step) for slot, step in zip(slots, steps)]
        for move in moves[0] + moves[-1] if len(moves) > 1 else moves[0]:
            move.start()
        for move in moves[0]:
            move.wait()

    staged = (
        stage_out, stage_back, stage_rows, stage_cotangent, stage_pre, stage_gated, stage_shared,
        stage_scaled,
    )

    def stores(block):
        targets = (
            out_part.at[block], back_part.at[block], slot_rows.at[:, block],
            slot_cotangent.at[:, block], grad_pre.at[:, :, block], gated.at[:, block],
            grad_shared_pre.at[:, block], scaled.at[block],
        )
        return [
            pltpu.make_async_copy(stage, target, store_sems.at[index])
            for index, (stage, target) in enumerate(zip(staged, targets))
        ]


    copies.arrive(LOCAL, 0)
    copies.arrive(LOCAL, 1)
    for piece in (own, other):
        copies.arrive(0, OVER_CORE, piece, 0)
    complete((0,), (0,))

    def turn(index, carry):
        far = (index + 1) // 2
        step = far * (1 - 2 * (index % 2)) + (index // 7) * 8
        block = ring_member((me.place + step + RING) % RING)
        slot = index % 2

        def between():
            for hop in (1, 2, 3, 4):

                @pl.when(index == max(0, 2 * hop - 3))
                def _():
                    hop_in(1, hop)

            @pl.when(index > 0)
            def _():
                for move in stores(0):
                    move.wait()

        def scalar_out(expert, values):
            row = scale_at if expert is None else first_expert + expert
            for quarter in range(4):
                part = values[:, quarter * count : (quarter + 1) * count]
                scalars[block, quarter, pl.ds(row, 1), :] = part

        rows_here = held_rows[slot].reshape(4 * count, width)
        cotangent_here = held_cotangent[slot].reshape(4 * count, width)
        quarters = [all_scales[block, quarter] for quarter in range(4)]
        columns = jnp.concatenate([jnp.swapaxes(values, 0, 1) for values in quarters], axis=0)
        gate_rows = [
            jnp.concatenate(
                [all_scales[block, quarter, pl.ds(first_expert + e, 1), :] for quarter in range(4)],
                axis=1,
            )
            for e in range(experts)
        ]
        feed_block(
            rank_row[block],
            rank_column[block],
            jnp.concatenate(gate_rows, axis=0),
            columns[:, scale_at : scale_at + 1],
            rows_here,
            cotangent_here,
            expert_in,
            expert_down,
            shared,
            staged,
            between,
            out_terms,
            back_terms,
            scalar_out,
        )
        for move in stores(block):
            move.start()

        for hop in (1, 2, 3, 4):

            @pl.when(index == max(0, 2 * hop - 3))
            def _():
                scales_in(hop)
                hop_in(0, hop)
                if hop > 1:
                    for move in load(0, hop - 1):
                        move.wait()

            @pl.when(index == 2 * hop - 2)
            def _():
                steps = (-hop, hop) if hop < 4 else (4,)
                over_x(1, steps)
                over_x(0, steps)
                complete(steps, (1, 0))

        return carry

    lax.fori_loop(0, RING, turn, 0)
    for move in stores(0):
        move.wait()
    copies.finish()


def me_scale_row(experts):
    return RING * experts


def gather_feed(
    rows, cotangent, scales, routes, expert_in, expert_down, shared, capacity, collective_id
):
    bf16, f32 = jnp.bfloat16, jnp.float32
    blocks, _, tokens = routes.shape
    experts = expert_in.shape[0]
    count, width = rows.shape
    hidden = expert_in.shape[1] // 2
    slice_hidden = shared.shape[2]
    shape = jax.ShapeDtypeStruct
    stages = (
        (tokens, width),
        (tokens, width),
        (experts, capacity, width),
        (experts, capacity, width),
        (2, experts, capacity, hidden),
        (experts, capacity, hidden),
        (2, tokens, slice_hidden),
        (tokens, slice_hidden),
    )
    return pl.pallas_call(
        gather_feed_kernel,
        out_shape=(
            shape((RING, 4, count, width), bf16),
            shape((RING, 4, count, width), bf16),
            shape((RING, 4) + scales.shape, f32),
            shape((blocks, tokens, width), bf16),
            shape((blocks, tokens, width), bf16),
            shape((experts, blocks, capacity, width), bf16),
            shape((experts, blocks, capacity, width), bf16),
            shape((2, experts, blocks, capacity, hidden), bf16),
            shape((experts, blocks, capacity, hidden), bf16),
            shape((2, blocks, tokens, slice_hidden), bf16),
            shape((blocks, tokens, slice_hidden), bf16),
            shape((RING, 4) + scales.shape, f32),
        ),
        in_specs=[IN_VMEM] * 7,
        out_specs=(IN_PLACE,) * 2 + (IN_VMEM,) + (IN_PLACE,) * 8 + (IN_VMEM,),
        scratch_shapes=[
            pltpu.VMEM((blocks, experts, tokens), jnp.int32),
            pltpu.VMEM((blocks, tokens, experts), jnp.int32),
            pltpu.VMEM((3, slice_hidden, width), bf16),
            pltpu.VMEM((experts * capacity + slice_hidden, width), bf16),
            pltpu.VMEM((experts * capacity + 2 * slice_hidden, width), bf16),
            pltpu.VMEM((2, 4, count, width), bf16),
            pltpu.VMEM((2, 4, count, width), bf16),
        ]
        + [pltpu.VMEM(stage, bf16) for stage in stages]
        + [pltpu.SemaphoreType.DMA((2, 2)), pltpu.SemaphoreType.DMA((len(stages),))]
        + semaphores(160),
        compiler_params=remote_params(collective_id, 62),
        name="gather_feed",
    )(rows, cotangent, scales, routes, expert_in, expert_down, shared)


def add_into(total, term, rows, tile=32):
    tile = min(tile, rows)

    def step(index, carry):
        here = pl.ds(pl.multiple_of(index * tile, tile), tile)
        summed = total[here, :].astype(jnp.float32) + term[here, :].astype(jnp.float32)
        total[here, :] = summed.astype(total.dtype)
        return carry

    lax.fori_loop(0, rows // tile, step, 0)


class WeightGrads:
    def __init__(self, jobs, left, right, sums, low, sems, out_sems):
        self.jobs, self.left, self.right = jobs, left, right
        self.sums, self.low, self.sems, self.out_sems = sums, low, sems, out_sems
        self.next = 0
        self.stores = {}
        self.fetch(0, 0, 0).start()

    def fetch(self, job, index, slot):
        left, right, _ = self.jobs[job]
        chunk, rows, columns, _ = self.size(job)
        here = pl.ds(pl.multiple_of(index * chunk, chunk), chunk)
        return Pair(
            pltpu.make_async_copy(
                left.at[here], self.left[rows].at[slot, pl.ds(0, chunk)], self.sems.at[slot, 0]
            ),
            pltpu.make_async_copy(
                right.at[here], self.right.at[slot, pl.ds(0, chunk)], self.sems.at[slot, 1]
            ),
        )

    def size(self, job):
        left, right, _ = self.jobs[job]
        depth, rows = left.shape
        chunk = min(self.right.shape[1], depth)
        while depth % (2 * chunk):
            chunk -= 128
        return chunk, rows, right.shape[1], depth // chunk

    def run(self, count=1):
        for job in range(self.next, min(self.next + count, len(self.jobs))):
            self.one(job)

    def one(self, job):
        self.next = job + 1
        chunk, rows, _, steps = self.size(job)
        which = job % 2
        if which in self.stores:
            self.stores.pop(which).wait()
        total = self.sums.at[which, pl.ds(0, rows)]

        def step(index, carry):
            slot = index % 2

            @pl.when(index + 1 < steps)
            def _():
                self.fetch(job, index + 1, 1 - slot).start()

            if job + 1 < len(self.jobs):

                @pl.when(index + 1 == steps)
                def _():
                    self.fetch(job + 1, 0, 0).start()

            self.fetch(job, index, slot).wait()
            term = product(
                self.left[rows][slot, pl.ds(0, chunk)], self.right[slot, pl.ds(0, chunk)], TN
            )

            @pl.when(index == 0)
            def _():
                total[...] = term

            @pl.when(index > 0)
            def _():
                total[...] += term

            return carry

        lax.fori_loop(0, steps, step, 0)
        out = self.jobs[job][2]
        source = self.low.at[which, pl.ds(0, rows)]
        source[...] = total[...].astype(out.dtype)
        if out.ndim == source.ndim:
            moves = [pltpu.make_async_copy(source, out, self.out_sems.at[which, 0])]
        else:
            across = out.shape[2]
            moves = [
                pltpu.make_async_copy(
                    source.at[:, pl.ds(place * across, across)], out.at[place], self.out_sems.at[which, place]
                )
                for place in range(out.shape[0])
            ]
        self.stores[which] = Pair(*moves)
        self.stores[which].start()

    def finish(self):
        self.run(len(self.jobs))
        for store in self.stores.values():
            store.wait()


class Pair:
    def __init__(self, *moves):
        self.moves = moves

    def start(self):
        for move in self.moves:
            move.start()

    def wait(self):
        for move in self.moves:
            move.wait()


def scatter_kernel(
    back_part, ffn_part, scalars, slot_rows, slot_cotangent, grad_pre, gated,
    all_rows, all_cotangent, grad_shared_pre, scaled,
    back_sum, ffn_sum, out_scalars, grad_expert_in, grad_expert_down, grad_shared,
    held, core_in, x_in, ring_q, ring_x, last_in,
    s_held, s_core, s_x, s_ring,
    job_left, job_short, job_right, job_sums, job_low, job_sems, job_out_sems,
    free, send_sems, recv_sems,
):
    me = Peers()
    copies = Copies(send_sems, recv_sems)
    parts, outs = (back_part, ffn_part), (back_sum, ffn_sum)
    count = back_part.shape[2]
    half, piece = count // 2, count // 4
    q, qx, qc, qd = me.quarter, me.x_quarter, me.core_quarter, me.far_quarter
    own, other, last = range(3)
    peers = {RIGHT: me.right, LEFT: me.left}
    greet([me.right, me.left, me.x_peer, me.core_peer])
    order = (4, 3, 5, 2, 6, 1, 7, 0)

    def load(kind):
        for k in order:
            for slot, mine in ((0, q), (1, qx)):
                copies.local(
                    (kind, LOCAL, k, slot), parts[kind].at[me.block(k), mine], held.at[kind, k, slot]
                )

    def swap_cores(kind):
        for k in order:
            for slot, theirs in ((0, qc), (1, qd)):
                target = core_in.at[k, slot]
                copies.send(
                    (kind, OVER_CORE, k, slot),
                    parts[kind].at[me.block(k), theirs],
                    target,
                    target,
                    me.core_peer,
                )

    swap_cores(0)
    load(0)
    for k in range(RING):
        for slot, mine, theirs in ((0, q, qc), (1, qx, qd)):
            copies.local((SCALARS, LOCAL, k, slot), scalars.at[me.block(k), mine], s_held.at[slot, k])
            target = s_core.at[slot, k]
            copies.send(
                (SCALARS, OVER_CORE, k, slot),
                scalars.at[me.block(k), theirs],
                target,
                target,
                me.core_peer,
            )

    def prepare(kind, *blocks):
        for k in blocks:
            for slot in (1, 0):
                copies.arrive(kind, LOCAL, k, slot)
                copies.arrive(kind, OVER_CORE, k, slot)
                add_into(held.at[kind, k, slot], core_in.at[k, slot], count)
                if slot == 1:
                    source = held.at[kind, k, 1, pl.ds(half, half)]
                    target = x_in.at[kind, k]
                    copies.send((kind, OVER_X, k), source, target, target, me.x_peer)

    def over_x(kind, *blocks):
        for k in blocks:
            copies.arrive(kind, OVER_X, k)
            add_into(held.at[kind, k, 0, pl.ds(half, half)], x_in.at[kind, k], half)

    def pass_on(kind, side, hop, k):
        if hop == 0:
            rows_q, rows_x = pl.ds(side * half, half), pl.ds(side * piece, piece)
        else:
            rows_q, rows_x = pl.ds(0, count), pl.ds(0, half)
        for which, landing, rows in ((own, ring_q, rows_q), (other, ring_x, rows_x)):
            target = landing.at[kind, side, hop, rows]
            source = held.at[kind, k, which, rows]
            copies.send((kind, side, which, hop), source, target, target, peers[side])

    def take_in(kind, side, hop, k):
        if hop == 0:
            span_q, span_x, at_q, at_x = half, piece, side * half, side * piece
        else:
            span_q, span_x, at_q, at_x = count, half, 0, 0
        for which, landing, span, at in (
            (own, ring_q, span_q, at_q),
            (other, ring_x, span_x, at_x),
        ):
            copies.arrive(kind, side, which, hop)
            rows = pl.ds(at, span)
            add_into(held.at[kind, k, which, rows], landing.at[kind, side, hop, rows], span)

    def hop_on(kind, hop):
        right_block, left_block = 4 - hop, 4 + hop
        if hop == 0:
            pass_on(kind, RIGHT, 0, 4)
            pass_on(kind, LEFT, 0, 4)
            return
        take_in(kind, RIGHT, hop - 1, right_block)
        pass_on(kind, RIGHT, hop, right_block)
        take_in(kind, LEFT, hop - 1, left_block)
        pass_on(kind, LEFT, hop, left_block)

    def pass_scalars(side, hop, k):
        target = s_ring.at[side, hop]
        copies.send((SCALARS, side, hop), s_held.at[0, k], target, target, peers[side])

    def take_scalars(side, hop, k):
        copies.arrive(SCALARS, side, hop)
        s_held[0, k] += s_ring[side, hop]

    def home(kind):
        take_in(kind, RIGHT, 3, 0)
        take_in(kind, LEFT, 3, 0)
        source, target = held.at[kind, 0, 1, pl.ds(0, half)], last_in.at[kind]
        copies.send((kind, OVER_X, last, last), source, target, target, me.x_peer)

    def home_out(kind):
        out = outs[kind]
        out[pl.ds(half, half), :] = held[kind, 0, 0, pl.ds(half, half), :].astype(out.dtype)
        copies.arrive(kind, OVER_X, last, last)
        out[pl.ds(0, half), :] = (
            held[kind, 0, 0, pl.ds(0, half), :].astype(jnp.float32)
            + last_in[kind].astype(jnp.float32)
        ).astype(out.dtype)

    experts = slot_rows.shape[0]
    jobs = []
    for expert in range(experts):
        for index in range(2):
            jobs.append(
                (grad_pre.at[index, expert], slot_rows.at[expert], grad_expert_in.at[expert, index])
            )
        jobs.append((gated.at[expert], slot_cotangent.at[expert], grad_expert_down.at[expert]))
    for index in range(2):
        jobs.append((grad_shared_pre.at[index], all_rows, grad_shared.at[:, index]))
    jobs.append((scaled, all_cotangent, grad_shared.at[:, 2]))
    prepare(0, 4, 3, 5)
    over_x(0, 4)
    hop_on(0, 0)
    prepare(0, 2, 6)
    for k in range(RING):
        for slot in (0, 1):
            copies.arrive(SCALARS, LOCAL, k, slot)
            copies.arrive(SCALARS, OVER_CORE, k, slot)
    s_held[...] += s_core[...]
    copies.send((SCALARS, OVER_X), s_held.at[1], s_x, s_x, me.x_peer)
    over_x(0, 3, 5)
    hop_on(0, 1)
    copies.arrive(SCALARS, OVER_X)
    s_held[0] += s_x[...]
    pass_scalars(RIGHT, 0, 4)
    prepare(0, 1, 7, 0)
    pl.semaphore_signal(free, inc=1, device_id=me.core_peer, device_id_type=MESH_ID)
    load(1)
    lefts = {job_left.shape[2]: job_left, job_short.shape[2]: job_short}
    grads = WeightGrads(jobs, lefts, job_right, job_sums, job_low, job_sems, job_out_sems)
    over_x(0, 2, 6)
    hop_on(0, 2)
    take_scalars(RIGHT, 0, 3)
    pass_scalars(RIGHT, 1, 3)
    pass_scalars(LEFT, 1, 5)
    pl.semaphore_wait(free, 1)
    swap_cores(1)
    over_x(0, 1, 7)
    grads.run(1)
    prepare(1, 4, 3, 5)
    hop_on(0, 3)
    take_scalars(RIGHT, 1, 2)
    take_scalars(LEFT, 1, 6)
    pass_scalars(RIGHT, 2, 2)
    pass_scalars(LEFT, 2, 6)
    over_x(0, 0)
    over_x(1, 4)
    hop_on(1, 0)
    prepare(1, 2, 6)
    over_x(1, 3, 5)
    grads.run(2)
    home(0)
    for side, k in ((RIGHT, 1), (LEFT, 7)):
        take_scalars(side, 2, k)
        pass_scalars(side, 3, k)
    hop_on(1, 1)
    home_out(0)
    prepare(1, 1, 7, 0)
    over_x(1, 2, 6)
    grads.run(2)
    hop_on(1, 2)
    over_x(1, 1, 7, 0)
    grads.run(2)
    hop_on(1, 3)
    take_scalars(RIGHT, 3, 0)
    take_scalars(LEFT, 3, 0)
    out_scalars[...] = s_held[0, 0]
    grads.finish()
    home(1)
    home_out(1)
    copies.finish()


def scatter_rows(back_part, ffn_part, scalars, fed, collective_id):
    slot_rows, slot_cotangent, grad_pre, gated, all_rows, all_cotangent, grad_shared_pre, scaled = fed
    _, _, count, width = back_part.shape
    half = count // 2
    dtype, f32 = back_part.dtype, jnp.float32
    s_shape = scalars.shape[2:]
    experts, hidden = gated.shape[0], gated.shape[2]
    shared_hidden = scaled.shape[1]
    shape = jax.ShapeDtypeStruct
    return pl.pallas_call(
        scatter_kernel,
        out_shape=(
            shape((count, width), f32),
            shape((count, width), f32),
            shape(s_shape, f32),
            shape((experts, 2, hidden, width), dtype),
            shape((experts, hidden, width), dtype),
            shape((RING, 3, shared_hidden, width // RING), dtype),
        ),
        in_specs=[IN_PLACE] * 11,
        out_specs=(IN_VMEM,) * 3 + (IN_PLACE,) * 3,
        scratch_shapes=[
            pltpu.VMEM((2, RING, 2, count, width), dtype),
            pltpu.VMEM((RING, 2, count, width), dtype),
            pltpu.VMEM((2, RING, half, width), dtype),
            pltpu.VMEM((2, 2, 4, count, width), dtype),
            pltpu.VMEM((2, 2, 4, half, width), dtype),
            pltpu.VMEM((2, half, width), dtype),
            pltpu.VMEM((2, RING) + s_shape, f32),
            pltpu.VMEM((2, RING) + s_shape, f32),
            pltpu.VMEM((RING,) + s_shape, f32),
            pltpu.VMEM((2, 4) + s_shape, f32),
            pltpu.VMEM((2, 640, hidden), dtype),
            pltpu.VMEM((2, 640, shared_hidden), dtype),
            pltpu.VMEM((2, 640, width), dtype),
            pltpu.VMEM((2, hidden, width), f32),
            pltpu.VMEM((2, hidden, width), dtype),
            pltpu.SemaphoreType.DMA((2, 2)),
            pltpu.SemaphoreType.DMA((2, RING)),
            pltpu.SemaphoreType.REGULAR,
        ]
        + semaphores(168),
        compiler_params=remote_params(collective_id, 62),
        name="scatter_rows",
    )(back_part, ffn_part, scalars, *fed)


def open_kernel(
    shard_in, shard_out, routes, rows, gain, bias, cosine, sine, shared_in, shared_down,
    full_in, full_out, full_routes, normed, queries, keys_values, shared_shards,
    sums, share_send, share_recv, send_sems, recv_sems,
):
    me = Peers()
    copies = Copies(send_sems, recv_sems)
    bf16, f32 = jnp.bfloat16, jnp.float32
    kinds, depth, width = shard_in.shape
    out_rows, columns = shard_out.shape
    tokens = rows.shape[0]
    sides = ((RIGHT, me.right, -1), (LEFT, me.left, 1))
    greet_along_z(me)

    def cell(kind, step, part, parts):
        block = me.block(step)
        if kind < kinds:
            return full_in.at[kind, block, pl.ds(part * (depth // parts), depth // parts)]
        if kind > kinds:
            return full_routes.at[block]
        across = pl.ds(pl.multiple_of(block * columns, columns), columns)
        return full_out.at[pl.ds(part * (out_rows // parts), out_rows // parts), across]

    def pass_on(side, peer, sign, kind, hop, source=None):
        if kind > kinds and hop == 3 and side == LEFT:
            return
        parts = 2 if hop == 3 else 1
        part = side if hop == 3 else 0
        step = sign * hop
        here = cell(kind, step, part, parts)
        copies.send(
            (side, kind, hop + 1),
            here if source is None else source,
            here,
            cell(kind, step + sign, part, parts),
            peer,
        )

    def hop_on(hop, order):
        for kind in order:
            source = None
            if hop == 0:
                source = shard_in.at[kind] if kind < kinds else shard_out if kind == kinds else routes
                cell(kind, 0, 0, 1)[...] = source[...]
            for side, peer, sign in sides:
                if hop > 0:
                    copies.arrive(side, kind, hop)
                pass_on(side, peer, sign, kind, hop, source)

    def multiply(kind, step):
        block = me.block(step)
        features = normed[:, pl.ds(pl.multiple_of(block * depth, depth), depth)]
        term = product(features, full_in[kind, block])
        if step == 0:
            sums[kind] = term + bias[kind : kind + 1, :]
        else:
            sums[kind] += term

    def go_round(order):
        taken = [kind for kind in order if kind < kinds]
        for hop in (1, 2, 3):
            hop_on(hop, order)
            for kind in taken:
                for step in (-hop, hop):
                    multiply(kind, step)
        for kind in order:
            for side, _, _ in sides:
                if kind <= kinds or side == RIGHT:
                    copies.arrive(side, kind, 4)
        for kind in taken:
            multiply(kind, 4)

    def heads_of(kind, turn):
        for start in range(0, width, HD):
            head = slice(start, start + HD)
            part = sums[kind, :, head]
            if turn:
                part = turned(part, cosine[...], sine[...])
            yield head, part.astype(bf16)

    first, second = (kinds + 1,) + tuple(range(kinds - 1, 0, -1)), (0, kinds)
    hop_on(0, first)
    _, scaled = rms_parts(rows[...].astype(f32))
    normed[...] = (scaled * gain[...]).astype(bf16)
    for kind in range(kinds):
        if kind:
            multiply(kind, 0)
    places, _, slice_hidden, across = shared_shards.shape
    for index in range(2):
        turned_shard = jnp.swapaxes(shared_in[index].astype(f32), 0, 1).astype(bf16)
        shared_shards[:, index] = turned_shard.reshape(places, slice_hidden, across)
    shared_shards[:, 2] = shared_down[...].reshape(places, slice_hidden, across)
    go_round(first)
    for index in range(2):
        for head, part in heads_of(index + 1, index == 0):
            keys_values[index, 2, :, head] = part
    pieces = 2
    size = tokens // pieces
    parts = [(kind, pl.ds(piece * size, size)) for kind in range(2) for piece in range(pieces)]
    count = len(parts)
    share = Copies(share_send, share_recv)

    def upward(index, kind, at):
        target = keys_values.at[kind, 0, at]
        return share.describe(keys_values.at[kind, 2, at], target, (me.ep + 2, me.tp), index)

    def sideways(index, kind, at):
        target = keys_values.at[kind, 1, at]
        return share.describe(keys_values.at[kind, 2, at], target, me.y_peer, count + index)

    def onward(index, kind, at):
        target = keys_values.at[kind, 1, at]
        return share.describe(keys_values.at[kind, 0, at], target, me.y_peer, count + index)

    def each(copy, action):
        for index, (kind, at) in enumerate(parts):
            action(copy(index, kind, at))

    @pl.when(me.z < 3)
    def _():
        each(upward, lambda copy: copy.start())

    @pl.when(me.y == 0)
    def _():
        each(sideways, lambda copy: copy.start())

    hop_on(0, second)
    multiply(0, 0)

    @pl.when(me.z == 0)
    def _():
        keys_values[:, 0] = jnp.zeros((2, tokens, width), bf16)

    @pl.when((me.z == 0) & (me.y == 0))
    def _():
        keys_values[:, 1] = jnp.zeros((2, tokens, width), bf16)

    @pl.when(me.z > 0)
    def _():
        for index, (kind, at) in enumerate(parts):
            upward(index, kind, at).wait_recv()

            @pl.when(me.y == 1)
            def _():
                onward(index, kind, at).start()

    go_round(second)
    for head, part in heads_of(0, True):
        queries[:, head] = part

    @pl.when((me.y == 1) | (me.z > 0))
    def _():
        each(sideways, lambda copy: copy.wait_recv())

    @pl.when(me.z < 3)
    def _():
        each(upward, lambda copy: copy.wait_send())

    @pl.when((me.y == 0) | (me.z > 0))
    def _():
        each(sideways, lambda copy: copy.wait_send())

    copies.finish()


def open_attention(
    shard_in, shard_out, routes, rows, gain, bias, cosine, sine, shared_in, shared_down, collective_id
):
    kinds, depth, width = shard_in.shape
    out_rows, columns = shard_out.shape
    tokens, features = rows.shape
    bf16 = jnp.bfloat16
    shape = jax.ShapeDtypeStruct
    return pl.pallas_call(
        open_kernel,
        out_shape=(
            shape((kinds, RING, depth, width), bf16),
            shape((out_rows, RING * columns), bf16),
            shape((RING,) + routes.shape, routes.dtype),
            shape((tokens, features), bf16),
            shape((tokens, width), bf16),
            shape((2, 3, tokens, width), bf16),
            shape((RING, 3, shared_in.shape[2] // RING, shared_in.shape[1]), bf16),
        ),
        in_specs=[IN_VMEM] * 10,
        out_specs=(IN_VMEM,) * 7,
        scratch_shapes=[pltpu.VMEM((kinds, tokens, width), jnp.float32)]
        + semaphores(8)
        + semaphores(8 * (kinds + 2)),
        compiler_params=remote_params(collective_id),
        name="open_attention",
    )(shard_in, shard_out, routes, rows, gain[None], bias, cosine, sine, shared_in, shared_down)


def finish_kernel(
    normed, grad_raw, heads, grad_attention, weights, gain, rows, grad_residual, tail,
    sum_in, sum_out, sum_tail, grad_input,
    held_in, held_out, ring_in, ring_out, tails, tail_sums,
    core_out, core_in, x_out, x_in, grad_rows, mine,
    send_sems, recv_sems,
):
    me = Peers()
    copies = Copies(send_sems, recv_sems)
    bf16, f32 = jnp.bfloat16, jnp.float32
    kinds = grad_raw.shape[0]
    depth, width = sum_in.shape[1], sum_in.shape[2]
    out_rows, columns = sum_out.shape
    count = rows.shape[0]
    peers = {RIGHT: me.right, LEFT: me.left}
    greet([me.right, me.left, me.x_peer, me.core_peer, me.far_peer])

    def held(kind, k):
        return held_in.at[k, kind] if kind < kinds else held_out.at[k]

    def ring(kind, side, hop):
        return ring_in.at[side, hop, kind] if kind < kinds else ring_out.at[side, hop]

    def span(kind, side, hop):
        whole = depth if kind < kinds else out_rows
        return (side * (whole // 2), whole // 2) if hop == 0 else (0, whole)

    def pass_on(side, hop, k, kind):
        at = pl.ds(*span(kind, side, hop))
        target = ring(kind, side, hop).at[at]
        copies.send((side, kind, hop), held(kind, k).at[at], target, target, peers[side])

    def take_in(side, hop, k, kind):
        copies.arrive(side, kind, hop)
        start, size = span(kind, side, hop)
        at = pl.ds(start, size)
        add_into(held(kind, k).at[at], ring(kind, side, hop).at[at], size)

    def work_out(*blocks):
        for k in blocks:
            block = me.block(k)
            features = normed[:, pl.ds(pl.multiple_of(block * depth, depth), depth)]
            for kind in range(kinds):
                held_in[k, kind] = product(features, grad_raw[kind], TN).astype(bf16)
            across = grad_attention[:, pl.ds(pl.multiple_of(block * columns, columns), columns)]
            held_out[k] = product(heads[...], across, TN).astype(bf16)

    def hop_on(hop):
        if hop == 0:
            for kind in range(kinds + 1):
                for side in (RIGHT, LEFT):
                    pass_on(side, 0, 4, kind)
            return
        for kind in range(kinds + 1):
            for side, k in ((RIGHT, 4 - hop), (LEFT, 4 + hop)):
                take_in(side, hop - 1, k, kind)
                pass_on(side, hop, k, kind)

    def quarter(index):
        here = pl.ds(pl.multiple_of(index * count, count), count)
        total = None
        for kind in range(kinds):
            term = product(grad_raw[kind, here, :], weights[kind], NT)
            total = term if total is None else total + term
        return total

    work_out(4)
    hop_on(0)
    for slot, index in ((1, me.far_quarter), (0, me.core_quarter)):
        core_out[slot] = quarter(index).astype(bf16)
        target = core_in.at[slot]
        copies.send((SCALARS, OVER_CORE, slot), core_out.at[slot], target, target, me.core_peer)
    mine[...] = quarter(me.x_quarter)
    copies.arrive(SCALARS, OVER_CORE, 1)
    x_out[...] = (mine[...] + core_in[1].astype(f32)).astype(bf16)
    copies.send((SCALARS, OVER_X), x_out, x_in, x_in, me.x_peer)
    work_out(3, 5)
    hop_on(1)
    mine[...] = quarter(me.quarter)
    copies.arrive(SCALARS, OVER_CORE, 0)
    work_out(2, 6)
    copies.arrive(SCALARS, OVER_X)
    total = mine[...] + core_in[0].astype(f32) + x_in[...].astype(f32)
    inverse, scaled_rows = rms_parts(rows[...].astype(f32))
    scaled = total * gain[...]
    slope = inverse * (
        scaled - scaled_rows * jnp.mean(scaled * scaled_rows, axis=-1, keepdims=True)
    )
    grad_rows[...] = (grad_residual[...] + slope).astype(bf16)
    here = grad_input.at[me.quarter]
    copies.send((SCALARS, RIGHT, OVER_X), grad_rows, here, grad_input.at[me.x_quarter], me.x_peer)
    copies.send(
        (SCALARS, RIGHT, OVER_CORE), grad_rows, here, grad_input.at[me.core_quarter], me.core_peer
    )
    copies.local((LOCAL,), grad_rows, here)
    gain_grad = jnp.sum(total * scaled_rows, axis=0, keepdims=True)
    tails[0, 0:kinds, :] = tail[...]
    for index in range(gain_grad.shape[1] // width):
        part = slice(index * width, (index + 1) * width)
        tails[0, kinds + index : kinds + index + 1, :] = gain_grad[:, part]
    tail_kind = kinds + 1

    def pass_tail(side, hop, place):
        sign = -1 if side == RIGHT else 1
        target = tails.at[(place + sign) % RING]
        copies.send((side, tail_kind, hop), tails.at[place], target, target, peers[side])

    pass_tail(RIGHT, 0, 0)
    pass_tail(LEFT, 0, 0)
    hop_on(2)
    work_out(1, 7)
    copies.arrive(SCALARS, RIGHT, OVER_X)
    beside = grad_input.at[me.x_quarter]
    copies.send(
        (SCALARS, LEFT, OVER_CORE), beside, beside, grad_input.at[me.far_quarter], me.core_peer
    )
    for side, place in ((RIGHT, 7), (LEFT, 1)):
        copies.arrive(side, tail_kind, 0)
        pass_tail(side, 1, place)
    hop_on(3)
    for side, place in ((RIGHT, 6), (LEFT, 2)):
        copies.arrive(side, tail_kind, 1)
        pass_tail(side, 2, place)
    work_out(0)
    copies.arrive(RIGHT, tail_kind, 2)
    pass_tail(RIGHT, 3, 5)
    copies.arrive(LEFT, tail_kind, 2)
    for kind in range(kinds + 1):
        for side in (RIGHT, LEFT):
            take_in(side, 3, 0, kind)
        if kind < kinds:
            sum_in[kind] = held_in[0, kind].astype(f32)
    sum_out[...] = held_out[0].astype(f32)
    copies.arrive(RIGHT, tail_kind, 3)
    total = tails[0]
    for place in range(1, RING):
        total = total + tails[place]
    tail_sums[me.tp] = total
    for way, peer, index in (
        (OVER_X, me.x_peer, me.x_quarter),
        (OVER_CORE, me.core_peer, me.core_quarter),
        (OVER_FAR, me.far_peer, me.far_quarter),
    ):
        copies.send(
            (way, tail_kind), tail_sums.at[me.tp], tail_sums.at[me.tp], tail_sums.at[index], peer
        )
    for way in (OVER_X, OVER_CORE, OVER_FAR):
        copies.arrive(way, tail_kind)
    sum_tail[...] = tail_sums[...]
    copies.finish()


def finish(
    normed, grad_raw, heads, grad_attention, weights, gain, rows, grad_residual, bias, collective_id
):
    tokens, width = normed.shape
    kinds, _, columns = grad_raw.shape
    count = rows.shape[0]
    depth = width // RING
    bf16, f32 = jnp.bfloat16, jnp.float32
    shape = jax.ShapeDtypeStruct
    tail_shape = (-(-(kinds + width // columns) // 8) * 8, columns)
    return pl.pallas_call(
        finish_kernel,
        out_shape=(
            shape((kinds, depth, columns), f32),
            shape((columns, depth), f32),
            shape((4,) + tail_shape, f32),
            shape((4, count, width), bf16),
        ),
        in_specs=[IN_VMEM] * 9,
        out_specs=(IN_VMEM,) * 3 + (IN_PLACE,),
        scratch_shapes=[
            pltpu.VMEM((RING, kinds, depth, columns), bf16),
            pltpu.VMEM((RING, columns, depth), bf16),
            pltpu.VMEM((2, 4, kinds, depth, columns), bf16),
            pltpu.VMEM((2, 4, columns, depth), bf16),
            pltpu.VMEM((RING,) + tail_shape, f32),
            pltpu.VMEM((4,) + tail_shape, f32),
            pltpu.VMEM((2, count, width), bf16),
            pltpu.VMEM((2, count, width), bf16),
            pltpu.VMEM((count, width), bf16),
            pltpu.VMEM((count, width), bf16),
            pltpu.VMEM((count, width), bf16),
            pltpu.VMEM((count, width), f32),
        ]
        + semaphores(56),
        compiler_params=remote_params(collective_id, 60),
        name="finish",
    )(normed, grad_raw, heads, grad_attention, weights, gain[None], rows, grad_residual, bias)


def greet_along_z(me, others=()):
    barrier = pltpu.get_barrier_semaphore()
    for peer in (me.y_peer,) + others:
        pl.semaphore_signal(barrier, inc=1, device_id=peer, device_id_type=MESH_ID)

    @pl.when(me.z > 0)
    def _():
        peer = (me.ep - 2, me.tp)
        pl.semaphore_signal(barrier, inc=1, device_id=peer, device_id_type=MESH_ID)

    @pl.when(me.z < 3)
    def _():
        peer = (me.ep + 2, me.tp)
        pl.semaphore_signal(barrier, inc=1, device_id=peer, device_id_type=MESH_ID)

    pl.semaphore_wait(barrier, 1 + len(others) + (me.z + 2) // 3 + (5 - me.z) // 3)


def back_kernel(
    rows, weights, valid, queries, keys_values, query_doc, key_doc, log_totals, cosine, sine,
    grad_attention, grad_raw,
    grad_heads, grads, total, from_y, from_z,
    y_send, y_recv, z_send, z_recv, send_sems, recv_sems,
):
    me = Peers()
    copies = Copies(send_sems, recv_sems)
    bf16, f32 = jnp.bfloat16, jnp.float32
    count = rows.shape[0]
    tokens, width = queries.shape
    blocks = keys_values.shape[1]
    head_count = width // HD
    greet_along_z(me, (me.x_peer, me.core_peer))

    mine = grad_attention.at[me.quarter]
    copies.send((OVER_X,), rows, mine, grad_attention.at[me.x_quarter], me.x_peer)
    copies.send((OVER_CORE, 0), rows, mine, grad_attention.at[me.core_quarter], me.core_peer)
    mine[...] = rows[...]

    def heads_of(quarter):
        at = pl.ds(pl.multiple_of(quarter * count, count), count)
        part = product(grad_attention[quarter], weights[...], NT) * valid[at, :]
        grad_heads[at, :] = part.astype(bf16)

    heads_of(me.quarter)
    copies.arrive(OVER_CORE, 0)
    heads_of(me.core_quarter)
    copies.arrive(OVER_X)
    beside = grad_attention.at[me.x_quarter]
    copies.send((OVER_CORE, 1), beside, beside, grad_attention.at[me.far_quarter], me.core_peer)
    heads_of(me.x_quarter)
    copies.arrive(OVER_CORE, 1)
    heads_of(me.far_quarter)

    across = Copies(y_send, y_recv)
    along = Copies(z_send, z_recv)

    def columns(head):
        return pl.ds(pl.multiple_of(head * HD, HD), HD)

    def sideways(head, kind):
        at = columns(head)
        source, target = grads.at[kind, 1, :, at], from_y.at[kind, :, at]
        return across.describe(source, target, me.y_peer, 2 * head + kind)

    def downward(head, kind, source):
        at = columns(head)
        return along.describe(
            source.at[kind, :, at], from_z.at[kind, :, at], (me.ep - 2, me.tp), 2 * head + kind
        )

    scale = 1.0 / math.sqrt(HD)

    def one_head(head, carry):
        at = columns(head)
        keys = keys_values[0, :, :, at].reshape(blocks * tokens, HD)
        values = keys_values[1, :, :, at].reshape(blocks * tokens, HD)
        query = queries[:, at]
        out_grads = grad_heads[:, at]
        scores = masked_scores(query, keys, query_doc[...], key_doc[...])
        probs = jnp.exp(scores - log_totals[head])
        slopes = product(out_grads, values, NT)
        slopes = probs * (slopes - jnp.sum(probs * slopes, axis=1, keepdims=True))
        grad_scores = slopes.astype(bf16)
        grad_keys = product(grad_scores, query, TN) * scale
        grads[0, :, :, at] = grad_keys.astype(bf16).reshape(blocks, tokens, HD)
        grad_values = product(probs.astype(bf16), out_grads, TN)
        grads[1, :, :, at] = grad_values.astype(bf16).reshape(blocks, tokens, HD)
        for kind in range(2):
            sideways(head, kind).start()

        @pl.when((me.z > 0) & (me.y == 0))
        def _():
            for kind in range(2):
                downward(head, kind, grads.at[:, 0]).start()

        turned_back = turned(product(grad_scores, keys) * scale, cosine[...], -sine[...])
        grad_raw[0, :, at] = turned_back.astype(bf16)
        return carry

    lax.fori_loop(0, head_count, one_head, 0)

    def from_beside(head, carry):
        at = columns(head)
        for kind in range(2):
            sideways(head, kind).wait_recv()
            here = grads[kind, 2, :, at].astype(f32)

            @pl.when(me.y == 0)
            def _():
                total[kind, :, at] = here + from_y[kind, :, at].astype(f32)

            @pl.when(me.y == 1)
            def _():
                total[kind, :, at] = here
                two_back = grads[kind, 0, :, at].astype(f32)
                summed = two_back + from_y[kind, :, at].astype(f32)
                from_y[kind, :, at] = summed.astype(bf16)

            @pl.when((me.z > 0) & (me.y == 1))
            def _():
                downward(head, kind, from_y).start()

        return carry

    lax.fori_loop(0, head_count, from_beside, 0)

    def from_above(head, carry):
        at = columns(head)

        @pl.when(me.z < 3)
        def _():
            for kind in range(2):
                downward(head, kind, from_y).wait_recv()
                total[kind, :, at] += from_z[kind, :, at].astype(f32)

        grad_raw[1, :, at] = turned(total[0, :, at], cosine[...], -sine[...]).astype(bf16)
        grad_raw[2, :, at] = total[1, :, at].astype(bf16)
        return carry

    lax.fori_loop(0, head_count, from_above, 0)

    def sent(head, carry):
        for kind in range(2):
            sideways(head, kind).wait_send()

        @pl.when(me.z > 0)
        def _():
            for kind in range(2):
                downward(head, kind, from_y).wait_send()

        return carry

    lax.fori_loop(0, head_count, sent, 0)
    copies.finish()


def back_attention(
    rows, weights, valid, queries, keys_values, query_doc, key_doc, log_totals, cosine, sine,
    collective_id,
):
    count, features = rows.shape
    tokens, width = queries.shape
    bf16, f32 = jnp.bfloat16, jnp.float32
    shape = jax.ShapeDtypeStruct
    pieces = 2 * (width // HD)
    return pl.pallas_call(
        back_kernel,
        out_shape=(shape((4, count, features), bf16), shape((3, tokens, width), bf16)),
        in_specs=[IN_VMEM] * 10,
        out_specs=(IN_VMEM,) * 2,
        scratch_shapes=[
            pltpu.VMEM((tokens, width), bf16),
            pltpu.VMEM(keys_values.shape, bf16),
            pltpu.VMEM((2, tokens, width), f32),
            pltpu.VMEM((2, tokens, width), bf16),
            pltpu.VMEM((2, tokens, width), bf16),
        ]
        + semaphores(pieces)
        + semaphores(pieces)
        + semaphores(3),
        compiler_params=remote_params(collective_id, 60),
        name="back_attention",
    )(rows, weights, valid, queries, keys_values, query_doc, key_doc, log_totals, cosine, sine)


def reduce_kernel(flip, left, right, out, core_out, core_in, x_out, x_in, send_sems, recv_sems):
    me = Peers()
    copies = Copies(send_sems, recv_sems)
    terms = left.shape[0]
    count = out.shape[0]
    f32 = jnp.float32
    greet([me.x_peer, me.core_peer])

    def quarter(index):
        rows = pl.ds(pl.multiple_of(index * count, count), count)
        total = None
        for term in range(terms):
            one = product(left[term, rows, :], right[term], NT if flip else NN)
            total = one if total is None else total + one
        return total

    for slot, index in ((1, me.far_quarter), (0, me.core_quarter)):
        core_out[slot] = quarter(index).astype(core_out.dtype)
        target = core_in.at[slot]
        copies.send((OVER_CORE, slot), core_out.at[slot], target, target, me.core_peer)
    mine = quarter(me.x_quarter)
    copies.arrive(OVER_CORE, 1)
    x_out[...] = (mine + core_in[1].astype(f32)).astype(x_out.dtype)
    copies.send((OVER_X,), x_out, x_in, x_in, me.x_peer)
    mine = quarter(me.quarter)
    copies.arrive(OVER_CORE, 0)
    out[...] = mine + core_in[0].astype(f32)
    copies.arrive(OVER_X)
    out[...] += x_in[...].astype(f32)
    copies.finish()


def product_to_owner(left, right, flip, collective_id):
    tokens = left.shape[1]
    width = right.shape[1] if flip else right.shape[2]
    count = tokens // 4
    bf16 = jnp.bfloat16
    return pl.pallas_call(
        functools.partial(reduce_kernel, flip),
        out_shape=jax.ShapeDtypeStruct((count, width), jnp.float32),
        in_specs=[IN_VMEM] * 2,
        out_specs=IN_VMEM,
        scratch_shapes=[
            pltpu.VMEM((2, count, width), bf16),
            pltpu.VMEM((2, count, width), bf16),
            pltpu.VMEM((count, width), bf16),
            pltpu.VMEM((count, width), bf16),
        ]
        + semaphores(3),
        compiler_params=remote_params(collective_id),
        name="product_to_owner",
    )(left, right)


def own_rows(block, tp_index, count):
    return lax.dynamic_slice_in_dim(block, tp_index * count, count, 0)


def per_device_dense(
    layer_input,
    attention_gain,
    attention_in,
    attention_bias,
    attention_out,
    feedforward_gain,
    shared_in,
    shared_down,
    shared_gate,
    router,
    expert_in,
    expert_down,
    routes,
    document_lengths,
    cotangent,
):
    bf16 = jnp.bfloat16
    f32 = jnp.float32
    both = (EP, TP)
    tok_count, model_width = layer_input.shape
    expert_count = router.shape[1]
    top_count = routes.shape[1]
    ep_size = lax.axis_size(EP)
    tp_size = lax.axis_size(TP)
    ep_index = lax.axis_index(EP)
    tp_index = lax.axis_index(TP)
    own_count = tok_count // tp_size
    all_count = tok_count * ep_size
    capacity = tp_size * (
        (5 * tok_count * top_count + 4 * expert_count * tp_size - 1) // (4 * expert_count * tp_size)
    )
    reach_back = min((WINDOW + tok_count - 2) // tok_count, ep_size - 1)
    local_experts = expert_in.shape[0]
    route_rows = jnp.concatenate(
        [routes.T, jnp.full((-top_count % 8, tok_count), -1, routes.dtype)]
    )
    positions = ep_index * tok_count + jnp.arange(tok_count, dtype=jnp.int32)
    key_count = (reach_back + 1) * tok_count
    key_positions = (ep_index - reach_back) * tok_count + jnp.arange(key_count, dtype=jnp.int32)
    query_doc, rope_pos, valid_mask = doc_table(document_lengths, positions)
    query_doc = query_doc[:, None]
    key_doc = doc_table(document_lengths, key_positions)[0][None, :]
    valid_rows = valid_mask.astype(f32)[:, None]
    cosine, sine = (part[:, 0] for part in rope_angles(rope_pos, HD))
    cosine = jnp.concatenate([cosine, cosine], axis=1)
    sine = jnp.concatenate([-sine, sine], axis=1)
    (
        in_blocks,
        out_full,
        all_routes,
        normed_attention,
        queries,
        keys_values,
        shared_shards,
    ) = open_attention(
        attention_in,
        attention_out,
        route_rows,
        layer_input,
        attention_gain,
        attention_bias,
        cosine,
        sine,
        shared_in,
        shared_down,
        0,
    )
    in_full = in_blocks.reshape(3, model_width, -1)
    shard_width = shared_in.shape[1]
    slice_hidden = shared_in.shape[2] // ep_size
    shared_slices = lax.all_to_all(shared_shards, EP, split_axis=0, concat_axis=0, tiled=True)
    heads_low, log_totals = attend(queries, keys_values, query_doc, key_doc, valid_rows)
    attention_sum = product_to_owner(heads_low[None], out_full[None], False, 2)
    input_rows = own_rows(layer_input, tp_index, own_count).astype(f32)
    residual = input_rows + attention_sum
    inverse_two, normed_two = rms_parts(residual)
    normed_ffn = normed_two * feedforward_gain
    normed_low = normed_ffn.astype(bf16)
    shared_scale = jax.nn.sigmoid(jnp.dot(normed_ffn, shared_gate, precision=HIGHEST))
    router_probs = jax.nn.softmax(jnp.dot(normed_ffn, router, precision=HIGHEST), axis=-1)
    routes_own = own_rows(routes, tp_index, own_count)
    expert_ids = jnp.arange(expert_count, dtype=jnp.int32)
    picked = jnp.any(routes_own[:, :, None] == expert_ids[None, None, :], axis=1)
    chosen = jnp.where(picked, router_probs, 0.0)
    chosen_total = jnp.sum(chosen, axis=1, keepdims=True)
    gates = chosen / chosen_total
    scale_count = -(-(expert_count + 1) // 8) * 8
    spare = jnp.zeros((scale_count - expert_count - 1, own_count), f32)
    scale_rows = jnp.concatenate([gates.T, shared_scale[None], spare])
    (
        all_rows,
        all_cotangent,
        all_scales,
        ffn_part,
        back_part,
        slot_rows,
        slot_cotangent,
        grad_pre,
        gated,
        grad_shared_pre,
        scaled_hidden,
        scalar_part,
    ) = gather_feed(
        normed_low,
        cotangent.reshape(tp_size, own_count, model_width),
        scale_rows,
        all_routes,
        jnp.swapaxes(expert_in, 2, 3).reshape(local_experts, -1, model_width),
        expert_down,
        shared_slices,
        capacity,
        3,
    )
    part_shape = (ep_size, tp_size, own_count, model_width)
    slot_count = ep_size * capacity
    fed = (
        slot_rows.reshape(local_experts, slot_count, model_width),
        slot_cotangent.reshape(local_experts, slot_count, model_width),
        grad_pre.reshape(2, local_experts, slot_count, -1),
        gated.reshape(local_experts, slot_count, -1),
        all_rows.reshape(all_count, model_width),
        all_cotangent.reshape(all_count, model_width),
        grad_shared_pre.reshape(2, all_count, slice_hidden),
        scaled_hidden.reshape(all_count, slice_hidden),
    )
    back_sum, ffn_sum, scalar_sum, grad_expert_in, grad_expert_down, shared_grads = scatter_rows(
        back_part.reshape(part_shape), ffn_part.reshape(part_shape), scalar_part, fed, 4
    )
    scalar_sum = scalar_sum.T
    grad_expert_in = jnp.swapaxes(grad_expert_in, 2, 3).astype(f32)
    grad_expert_down = grad_expert_down.astype(f32)
    layer_output = lax.all_gather((residual + ffn_sum).astype(bf16), TP, axis=0, tiled=True)
    shared_grads = lax.all_to_all(shared_grads, EP, split_axis=0, concat_axis=0, tiled=True)
    shared_grads = (
        jnp.swapaxes(shared_grads, 0, 1).reshape(3, -1, shard_width).astype(f32)
    )
    grad_shared_in = jnp.swapaxes(shared_grads[:2], 1, 2)
    grad_shared_down = shared_grads[2]

    grad_gates = scalar_sum[:, :expert_count]
    grad_probs = jnp.where(
        picked,
        (grad_gates - jnp.sum(grad_gates * gates, axis=1, keepdims=True)) / chosen_total,
        0.0,
    )
    grad_logits = router_probs * (
        grad_probs - jnp.sum(grad_probs * router_probs, axis=1, keepdims=True)
    )
    grad_router = jnp.einsum("td,te->de", normed_ffn, grad_logits, precision=HIGHEST)
    grad_scale_pre = scalar_sum[:, expert_count] * shared_scale * (1.0 - shared_scale)
    grad_shared_gate = jnp.dot(grad_scale_pre, normed_ffn, precision=HIGHEST)
    grad_normed = (
        back_sum
        + jnp.einsum("te,de->td", grad_logits, router, precision=HIGHEST)
        + grad_scale_pre[:, None] * shared_gate[None, :]
    )
    grad_mid_norm, grad_feedforward_gain = norm_back(
        grad_normed, feedforward_gain, inverse_two, normed_two
    )
    small = jnp.concatenate([grad_feedforward_gain[None], grad_shared_gate[None], grad_router.T])
    small = lax.psum(small, both)
    grad_residual = own_rows(cotangent, tp_index, own_count).astype(f32) + grad_mid_norm
    grad_attention, grad_raw = back_attention(
        grad_residual.astype(bf16),
        out_full,
        valid_rows,
        queries,
        keys_values,
        query_doc,
        key_doc,
        log_totals,
        cosine,
        sine,
        5,
    )
    grad_attention = grad_attention.reshape(tok_count, model_width)
    grad_attention_bias = jnp.sum(grad_raw.astype(f32), axis=1)
    grad_attention_in, grad_attention_out, tails, grad_input = finish(
        normed_attention,
        grad_raw,
        heads_low,
        grad_attention,
        in_full,
        attention_gain,
        own_rows(layer_input, tp_index, own_count),
        grad_residual,
        grad_attention_bias,
        7,
    )
    grad_attention_bias = lax.dynamic_index_in_dim(tails, tp_index, 0, keepdims=False)[:3]
    grad_attention_gain = jnp.sum(tails[:, 3:], axis=0)[: model_width // tails.shape[2]].reshape(-1)
    return (
        layer_output,
        grad_input.reshape(tok_count, model_width),
        grad_attention_gain,
        grad_attention_in,
        grad_attention_bias,
        grad_attention_out,
        small[0],
        grad_shared_in,
        grad_shared_down,
        small[1],
        small[2:].T,
        grad_expert_in,
        grad_expert_down,
    )


def per_device(*arguments):
    small_slice = lax.axis_size(EP) == RING and lax.axis_size(TP) == 4
    return (per_device_dense if small_slice else per_device_sparse)(*arguments)


def per_device_sparse(
    layer_input,
    attention_gain,
    attention_in,
    attention_bias,
    attention_out,
    feedforward_gain,
    shared_in,
    shared_down,
    shared_gate,
    router,
    expert_in,
    expert_down,
    routes,
    document_lengths,
    cotangent,
):
    bf16 = jnp.bfloat16
    f32 = jnp.float32
    tok_count = layer_input.shape[0]
    model_width = layer_input.shape[1]
    expert_count = router.shape[1]
    top_count = routes.shape[1]
    ep_size = lax.axis_size(EP)
    tp_size = lax.axis_size(TP)
    capacity = tp_size * (
        (5 * tok_count * top_count + 4 * expert_count * tp_size - 1) // (4 * expert_count * tp_size)
    )
    reach_back = min((WINDOW + tok_count - 2) // tok_count, ep_size - 1)
    head_dim = HD
    local_heads = attention_in.shape[2] // head_dim
    score_scale = 1.0 / math.sqrt(head_dim)
    in_full, out_full, shared_in_full, shared_down_full = (
        lax.all_gather(attention_in, EP, axis=1, tiled=True),
        lax.all_gather(attention_out, EP, axis=1, tiled=True),
        lax.all_gather(shared_in, EP, axis=1, tiled=True),
        lax.all_gather(shared_down, EP, axis=1, tiled=True),
    )
    ep_index = lax.axis_index(EP)
    positions = ep_index * tok_count + jnp.arange(tok_count, dtype=jnp.int32)
    key_count = (reach_back + 1) * tok_count
    key_positions = (ep_index - reach_back) * tok_count + jnp.arange(key_count, dtype=jnp.int32)
    query_doc, rope_pos, valid_mask = doc_table(document_lengths, positions)
    key_doc = doc_table(document_lengths, key_positions)[0]
    distance = positions[:, None] - key_positions[None, :]
    allowed = (query_doc[:, None] == key_doc[None, :]) & (distance >= 0) & (distance < WINDOW)
    valid_rows = valid_mask.astype(f32)[:, None]
    cosine, sine_part = rope_angles(rope_pos, head_dim)
    input_rows = layer_input.astype(f32)
    inverse_one, normed_one = rms_parts(input_rows)
    normed_attention = (normed_one * attention_gain).astype(bf16)
    raw_proj = (
        jnp.einsum("td,sde->ste", normed_attention, in_full, preferred_element_type=f32)
        + attention_bias[:, None, :]
    )
    queries = rotate(
        raw_proj[0].reshape(tok_count, local_heads, head_dim), cosine, sine_part, 1.0
    ).astype(bf16)
    keys_own = rotate(
        raw_proj[1].reshape(tok_count, local_heads, head_dim), cosine, sine_part, 1.0
    ).astype(bf16)
    values_own = raw_proj[2].reshape(tok_count, local_heads, head_dim).astype(bf16)
    key_value = jnp.stack([keys_own, values_own])
    earlier = []
    for hop_count in range(reach_back, 0, -1):
        earlier.append(shifted(key_value, EP, hop_count))
    all_kv = jnp.concatenate(earlier + [key_value], axis=1)
    all_keys = all_kv[0]
    all_values = all_kv[1]
    scores = jnp.einsum("qhe,khe->hqk", queries, all_keys, preferred_element_type=f32) * score_scale
    scores = jnp.where(allowed[None], scores, MASKED)
    row_max = jnp.max(scores, axis=-1, keepdims=True)
    exp_terms = jnp.exp(scores - row_max)
    row_total = jnp.sum(exp_terms, axis=-1, keepdims=True)
    log_total = row_max + jnp.log(row_total)
    weights = (exp_terms / row_total).astype(bf16)
    heads_out = jnp.einsum("hqk,khe->qhe", weights, all_values, preferred_element_type=f32).reshape(
        tok_count, -1
    )
    heads_low = (heads_out * valid_rows).astype(bf16)
    attention_sum = tensor_total(jnp.dot(heads_low, out_full, preferred_element_type=f32))
    residual = input_rows + attention_sum
    inverse_two, normed_two = rms_parts(residual)
    normed_ffn = normed_two * feedforward_gain
    normed_low = normed_ffn.astype(bf16)
    shared_pre = jnp.einsum("td,sdf->stf", normed_low, shared_in_full, preferred_element_type=f32)
    shared_silu, shared_slope = silu_parts(shared_pre[0])
    shared_hidden = (shared_silu * shared_pre[1]).astype(bf16)
    shared_out = tensor_total(jnp.dot(shared_hidden, shared_down_full, preferred_element_type=f32))
    shared_scale = jax.nn.sigmoid(jnp.dot(normed_ffn, shared_gate, precision=HIGHEST))
    router_probs = jax.nn.softmax(jnp.dot(normed_ffn, router, precision=HIGHEST), axis=-1)
    chosen = jnp.take_along_axis(router_probs, routes, axis=1)
    chosen_total = jnp.sum(chosen, axis=1, keepdims=True)
    gate_values = chosen / chosen_total
    assign_count = tok_count * top_count
    flat_routes = routes.reshape(-1)
    expert_ids = jnp.arange(expert_count, dtype=jnp.int32)
    one_hot = (flat_routes[:, None] == expert_ids[None, :]).astype(jnp.int32)
    arrival_rank = jnp.sum((jnp.cumsum(one_hot, axis=0) - one_hot) * one_hot, axis=1)
    slot_count = expert_count * capacity
    slot_index = jnp.where(
        arrival_rank < capacity, flat_routes * capacity + arrival_rank, slot_count
    )
    slot_assign = (
        jnp.full((slot_count + 1,), assign_count, jnp.int32)
        .at[slot_index]
        .set(jnp.arange(assign_count, dtype=jnp.int32))[:slot_count]
    )
    slot_token = slot_assign // top_count
    padded_rows = jnp.concatenate([normed_low, jnp.zeros((1, model_width), bf16)])
    send_rows = padded_rows[slot_token].reshape(expert_count, capacity, model_width)

    def expert_trip(outgoing, work):
        row_block = lax.all_to_all(outgoing, EP, split_axis=0, concat_axis=1, tiled=True)
        partial_rows, extras = work(row_block)
        share_rows = lax.psum_scatter(partial_rows, TP, scatter_dimension=1, tiled=True).astype(
            bf16
        )
        whole_rows = lax.all_gather(share_rows, TP, axis=1, tiled=True)
        return (lax.all_to_all(whole_rows, EP, split_axis=1, concat_axis=0, tiled=True), extras)

    def expert_forward(row_block):
        pre_acts = jnp.einsum("erd,esdf->serf", row_block, expert_in, preferred_element_type=f32)
        gate_silu, gate_slope = silu_parts(pre_acts[0])
        hidden = (gate_silu * pre_acts[1]).astype(bf16)
        partial_rows = jnp.einsum("erf,efd->erd", hidden, expert_down, preferred_element_type=f32)
        return (partial_rows, (row_block, pre_acts, hidden, gate_silu, gate_slope))

    returned_rows, kept_state = expert_trip(send_rows, expert_forward)
    expert_rows, expert_pre, expert_hidden, expert_silu, expert_slope = kept_state
    padded_back = jnp.concatenate(
        [returned_rows.reshape(slot_count, model_width), jnp.zeros((1, model_width), bf16)]
    )
    picked = padded_back[slot_index].reshape(tok_count, top_count, model_width).astype(f32)
    moe_sum = jnp.sum(gate_values[:, :, None] * picked, axis=1)
    layer_output = (residual + shared_scale[:, None] * shared_out + moe_sum).astype(bf16)
    grad_rows = cotangent.astype(f32)
    padded_grad = jnp.concatenate([grad_rows, jnp.zeros((1, model_width), f32)])
    padded_gates = jnp.concatenate([gate_values.reshape(-1), jnp.zeros((1,), f32)])
    grad_send = (padded_gates[slot_assign][:, None] * padded_grad[slot_token]).astype(bf16)
    grad_send = grad_send.reshape(expert_count, capacity, model_width)

    def expert_backward(grad_block):
        grad_down = jnp.einsum(
            "erf,erd->efd", expert_hidden, grad_block, preferred_element_type=f32
        )
        grad_hidden = jnp.einsum(
            "erd,efd->erf", grad_block, expert_down, preferred_element_type=f32
        )
        grad_pre = jnp.stack(
            [grad_hidden * expert_pre[1] * expert_slope, grad_hidden * expert_silu]
        ).astype(bf16)
        grad_weights_in = jnp.einsum(
            "erd,serf->esdf", expert_rows, grad_pre, preferred_element_type=f32
        )
        grad_back_rows = jnp.einsum(
            "serf,esdf->erd", grad_pre, expert_in, preferred_element_type=f32
        )
        return (grad_back_rows, (grad_weights_in, grad_down))

    grad_returned, expert_grads = expert_trip(grad_send, expert_backward)
    grad_expert_in, grad_expert_down = expert_grads
    grad_gate_values = jnp.sum(picked * grad_rows[:, None, :], axis=2)
    grad_chosen = (
        grad_gate_values - jnp.sum(grad_gate_values * gate_values, axis=1, keepdims=True)
    ) / chosen_total
    grad_probs = jnp.sum(
        jnp.where(routes[:, :, None] == expert_ids[None, None, :], grad_chosen[:, :, None], 0.0),
        axis=1,
    )
    grad_logits = router_probs * (
        grad_probs - jnp.sum(grad_probs * router_probs, axis=1, keepdims=True)
    )
    grad_router = jnp.einsum("td,te->de", normed_ffn, grad_logits, precision=HIGHEST)
    grad_shared_out = (shared_scale[:, None] * grad_rows).astype(bf16)
    grad_shared_down = jnp.einsum(
        "tf,td->fd", shared_hidden, grad_shared_out, preferred_element_type=f32
    )
    grad_shared_hidden = jnp.einsum(
        "td,fd->tf", grad_shared_out, shared_down_full, preferred_element_type=f32
    )
    grad_shared_pre = jnp.stack(
        [grad_shared_hidden * shared_pre[1] * shared_slope, grad_shared_hidden * shared_silu]
    ).astype(bf16)
    grad_shared_in = jnp.einsum(
        "td,stf->sdf", normed_low, grad_shared_pre, preferred_element_type=f32
    )
    shared_back = jnp.einsum(
        "stf,sdf->td", grad_shared_pre, shared_in_full, preferred_element_type=f32
    )
    grad_scale_pre = jnp.sum(grad_rows * shared_out, axis=1) * shared_scale * (1.0 - shared_scale)
    grad_shared_gate = jnp.dot(grad_scale_pre, normed_ffn, precision=HIGHEST)
    padded_return = jnp.concatenate(
        [grad_returned.reshape(slot_count, model_width), jnp.zeros((1, model_width), bf16)]
    )
    moe_back = jnp.sum(
        padded_return[slot_index].reshape(tok_count, top_count, model_width).astype(f32), axis=1
    )
    grad_normed = (
        tensor_total(shared_back)
        + moe_back
        + jnp.einsum("te,de->td", grad_logits, router, precision=HIGHEST)
        + grad_scale_pre[:, None] * shared_gate[None, :]
    )
    grad_mid_norm, grad_feedforward_gain = norm_back(
        grad_normed, feedforward_gain, inverse_two, normed_two
    )
    grad_residual = grad_rows + grad_mid_norm
    grad_attention = grad_residual.astype(bf16)
    grad_attention_out = jnp.einsum(
        "tf,td->fd", heads_low, grad_attention, preferred_element_type=f32
    )
    grad_heads = jnp.einsum(
        "td,fd->tf", grad_attention, out_full, preferred_element_type=f32
    ).astype(bf16)
    grad_heads = (grad_heads * valid_rows.astype(bf16)).reshape(tok_count, local_heads, head_dim)
    scores_again = (
        jnp.einsum("qhe,khe->hqk", queries, all_keys, preferred_element_type=f32) * score_scale
    )
    scores_again = jnp.where(allowed[None], scores_again, MASKED)
    softmax_out = jnp.exp(scores_again - log_total)
    weights_again = softmax_out.astype(bf16)
    grad_weights = jnp.einsum("qhe,khe->hqk", grad_heads, all_values, preferred_element_type=f32)
    grad_scores = (
        softmax_out * (grad_weights - jnp.sum(softmax_out * grad_weights, axis=-1, keepdims=True))
    ).astype(bf16)
    grad_queries = (
        jnp.einsum("hqk,khe->qhe", grad_scores, all_keys, preferred_element_type=f32) * score_scale
    )
    grad_keys = (
        jnp.einsum("hqk,qhe->khe", grad_scores, queries, preferred_element_type=f32) * score_scale
    )
    grad_values = jnp.einsum("hqk,qhe->khe", weights_again, grad_heads, preferred_element_type=f32)
    grad_kv = jnp.stack([grad_keys, grad_values])
    own_part = grad_kv[:, reach_back * tok_count :]
    for hop_count in range(1, reach_back + 1):
        segment_start = (reach_back - hop_count) * tok_count
        segment = grad_kv[:, segment_start : segment_start + tok_count]
        own_part = own_part + shifted(segment, EP, -hop_count)
    grad_raw = (
        jnp.stack(
            [
                rotate(grad_queries, cosine, sine_part, -1.0),
                rotate(own_part[0], cosine, sine_part, -1.0),
                own_part[1],
            ]
        )
        .reshape(3, tok_count, -1)
        .astype(bf16)
    )
    grad_attention_bias = jnp.sum(grad_raw.astype(f32), axis=1)
    grad_attention_in = jnp.einsum(
        "td,ste->sde", normed_attention, grad_raw, preferred_element_type=f32
    )
    grad_normed_attention = tensor_total(
        jnp.einsum("ste,sde->td", grad_raw, in_full, preferred_element_type=f32)
    )
    grad_in_norm, grad_attention_gain = norm_back(
        grad_normed_attention, attention_gain, inverse_one, normed_one
    )
    grad_input = (grad_residual + grad_in_norm).astype(bf16)
    grad_attention_in, grad_attention_out, grad_shared_in, grad_shared_down = (
        lax.psum_scatter(
            grad_attention_in.astype(jnp.bfloat16), EP, scatter_dimension=1, tiled=True
        ).astype(jnp.float32),
        lax.psum_scatter(
            grad_attention_out.astype(jnp.bfloat16), EP, scatter_dimension=1, tiled=True
        ).astype(jnp.float32),
        lax.psum_scatter(
            grad_shared_in.astype(jnp.bfloat16), EP, scatter_dimension=1, tiled=True
        ).astype(jnp.float32),
        lax.psum_scatter(
            grad_shared_down.astype(jnp.bfloat16), EP, scatter_dimension=1, tiled=True
        ).astype(jnp.float32),
    )
    (
        grad_attention_gain,
        grad_attention_bias,
        grad_feedforward_gain,
        grad_shared_gate,
        grad_router,
    ) = (
        lax.psum(grad_attention_gain.astype(jnp.bfloat16), EP).astype(jnp.float32),
        lax.psum(grad_attention_bias.astype(jnp.bfloat16), EP).astype(jnp.float32),
        lax.psum(grad_feedforward_gain.astype(jnp.bfloat16), EP).astype(jnp.float32),
        lax.psum(grad_shared_gate.astype(jnp.bfloat16), EP).astype(jnp.float32),
        lax.psum(grad_router.astype(jnp.bfloat16), EP).astype(jnp.float32),
    )
    return (
        layer_output,
        grad_input,
        grad_attention_gain,
        grad_attention_in,
        grad_attention_bias,
        grad_attention_out,
        grad_feedforward_gain,
        grad_shared_in,
        grad_shared_down,
        grad_shared_gate,
        grad_router,
        grad_expert_in,
        grad_expert_down,
    )


def solution(mesh):
    return jax.shard_map(
        per_device,
        mesh=mesh,
        in_specs=(
            P(EP, None),
            P(),
            P(None, EP, TP),
            P(None, TP),
            P(TP, EP),
            P(),
            P(None, EP, TP),
            P(TP, EP),
            P(),
            P(),
            P(EP, None, None, TP),
            P(EP, TP, None),
            P(EP, None),
            P(),
            P(EP, None),
        ),
        out_specs=(
            P(EP, None),
            P(EP, None),
            P(),
            P(None, EP, TP),
            P(None, TP),
            P(TP, EP),
            P(),
            P(None, EP, TP),
            P(TP, EP),
            P(),
            P(),
            P(EP, None, None, TP),
            P(EP, TP, None),
        ),
        check_vma=False,
    )
```

```python
import functools
import math

import jax
import jax.numpy as jnp
from jax import lax
from jax.experimental import pallas as pl
from jax.experimental.pallas import tpu as pltpu
from jax.sharding import PartitionSpec as P

EP, TP = "ep", "tp"
HD = 128
WINDOW = 1024


HIGHEST = lax.Precision.HIGHEST
EPSILON = 1e-06
ROPE_BASE = 1000000.0
MASKED = -1000000000.0


def shifted(value, axis, steps):
    count = lax.axis_size(axis)
    leading, last = (max(0, -steps), min(count, count - steps))
    return lax.ppermute(value, axis, [(source, source + steps) for source in range(leading, last)])


def tensor_total(partial_sum):
    return lax.psum(partial_sum, TP)


def rms_parts(values):
    inverse = lax.rsqrt(jnp.mean(values * values, axis=-1, keepdims=True) + EPSILON)
    return (inverse, values * inverse)


def norm_back(grad_rows, gain_vec, inverse, normed):
    scaled = grad_rows * gain_vec
    grad_in = inverse * (scaled - normed * jnp.mean(scaled * normed, axis=-1, keepdims=True))
    return (grad_in, jnp.sum(grad_rows * normed, axis=0))


def doc_table(document_lengths, positions):
    doc_ends = jnp.cumsum(document_lengths)
    starts_all = jnp.concatenate([doc_ends - document_lengths, doc_ends[-1:]])
    doc_ids = jnp.sum((positions[:, None] >= doc_ends[None, :]).astype(jnp.int32), axis=1)
    matches = (
        doc_ids[:, None] == jnp.arange(document_lengths.shape[0] + 1, dtype=jnp.int32)[None, :]
    )
    doc_begin = jnp.sum(jnp.where(matches, starts_all[None, :], 0), axis=1)
    rope_pos = positions - doc_begin
    valid_mask = positions < doc_ends[-1]
    doc_ids = jnp.where(positions < 0, -1, doc_ids)
    return (doc_ids, rope_pos, valid_mask)


def rope_angles(rope_pos, head_dim):
    half_width = head_dim // 2
    freqs = jnp.power(ROPE_BASE, -2.0 * jnp.arange(half_width, dtype=jnp.float32) / head_dim)
    angles = rope_pos.astype(jnp.float32)[:, None] * freqs[None, :]
    return (jnp.cos(angles)[:, None, :], jnp.sin(angles)[:, None, :])


def rotate(values, cosine, sine_part, turn_sign):
    half_width = values.shape[-1] // 2
    first_part = values[..., :half_width]
    second_part = values[..., half_width:]
    return jnp.concatenate(
        [
            first_part * cosine - turn_sign * second_part * sine_part,
            second_part * cosine + turn_sign * first_part * sine_part,
        ],
        axis=-1,
    )


def silu_parts(gate_pre):
    sig_gate = jax.nn.sigmoid(gate_pre)
    return (gate_pre * sig_gate, sig_gate * (1.0 + gate_pre * (1.0 - sig_gate)))


NN = (((1,), (0,)), ((), ()))
NT = (((1,), (1,)), ((), ()))
TN = (((0,), (0,)), ((), ()))


def product(left, right, dims=NN):
    return lax.dot_general(left, right, dims, preferred_element_type=jnp.float32)


def turned(values, cosine, sine):
    half = values.shape[1] // 2
    swapped = jnp.concatenate([values[:, half:], values[:, :half]], axis=1)
    return values * cosine + swapped * sine


def masked_scores(queries, keys, query_doc, key_doc):
    tokens, count = queries.shape[0], keys.shape[0]
    scores = product(queries, keys, NT) * (1.0 / math.sqrt(HD))
    ahead = lax.broadcasted_iota(jnp.int32, (tokens, count), 0) + (count - tokens)
    distance = ahead - lax.broadcasted_iota(jnp.int32, (tokens, count), 1)
    allowed = (query_doc == key_doc) & (distance >= 0) & (distance < WINDOW)
    return jnp.where(allowed, scores, MASKED)


def attend_kernel(queries, keys, values, query_doc, key_doc, valid, heads, log_totals):
    count = keys.shape[1] * keys.shape[2]
    keys, values = keys[0].reshape(count, HD), values[0].reshape(count, HD)
    scores = masked_scores(queries[...], keys, query_doc[...], key_doc[...])
    row_max = jnp.max(scores, axis=1, keepdims=True)
    terms = jnp.exp(scores - row_max)
    total = jnp.sum(terms, axis=1, keepdims=True)
    weights = (terms / total).astype(jnp.bfloat16)
    heads[...] = (product(weights, values) * valid[...]).astype(jnp.bfloat16)
    log_totals[0] = row_max + jnp.log(total)


def attention_specs(tokens, blocks):
    def column(*dims):
        return pl.BlockSpec(dims, lambda h: (0,) * len(dims))

    head = pl.BlockSpec((tokens, HD), lambda h: (0, h))
    keys = pl.BlockSpec((1, blocks, tokens, HD), lambda h: (0, 0, 0, h))
    values = pl.BlockSpec((1, blocks, tokens, HD), lambda h: (1, 0, 0, h))
    logs = pl.BlockSpec((1, tokens, 1), lambda h: (h, 0, 0))
    return head, keys, values, column(tokens, 1), column(1, blocks * tokens), logs


def attend(queries, keys_values, query_doc, key_doc, valid):
    tokens, columns = queries.shape
    blocks = keys_values.shape[1]
    head, keys, values, column, row, logs = attention_specs(tokens, blocks)
    shape = jax.ShapeDtypeStruct
    return pl.pallas_call(
        attend_kernel,
        grid=(columns // HD,),
        in_specs=[head, keys, values, column, row, column],
        out_specs=(head, logs),
        out_shape=(
            shape((tokens, columns), jnp.bfloat16),
            shape((columns // HD, tokens, 1), jnp.float32),
        ),
        compiler_params=pltpu.CompilerParams(vmem_limit_bytes=40 * 2**20),
        name="attend",
    )(queries, keys_values, keys_values, query_doc, key_doc, valid)


RING = 8
NO_SLOT = 1 << 20
RIGHT, LEFT, OVER_X, OVER_CORE, OVER_FAR, LOCAL, SCALARS = range(7)
MESH_ID = pl.DeviceIdType.MESH


def ring_place(ep):
    z, y = ep // 2, ep % 2
    return z + y * (7 - 2 * z)


def ring_member(place):
    upper = place // 4
    return 2 * place + upper * (15 - 4 * place)


class Peers:
    def __init__(self):
        self.ep, self.tp = lax.axis_index(EP), lax.axis_index(TP)
        self.x, self.core = self.tp // 2, self.tp % 2
        self.z, self.y = self.ep // 2, self.ep % 2
        self.place = ring_place(self.ep)
        self.right = (self.block(1), self.tp)
        self.left = (self.block(RING - 1), self.tp)
        self.quarter = self.tp
        self.x_quarter = (1 - self.x) * 2 + self.core
        self.core_quarter = self.x * 2 + 1 - self.core
        self.far_quarter = (1 - self.x) * 2 + 1 - self.core
        self.x_peer = (self.ep, self.x_quarter)
        self.core_peer = (self.ep, self.core_quarter)
        self.far_peer = (self.ep, self.far_quarter)
        self.y_peer = (self.z * 2 + 1 - self.y, self.tp)

    def block(self, step):
        return ring_member((self.place + step + RING) % RING)


def greet(peers):
    barrier = pltpu.get_barrier_semaphore()
    for peer in peers:
        pl.semaphore_signal(barrier, inc=1, device_id=peer, device_id_type=MESH_ID)
    pl.semaphore_wait(barrier, len(peers))


class Copies:
    def __init__(self, send_sems, recv_sems):
        self.send_sems, self.recv_sems = send_sems, recv_sems
        self.count = 0
        self.sent = []
        self.landing = {}

    def describe(self, source, target, peer, index):
        return pltpu.make_async_remote_copy(
            src_ref=source,
            dst_ref=target,
            send_sem=self.send_sems.at[index],
            recv_sem=self.recv_sems.at[index],
            device_id=peer,
            device_id_type=MESH_ID,
        )

    def send(self, key, source, target, landing, peer):
        index = self.count
        self.count += 1
        copy = self.describe(source, target, peer, index)
        copy.start()
        self.sent.append(copy)
        self.landing[key] = self.describe(landing, landing, peer, index).wait_recv

    def local(self, key, source, target):
        index = self.count
        self.count += 1
        copy = pltpu.make_async_copy(source, target, self.send_sems.at[index])
        copy.start()
        self.landing[key] = copy.wait

    def arrive(self, *key):
        self.landing.pop(key)()

    def finish(self):
        for wait in self.landing.values():
            wait()
        for copy in self.sent:
            copy.wait_send()


def remote_params(collective_id, vmem=48):
    return pltpu.CompilerParams(
        collective_id=collective_id, has_side_effects=True, vmem_limit_bytes=vmem * 2**20
    )


def semaphores(count):
    return [pltpu.SemaphoreType.DMA((count,))] * 2


IN_PLACE = pl.BlockSpec(memory_space=pl.ANY)
IN_VMEM = pl.BlockSpec(memory_space=pltpu.VMEM)


class LateCopies(Copies):
    def send(self, key, source, target, landing, peer):
        index = self.count
        self.count += 1
        self.describe(source(), target(), peer, index).start()
        self.sent.append(lambda: self.describe(source(), target(), peer, index).wait_send())
        self.landing[key] = lambda: self.describe(landing(), landing(), peer, index).wait_recv()

    def local(self, key, source, target):
        index = self.count
        self.count += 1

        def copy():
            return pltpu.make_async_copy(source(), target(), self.send_sems.at[index])

        copy().start()
        self.landing[key] = lambda: copy().wait()

    def finish(self):
        for wait in list(self.landing.values()) + self.sent:
            wait()


def feed_block(
    rank_row, rank_column, gate_rows, scale, token_rows, token_cotangent,
    expert_in, expert_down, shared, staged, between, out_terms, back_terms, scalar_out,
):
    (
        out_part, back_part, slot_rows, slot_cotangent, grad_pre, gated, grad_shared_pre, scaled,
    ) = staged
    bf16, f32 = jnp.bfloat16, jnp.float32
    experts, slots, _ = slot_rows.shape
    tokens = token_rows.shape[0]
    hidden_count = gated.shape[2]
    all_slots = experts * slots
    silu, slope = silu_parts(product(token_rows, shared[0], NT))
    up = product(token_rows, shared[1], NT)
    hidden = (silu * up).astype(bf16).astype(f32)
    scaled_hidden = (scale * hidden).astype(bf16)
    back = product(token_cotangent, shared[2], NT)
    scalar_out(None, jnp.sum(jnp.swapaxes(hidden * back, 0, 1), axis=0, keepdims=True))
    back = scale * back
    gate_grad = (back * up * slope).astype(bf16)
    up_grad = (back * silu).astype(bf16)
    between()
    scaled[...] = scaled_hidden
    grad_shared_pre[0] = gate_grad
    grad_shared_pre[1] = up_grad
    order = lax.broadcasted_iota(jnp.int32, (all_slots, tokens), 0)
    spread_order = lax.broadcasted_iota(jnp.int32, (tokens, all_slots), 1)
    hits, spread = None, None
    for expert in range(experts):
        row_hits = order == rank_row[expert : expert + 1, :] + expert * slots
        column_hits = spread_order == rank_column[:, expert : expert + 1] + expert * slots
        hits = row_hits if hits is None else hits | row_hits
        spread = column_hits if spread is None else spread | column_hits
    place = hits.astype(bf16)
    taken = product(place, token_rows).astype(bf16)
    taken_cotangent = product(place, token_cotangent).astype(bf16)
    for ref, values in ((slot_rows, taken), (slot_cotangent, taken_cotangent)):
        for expert in range(experts):
            ref[expert] = values[expert * slots : (expert + 1) * slots]
    for expert in range(experts):
        mine = slice(expert * slots, (expert + 1) * slots)
        gate = jnp.sum(
            jnp.where(hits[mine], gate_rows[expert : expert + 1], 0.0), axis=1, keepdims=True
        )
        pre = product(taken[mine], expert_in[expert], NT)
        silu, slope = silu_parts(pre[:, :hidden_count])
        up = pre[:, hidden_count:]
        hidden = (silu * up).astype(bf16).astype(f32)
        gated_hidden = (gate * hidden).astype(bf16)
        gated[expert] = gated_hidden
        back = product(taken_cotangent[mine], expert_down[expert], NT)
        slot_grad = jnp.sum(hidden * back, axis=1, keepdims=True)
        scalar_out(
            expert, jnp.sum(jnp.where(hits[mine], slot_grad, 0.0), axis=0, keepdims=True)
        )
        back = gate * back
        gate_grad_e = (back * up * slope).astype(bf16)
        up_grad_e = (back * silu).astype(bf16)
        grad_pre[0, expert] = gate_grad_e
        grad_pre[1, expert] = up_grad_e
        out_terms[mine, :] = product(gated_hidden, expert_down[expert]).astype(bf16)
        both_grads = jnp.concatenate([gate_grad_e, up_grad_e], axis=1)
        back_terms[mine, :] = product(both_grads, expert_in[expert]).astype(bf16)
    spread = spread.astype(bf16)
    out_part[...] = product(
        jnp.concatenate([spread, scaled_hidden], axis=1), out_terms[...]
    ).astype(bf16)
    back_part[...] = product(
        jnp.concatenate([spread, gate_grad, up_grad], axis=1), back_terms[...]
    ).astype(bf16)


def gather_feed_kernel(
    rows, cotangent, scales, routes, expert_in, expert_down, shared_blocks,
    all_rows, all_cotangent, all_scales,
    out_part, back_part, slot_rows, slot_cotangent, grad_pre, gated, grad_shared_pre, scaled,
    scalars,
    rank_row, rank_column, shared, out_terms, back_terms, held_rows, held_cotangent,
    stage_out, stage_back, stage_rows, stage_cotangent, stage_pre, stage_gated, stage_shared,
    stage_scaled,
    load_sems, store_sems, send_sems, recv_sems,
):
    me = Peers()
    copies = LateCopies(send_sems, recv_sems)
    count = rows.shape[0]
    half, part = count // 2, count // 4
    first_rows = (half, half - count // 8)
    q, qx, qc, qd = me.quarter, me.x_quarter, me.core_quarter, me.far_quarter
    blocks = {step: me.block(step) for step in range(-4, 5)}
    low = [pl.ds(0, rows_low) for rows_low in first_rows]
    high = [pl.ds(rows_low, count - rows_low) for rows_low in first_rows]
    whole = pl.ds(0, count)
    own, other, scale = range(3)
    full = (all_rows, all_cotangent)
    sides = ((RIGHT, me.right, -1, 0), (LEFT, me.left, 1, 1))
    greet([me.right, me.left, me.x_peer, me.core_peer, me.far_peer])

    def push(key, kind, step, quarter, which, peer, landing_step, landing_quarter, source=None):
        def cell():
            return full[kind].at[blocks[step], quarter, which]

        def landing():
            return full[kind].at[blocks[landing_step], landing_quarter, which]

        copies.send((kind,) + key, source or cell, cell, landing, peer)

    push((OVER_X, other, 0), 0, 0, q, low[0], me.x_peer, 0, qx, lambda: rows.at[low[0]])
    for side, peer, sign, keep in sides:
        push((side, own, 1), 1, 0, q, whole, peer, sign, q, lambda: cotangent.at[q])
        push((side, other, 1), 1, 0, qx, low[1], peer, sign, qx, lambda: cotangent.at[qx, low[1]])
    push((OVER_X, own, 0), 0, 0, q, high[0], me.x_peer, 0, qx, lambda: rows.at[high[0]])
    push((OVER_CORE, own, 0), 0, 0, q, whole, me.core_peer, 0, qc, lambda: rows)
    for side, peer, sign, keep in sides:
        push((side, own, 1), 0, 0, q, whole, peer, sign, q, lambda: rows)
    copies.local((LOCAL, 0), lambda: rows, lambda: all_rows.at[blocks[0], q])
    copies.local((LOCAL, 1), lambda: cotangent, lambda: all_cotangent.at[blocks[0]])

    def scales_of(quarter):
        return lambda: all_scales.at[blocks[0], quarter]

    for way, peer, quarter in (
        (OVER_X, me.x_peer, qx),
        (OVER_CORE, me.core_peer, qc),
        (OVER_FAR, me.far_peer, qd),
    ):
        copies.send((way, scale, 0), lambda: scales, scales_of(q), scales_of(quarter), peer)
    copies.local((LOCAL, scale), lambda: scales, scales_of(q))
    experts, _, width = expert_in.shape
    all_slots = experts * slot_rows.shape[2]
    shared_count, across = shared.shape[1], shared_blocks.shape[3]
    for block in range(RING):
        shared[:, :, block * across : (block + 1) * across] = shared_blocks[block]
    out_terms[all_slots:, :] = shared[2]
    back_terms[all_slots : all_slots + shared_count, :] = shared[0]
    back_terms[all_slots + shared_count :, :] = shared[1]
    first_expert, scale_at = me.ep * experts, me_scale_row(experts)
    tokens = routes.shape[2]
    taken = []
    for block in range(RING):
        for expert in range(experts):
            chosen = routes[block] == first_expert + expert
            taken.append(jnp.max(chosen.astype(jnp.float32), axis=0, keepdims=True))
    taken = jnp.concatenate(taken, axis=0)
    down = lax.broadcasted_iota(jnp.int32, (tokens, tokens), 0)
    right = lax.broadcasted_iota(jnp.int32, (tokens, tokens), 1)
    rank = product(taken.astype(jnp.bfloat16), (right < down).astype(jnp.bfloat16), NT)
    kept = (taken > 0.0) & (rank < slot_rows.shape[2])
    rank = jnp.where(kept, rank, float(NO_SLOT))
    column = product((right == down).astype(jnp.bfloat16), rank.astype(jnp.bfloat16), NT)
    for block in range(RING):
        mine = slice(block * experts, (block + 1) * experts)
        rank_row[block] = rank[mine].astype(jnp.int32)
        rank_column[block] = column[:, mine].astype(jnp.int32)
    scalars[...] = jnp.zeros_like(scalars)
    copies.arrive(0, OVER_X, other, 0)
    for side, peer, sign, keep in sides:
        push((side, other, 1), 0, 0, qx, low[0], peer, sign, qx)
    for way in (OVER_X, OVER_CORE, OVER_FAR):
        copies.arrive(way, scale, 0)
    copies.arrive(LOCAL, scale)

    def push_scales(step, side, peer, sign):
        def cell():
            return all_scales.at[blocks[step]]

        copies.send(
            (side, scale, abs(step) + 1), cell, cell, lambda: all_scales.at[blocks[step + sign]], peer
        )

    for side, peer, sign, keep in sides:
        push_scales(0, side, peer, sign)
    copies.arrive(0, OVER_X, own, 0)
    push((OVER_CORE, other, 0), 0, 0, qx, whole, me.core_peer, 0, qd)

    def hop_in(kind, hop):
        for side, peer, sign, keep in sides:
            step = sign * hop
            if hop < 4:
                copies.arrive(kind, side, own, hop)
                which = whole if hop < 3 else pl.ds(keep * half, half)
                push((side, own, hop + 1), kind, step, q, which, peer, step + sign, q)
                push((OVER_X, own, step), kind, step, q, high[kind], me.x_peer, step, qx)
                push((OVER_CORE, own, step), kind, step, q, whole, me.core_peer, step, qc)
                copies.arrive(kind, side, other, hop)
                last = pl.ds(part, first_rows[kind] - part) if keep else pl.ds(0, part)
                which = low[kind] if hop < 3 else last
                push((side, other, hop + 1), kind, step, qx, which, peer, step + sign, qx)
                push((OVER_CORE, other, step), kind, step, qx, low[kind], me.core_peer, step, qd)
        if hop == 4:
            copies.arrive(kind, LEFT, own, 4)
            copies.arrive(kind, RIGHT, own, 4)
            push((OVER_X, own, 4), kind, 4, q, high[kind], me.x_peer, 4, qx)
            push((OVER_CORE, own, 4), kind, 4, q, whole, me.core_peer, 4, qc)
            copies.arrive(kind, LEFT, other, 4)
            copies.arrive(kind, RIGHT, other, 4)
            push((OVER_CORE, other, 4), kind, 4, qx, low[kind], me.core_peer, 4, qd)

    def over_x(kind, steps):
        for step in steps:
            copies.arrive(kind, OVER_X, own, step)
            push((OVER_CORE, scale, step), kind, step, qx, high[kind], me.core_peer, step, qd)

    def scales_in(hop):
        for side, peer, sign, keep in sides:
            if hop < 4 or side == RIGHT:
                copies.arrive(side, scale, hop)
                if hop < 3 or (hop == 3 and side == RIGHT):
                    push_scales(sign * hop, side, peer, sign)

    def load(slot, step):
        pairs = ((all_rows, held_rows), (all_cotangent, held_cotangent))
        return [
            pltpu.make_async_copy(source.at[blocks[step]], held.at[slot], load_sems.at[slot, kind])
            for kind, (source, held) in enumerate(pairs)
        ]

    def complete(steps, slots):
        for step in steps:
            for kind in range(2):
                if step != 0:
                    for piece in (own, other, scale):
                        copies.arrive(kind, OVER_CORE, piece, step)
        moves = [load(slot, step) for slot, step in zip(slots, steps)]
        for move in moves[0] + moves[-1] if len(moves) > 1 else moves[0]:
            move.start()
        for move in moves[0]:
            move.wait()

    staged = (
        stage_out, stage_back, stage_rows, stage_cotangent, stage_pre, stage_gated, stage_shared,
        stage_scaled,
    )

    def stores(block):
        targets = (
            out_part.at[block], back_part.at[block], slot_rows.at[:, block],
            slot_cotangent.at[:, block], grad_pre.at[:, :, block], gated.at[:, block],
            grad_shared_pre.at[:, block], scaled.at[block],
        )
        return [
            pltpu.make_async_copy(stage, target, store_sems.at[index])
            for index, (stage, target) in enumerate(zip(staged, targets))
        ]


    copies.arrive(LOCAL, 0)
    copies.arrive(LOCAL, 1)
    for piece in (own, other):
        copies.arrive(0, OVER_CORE, piece, 0)
    complete((0,), (0,))

    def turn(index, carry):
        far = (index + 1) // 2
        step = far * (1 - 2 * (index % 2)) + (index // 7) * 8
        block = ring_member((me.place + step + RING) % RING)
        slot = index % 2

        def between():
            for hop in (1, 2, 3, 4):

                @pl.when(index == max(0, 2 * hop - 3))
                def _():
                    hop_in(1, hop)

            @pl.when(index > 0)
            def _():
                for move in stores(0):
                    move.wait()

        def scalar_out(expert, values):
            row = scale_at if expert is None else first_expert + expert
            for quarter in range(4):
                part = values[:, quarter * count : (quarter + 1) * count]
                scalars[block, quarter, pl.ds(row, 1), :] = part

        rows_here = held_rows[slot].reshape(4 * count, width)
        cotangent_here = held_cotangent[slot].reshape(4 * count, width)
        quarters = [all_scales[block, quarter] for quarter in range(4)]
        columns = jnp.concatenate([jnp.swapaxes(values, 0, 1) for values in quarters], axis=0)
        gate_rows = [
            jnp.concatenate(
                [all_scales[block, quarter, pl.ds(first_expert + e, 1), :] for quarter in range(4)],
                axis=1,
            )
            for e in range(experts)
        ]
        feed_block(
            rank_row[block],
            rank_column[block],
            jnp.concatenate(gate_rows, axis=0),
            columns[:, scale_at : scale_at + 1],
            rows_here,
            cotangent_here,
            expert_in,
            expert_down,
            shared,
            staged,
            between,
            out_terms,
            back_terms,
            scalar_out,
        )
        for move in stores(block):
            move.start()

        for hop in (1, 2, 3, 4):

            @pl.when(index == max(0, 2 * hop - 3))
            def _():
                scales_in(hop)
                hop_in(0, hop)
                if hop > 1:
                    for move in load(0, hop - 1):
                        move.wait()

            @pl.when(index == 2 * hop - 2)
            def _():
                steps = (-hop, hop) if hop < 4 else (4,)
                over_x(1, steps)
                over_x(0, steps)
                complete(steps, (1, 0))

        return carry

    lax.fori_loop(0, RING, turn, 0)
    for move in stores(0):
        move.wait()
    copies.finish()


def me_scale_row(experts):
    return RING * experts


def gather_feed(
    rows, cotangent, scales, routes, expert_in, expert_down, shared, capacity, collective_id
):
    bf16, f32 = jnp.bfloat16, jnp.float32
    blocks, _, tokens = routes.shape
    experts = expert_in.shape[0]
    count, width = rows.shape
    hidden = expert_in.shape[1] // 2
    slice_hidden = shared.shape[2]
    shape = jax.ShapeDtypeStruct
    stages = (
        (tokens, width),
        (tokens, width),
        (experts, capacity, width),
        (experts, capacity, width),
        (2, experts, capacity, hidden),
        (experts, capacity, hidden),
        (2, tokens, slice_hidden),
        (tokens, slice_hidden),
    )
    return pl.pallas_call(
        gather_feed_kernel,
        out_shape=(
            shape((RING, 4, count, width), bf16),
            shape((RING, 4, count, width), bf16),
            shape((RING, 4) + scales.shape, f32),
            shape((blocks, tokens, width), bf16),
            shape((blocks, tokens, width), bf16),
            shape((experts, blocks, capacity, width), bf16),
            shape((experts, blocks, capacity, width), bf16),
            shape((2, experts, blocks, capacity, hidden), bf16),
            shape((experts, blocks, capacity, hidden), bf16),
            shape((2, blocks, tokens, slice_hidden), bf16),
            shape((blocks, tokens, slice_hidden), bf16),
            shape((RING, 4) + scales.shape, f32),
        ),
        in_specs=[IN_VMEM] * 7,
        out_specs=(IN_PLACE,) * 2 + (IN_VMEM,) + (IN_PLACE,) * 8 + (IN_VMEM,),
        scratch_shapes=[
            pltpu.VMEM((blocks, experts, tokens), jnp.int32),
            pltpu.VMEM((blocks, tokens, experts), jnp.int32),
            pltpu.VMEM((3, slice_hidden, width), bf16),
            pltpu.VMEM((experts * capacity + slice_hidden, width), bf16),
            pltpu.VMEM((experts * capacity + 2 * slice_hidden, width), bf16),
            pltpu.VMEM((2, 4, count, width), bf16),
            pltpu.VMEM((2, 4, count, width), bf16),
        ]
        + [pltpu.VMEM(stage, bf16) for stage in stages]
        + [pltpu.SemaphoreType.DMA((2, 2)), pltpu.SemaphoreType.DMA((len(stages),))]
        + semaphores(160),
        compiler_params=remote_params(collective_id, 62),
        name="gather_feed",
    )(rows, cotangent, scales, routes, expert_in, expert_down, shared)


def add_into(total, term, rows, tile=32):
    tile = min(tile, rows)

    def step(index, carry):
        here = pl.ds(pl.multiple_of(index * tile, tile), tile)
        summed = total[here, :].astype(jnp.float32) + term[here, :].astype(jnp.float32)
        total[here, :] = summed.astype(total.dtype)
        return carry

    lax.fori_loop(0, rows // tile, step, 0)


class WeightGrads:
    def __init__(self, jobs, left, right, sums, low, sems, out_sems):
        self.jobs, self.left, self.right = jobs, left, right
        self.sums, self.low, self.sems, self.out_sems = sums, low, sems, out_sems
        self.next = 0
        self.stores = {}
        self.fetch(0, 0, 0).start()

    def fetch(self, job, index, slot):
        left, right, _ = self.jobs[job]
        chunk, rows, columns, _ = self.size(job)
        here = pl.ds(pl.multiple_of(index * chunk, chunk), chunk)
        return Pair(
            pltpu.make_async_copy(
                left.at[here], self.left[rows].at[slot, pl.ds(0, chunk)], self.sems.at[slot, 0]
            ),
            pltpu.make_async_copy(
                right.at[here], self.right.at[slot, pl.ds(0, chunk)], self.sems.at[slot, 1]
            ),
        )

    def size(self, job):
        left, right, _ = self.jobs[job]
        depth, rows = left.shape
        chunk = min(self.right.shape[1], depth)
        while depth % (2 * chunk):
            chunk -= 128
        return chunk, rows, right.shape[1], depth // chunk

    def run(self, count=1):
        for job in range(self.next, min(self.next + count, len(self.jobs))):
            self.one(job)

    def one(self, job):
        self.next = job + 1
        chunk, rows, _, steps = self.size(job)
        which = job % 2
        if which in self.stores:
            self.stores.pop(which).wait()
        total = self.sums.at[which, pl.ds(0, rows)]

        def step(index, carry):
            slot = index % 2

            @pl.when(index + 1 < steps)
            def _():
                self.fetch(job, index + 1, 1 - slot).start()

            if job + 1 < len(self.jobs):

                @pl.when(index + 1 == steps)
                def _():
                    self.fetch(job + 1, 0, 0).start()

            self.fetch(job, index, slot).wait()
            term = product(
                self.left[rows][slot, pl.ds(0, chunk)], self.right[slot, pl.ds(0, chunk)], TN
            )

            @pl.when(index == 0)
            def _():
                total[...] = term

            @pl.when(index > 0)
            def _():
                total[...] += term

            return carry

        lax.fori_loop(0, steps, step, 0)
        out = self.jobs[job][2]
        source = self.low.at[which, pl.ds(0, rows)]
        source[...] = total[...].astype(out.dtype)
        if out.ndim == source.ndim:
            moves = [pltpu.make_async_copy(source, out, self.out_sems.at[which, 0])]
        else:
            across = out.shape[2]
            moves = [
                pltpu.make_async_copy(
                    source.at[:, pl.ds(place * across, across)], out.at[place], self.out_sems.at[which, place]
                )
                for place in range(out.shape[0])
            ]
        self.stores[which] = Pair(*moves)
        self.stores[which].start()

    def finish(self):
        self.run(len(self.jobs))
        for store in self.stores.values():
            store.wait()


class Pair:
    def __init__(self, *moves):
        self.moves = moves

    def start(self):
        for move in self.moves:
            move.start()

    def wait(self):
        for move in self.moves:
            move.wait()


def scatter_kernel(
    back_part, ffn_part, scalars, slot_rows, slot_cotangent, grad_pre, gated,
    all_rows, all_cotangent, grad_shared_pre, scaled,
    back_sum, ffn_sum, out_scalars, grad_experts, grad_shared,
    held, core_in, x_in, ring_q, ring_x, last_in,
    s_held, s_core, s_x, s_ring,
    job_left, job_short, job_right, job_sums, job_low, job_sems, job_out_sems,
    free, send_sems, recv_sems,
):
    me = Peers()
    copies = Copies(send_sems, recv_sems)
    parts, outs = (back_part, ffn_part), (back_sum, ffn_sum)
    count = back_part.shape[2]
    half, piece = count // 2, count // 4
    q, qx, qc, qd = me.quarter, me.x_quarter, me.core_quarter, me.far_quarter
    own, other, last = range(3)
    peers = {RIGHT: me.right, LEFT: me.left}
    greet([me.right, me.left, me.x_peer, me.core_peer])
    order = (4, 3, 5, 2, 6, 1, 7, 0)

    def load(kind):
        for k in order:
            for slot, mine in ((0, q), (1, qx)):
                copies.local(
                    (kind, LOCAL, k, slot), parts[kind].at[me.block(k), mine], held.at[kind, k, slot]
                )

    def swap_cores(kind):
        for k in order:
            for slot, theirs in ((0, qc), (1, qd)):
                target = core_in.at[k, slot]
                copies.send(
                    (kind, OVER_CORE, k, slot),
                    parts[kind].at[me.block(k), theirs],
                    target,
                    target,
                    me.core_peer,
                )

    swap_cores(0)
    load(0)
    for k in range(RING):
        for slot, mine, theirs in ((0, q, qc), (1, qx, qd)):
            copies.local((SCALARS, LOCAL, k, slot), scalars.at[me.block(k), mine], s_held.at[slot, k])
            target = s_core.at[slot, k]
            copies.send(
                (SCALARS, OVER_CORE, k, slot),
                scalars.at[me.block(k), theirs],
                target,
                target,
                me.core_peer,
            )

    def prepare(kind, *blocks):
        for k in blocks:
            for slot in (1, 0):
                copies.arrive(kind, LOCAL, k, slot)
                copies.arrive(kind, OVER_CORE, k, slot)
                add_into(held.at[kind, k, slot], core_in.at[k, slot], count)
                if slot == 1:
                    source = held.at[kind, k, 1, pl.ds(half, half)]
                    target = x_in.at[kind, k]
                    copies.send((kind, OVER_X, k), source, target, target, me.x_peer)

    def over_x(kind, *blocks):
        for k in blocks:
            copies.arrive(kind, OVER_X, k)
            add_into(held.at[kind, k, 0, pl.ds(half, half)], x_in.at[kind, k], half)

    def pass_on(kind, side, hop, k):
        if hop == 0:
            rows_q, rows_x = pl.ds(side * half, half), pl.ds(side * piece, piece)
        else:
            rows_q, rows_x = pl.ds(0, count), pl.ds(0, half)
        for which, landing, rows in ((own, ring_q, rows_q), (other, ring_x, rows_x)):
            target = landing.at[kind, side, hop, rows]
            source = held.at[kind, k, which, rows]
            copies.send((kind, side, which, hop), source, target, target, peers[side])

    def take_in(kind, side, hop, k):
        if hop == 0:
            span_q, span_x, at_q, at_x = half, piece, side * half, side * piece
        else:
            span_q, span_x, at_q, at_x = count, half, 0, 0
        for which, landing, span, at in (
            (own, ring_q, span_q, at_q),
            (other, ring_x, span_x, at_x),
        ):
            copies.arrive(kind, side, which, hop)
            rows = pl.ds(at, span)
            add_into(held.at[kind, k, which, rows], landing.at[kind, side, hop, rows], span)

    def hop_on(kind, hop):
        right_block, left_block = 4 - hop, 4 + hop
        if hop == 0:
            pass_on(kind, RIGHT, 0, 4)
            pass_on(kind, LEFT, 0, 4)
            return
        take_in(kind, RIGHT, hop - 1, right_block)
        pass_on(kind, RIGHT, hop, right_block)
        take_in(kind, LEFT, hop - 1, left_block)
        pass_on(kind, LEFT, hop, left_block)

    def pass_scalars(side, hop, k):
        target = s_ring.at[side, hop]
        copies.send((SCALARS, side, hop), s_held.at[0, k], target, target, peers[side])

    def take_scalars(side, hop, k):
        copies.arrive(SCALARS, side, hop)
        s_held[0, k] += s_ring[side, hop]

    def home(kind):
        take_in(kind, RIGHT, 3, 0)
        take_in(kind, LEFT, 3, 0)
        source, target = held.at[kind, 0, 1, pl.ds(0, half)], last_in.at[kind]
        copies.send((kind, OVER_X, last, last), source, target, target, me.x_peer)

    def home_out(kind):
        out = outs[kind]
        out[pl.ds(half, half), :] = held[kind, 0, 0, pl.ds(half, half), :].astype(out.dtype)
        copies.arrive(kind, OVER_X, last, last)
        out[pl.ds(0, half), :] = (
            held[kind, 0, 0, pl.ds(0, half), :].astype(jnp.float32)
            + last_in[kind].astype(jnp.float32)
        ).astype(out.dtype)

    experts = slot_rows.shape[0]
    jobs = []
    for expert in range(experts):
        for index in range(2):
            jobs.append(
                (grad_pre.at[index, expert], slot_rows.at[expert], grad_experts.at[expert, index])
            )
        jobs.append((gated.at[expert], slot_cotangent.at[expert], grad_experts.at[expert, 2]))
    for index in range(2):
        jobs.append((grad_shared_pre.at[index], all_rows, grad_shared.at[:, index]))
    jobs.append((scaled, all_cotangent, grad_shared.at[:, 2]))
    prepare(0, 4, 3, 5)
    over_x(0, 4)
    hop_on(0, 0)
    prepare(0, 2, 6)
    for k in range(RING):
        for slot in (0, 1):
            copies.arrive(SCALARS, LOCAL, k, slot)
            copies.arrive(SCALARS, OVER_CORE, k, slot)
    s_held[...] += s_core[...]
    copies.send((SCALARS, OVER_X), s_held.at[1], s_x, s_x, me.x_peer)
    over_x(0, 3, 5)
    hop_on(0, 1)
    copies.arrive(SCALARS, OVER_X)
    s_held[0] += s_x[...]
    pass_scalars(RIGHT, 0, 4)
    prepare(0, 1, 7, 0)
    pl.semaphore_signal(free, inc=1, device_id=me.core_peer, device_id_type=MESH_ID)
    load(1)
    lefts = {job_left.shape[2]: job_left, job_short.shape[2]: job_short}
    grads = WeightGrads(jobs, lefts, job_right, job_sums, job_low, job_sems, job_out_sems)
    over_x(0, 2, 6)
    hop_on(0, 2)
    take_scalars(RIGHT, 0, 3)
    pass_scalars(RIGHT, 1, 3)
    pass_scalars(LEFT, 1, 5)
    pl.semaphore_wait(free, 1)
    swap_cores(1)
    over_x(0, 1, 7)
    grads.run(1)
    prepare(1, 4, 3, 5)
    hop_on(0, 3)
    take_scalars(RIGHT, 1, 2)
    take_scalars(LEFT, 1, 6)
    pass_scalars(RIGHT, 2, 2)
    pass_scalars(LEFT, 2, 6)
    over_x(0, 0)
    over_x(1, 4)
    hop_on(1, 0)
    prepare(1, 2, 6)
    over_x(1, 3, 5)
    grads.run(2)
    home(0)
    for side, k in ((RIGHT, 1), (LEFT, 7)):
        take_scalars(side, 2, k)
        pass_scalars(side, 3, k)
    hop_on(1, 1)
    home_out(0)
    prepare(1, 1, 7, 0)
    over_x(1, 2, 6)
    grads.run(2)
    hop_on(1, 2)
    over_x(1, 1, 7, 0)
    grads.run(2)
    hop_on(1, 3)
    take_scalars(RIGHT, 3, 0)
    take_scalars(LEFT, 3, 0)
    out_scalars[...] = s_held[0, 0]
    grads.finish()
    home(1)
    home_out(1)
    copies.finish()


def scatter_rows(back_part, ffn_part, scalars, fed, collective_id):
    slot_rows, slot_cotangent, grad_pre, gated, all_rows, all_cotangent, grad_shared_pre, scaled = fed
    _, _, count, width = back_part.shape
    half = count // 2
    dtype, f32 = back_part.dtype, jnp.float32
    s_shape = scalars.shape[2:]
    experts, hidden = gated.shape[0], gated.shape[2]
    shared_hidden = scaled.shape[1]
    shape = jax.ShapeDtypeStruct
    return pl.pallas_call(
        scatter_kernel,
        out_shape=(
            shape((count, width), f32),
            shape((count, width), f32),
            shape(s_shape, f32),
            shape((experts, 3, hidden, width), dtype),
            shape((RING, 3, shared_hidden, width // RING), dtype),
        ),
        in_specs=[IN_PLACE] * 11,
        out_specs=(IN_VMEM,) * 3 + (IN_PLACE,) * 2,
        scratch_shapes=[
            pltpu.VMEM((2, RING, 2, count, width), dtype),
            pltpu.VMEM((RING, 2, count, width), dtype),
            pltpu.VMEM((2, RING, half, width), dtype),
            pltpu.VMEM((2, 2, 4, count, width), dtype),
            pltpu.VMEM((2, 2, 4, half, width), dtype),
            pltpu.VMEM((2, half, width), dtype),
            pltpu.VMEM((2, RING) + s_shape, f32),
            pltpu.VMEM((2, RING) + s_shape, f32),
            pltpu.VMEM((RING,) + s_shape, f32),
            pltpu.VMEM((2, 4) + s_shape, f32),
            pltpu.VMEM((2, 640, hidden), dtype),
            pltpu.VMEM((2, 640, shared_hidden), dtype),
            pltpu.VMEM((2, 640, width), dtype),
            pltpu.VMEM((2, hidden, width), f32),
            pltpu.VMEM((2, hidden, width), dtype),
            pltpu.SemaphoreType.DMA((2, 2)),
            pltpu.SemaphoreType.DMA((2, RING)),
            pltpu.SemaphoreType.REGULAR,
        ]
        + semaphores(168),
        compiler_params=remote_params(collective_id, 62),
        name="scatter_rows",
    )(back_part, ffn_part, scalars, *fed)


def open_kernel(
    shard_in, shard_out, routes, rows, gain, bias, cosine, sine, shared_in, shared_down,
    full_in, full_out, full_routes, normed, queries, keys_values, shared_shards,
    sums, share_send, share_recv, send_sems, recv_sems,
):
    me = Peers()
    copies = Copies(send_sems, recv_sems)
    bf16, f32 = jnp.bfloat16, jnp.float32
    kinds, depth, width = shard_in.shape
    out_rows, columns = shard_out.shape
    tokens = rows.shape[0]
    sides = ((RIGHT, me.right, -1), (LEFT, me.left, 1))
    greet_along_z(me)

    def cell(kind, step, part, parts):
        block = me.block(step)
        if kind < kinds:
            return full_in.at[kind, block, pl.ds(part * (depth // parts), depth // parts)]
        if kind > kinds:
            return full_routes.at[block]
        across = pl.ds(pl.multiple_of(block * columns, columns), columns)
        return full_out.at[pl.ds(part * (out_rows // parts), out_rows // parts), across]

    def pass_on(side, peer, sign, kind, hop, source=None):
        if kind > kinds and hop == 3 and side == LEFT:
            return
        parts = 2 if hop == 3 else 1
        part = side if hop == 3 else 0
        step = sign * hop
        here = cell(kind, step, part, parts)
        copies.send(
            (side, kind, hop + 1),
            here if source is None else source,
            here,
            cell(kind, step + sign, part, parts),
            peer,
        )

    def hop_on(hop, order):
        for kind in order:
            source = None
            if hop == 0:
                source = shard_in.at[kind] if kind < kinds else shard_out if kind == kinds else routes
                cell(kind, 0, 0, 1)[...] = source[...]
            for side, peer, sign in sides:
                if hop > 0:
                    copies.arrive(side, kind, hop)
                pass_on(side, peer, sign, kind, hop, source)

    def multiply(kind, step):
        block = me.block(step)
        features = normed[:, pl.ds(pl.multiple_of(block * depth, depth), depth)]
        term = product(features, full_in[kind, block])
        if step == 0:
            sums[kind] = term + bias[kind : kind + 1, :]
        else:
            sums[kind] += term

    def go_round(order):
        taken = [kind for kind in order if kind < kinds]
        for hop in (1, 2, 3):
            hop_on(hop, order)
            for kind in taken:
                for step in (-hop, hop):
                    multiply(kind, step)
        for kind in order:
            for side, _, _ in sides:
                if kind <= kinds or side == RIGHT:
                    copies.arrive(side, kind, 4)
        for kind in taken:
            multiply(kind, 4)

    def heads_of(kind, turn):
        for start in range(0, width, HD):
            head = slice(start, start + HD)
            part = sums[kind, :, head]
            if turn:
                part = turned(part, cosine[...], sine[...])
            yield head, part.astype(bf16)

    first, second = (kinds + 1,) + tuple(range(kinds - 1, 0, -1)), (0, kinds)
    hop_on(0, first)
    _, scaled = rms_parts(rows[...].astype(f32))
    normed[...] = (scaled * gain[...]).astype(bf16)
    for kind in range(kinds):
        if kind:
            multiply(kind, 0)
    places, _, slice_hidden, across = shared_shards.shape
    for index in range(2):
        turned_shard = jnp.swapaxes(shared_in[index].astype(f32), 0, 1).astype(bf16)
        shared_shards[:, index] = turned_shard.reshape(places, slice_hidden, across)
    shared_shards[:, 2] = shared_down[...].reshape(places, slice_hidden, across)
    go_round(first)
    for index in range(2):
        for head, part in heads_of(index + 1, index == 0):
            keys_values[index, 2, :, head] = part
    pieces = 2
    size = tokens // pieces
    parts = [(kind, pl.ds(piece * size, size)) for kind in range(2) for piece in range(pieces)]
    count = len(parts)
    share = Copies(share_send, share_recv)

    def upward(index, kind, at):
        target = keys_values.at[kind, 0, at]
        return share.describe(keys_values.at[kind, 2, at], target, (me.ep + 2, me.tp), index)

    def sideways(index, kind, at):
        target = keys_values.at[kind, 1, at]
        return share.describe(keys_values.at[kind, 2, at], target, me.y_peer, count + index)

    def onward(index, kind, at):
        target = keys_values.at[kind, 1, at]
        return share.describe(keys_values.at[kind, 0, at], target, me.y_peer, count + index)

    def each(copy, action):
        for index, (kind, at) in enumerate(parts):
            action(copy(index, kind, at))

    @pl.when(me.z < 3)
    def _():
        each(upward, lambda copy: copy.start())

    @pl.when(me.y == 0)
    def _():
        each(sideways, lambda copy: copy.start())

    hop_on(0, second)
    multiply(0, 0)

    @pl.when(me.z == 0)
    def _():
        keys_values[:, 0] = jnp.zeros((2, tokens, width), bf16)

    @pl.when((me.z == 0) & (me.y == 0))
    def _():
        keys_values[:, 1] = jnp.zeros((2, tokens, width), bf16)

    @pl.when(me.z > 0)
    def _():
        for index, (kind, at) in enumerate(parts):
            upward(index, kind, at).wait_recv()

            @pl.when(me.y == 1)
            def _():
                onward(index, kind, at).start()

    go_round(second)
    for head, part in heads_of(0, True):
        queries[:, head] = part

    @pl.when((me.y == 1) | (me.z > 0))
    def _():
        each(sideways, lambda copy: copy.wait_recv())

    @pl.when(me.z < 3)
    def _():
        each(upward, lambda copy: copy.wait_send())

    @pl.when((me.y == 0) | (me.z > 0))
    def _():
        each(sideways, lambda copy: copy.wait_send())

    copies.finish()


def open_attention(
    shard_in, shard_out, routes, rows, gain, bias, cosine, sine, shared_in, shared_down, collective_id
):
    kinds, depth, width = shard_in.shape
    out_rows, columns = shard_out.shape
    tokens, features = rows.shape
    bf16 = jnp.bfloat16
    shape = jax.ShapeDtypeStruct
    return pl.pallas_call(
        open_kernel,
        out_shape=(
            shape((kinds, RING, depth, width), bf16),
            shape((out_rows, RING * columns), bf16),
            shape((RING,) + routes.shape, routes.dtype),
            shape((tokens, features), bf16),
            shape((tokens, width), bf16),
            shape((2, 3, tokens, width), bf16),
            shape((RING, 3, shared_in.shape[2] // RING, shared_in.shape[1]), bf16),
        ),
        in_specs=[IN_VMEM] * 10,
        out_specs=(IN_VMEM,) * 7,
        scratch_shapes=[pltpu.VMEM((kinds, tokens, width), jnp.float32)]
        + semaphores(8)
        + semaphores(8 * (kinds + 2)),
        compiler_params=remote_params(collective_id),
        name="open_attention",
    )(shard_in, shard_out, routes, rows, gain[None], bias, cosine, sine, shared_in, shared_down)


def finish_kernel(
    normed, grad_raw, heads, grad_attention, weights, gain, rows, grad_residual, tail,
    sum_in, sum_out, sum_tail, grad_input,
    held_in, held_out, ring_in, ring_out, tails, tail_sums,
    core_out, core_in, x_out, x_in, grad_rows, mine,
    send_sems, recv_sems,
):
    me = Peers()
    copies = Copies(send_sems, recv_sems)
    bf16, f32 = jnp.bfloat16, jnp.float32
    kinds = grad_raw.shape[0]
    depth, width = sum_in.shape[1], sum_in.shape[2]
    out_rows, columns = sum_out.shape
    count = rows.shape[0]
    peers = {RIGHT: me.right, LEFT: me.left}
    greet([me.right, me.left, me.x_peer, me.core_peer, me.far_peer])

    def held(kind, k):
        return held_in.at[k, kind] if kind < kinds else held_out.at[k]

    def ring(kind, side, hop):
        return ring_in.at[side, hop, kind] if kind < kinds else ring_out.at[side, hop]

    def span(kind, side, hop):
        whole = depth if kind < kinds else out_rows
        return (side * (whole // 2), whole // 2) if hop == 0 else (0, whole)

    def pass_on(side, hop, k, kind):
        at = pl.ds(*span(kind, side, hop))
        target = ring(kind, side, hop).at[at]
        copies.send((side, kind, hop), held(kind, k).at[at], target, target, peers[side])

    def take_in(side, hop, k, kind):
        copies.arrive(side, kind, hop)
        start, size = span(kind, side, hop)
        at = pl.ds(start, size)
        add_into(held(kind, k).at[at], ring(kind, side, hop).at[at], size)

    def work_out(*blocks):
        for k in blocks:
            block = me.block(k)
            features = normed[:, pl.ds(pl.multiple_of(block * depth, depth), depth)]
            for kind in range(kinds):
                held_in[k, kind] = product(features, grad_raw[kind], TN).astype(bf16)
            across = grad_attention[:, pl.ds(pl.multiple_of(block * columns, columns), columns)]
            held_out[k] = product(heads[...], across, TN).astype(bf16)

    def hop_on(hop):
        if hop == 0:
            for kind in range(kinds + 1):
                for side in (RIGHT, LEFT):
                    pass_on(side, 0, 4, kind)
            return
        for kind in range(kinds + 1):
            for side, k in ((RIGHT, 4 - hop), (LEFT, 4 + hop)):
                take_in(side, hop - 1, k, kind)
                pass_on(side, hop, k, kind)

    def quarter(index):
        here = pl.ds(pl.multiple_of(index * count, count), count)
        total = None
        for kind in range(kinds):
            term = product(grad_raw[kind, here, :], weights[kind], NT)
            total = term if total is None else total + term
        return total

    work_out(4)
    hop_on(0)
    for slot, index in ((1, me.far_quarter), (0, me.core_quarter)):
        core_out[slot] = quarter(index).astype(bf16)
        target = core_in.at[slot]
        copies.send((SCALARS, OVER_CORE, slot), core_out.at[slot], target, target, me.core_peer)
    mine[...] = quarter(me.x_quarter)
    copies.arrive(SCALARS, OVER_CORE, 1)
    x_out[...] = (mine[...] + core_in[1].astype(f32)).astype(bf16)
    copies.send((SCALARS, OVER_X), x_out, x_in, x_in, me.x_peer)
    work_out(3, 5)
    hop_on(1)
    mine[...] = quarter(me.quarter)
    copies.arrive(SCALARS, OVER_CORE, 0)
    work_out(2, 6)
    copies.arrive(SCALARS, OVER_X)
    total = mine[...] + core_in[0].astype(f32) + x_in[...].astype(f32)
    inverse, scaled_rows = rms_parts(rows[...].astype(f32))
    scaled = total * gain[...]
    slope = inverse * (
        scaled - scaled_rows * jnp.mean(scaled * scaled_rows, axis=-1, keepdims=True)
    )
    grad_rows[...] = (grad_residual[...] + slope).astype(bf16)
    here = grad_input.at[me.quarter]
    copies.send((SCALARS, RIGHT, OVER_X), grad_rows, here, grad_input.at[me.x_quarter], me.x_peer)
    copies.send(
        (SCALARS, RIGHT, OVER_CORE), grad_rows, here, grad_input.at[me.core_quarter], me.core_peer
    )
    copies.local((LOCAL,), grad_rows, here)
    gain_grad = jnp.sum(total * scaled_rows, axis=0, keepdims=True)
    tails[0, 0:kinds, :] = tail[...]
    for index in range(gain_grad.shape[1] // width):
        part = slice(index * width, (index + 1) * width)
        tails[0, kinds + index : kinds + index + 1, :] = gain_grad[:, part]
    tail_kind = kinds + 1

    def pass_tail(side, hop, place):
        sign = -1 if side == RIGHT else 1
        target = tails.at[(place + sign) % RING]
        copies.send((side, tail_kind, hop), tails.at[place], target, target, peers[side])

    pass_tail(RIGHT, 0, 0)
    pass_tail(LEFT, 0, 0)
    hop_on(2)
    work_out(1, 7)
    copies.arrive(SCALARS, RIGHT, OVER_X)
    beside = grad_input.at[me.x_quarter]
    copies.send(
        (SCALARS, LEFT, OVER_CORE), beside, beside, grad_input.at[me.far_quarter], me.core_peer
    )
    for side, place in ((RIGHT, 7), (LEFT, 1)):
        copies.arrive(side, tail_kind, 0)
        pass_tail(side, 1, place)
    hop_on(3)
    for side, place in ((RIGHT, 6), (LEFT, 2)):
        copies.arrive(side, tail_kind, 1)
        pass_tail(side, 2, place)
    work_out(0)
    copies.arrive(RIGHT, tail_kind, 2)
    pass_tail(RIGHT, 3, 5)
    copies.arrive(LEFT, tail_kind, 2)
    for kind in range(kinds + 1):
        for side in (RIGHT, LEFT):
            take_in(side, 3, 0, kind)
        if kind < kinds:
            sum_in[kind] = held_in[0, kind].astype(f32)
    sum_out[...] = held_out[0].astype(f32)
    copies.arrive(RIGHT, tail_kind, 3)
    total = tails[0]
    for place in range(1, RING):
        total = total + tails[place]
    tail_sums[me.tp] = total
    for way, peer, index in (
        (OVER_X, me.x_peer, me.x_quarter),
        (OVER_CORE, me.core_peer, me.core_quarter),
        (OVER_FAR, me.far_peer, me.far_quarter),
    ):
        copies.send(
            (way, tail_kind), tail_sums.at[me.tp], tail_sums.at[me.tp], tail_sums.at[index], peer
        )
    for way in (OVER_X, OVER_CORE, OVER_FAR):
        copies.arrive(way, tail_kind)
    sum_tail[...] = tail_sums[...]
    copies.finish()


def finish(
    normed, grad_raw, heads, grad_attention, weights, gain, rows, grad_residual, bias, collective_id
):
    tokens, width = normed.shape
    kinds, _, columns = grad_raw.shape
    count = rows.shape[0]
    depth = width // RING
    bf16, f32 = jnp.bfloat16, jnp.float32
    shape = jax.ShapeDtypeStruct
    tail_shape = (-(-(kinds + width // columns) // 8) * 8, columns)
    return pl.pallas_call(
        finish_kernel,
        out_shape=(
            shape((kinds, depth, columns), f32),
            shape((columns, depth), f32),
            shape((4,) + tail_shape, f32),
            shape((4, count, width), bf16),
        ),
        in_specs=[IN_VMEM] * 9,
        out_specs=(IN_VMEM,) * 3 + (IN_PLACE,),
        scratch_shapes=[
            pltpu.VMEM((RING, kinds, depth, columns), bf16),
            pltpu.VMEM((RING, columns, depth), bf16),
            pltpu.VMEM((2, 4, kinds, depth, columns), bf16),
            pltpu.VMEM((2, 4, columns, depth), bf16),
            pltpu.VMEM((RING,) + tail_shape, f32),
            pltpu.VMEM((4,) + tail_shape, f32),
            pltpu.VMEM((2, count, width), bf16),
            pltpu.VMEM((2, count, width), bf16),
            pltpu.VMEM((count, width), bf16),
            pltpu.VMEM((count, width), bf16),
            pltpu.VMEM((count, width), bf16),
            pltpu.VMEM((count, width), f32),
        ]
        + semaphores(56),
        compiler_params=remote_params(collective_id, 60),
        name="finish",
    )(normed, grad_raw, heads, grad_attention, weights, gain[None], rows, grad_residual, bias)


def widen_kernel(
    experts, shared, rows, expert_in, expert_down, shared_in, shared_down, rows_out
):
    f32 = jnp.float32
    expert_in[...] = experts[:, :2].astype(f32)
    expert_down[...] = experts[:, 2].astype(f32)
    rows_out[...] = rows[0]

    @pl.when(pl.program_id(0) == 0)
    def _():
        places, _, hidden, across = shared.shape
        for index in range(2):
            slices = shared[:, index].astype(f32).reshape(places * hidden, across)
            shared_in[index] = jnp.swapaxes(slices, 0, 1)
        shared_down[...] = shared[:, 2].astype(f32).reshape(places * hidden, across)


def widen(experts, shared, rows):
    count, _, hidden, width = experts.shape
    places, _, slice_hidden, across = shared.shape
    quarters, own, _ = rows.shape
    parts = places // count
    columns = width // parts
    step = quarters * own // places
    f32 = jnp.float32
    shape = jax.ShapeDtypeStruct
    shared_hidden = places * slice_hidden
    return pl.pallas_call(
        widen_kernel,
        grid=(places,),
        in_specs=[
            pl.BlockSpec((1, 3, hidden, columns), lambda i: (i // parts, 0, 0, i % parts)),
            pl.BlockSpec(shared.shape, lambda i: (0, 0, 0, 0)),
            pl.BlockSpec((1, step, width), lambda i: (i * step // own, i % (own // step), 0)),
        ],
        out_specs=(
            pl.BlockSpec((1, 2, hidden, columns), lambda i: (i // parts, 0, 0, i % parts)),
            pl.BlockSpec((1, hidden, columns), lambda i: (i // parts, 0, i % parts)),
            pl.BlockSpec((2, across, shared_hidden), lambda i: (0, 0, 0)),
            pl.BlockSpec((shared_hidden, across), lambda i: (0, 0)),
            pl.BlockSpec((step, width), lambda i: (i, 0)),
        ),
        out_shape=(
            shape((count, 2, hidden, width), f32),
            shape((count, hidden, width), f32),
            shape((2, across, shared_hidden), f32),
            shape((shared_hidden, across), f32),
            shape((quarters * own, width), rows.dtype),
        ),
        compiler_params=pltpu.CompilerParams(vmem_limit_bytes=60 * 2**20),
        name="widen",
    )(experts, shared, rows)


def greet_along_z(me, others=()):
    barrier = pltpu.get_barrier_semaphore()
    for peer in (me.y_peer,) + others:
        pl.semaphore_signal(barrier, inc=1, device_id=peer, device_id_type=MESH_ID)

    @pl.when(me.z > 0)
    def _():
        peer = (me.ep - 2, me.tp)
        pl.semaphore_signal(barrier, inc=1, device_id=peer, device_id_type=MESH_ID)

    @pl.when(me.z < 3)
    def _():
        peer = (me.ep + 2, me.tp)
        pl.semaphore_signal(barrier, inc=1, device_id=peer, device_id_type=MESH_ID)

    pl.semaphore_wait(barrier, 1 + len(others) + (me.z + 2) // 3 + (5 - me.z) // 3)


def back_kernel(
    rows, weights, valid, queries, keys_values, query_doc, key_doc, log_totals, cosine, sine,
    grad_attention, grad_raw,
    grad_heads, grads, total, from_y, from_z,
    y_send, y_recv, z_send, z_recv, send_sems, recv_sems,
):
    me = Peers()
    copies = Copies(send_sems, recv_sems)
    bf16, f32 = jnp.bfloat16, jnp.float32
    count = rows.shape[0]
    tokens, width = queries.shape
    blocks = keys_values.shape[1]
    head_count = width // HD
    greet_along_z(me, (me.x_peer, me.core_peer))

    mine = grad_attention.at[me.quarter]
    copies.send((OVER_X,), rows, mine, grad_attention.at[me.x_quarter], me.x_peer)
    copies.send((OVER_CORE, 0), rows, mine, grad_attention.at[me.core_quarter], me.core_peer)
    mine[...] = rows[...]

    def heads_of(quarter):
        at = pl.ds(pl.multiple_of(quarter * count, count), count)
        part = product(grad_attention[quarter], weights[...], NT) * valid[at, :]
        grad_heads[at, :] = part.astype(bf16)

    heads_of(me.quarter)
    copies.arrive(OVER_CORE, 0)
    heads_of(me.core_quarter)
    copies.arrive(OVER_X)
    beside = grad_attention.at[me.x_quarter]
    copies.send((OVER_CORE, 1), beside, beside, grad_attention.at[me.far_quarter], me.core_peer)
    heads_of(me.x_quarter)
    copies.arrive(OVER_CORE, 1)
    heads_of(me.far_quarter)

    across = Copies(y_send, y_recv)
    along = Copies(z_send, z_recv)

    def columns(head):
        return pl.ds(pl.multiple_of(head * HD, HD), HD)

    def sideways(head, kind):
        at = columns(head)
        source, target = grads.at[kind, 1, :, at], from_y.at[kind, :, at]
        return across.describe(source, target, me.y_peer, 2 * head + kind)

    def downward(head, kind, source):
        at = columns(head)
        return along.describe(
            source.at[kind, :, at], from_z.at[kind, :, at], (me.ep - 2, me.tp), 2 * head + kind
        )

    scale = 1.0 / math.sqrt(HD)

    def one_head(head, carry):
        at = columns(head)
        keys = keys_values[0, :, :, at].reshape(blocks * tokens, HD)
        values = keys_values[1, :, :, at].reshape(blocks * tokens, HD)
        query = queries[:, at]
        out_grads = grad_heads[:, at]
        scores = masked_scores(query, keys, query_doc[...], key_doc[...])
        probs = jnp.exp(scores - log_totals[head])
        slopes = product(out_grads, values, NT)
        slopes = probs * (slopes - jnp.sum(probs * slopes, axis=1, keepdims=True))
        grad_scores = slopes.astype(bf16)
        grad_keys = product(grad_scores, query, TN) * scale
        grads[0, :, :, at] = grad_keys.astype(bf16).reshape(blocks, tokens, HD)
        grad_values = product(probs.astype(bf16), out_grads, TN)
        grads[1, :, :, at] = grad_values.astype(bf16).reshape(blocks, tokens, HD)
        for kind in range(2):
            sideways(head, kind).start()

        @pl.when((me.z > 0) & (me.y == 0))
        def _():
            for kind in range(2):
                downward(head, kind, grads.at[:, 0]).start()

        turned_back = turned(product(grad_scores, keys) * scale, cosine[...], -sine[...])
        grad_raw[0, :, at] = turned_back.astype(bf16)
        return carry

    lax.fori_loop(0, head_count, one_head, 0)

    def from_beside(head, carry):
        at = columns(head)
        for kind in range(2):
            sideways(head, kind).wait_recv()
            here = grads[kind, 2, :, at].astype(f32)

            @pl.when(me.y == 0)
            def _():
                total[kind, :, at] = here + from_y[kind, :, at].astype(f32)

            @pl.when(me.y == 1)
            def _():
                total[kind, :, at] = here
                two_back = grads[kind, 0, :, at].astype(f32)
                summed = two_back + from_y[kind, :, at].astype(f32)
                from_y[kind, :, at] = summed.astype(bf16)

            @pl.when((me.z > 0) & (me.y == 1))
            def _():
                downward(head, kind, from_y).start()

        return carry

    lax.fori_loop(0, head_count, from_beside, 0)

    def from_above(head, carry):
        at = columns(head)

        @pl.when(me.z < 3)
        def _():
            for kind in range(2):
                downward(head, kind, from_y).wait_recv()
                total[kind, :, at] += from_z[kind, :, at].astype(f32)

        grad_raw[1, :, at] = turned(total[0, :, at], cosine[...], -sine[...]).astype(bf16)
        grad_raw[2, :, at] = total[1, :, at].astype(bf16)
        return carry

    lax.fori_loop(0, head_count, from_above, 0)

    def sent(head, carry):
        for kind in range(2):
            sideways(head, kind).wait_send()

        @pl.when(me.z > 0)
        def _():
            for kind in range(2):
                downward(head, kind, from_y).wait_send()

        return carry

    lax.fori_loop(0, head_count, sent, 0)
    copies.finish()


def back_attention(
    rows, weights, valid, queries, keys_values, query_doc, key_doc, log_totals, cosine, sine,
    collective_id,
):
    count, features = rows.shape
    tokens, width = queries.shape
    bf16, f32 = jnp.bfloat16, jnp.float32
    shape = jax.ShapeDtypeStruct
    pieces = 2 * (width // HD)
    return pl.pallas_call(
        back_kernel,
        out_shape=(shape((4, count, features), bf16), shape((3, tokens, width), bf16)),
        in_specs=[IN_VMEM] * 10,
        out_specs=(IN_VMEM,) * 2,
        scratch_shapes=[
            pltpu.VMEM((tokens, width), bf16),
            pltpu.VMEM(keys_values.shape, bf16),
            pltpu.VMEM((2, tokens, width), f32),
            pltpu.VMEM((2, tokens, width), bf16),
            pltpu.VMEM((2, tokens, width), bf16),
        ]
        + semaphores(pieces)
        + semaphores(pieces)
        + semaphores(3),
        compiler_params=remote_params(collective_id, 60),
        name="back_attention",
    )(rows, weights, valid, queries, keys_values, query_doc, key_doc, log_totals, cosine, sine)


def reduce_kernel(flip, left, right, out, core_out, core_in, x_out, x_in, send_sems, recv_sems):
    me = Peers()
    copies = Copies(send_sems, recv_sems)
    terms = left.shape[0]
    count = out.shape[0]
    f32 = jnp.float32
    greet([me.x_peer, me.core_peer])

    def quarter(index):
        rows = pl.ds(pl.multiple_of(index * count, count), count)
        total = None
        for term in range(terms):
            one = product(left[term, rows, :], right[term], NT if flip else NN)
            total = one if total is None else total + one
        return total

    for slot, index in ((1, me.far_quarter), (0, me.core_quarter)):
        core_out[slot] = quarter(index).astype(core_out.dtype)
        target = core_in.at[slot]
        copies.send((OVER_CORE, slot), core_out.at[slot], target, target, me.core_peer)
    mine = quarter(me.x_quarter)
    copies.arrive(OVER_CORE, 1)
    x_out[...] = (mine + core_in[1].astype(f32)).astype(x_out.dtype)
    copies.send((OVER_X,), x_out, x_in, x_in, me.x_peer)
    mine = quarter(me.quarter)
    copies.arrive(OVER_CORE, 0)
    out[...] = mine + core_in[0].astype(f32)
    copies.arrive(OVER_X)
    out[...] += x_in[...].astype(f32)
    copies.finish()


def product_to_owner(left, right, flip, collective_id):
    tokens = left.shape[1]
    width = right.shape[1] if flip else right.shape[2]
    count = tokens // 4
    bf16 = jnp.bfloat16
    return pl.pallas_call(
        functools.partial(reduce_kernel, flip),
        out_shape=jax.ShapeDtypeStruct((count, width), jnp.float32),
        in_specs=[IN_VMEM] * 2,
        out_specs=IN_VMEM,
        scratch_shapes=[
            pltpu.VMEM((2, count, width), bf16),
            pltpu.VMEM((2, count, width), bf16),
            pltpu.VMEM((count, width), bf16),
            pltpu.VMEM((count, width), bf16),
        ]
        + semaphores(3),
        compiler_params=remote_params(collective_id),
        name="product_to_owner",
    )(left, right)


def own_rows(block, tp_index, count):
    return lax.dynamic_slice_in_dim(block, tp_index * count, count, 0)


def per_device_dense(
    layer_input,
    attention_gain,
    attention_in,
    attention_bias,
    attention_out,
    feedforward_gain,
    shared_in,
    shared_down,
    shared_gate,
    router,
    expert_in,
    expert_down,
    routes,
    document_lengths,
    cotangent,
):
    bf16 = jnp.bfloat16
    f32 = jnp.float32
    both = (EP, TP)
    tok_count, model_width = layer_input.shape
    expert_count = router.shape[1]
    top_count = routes.shape[1]
    ep_size = lax.axis_size(EP)
    tp_size = lax.axis_size(TP)
    ep_index = lax.axis_index(EP)
    tp_index = lax.axis_index(TP)
    own_count = tok_count // tp_size
    all_count = tok_count * ep_size
    capacity = tp_size * (
        (5 * tok_count * top_count + 4 * expert_count * tp_size - 1) // (4 * expert_count * tp_size)
    )
    reach_back = min((WINDOW + tok_count - 2) // tok_count, ep_size - 1)
    local_experts = expert_in.shape[0]
    route_rows = jnp.concatenate(
        [routes.T, jnp.full((-top_count % 8, tok_count), -1, routes.dtype)]
    )
    positions = ep_index * tok_count + jnp.arange(tok_count, dtype=jnp.int32)
    key_count = (reach_back + 1) * tok_count
    key_positions = (ep_index - reach_back) * tok_count + jnp.arange(key_count, dtype=jnp.int32)
    query_doc, rope_pos, valid_mask = doc_table(document_lengths, positions)
    query_doc = query_doc[:, None]
    key_doc = doc_table(document_lengths, key_positions)[0][None, :]
    valid_rows = valid_mask.astype(f32)[:, None]
    cosine, sine = (part[:, 0] for part in rope_angles(rope_pos, HD))
    cosine = jnp.concatenate([cosine, cosine], axis=1)
    sine = jnp.concatenate([-sine, sine], axis=1)
    (
        in_blocks,
        out_full,
        all_routes,
        normed_attention,
        queries,
        keys_values,
        shared_shards,
    ) = open_attention(
        attention_in,
        attention_out,
        route_rows,
        layer_input,
        attention_gain,
        attention_bias,
        cosine,
        sine,
        shared_in,
        shared_down,
        0,
    )
    in_full = in_blocks.reshape(3, model_width, -1)
    shard_width = shared_in.shape[1]
    slice_hidden = shared_in.shape[2] // ep_size
    shared_slices = lax.all_to_all(shared_shards, EP, split_axis=0, concat_axis=0, tiled=True)
    heads_low, log_totals = attend(queries, keys_values, query_doc, key_doc, valid_rows)
    attention_sum = product_to_owner(heads_low[None], out_full[None], False, 2)
    input_rows = own_rows(layer_input, tp_index, own_count).astype(f32)
    residual = input_rows + attention_sum
    inverse_two, normed_two = rms_parts(residual)
    normed_ffn = normed_two * feedforward_gain
    normed_low = normed_ffn.astype(bf16)
    shared_scale = jax.nn.sigmoid(jnp.dot(normed_ffn, shared_gate, precision=HIGHEST))
    router_probs = jax.nn.softmax(jnp.dot(normed_ffn, router, precision=HIGHEST), axis=-1)
    routes_own = own_rows(routes, tp_index, own_count)
    expert_ids = jnp.arange(expert_count, dtype=jnp.int32)
    picked = jnp.any(routes_own[:, :, None] == expert_ids[None, None, :], axis=1)
    chosen = jnp.where(picked, router_probs, 0.0)
    chosen_total = jnp.sum(chosen, axis=1, keepdims=True)
    gates = chosen / chosen_total
    scale_count = -(-(expert_count + 1) // 8) * 8
    spare = jnp.zeros((scale_count - expert_count - 1, own_count), f32)
    scale_rows = jnp.concatenate([gates.T, shared_scale[None], spare])
    (
        all_rows,
        all_cotangent,
        all_scales,
        ffn_part,
        back_part,
        slot_rows,
        slot_cotangent,
        grad_pre,
        gated,
        grad_shared_pre,
        scaled_hidden,
        scalar_part,
    ) = gather_feed(
        normed_low,
        cotangent.reshape(tp_size, own_count, model_width),
        scale_rows,
        all_routes,
        jnp.swapaxes(expert_in, 2, 3).reshape(local_experts, -1, model_width),
        expert_down,
        shared_slices,
        capacity,
        3,
    )
    part_shape = (ep_size, tp_size, own_count, model_width)
    slot_count = ep_size * capacity
    fed = (
        slot_rows.reshape(local_experts, slot_count, model_width),
        slot_cotangent.reshape(local_experts, slot_count, model_width),
        grad_pre.reshape(2, local_experts, slot_count, -1),
        gated.reshape(local_experts, slot_count, -1),
        all_rows.reshape(all_count, model_width),
        all_cotangent.reshape(all_count, model_width),
        grad_shared_pre.reshape(2, all_count, slice_hidden),
        scaled_hidden.reshape(all_count, slice_hidden),
    )
    back_sum, ffn_sum, scalar_sum, grad_experts, shared_grads = scatter_rows(
        back_part.reshape(part_shape), ffn_part.reshape(part_shape), scalar_part, fed, 4
    )
    scalar_sum = scalar_sum.T
    layer_output = lax.all_gather((residual + ffn_sum).astype(bf16), TP, axis=0, tiled=True)
    shared_grads = lax.all_to_all(shared_grads, EP, split_axis=0, concat_axis=0, tiled=True)
    grad_gates = scalar_sum[:, :expert_count]
    grad_probs = jnp.where(
        picked,
        (grad_gates - jnp.sum(grad_gates * gates, axis=1, keepdims=True)) / chosen_total,
        0.0,
    )
    grad_logits = router_probs * (
        grad_probs - jnp.sum(grad_probs * router_probs, axis=1, keepdims=True)
    )
    grad_router = jnp.einsum("td,te->de", normed_ffn, grad_logits, precision=HIGHEST)
    grad_scale_pre = scalar_sum[:, expert_count] * shared_scale * (1.0 - shared_scale)
    grad_shared_gate = jnp.dot(grad_scale_pre, normed_ffn, precision=HIGHEST)
    grad_normed = (
        back_sum
        + jnp.einsum("te,de->td", grad_logits, router, precision=HIGHEST)
        + grad_scale_pre[:, None] * shared_gate[None, :]
    )
    grad_mid_norm, grad_feedforward_gain = norm_back(
        grad_normed, feedforward_gain, inverse_two, normed_two
    )
    small = jnp.concatenate([grad_feedforward_gain[None], grad_shared_gate[None], grad_router.T])
    small = lax.psum(small, both)
    grad_residual = own_rows(cotangent, tp_index, own_count).astype(f32) + grad_mid_norm
    grad_attention, grad_raw = back_attention(
        grad_residual.astype(bf16),
        out_full,
        valid_rows,
        queries,
        keys_values,
        query_doc,
        key_doc,
        log_totals,
        cosine,
        sine,
        5,
    )
    grad_attention = grad_attention.reshape(tok_count, model_width)
    grad_attention_bias = jnp.sum(grad_raw.astype(f32), axis=1)
    grad_attention_in, grad_attention_out, tails, grad_input = finish(
        normed_attention,
        grad_raw,
        heads_low,
        grad_attention,
        in_full,
        attention_gain,
        own_rows(layer_input, tp_index, own_count),
        grad_residual,
        grad_attention_bias,
        7,
    )
    grad_attention_bias = lax.dynamic_index_in_dim(tails, tp_index, 0, keepdims=False)[:3]
    grad_attention_gain = jnp.sum(tails[:, 3:], axis=0)[: model_width // tails.shape[2]].reshape(-1)
    grad_expert_in, grad_expert_down, grad_shared_in, grad_shared_down, grad_input = widen(
        grad_experts, shared_grads, grad_input
    )
    return (
        layer_output,
        grad_input,
        grad_attention_gain,
        grad_attention_in,
        grad_attention_bias,
        grad_attention_out,
        small[0],
        grad_shared_in,
        grad_shared_down,
        small[1],
        small[2:].T,
        jnp.swapaxes(grad_expert_in, 2, 3),
        grad_expert_down,
    )


def per_device(*arguments):
    small_slice = lax.axis_size(EP) == RING and lax.axis_size(TP) == 4
    return (per_device_dense if small_slice else per_device_sparse)(*arguments)


def per_device_sparse(
    layer_input,
    attention_gain,
    attention_in,
    attention_bias,
    attention_out,
    feedforward_gain,
    shared_in,
    shared_down,
    shared_gate,
    router,
    expert_in,
    expert_down,
    routes,
    document_lengths,
    cotangent,
):
    bf16 = jnp.bfloat16
    f32 = jnp.float32
    tok_count = layer_input.shape[0]
    model_width = layer_input.shape[1]
    expert_count = router.shape[1]
    top_count = routes.shape[1]
    ep_size = lax.axis_size(EP)
    tp_size = lax.axis_size(TP)
    capacity = tp_size * (
        (5 * tok_count * top_count + 4 * expert_count * tp_size - 1) // (4 * expert_count * tp_size)
    )
    reach_back = min((WINDOW + tok_count - 2) // tok_count, ep_size - 1)
    head_dim = HD
    local_heads = attention_in.shape[2] // head_dim
    score_scale = 1.0 / math.sqrt(head_dim)
    in_full, out_full, shared_in_full, shared_down_full = (
        lax.all_gather(attention_in, EP, axis=1, tiled=True),
        lax.all_gather(attention_out, EP, axis=1, tiled=True),
        lax.all_gather(shared_in, EP, axis=1, tiled=True),
        lax.all_gather(shared_down, EP, axis=1, tiled=True),
    )
    ep_index = lax.axis_index(EP)
    positions = ep_index * tok_count + jnp.arange(tok_count, dtype=jnp.int32)
    key_count = (reach_back + 1) * tok_count
    key_positions = (ep_index - reach_back) * tok_count + jnp.arange(key_count, dtype=jnp.int32)
    query_doc, rope_pos, valid_mask = doc_table(document_lengths, positions)
    key_doc = doc_table(document_lengths, key_positions)[0]
    distance = positions[:, None] - key_positions[None, :]
    allowed = (query_doc[:, None] == key_doc[None, :]) & (distance >= 0) & (distance < WINDOW)
    valid_rows = valid_mask.astype(f32)[:, None]
    cosine, sine_part = rope_angles(rope_pos, head_dim)
    input_rows = layer_input.astype(f32)
    inverse_one, normed_one = rms_parts(input_rows)
    normed_attention = (normed_one * attention_gain).astype(bf16)
    raw_proj = (
        jnp.einsum("td,sde->ste", normed_attention, in_full, preferred_element_type=f32)
        + attention_bias[:, None, :]
    )
    queries = rotate(
        raw_proj[0].reshape(tok_count, local_heads, head_dim), cosine, sine_part, 1.0
    ).astype(bf16)
    keys_own = rotate(
        raw_proj[1].reshape(tok_count, local_heads, head_dim), cosine, sine_part, 1.0
    ).astype(bf16)
    values_own = raw_proj[2].reshape(tok_count, local_heads, head_dim).astype(bf16)
    key_value = jnp.stack([keys_own, values_own])
    earlier = []
    for hop_count in range(reach_back, 0, -1):
        earlier.append(shifted(key_value, EP, hop_count))
    all_kv = jnp.concatenate(earlier + [key_value], axis=1)
    all_keys = all_kv[0]
    all_values = all_kv[1]
    scores = jnp.einsum("qhe,khe->hqk", queries, all_keys, preferred_element_type=f32) * score_scale
    scores = jnp.where(allowed[None], scores, MASKED)
    row_max = jnp.max(scores, axis=-1, keepdims=True)
    exp_terms = jnp.exp(scores - row_max)
    row_total = jnp.sum(exp_terms, axis=-1, keepdims=True)
    log_total = row_max + jnp.log(row_total)
    weights = (exp_terms / row_total).astype(bf16)
    heads_out = jnp.einsum("hqk,khe->qhe", weights, all_values, preferred_element_type=f32).reshape(
        tok_count, -1
    )
    heads_low = (heads_out * valid_rows).astype(bf16)
    attention_sum = tensor_total(jnp.dot(heads_low, out_full, preferred_element_type=f32))
    residual = input_rows + attention_sum
    inverse_two, normed_two = rms_parts(residual)
    normed_ffn = normed_two * feedforward_gain
    normed_low = normed_ffn.astype(bf16)
    shared_pre = jnp.einsum("td,sdf->stf", normed_low, shared_in_full, preferred_element_type=f32)
    shared_silu, shared_slope = silu_parts(shared_pre[0])
    shared_hidden = (shared_silu * shared_pre[1]).astype(bf16)
    shared_out = tensor_total(jnp.dot(shared_hidden, shared_down_full, preferred_element_type=f32))
    shared_scale = jax.nn.sigmoid(jnp.dot(normed_ffn, shared_gate, precision=HIGHEST))
    router_probs = jax.nn.softmax(jnp.dot(normed_ffn, router, precision=HIGHEST), axis=-1)
    chosen = jnp.take_along_axis(router_probs, routes, axis=1)
    chosen_total = jnp.sum(chosen, axis=1, keepdims=True)
    gate_values = chosen / chosen_total
    assign_count = tok_count * top_count
    flat_routes = routes.reshape(-1)
    expert_ids = jnp.arange(expert_count, dtype=jnp.int32)
    one_hot = (flat_routes[:, None] == expert_ids[None, :]).astype(jnp.int32)
    arrival_rank = jnp.sum((jnp.cumsum(one_hot, axis=0) - one_hot) * one_hot, axis=1)
    slot_count = expert_count * capacity
    slot_index = jnp.where(
        arrival_rank < capacity, flat_routes * capacity + arrival_rank, slot_count
    )
    slot_assign = (
        jnp.full((slot_count + 1,), assign_count, jnp.int32)
        .at[slot_index]
        .set(jnp.arange(assign_count, dtype=jnp.int32))[:slot_count]
    )
    slot_token = slot_assign // top_count
    padded_rows = jnp.concatenate([normed_low, jnp.zeros((1, model_width), bf16)])
    send_rows = padded_rows[slot_token].reshape(expert_count, capacity, model_width)

    def expert_trip(outgoing, work):
        row_block = lax.all_to_all(outgoing, EP, split_axis=0, concat_axis=1, tiled=True)
        partial_rows, extras = work(row_block)
        share_rows = lax.psum_scatter(partial_rows, TP, scatter_dimension=1, tiled=True).astype(
            bf16
        )
        whole_rows = lax.all_gather(share_rows, TP, axis=1, tiled=True)
        return (lax.all_to_all(whole_rows, EP, split_axis=1, concat_axis=0, tiled=True), extras)

    def expert_forward(row_block):
        pre_acts = jnp.einsum("erd,esdf->serf", row_block, expert_in, preferred_element_type=f32)
        gate_silu, gate_slope = silu_parts(pre_acts[0])
        hidden = (gate_silu * pre_acts[1]).astype(bf16)
        partial_rows = jnp.einsum("erf,efd->erd", hidden, expert_down, preferred_element_type=f32)
        return (partial_rows, (row_block, pre_acts, hidden, gate_silu, gate_slope))

    returned_rows, kept_state = expert_trip(send_rows, expert_forward)
    expert_rows, expert_pre, expert_hidden, expert_silu, expert_slope = kept_state
    padded_back = jnp.concatenate(
        [returned_rows.reshape(slot_count, model_width), jnp.zeros((1, model_width), bf16)]
    )
    picked = padded_back[slot_index].reshape(tok_count, top_count, model_width).astype(f32)
    moe_sum = jnp.sum(gate_values[:, :, None] * picked, axis=1)
    layer_output = (residual + shared_scale[:, None] * shared_out + moe_sum).astype(bf16)
    grad_rows = cotangent.astype(f32)
    padded_grad = jnp.concatenate([grad_rows, jnp.zeros((1, model_width), f32)])
    padded_gates = jnp.concatenate([gate_values.reshape(-1), jnp.zeros((1,), f32)])
    grad_send = (padded_gates[slot_assign][:, None] * padded_grad[slot_token]).astype(bf16)
    grad_send = grad_send.reshape(expert_count, capacity, model_width)

    def expert_backward(grad_block):
        grad_down = jnp.einsum(
            "erf,erd->efd", expert_hidden, grad_block, preferred_element_type=f32
        )
        grad_hidden = jnp.einsum(
            "erd,efd->erf", grad_block, expert_down, preferred_element_type=f32
        )
        grad_pre = jnp.stack(
            [grad_hidden * expert_pre[1] * expert_slope, grad_hidden * expert_silu]
        ).astype(bf16)
        grad_weights_in = jnp.einsum(
            "erd,serf->esdf", expert_rows, grad_pre, preferred_element_type=f32
        )
        grad_back_rows = jnp.einsum(
            "serf,esdf->erd", grad_pre, expert_in, preferred_element_type=f32
        )
        return (grad_back_rows, (grad_weights_in, grad_down))

    grad_returned, expert_grads = expert_trip(grad_send, expert_backward)
    grad_expert_in, grad_expert_down = expert_grads
    grad_gate_values = jnp.sum(picked * grad_rows[:, None, :], axis=2)
    grad_chosen = (
        grad_gate_values - jnp.sum(grad_gate_values * gate_values, axis=1, keepdims=True)
    ) / chosen_total
    grad_probs = jnp.sum(
        jnp.where(routes[:, :, None] == expert_ids[None, None, :], grad_chosen[:, :, None], 0.0),
        axis=1,
    )
    grad_logits = router_probs * (
        grad_probs - jnp.sum(grad_probs * router_probs, axis=1, keepdims=True)
    )
    grad_router = jnp.einsum("td,te->de", normed_ffn, grad_logits, precision=HIGHEST)
    grad_shared_out = (shared_scale[:, None] * grad_rows).astype(bf16)
    grad_shared_down = jnp.einsum(
        "tf,td->fd", shared_hidden, grad_shared_out, preferred_element_type=f32
    )
    grad_shared_hidden = jnp.einsum(
        "td,fd->tf", grad_shared_out, shared_down_full, preferred_element_type=f32
    )
    grad_shared_pre = jnp.stack(
        [grad_shared_hidden * shared_pre[1] * shared_slope, grad_shared_hidden * shared_silu]
    ).astype(bf16)
    grad_shared_in = jnp.einsum(
        "td,stf->sdf", normed_low, grad_shared_pre, preferred_element_type=f32
    )
    shared_back = jnp.einsum(
        "stf,sdf->td", grad_shared_pre, shared_in_full, preferred_element_type=f32
    )
    grad_scale_pre = jnp.sum(grad_rows * shared_out, axis=1) * shared_scale * (1.0 - shared_scale)
    grad_shared_gate = jnp.dot(grad_scale_pre, normed_ffn, precision=HIGHEST)
    padded_return = jnp.concatenate(
        [grad_returned.reshape(slot_count, model_width), jnp.zeros((1, model_width), bf16)]
    )
    moe_back = jnp.sum(
        padded_return[slot_index].reshape(tok_count, top_count, model_width).astype(f32), axis=1
    )
    grad_normed = (
        tensor_total(shared_back)
        + moe_back
        + jnp.einsum("te,de->td", grad_logits, router, precision=HIGHEST)
        + grad_scale_pre[:, None] * shared_gate[None, :]
    )
    grad_mid_norm, grad_feedforward_gain = norm_back(
        grad_normed, feedforward_gain, inverse_two, normed_two
    )
    grad_residual = grad_rows + grad_mid_norm
    grad_attention = grad_residual.astype(bf16)
    grad_attention_out = jnp.einsum(
        "tf,td->fd", heads_low, grad_attention, preferred_element_type=f32
    )
    grad_heads = jnp.einsum(
        "td,fd->tf", grad_attention, out_full, preferred_element_type=f32
    ).astype(bf16)
    grad_heads = (grad_heads * valid_rows.astype(bf16)).reshape(tok_count, local_heads, head_dim)
    scores_again = (
        jnp.einsum("qhe,khe->hqk", queries, all_keys, preferred_element_type=f32) * score_scale
    )
    scores_again = jnp.where(allowed[None], scores_again, MASKED)
    softmax_out = jnp.exp(scores_again - log_total)
    weights_again = softmax_out.astype(bf16)
    grad_weights = jnp.einsum("qhe,khe->hqk", grad_heads, all_values, preferred_element_type=f32)
    grad_scores = (
        softmax_out * (grad_weights - jnp.sum(softmax_out * grad_weights, axis=-1, keepdims=True))
    ).astype(bf16)
    grad_queries = (
        jnp.einsum("hqk,khe->qhe", grad_scores, all_keys, preferred_element_type=f32) * score_scale
    )
    grad_keys = (
        jnp.einsum("hqk,qhe->khe", grad_scores, queries, preferred_element_type=f32) * score_scale
    )
    grad_values = jnp.einsum("hqk,qhe->khe", weights_again, grad_heads, preferred_element_type=f32)
    grad_kv = jnp.stack([grad_keys, grad_values])
    own_part = grad_kv[:, reach_back * tok_count :]
    for hop_count in range(1, reach_back + 1):
        segment_start = (reach_back - hop_count) * tok_count
        segment = grad_kv[:, segment_start : segment_start + tok_count]
        own_part = own_part + shifted(segment, EP, -hop_count)
    grad_raw = (
        jnp.stack(
            [
                rotate(grad_queries, cosine, sine_part, -1.0),
                rotate(own_part[0], cosine, sine_part, -1.0),
                own_part[1],
            ]
        )
        .reshape(3, tok_count, -1)
        .astype(bf16)
    )
    grad_attention_bias = jnp.sum(grad_raw.astype(f32), axis=1)
    grad_attention_in = jnp.einsum(
        "td,ste->sde", normed_attention, grad_raw, preferred_element_type=f32
    )
    grad_normed_attention = tensor_total(
        jnp.einsum("ste,sde->td", grad_raw, in_full, preferred_element_type=f32)
    )
    grad_in_norm, grad_attention_gain = norm_back(
        grad_normed_attention, attention_gain, inverse_one, normed_one
    )
    grad_input = (grad_residual + grad_in_norm).astype(bf16)
    grad_attention_in, grad_attention_out, grad_shared_in, grad_shared_down = (
        lax.psum_scatter(
            grad_attention_in.astype(jnp.bfloat16), EP, scatter_dimension=1, tiled=True
        ).astype(jnp.float32),
        lax.psum_scatter(
            grad_attention_out.astype(jnp.bfloat16), EP, scatter_dimension=1, tiled=True
        ).astype(jnp.float32),
        lax.psum_scatter(
            grad_shared_in.astype(jnp.bfloat16), EP, scatter_dimension=1, tiled=True
        ).astype(jnp.float32),
        lax.psum_scatter(
            grad_shared_down.astype(jnp.bfloat16), EP, scatter_dimension=1, tiled=True
        ).astype(jnp.float32),
    )
    (
        grad_attention_gain,
        grad_attention_bias,
        grad_feedforward_gain,
        grad_shared_gate,
        grad_router,
    ) = (
        lax.psum(grad_attention_gain.astype(jnp.bfloat16), EP).astype(jnp.float32),
        lax.psum(grad_attention_bias.astype(jnp.bfloat16), EP).astype(jnp.float32),
        lax.psum(grad_feedforward_gain.astype(jnp.bfloat16), EP).astype(jnp.float32),
        lax.psum(grad_shared_gate.astype(jnp.bfloat16), EP).astype(jnp.float32),
        lax.psum(grad_router.astype(jnp.bfloat16), EP).astype(jnp.float32),
    )
    return (
        layer_output,
        grad_input,
        grad_attention_gain,
        grad_attention_in,
        grad_attention_bias,
        grad_attention_out,
        grad_feedforward_gain,
        grad_shared_in,
        grad_shared_down,
        grad_shared_gate,
        grad_router,
        grad_expert_in,
        grad_expert_down,
    )


def solution(mesh):
    return jax.shard_map(
        per_device,
        mesh=mesh,
        in_specs=(
            P(EP, None),
            P(),
            P(None, EP, TP),
            P(None, TP),
            P(TP, EP),
            P(),
            P(None, EP, TP),
            P(TP, EP),
            P(),
            P(),
            P(EP, None, None, TP),
            P(EP, TP, None),
            P(EP, None),
            P(),
            P(EP, None),
        ),
        out_specs=(
            P(EP, None),
            P(EP, None),
            P(),
            P(None, EP, TP),
            P(None, TP),
            P(TP, EP),
            P(),
            P(None, EP, TP),
            P(TP, EP),
            P(),
            P(),
            P(EP, None, None, TP),
            P(EP, TP, None),
        ),
        check_vma=False,
    )
```

```python
import functools
import math

import jax
import jax.numpy as jnp
from jax import lax
from jax.experimental import pallas as pl
from jax.experimental.pallas import tpu as pltpu
from jax.sharding import PartitionSpec as P

EP, TP = "ep", "tp"
HD = 128
WINDOW = 1024


HIGHEST = lax.Precision.HIGHEST
EPSILON = 1e-06
ROPE_BASE = 1000000.0
MASKED = -1000000000.0


def shifted(value, axis, steps):
    count = lax.axis_size(axis)
    leading, last = (max(0, -steps), min(count, count - steps))
    return lax.ppermute(value, axis, [(source, source + steps) for source in range(leading, last)])


def tensor_total(partial_sum):
    return lax.psum(partial_sum, TP)


def rms_parts(values):
    inverse = lax.rsqrt(jnp.mean(values * values, axis=-1, keepdims=True) + EPSILON)
    return (inverse, values * inverse)


def norm_back(grad_rows, gain_vec, inverse, normed):
    scaled = grad_rows * gain_vec
    grad_in = inverse * (scaled - normed * jnp.mean(scaled * normed, axis=-1, keepdims=True))
    return (grad_in, jnp.sum(grad_rows * normed, axis=0))


def doc_table(document_lengths, positions):
    doc_ends = jnp.cumsum(document_lengths)
    starts_all = jnp.concatenate([doc_ends - document_lengths, doc_ends[-1:]])
    doc_ids = jnp.sum((positions[:, None] >= doc_ends[None, :]).astype(jnp.int32), axis=1)
    matches = (
        doc_ids[:, None] == jnp.arange(document_lengths.shape[0] + 1, dtype=jnp.int32)[None, :]
    )
    doc_begin = jnp.sum(jnp.where(matches, starts_all[None, :], 0), axis=1)
    rope_pos = positions - doc_begin
    valid_mask = positions < doc_ends[-1]
    doc_ids = jnp.where(positions < 0, -1, doc_ids)
    return (doc_ids, rope_pos, valid_mask)


def rope_angles(rope_pos, head_dim):
    half_width = head_dim // 2
    freqs = jnp.power(ROPE_BASE, -2.0 * jnp.arange(half_width, dtype=jnp.float32) / head_dim)
    angles = rope_pos.astype(jnp.float32)[:, None] * freqs[None, :]
    return (jnp.cos(angles)[:, None, :], jnp.sin(angles)[:, None, :])


def rotate(values, cosine, sine_part, turn_sign):
    half_width = values.shape[-1] // 2
    first_part = values[..., :half_width]
    second_part = values[..., half_width:]
    return jnp.concatenate(
        [
            first_part * cosine - turn_sign * second_part * sine_part,
            second_part * cosine + turn_sign * first_part * sine_part,
        ],
        axis=-1,
    )


def silu_parts(gate_pre):
    sig_gate = jax.nn.sigmoid(gate_pre)
    return (gate_pre * sig_gate, sig_gate * (1.0 + gate_pre * (1.0 - sig_gate)))


NN = (((1,), (0,)), ((), ()))
NT = (((1,), (1,)), ((), ()))
TN = (((0,), (0,)), ((), ()))


def product(left, right, dims=NN):
    return lax.dot_general(left, right, dims, preferred_element_type=jnp.float32)


def turned(values, cosine, sine):
    half = values.shape[1] // 2
    swapped = jnp.concatenate([values[:, half:], values[:, :half]], axis=1)
    return values * cosine + swapped * sine


def masked_scores(queries, keys, query_doc, key_doc):
    tokens, count = queries.shape[0], keys.shape[0]
    scores = product(queries, keys, NT) * (1.0 / math.sqrt(HD))
    ahead = lax.broadcasted_iota(jnp.int32, (tokens, count), 0) + (count - tokens)
    distance = ahead - lax.broadcasted_iota(jnp.int32, (tokens, count), 1)
    allowed = (query_doc == key_doc) & (distance >= 0) & (distance < WINDOW)
    return jnp.where(allowed, scores, MASKED)


def attend_kernel(queries, keys, values, query_doc, key_doc, valid, heads, log_totals):
    count = keys.shape[1] * keys.shape[2]
    keys, values = keys[0].reshape(count, HD), values[0].reshape(count, HD)
    scores = masked_scores(queries[...], keys, query_doc[...], key_doc[...])
    row_max = jnp.max(scores, axis=1, keepdims=True)
    terms = jnp.exp(scores - row_max)
    total = jnp.sum(terms, axis=1, keepdims=True)
    weights = (terms / total).astype(jnp.bfloat16)
    heads[...] = (product(weights, values) * valid[...]).astype(jnp.bfloat16)
    log_totals[0] = row_max + jnp.log(total)


def attention_specs(tokens, blocks):
    def column(*dims):
        return pl.BlockSpec(dims, lambda h: (0,) * len(dims))

    head = pl.BlockSpec((tokens, HD), lambda h: (0, h))
    keys = pl.BlockSpec((1, blocks, tokens, HD), lambda h: (0, 0, 0, h))
    values = pl.BlockSpec((1, blocks, tokens, HD), lambda h: (1, 0, 0, h))
    logs = pl.BlockSpec((1, tokens, 1), lambda h: (h, 0, 0))
    return head, keys, values, column(tokens, 1), column(1, blocks * tokens), logs


def attend(queries, keys_values, query_doc, key_doc, valid):
    tokens, columns = queries.shape
    blocks = keys_values.shape[1]
    head, keys, values, column, row, logs = attention_specs(tokens, blocks)
    shape = jax.ShapeDtypeStruct
    return pl.pallas_call(
        attend_kernel,
        grid=(columns // HD,),
        in_specs=[head, keys, values, column, row, column],
        out_specs=(head, logs),
        out_shape=(
            shape((tokens, columns), jnp.bfloat16),
            shape((columns // HD, tokens, 1), jnp.float32),
        ),
        compiler_params=pltpu.CompilerParams(vmem_limit_bytes=40 * 2**20),
        name="attend",
    )(queries, keys_values, keys_values, query_doc, key_doc, valid)


RING = 8
NO_SLOT = 1 << 20
RIGHT, LEFT, OVER_X, OVER_CORE, OVER_FAR, LOCAL, SCALARS = range(7)
MESH_ID = pl.DeviceIdType.MESH


def ring_place(ep):
    z, y = ep // 2, ep % 2
    return z + y * (7 - 2 * z)


def ring_member(place):
    upper = place // 4
    return 2 * place + upper * (15 - 4 * place)


class Peers:
    def __init__(self):
        self.ep, self.tp = lax.axis_index(EP), lax.axis_index(TP)
        self.x, self.core = self.tp // 2, self.tp % 2
        self.z, self.y = self.ep // 2, self.ep % 2
        self.place = ring_place(self.ep)
        self.right = (self.block(1), self.tp)
        self.left = (self.block(RING - 1), self.tp)
        self.quarter = self.tp
        self.x_quarter = (1 - self.x) * 2 + self.core
        self.core_quarter = self.x * 2 + 1 - self.core
        self.far_quarter = (1 - self.x) * 2 + 1 - self.core
        self.x_peer = (self.ep, self.x_quarter)
        self.core_peer = (self.ep, self.core_quarter)
        self.far_peer = (self.ep, self.far_quarter)
        self.y_peer = (self.z * 2 + 1 - self.y, self.tp)

    def block(self, step):
        return ring_member((self.place + step + RING) % RING)


def greet(peers):
    barrier = pltpu.get_barrier_semaphore()
    for peer in peers:
        pl.semaphore_signal(barrier, inc=1, device_id=peer, device_id_type=MESH_ID)
    pl.semaphore_wait(barrier, len(peers))


class Copies:
    def __init__(self, send_sems, recv_sems):
        self.send_sems, self.recv_sems = send_sems, recv_sems
        self.count = 0
        self.sent = []
        self.landing = {}

    def describe(self, source, target, peer, index):
        return pltpu.make_async_remote_copy(
            src_ref=source,
            dst_ref=target,
            send_sem=self.send_sems.at[index],
            recv_sem=self.recv_sems.at[index],
            device_id=peer,
            device_id_type=MESH_ID,
        )

    def send(self, key, source, target, landing, peer):
        index = self.count
        self.count += 1
        copy = self.describe(source, target, peer, index)
        copy.start()
        self.sent.append(copy)
        self.landing[key] = self.describe(landing, landing, peer, index).wait_recv

    def local(self, key, source, target):
        index = self.count
        self.count += 1
        copy = pltpu.make_async_copy(source, target, self.send_sems.at[index])
        copy.start()
        self.landing[key] = copy.wait

    def arrive(self, *key):
        self.landing.pop(key)()

    def finish(self):
        for wait in self.landing.values():
            wait()
        for copy in self.sent:
            copy.wait_send()


def remote_params(collective_id, vmem=48):
    return pltpu.CompilerParams(
        collective_id=collective_id, has_side_effects=True, vmem_limit_bytes=vmem * 2**20
    )


def semaphores(count):
    return [pltpu.SemaphoreType.DMA((count,))] * 2


IN_PLACE = pl.BlockSpec(memory_space=pl.ANY)
IN_VMEM = pl.BlockSpec(memory_space=pltpu.VMEM)


class LateCopies(Copies):
    def send(self, key, source, target, landing, peer):
        index = self.count
        self.count += 1
        self.describe(source(), target(), peer, index).start()
        self.sent.append(lambda: self.describe(source(), target(), peer, index).wait_send())
        self.landing[key] = lambda: self.describe(landing(), landing(), peer, index).wait_recv()

    def local(self, key, source, target):
        index = self.count
        self.count += 1

        def copy():
            return pltpu.make_async_copy(source(), target(), self.send_sems.at[index])

        copy().start()
        self.landing[key] = lambda: copy().wait()

    def finish(self):
        for wait in list(self.landing.values()) + self.sent:
            wait()


def feed_block(
    rank_row, rank_column, gate_rows, scale, token_rows, token_cotangent,
    expert_in, expert_down, shared, staged, between, out_terms, back_terms, scalar_out,
):
    (
        out_part, back_part, slot_rows, slot_cotangent, grad_pre, gated, grad_shared_pre, scaled,
    ) = staged
    bf16, f32 = jnp.bfloat16, jnp.float32
    experts, slots, _ = slot_rows.shape
    tokens = token_rows.shape[0]
    hidden_count = gated.shape[2]
    all_slots = experts * slots
    silu, slope = silu_parts(product(token_rows, shared[0], NT))
    up = product(token_rows, shared[1], NT)
    hidden = (silu * up).astype(bf16).astype(f32)
    scaled_hidden = (scale * hidden).astype(bf16)
    back = product(token_cotangent, shared[2], NT)
    scalar_out(None, jnp.sum(jnp.swapaxes(hidden * back, 0, 1), axis=0, keepdims=True))
    back = scale * back
    gate_grad = (back * up * slope).astype(bf16)
    up_grad = (back * silu).astype(bf16)
    between()
    scaled[...] = scaled_hidden
    grad_shared_pre[0] = gate_grad
    grad_shared_pre[1] = up_grad
    order = lax.broadcasted_iota(jnp.int32, (all_slots, tokens), 0)
    spread_order = lax.broadcasted_iota(jnp.int32, (tokens, all_slots), 1)
    hits, spread = None, None
    for expert in range(experts):
        row_hits = order == rank_row[expert : expert + 1, :] + expert * slots
        column_hits = spread_order == rank_column[:, expert : expert + 1] + expert * slots
        hits = row_hits if hits is None else hits | row_hits
        spread = column_hits if spread is None else spread | column_hits
    place = hits.astype(bf16)
    taken = product(place, token_rows).astype(bf16)
    taken_cotangent = product(place, token_cotangent).astype(bf16)
    for ref, values in ((slot_rows, taken), (slot_cotangent, taken_cotangent)):
        for expert in range(experts):
            ref[expert] = values[expert * slots : (expert + 1) * slots]
    for expert in range(experts):
        mine = slice(expert * slots, (expert + 1) * slots)
        gate = jnp.sum(
            jnp.where(hits[mine], gate_rows[expert : expert + 1], 0.0), axis=1, keepdims=True
        )
        pre = product(taken[mine], expert_in[expert], NT)
        silu, slope = silu_parts(pre[:, :hidden_count])
        up = pre[:, hidden_count:]
        hidden = (silu * up).astype(bf16).astype(f32)
        gated_hidden = (gate * hidden).astype(bf16)
        gated[expert] = gated_hidden
        back = product(taken_cotangent[mine], expert_down[expert], NT)
        slot_grad = jnp.sum(hidden * back, axis=1, keepdims=True)
        scalar_out(
            expert, jnp.sum(jnp.where(hits[mine], slot_grad, 0.0), axis=0, keepdims=True)
        )
        back = gate * back
        gate_grad_e = (back * up * slope).astype(bf16)
        up_grad_e = (back * silu).astype(bf16)
        grad_pre[0, expert] = gate_grad_e
        grad_pre[1, expert] = up_grad_e
        out_terms[mine, :] = product(gated_hidden, expert_down[expert]).astype(bf16)
        both_grads = jnp.concatenate([gate_grad_e, up_grad_e], axis=1)
        back_terms[mine, :] = product(both_grads, expert_in[expert]).astype(bf16)
    spread = spread.astype(bf16)
    out_part[...] = product(
        jnp.concatenate([spread, scaled_hidden], axis=1), out_terms[...]
    ).astype(bf16)
    back_part[...] = product(
        jnp.concatenate([spread, gate_grad, up_grad], axis=1), back_terms[...]
    ).astype(bf16)


def gather_feed_kernel(
    rows, cotangent, scales, routes, expert_in, expert_down, shared_blocks,
    all_rows, all_cotangent, all_scales,
    out_part, back_part, slot_rows, slot_cotangent, grad_pre, gated, grad_shared_pre, scaled,
    scalars,
    rank_row, rank_column, shared, out_terms, back_terms, held_rows, held_cotangent,
    stage_out, stage_back, stage_rows, stage_cotangent, stage_pre, stage_gated, stage_shared,
    stage_scaled,
    load_sems, store_sems, send_sems, recv_sems,
):
    me = Peers()
    copies = LateCopies(send_sems, recv_sems)
    count = rows.shape[0]
    half, part = count // 2, count // 4
    first_rows = (half, half - count // 8)
    q, qx, qc, qd = me.quarter, me.x_quarter, me.core_quarter, me.far_quarter
    blocks = {step: me.block(step) for step in range(-4, 5)}
    low = [pl.ds(0, rows_low) for rows_low in first_rows]
    high = [pl.ds(rows_low, count - rows_low) for rows_low in first_rows]
    whole = pl.ds(0, count)
    own, other, scale = range(3)
    full = (all_rows, all_cotangent)
    sides = ((RIGHT, me.right, -1, 0), (LEFT, me.left, 1, 1))
    greet([me.right, me.left, me.x_peer, me.core_peer, me.far_peer])

    def push(key, kind, step, quarter, which, peer, landing_step, landing_quarter, source=None):
        def cell():
            return full[kind].at[blocks[step], quarter, which]

        def landing():
            return full[kind].at[blocks[landing_step], landing_quarter, which]

        copies.send((kind,) + key, source or cell, cell, landing, peer)

    push((OVER_X, other, 0), 0, 0, q, low[0], me.x_peer, 0, qx, lambda: rows.at[low[0]])
    for side, peer, sign, keep in sides:
        push((side, own, 1), 1, 0, q, whole, peer, sign, q, lambda: cotangent.at[q])
        push((side, other, 1), 1, 0, qx, low[1], peer, sign, qx, lambda: cotangent.at[qx, low[1]])
    push((OVER_X, own, 0), 0, 0, q, high[0], me.x_peer, 0, qx, lambda: rows.at[high[0]])
    push((OVER_CORE, own, 0), 0, 0, q, whole, me.core_peer, 0, qc, lambda: rows)
    for side, peer, sign, keep in sides:
        push((side, own, 1), 0, 0, q, whole, peer, sign, q, lambda: rows)
    copies.local((LOCAL, 0), lambda: rows, lambda: all_rows.at[blocks[0], q])
    copies.local((LOCAL, 1), lambda: cotangent, lambda: all_cotangent.at[blocks[0]])

    def scales_of(quarter):
        return lambda: all_scales.at[blocks[0], quarter]

    for way, peer, quarter in (
        (OVER_X, me.x_peer, qx),
        (OVER_CORE, me.core_peer, qc),
        (OVER_FAR, me.far_peer, qd),
    ):
        copies.send((way, scale, 0), lambda: scales, scales_of(q), scales_of(quarter), peer)
    copies.local((LOCAL, scale), lambda: scales, scales_of(q))
    experts, _, width = expert_in.shape
    all_slots = experts * slot_rows.shape[2]
    shared_count, across = shared.shape[1], shared_blocks.shape[3]
    for block in range(RING):
        shared[:, :, block * across : (block + 1) * across] = shared_blocks[block]
    out_terms[all_slots:, :] = shared[2]
    back_terms[all_slots : all_slots + shared_count, :] = shared[0]
    back_terms[all_slots + shared_count :, :] = shared[1]
    first_expert, scale_at = me.ep * experts, me_scale_row(experts)
    tokens = routes.shape[2]
    taken = []
    for block in range(RING):
        for expert in range(experts):
            chosen = routes[block] == first_expert + expert
            taken.append(jnp.max(chosen.astype(jnp.float32), axis=0, keepdims=True))
    taken = jnp.concatenate(taken, axis=0)
    down = lax.broadcasted_iota(jnp.int32, (tokens, tokens), 0)
    right = lax.broadcasted_iota(jnp.int32, (tokens, tokens), 1)
    rank = product(taken.astype(jnp.bfloat16), (right < down).astype(jnp.bfloat16), NT)
    kept = (taken > 0.0) & (rank < slot_rows.shape[2])
    rank = jnp.where(kept, rank, float(NO_SLOT))
    column = product((right == down).astype(jnp.bfloat16), rank.astype(jnp.bfloat16), NT)
    for block in range(RING):
        mine = slice(block * experts, (block + 1) * experts)
        rank_row[block] = rank[mine].astype(jnp.int32)
        rank_column[block] = column[:, mine].astype(jnp.int32)
    scalars[...] = jnp.zeros_like(scalars)
    copies.arrive(0, OVER_X, other, 0)
    for side, peer, sign, keep in sides:
        push((side, other, 1), 0, 0, qx, low[0], peer, sign, qx)
    for way in (OVER_X, OVER_CORE, OVER_FAR):
        copies.arrive(way, scale, 0)
    copies.arrive(LOCAL, scale)

    def push_scales(step, side, peer, sign):
        def cell():
            return all_scales.at[blocks[step]]

        copies.send(
            (side, scale, abs(step) + 1), cell, cell, lambda: all_scales.at[blocks[step + sign]], peer
        )

    for side, peer, sign, keep in sides:
        push_scales(0, side, peer, sign)
    copies.arrive(0, OVER_X, own, 0)
    push((OVER_CORE, other, 0), 0, 0, qx, whole, me.core_peer, 0, qd)

    def hop_in(kind, hop):
        for side, peer, sign, keep in sides:
            step = sign * hop
            if hop < 4:
                copies.arrive(kind, side, own, hop)
                which = whole if hop < 3 else pl.ds(keep * half, half)
                push((side, own, hop + 1), kind, step, q, which, peer, step + sign, q)
                push((OVER_X, own, step), kind, step, q, high[kind], me.x_peer, step, qx)
                push((OVER_CORE, own, step), kind, step, q, whole, me.core_peer, step, qc)
                copies.arrive(kind, side, other, hop)
                last = pl.ds(part, first_rows[kind] - part) if keep else pl.ds(0, part)
                which = low[kind] if hop < 3 else last
                push((side, other, hop + 1), kind, step, qx, which, peer, step + sign, qx)
                push((OVER_CORE, other, step), kind, step, qx, low[kind], me.core_peer, step, qd)
        if hop == 4:
            copies.arrive(kind, LEFT, own, 4)
            copies.arrive(kind, RIGHT, own, 4)
            push((OVER_X, own, 4), kind, 4, q, high[kind], me.x_peer, 4, qx)
            push((OVER_CORE, own, 4), kind, 4, q, whole, me.core_peer, 4, qc)
            copies.arrive(kind, LEFT, other, 4)
            copies.arrive(kind, RIGHT, other, 4)
            push((OVER_CORE, other, 4), kind, 4, qx, low[kind], me.core_peer, 4, qd)

    def over_x(kind, steps):
        for step in steps:
            copies.arrive(kind, OVER_X, own, step)
            push((OVER_CORE, scale, step), kind, step, qx, high[kind], me.core_peer, step, qd)

    def scales_in(hop):
        for side, peer, sign, keep in sides:
            if hop < 4 or side == RIGHT:
                copies.arrive(side, scale, hop)
                if hop < 3 or (hop == 3 and side == RIGHT):
                    push_scales(sign * hop, side, peer, sign)

    def load(slot, step):
        pairs = ((all_rows, held_rows), (all_cotangent, held_cotangent))
        return [
            pltpu.make_async_copy(source.at[blocks[step]], held.at[slot], load_sems.at[slot, kind])
            for kind, (source, held) in enumerate(pairs)
        ]

    def complete(steps, slots):
        for step in steps:
            for kind in range(2):
                if step != 0:
                    for piece in (own, other, scale):
                        copies.arrive(kind, OVER_CORE, piece, step)
        moves = [load(slot, step) for slot, step in zip(slots, steps)]
        for move in moves[0] + moves[-1] if len(moves) > 1 else moves[0]:
            move.start()
        for move in moves[0]:
            move.wait()

    staged = (
        stage_out, stage_back, stage_rows, stage_cotangent, stage_pre, stage_gated, stage_shared,
        stage_scaled,
    )

    def stores(block):
        targets = (
            out_part.at[block], back_part.at[block], slot_rows.at[:, block],
            slot_cotangent.at[:, block], grad_pre.at[:, :, block], gated.at[:, block],
            grad_shared_pre.at[:, block], scaled.at[block],
        )
        return [
            pltpu.make_async_copy(stage, target, store_sems.at[index])
            for index, (stage, target) in enumerate(zip(staged, targets))
        ]


    copies.arrive(LOCAL, 0)
    copies.arrive(LOCAL, 1)
    for piece in (own, other):
        copies.arrive(0, OVER_CORE, piece, 0)
    complete((0,), (0,))

    def turn(index, carry):
        far = (index + 1) // 2
        step = far * (1 - 2 * (index % 2)) + (index // 7) * 8
        block = ring_member((me.place + step + RING) % RING)
        slot = index % 2

        def between():
            for hop in (1, 2, 3, 4):

                @pl.when(index == max(0, 2 * hop - 3))
                def _():
                    hop_in(1, hop)

            @pl.when(index > 0)
            def _():
                for move in stores(0):
                    move.wait()

        def scalar_out(expert, values):
            row = scale_at if expert is None else first_expert + expert
            for quarter in range(4):
                part = values[:, quarter * count : (quarter + 1) * count]
                scalars[block, quarter, pl.ds(row, 1), :] = part

        rows_here = held_rows[slot].reshape(4 * count, width)
        cotangent_here = held_cotangent[slot].reshape(4 * count, width)
        quarters = [all_scales[block, quarter] for quarter in range(4)]
        columns = jnp.concatenate([jnp.swapaxes(values, 0, 1) for values in quarters], axis=0)
        gate_rows = [
            jnp.concatenate(
                [all_scales[block, quarter, pl.ds(first_expert + e, 1), :] for quarter in range(4)],
                axis=1,
            )
            for e in range(experts)
        ]
        feed_block(
            rank_row[block],
            rank_column[block],
            jnp.concatenate(gate_rows, axis=0),
            columns[:, scale_at : scale_at + 1],
            rows_here,
            cotangent_here,
            expert_in,
            expert_down,
            shared,
            staged,
            between,
            out_terms,
            back_terms,
            scalar_out,
        )
        for move in stores(block):
            move.start()

        for hop in (1, 2, 3, 4):

            @pl.when(index == max(0, 2 * hop - 3))
            def _():
                scales_in(hop)
                hop_in(0, hop)
                if hop > 1:
                    for move in load(0, hop - 1):
                        move.wait()

            @pl.when(index == 2 * hop - 2)
            def _():
                steps = (-hop, hop) if hop < 4 else (4,)
                over_x(1, steps)
                over_x(0, steps)
                complete(steps, (1, 0))

        return carry

    lax.fori_loop(0, RING, turn, 0)
    for move in stores(0):
        move.wait()
    copies.finish()


def me_scale_row(experts):
    return RING * experts


def gather_feed(
    rows, cotangent, scales, routes, expert_in, expert_down, shared, capacity, collective_id
):
    bf16, f32 = jnp.bfloat16, jnp.float32
    blocks, _, tokens = routes.shape
    experts = expert_in.shape[0]
    count, width = rows.shape
    hidden = expert_in.shape[1] // 2
    slice_hidden = shared.shape[2]
    shape = jax.ShapeDtypeStruct
    stages = (
        (tokens, width),
        (tokens, width),
        (experts, capacity, width),
        (experts, capacity, width),
        (2, experts, capacity, hidden),
        (experts, capacity, hidden),
        (2, tokens, slice_hidden),
        (tokens, slice_hidden),
    )
    return pl.pallas_call(
        gather_feed_kernel,
        out_shape=(
            shape((RING, 4, count, width), bf16),
            shape((RING, 4, count, width), bf16),
            shape((RING, 4) + scales.shape, f32),
            shape((blocks, tokens, width), bf16),
            shape((blocks, tokens, width), bf16),
            shape((experts, blocks, capacity, width), bf16),
            shape((experts, blocks, capacity, width), bf16),
            shape((2, experts, blocks, capacity, hidden), bf16),
            shape((experts, blocks, capacity, hidden), bf16),
            shape((2, blocks, tokens, slice_hidden), bf16),
            shape((blocks, tokens, slice_hidden), bf16),
            shape((RING, 4) + scales.shape, f32),
        ),
        in_specs=[IN_VMEM] * 7,
        out_specs=(IN_PLACE,) * 2 + (IN_VMEM,) + (IN_PLACE,) * 8 + (IN_VMEM,),
        scratch_shapes=[
            pltpu.VMEM((blocks, experts, tokens), jnp.int32),
            pltpu.VMEM((blocks, tokens, experts), jnp.int32),
            pltpu.VMEM((3, slice_hidden, width), bf16),
            pltpu.VMEM((experts * capacity + slice_hidden, width), bf16),
            pltpu.VMEM((experts * capacity + 2 * slice_hidden, width), bf16),
            pltpu.VMEM((2, 4, count, width), bf16),
            pltpu.VMEM((2, 4, count, width), bf16),
        ]
        + [pltpu.VMEM(stage, bf16) for stage in stages]
        + [pltpu.SemaphoreType.DMA((2, 2)), pltpu.SemaphoreType.DMA((len(stages),))]
        + semaphores(160),
        compiler_params=remote_params(collective_id, 62),
        name="gather_feed",
    )(rows, cotangent, scales, routes, expert_in, expert_down, shared)


def add_into(total, term, rows, tile=32):
    tile = min(tile, rows)

    def step(index, carry):
        here = pl.ds(pl.multiple_of(index * tile, tile), tile)
        summed = total[here, :].astype(jnp.float32) + term[here, :].astype(jnp.float32)
        total[here, :] = summed.astype(total.dtype)
        return carry

    lax.fori_loop(0, rows // tile, step, 0)


class WeightGrads:
    def __init__(self, jobs, left, right, sums, low, sems, out_sems):
        self.jobs, self.left, self.right = jobs, left, right
        self.sums, self.low, self.sems, self.out_sems = sums, low, sems, out_sems
        self.next = 0
        self.stores = {}
        self.fetch(0, 0, 0).start()

    def fetch(self, job, index, slot):
        left, right, _ = self.jobs[job]
        chunk, rows, columns, _ = self.size(job)
        here = pl.ds(pl.multiple_of(index * chunk, chunk), chunk)
        return Pair(
            pltpu.make_async_copy(
                left.at[here], self.left[rows].at[slot, pl.ds(0, chunk)], self.sems.at[slot, 0]
            ),
            pltpu.make_async_copy(
                right.at[here], self.right.at[slot, pl.ds(0, chunk)], self.sems.at[slot, 1]
            ),
        )

    def size(self, job):
        left, right, _ = self.jobs[job]
        depth, rows = left.shape
        chunk = min(self.right.shape[1], depth)
        while depth % (2 * chunk):
            chunk -= 128
        return chunk, rows, right.shape[1], depth // chunk

    def run(self, count=1):
        for job in range(self.next, min(self.next + count, len(self.jobs))):
            self.one(job)

    def one(self, job):
        self.next = job + 1
        chunk, rows, _, steps = self.size(job)
        which = job % 2
        if which in self.stores:
            self.stores.pop(which).wait()
        total = self.sums.at[which, pl.ds(0, rows)]

        def step(index, carry):
            slot = index % 2

            @pl.when(index + 1 < steps)
            def _():
                self.fetch(job, index + 1, 1 - slot).start()

            if job + 1 < len(self.jobs):

                @pl.when(index + 1 == steps)
                def _():
                    self.fetch(job + 1, 0, 0).start()

            self.fetch(job, index, slot).wait()
            term = product(
                self.left[rows][slot, pl.ds(0, chunk)], self.right[slot, pl.ds(0, chunk)], TN
            )

            @pl.when(index == 0)
            def _():
                total[...] = term

            @pl.when(index > 0)
            def _():
                total[...] += term

            return carry

        lax.fori_loop(0, steps, step, 0)
        out = self.jobs[job][2]
        source = self.low.at[which, pl.ds(0, rows)]
        source[...] = total[...].astype(out.dtype)
        if out.ndim == source.ndim:
            moves = [pltpu.make_async_copy(source, out, self.out_sems.at[which, 0])]
        else:
            across = out.shape[2]
            moves = [
                pltpu.make_async_copy(
                    source.at[:, pl.ds(place * across, across)], out.at[place], self.out_sems.at[which, place]
                )
                for place in range(out.shape[0])
            ]
        self.stores[which] = Pair(*moves)
        self.stores[which].start()

    def finish(self):
        self.run(len(self.jobs))
        for store in self.stores.values():
            store.wait()


class Pair:
    def __init__(self, *moves):
        self.moves = moves

    def start(self):
        for move in self.moves:
            move.start()

    def wait(self):
        for move in self.moves:
            move.wait()


def scatter_kernel(
    back_part, ffn_part, scalars, slot_rows, slot_cotangent, grad_pre, gated,
    all_rows, all_cotangent, grad_shared_pre, scaled,
    back_sum, ffn_sum, out_scalars, grad_experts, grad_shared,
    held, core_in, x_in, ring_q, ring_x, last_in,
    s_held, s_core, s_x, s_ring,
    job_left, job_short, job_right, job_sums, job_low, job_sems, job_out_sems,
    free, send_sems, recv_sems,
):
    me = Peers()
    copies = Copies(send_sems, recv_sems)
    parts, outs = (back_part, ffn_part), (back_sum, ffn_sum)
    count = back_part.shape[2]
    half, piece = count // 2, count // 4
    q, qx, qc, qd = me.quarter, me.x_quarter, me.core_quarter, me.far_quarter
    own, other, last = range(3)
    peers = {RIGHT: me.right, LEFT: me.left}
    greet([me.right, me.left, me.x_peer, me.core_peer])
    order = (4, 3, 5, 2, 6, 1, 7, 0)

    def load(kind):
        for k in order:
            for slot, mine in ((0, q), (1, qx)):
                copies.local(
                    (kind, LOCAL, k, slot), parts[kind].at[me.block(k), mine], held.at[kind, k, slot]
                )

    def swap_cores(kind):
        for k in order:
            for slot, theirs in ((0, qc), (1, qd)):
                target = core_in.at[k, slot]
                copies.send(
                    (kind, OVER_CORE, k, slot),
                    parts[kind].at[me.block(k), theirs],
                    target,
                    target,
                    me.core_peer,
                )

    swap_cores(0)
    load(0)
    for k in range(RING):
        for slot, mine, theirs in ((0, q, qc), (1, qx, qd)):
            copies.local((SCALARS, LOCAL, k, slot), scalars.at[me.block(k), mine], s_held.at[slot, k])
            target = s_core.at[slot, k]
            copies.send(
                (SCALARS, OVER_CORE, k, slot),
                scalars.at[me.block(k), theirs],
                target,
                target,
                me.core_peer,
            )

    def prepare(kind, *blocks):
        for k in blocks:
            for slot in (1, 0):
                copies.arrive(kind, LOCAL, k, slot)
                copies.arrive(kind, OVER_CORE, k, slot)
                add_into(held.at[kind, k, slot], core_in.at[k, slot], count)
                if slot == 1:
                    source = held.at[kind, k, 1, pl.ds(half, half)]
                    target = x_in.at[kind, k]
                    copies.send((kind, OVER_X, k), source, target, target, me.x_peer)

    def over_x(kind, *blocks):
        for k in blocks:
            copies.arrive(kind, OVER_X, k)
            add_into(held.at[kind, k, 0, pl.ds(half, half)], x_in.at[kind, k], half)

    def pass_on(kind, side, hop, k):
        if hop == 0:
            rows_q, rows_x = pl.ds(side * half, half), pl.ds(side * piece, piece)
        else:
            rows_q, rows_x = pl.ds(0, count), pl.ds(0, half)
        for which, landing, rows in ((own, ring_q, rows_q), (other, ring_x, rows_x)):
            target = landing.at[kind, side, hop, rows]
            source = held.at[kind, k, which, rows]
            copies.send((kind, side, which, hop), source, target, target, peers[side])

    def take_in(kind, side, hop, k):
        if hop == 0:
            span_q, span_x, at_q, at_x = half, piece, side * half, side * piece
        else:
            span_q, span_x, at_q, at_x = count, half, 0, 0
        for which, landing, span, at in (
            (own, ring_q, span_q, at_q),
            (other, ring_x, span_x, at_x),
        ):
            copies.arrive(kind, side, which, hop)
            rows = pl.ds(at, span)
            add_into(held.at[kind, k, which, rows], landing.at[kind, side, hop, rows], span)

    def hop_on(kind, hop):
        right_block, left_block = 4 - hop, 4 + hop
        if hop == 0:
            pass_on(kind, RIGHT, 0, 4)
            pass_on(kind, LEFT, 0, 4)
            return
        take_in(kind, RIGHT, hop - 1, right_block)
        pass_on(kind, RIGHT, hop, right_block)
        take_in(kind, LEFT, hop - 1, left_block)
        pass_on(kind, LEFT, hop, left_block)

    def pass_scalars(side, hop, k):
        target = s_ring.at[side, hop]
        copies.send((SCALARS, side, hop), s_held.at[0, k], target, target, peers[side])

    def take_scalars(side, hop, k):
        copies.arrive(SCALARS, side, hop)
        s_held[0, k] += s_ring[side, hop]

    def home(kind):
        take_in(kind, RIGHT, 3, 0)
        take_in(kind, LEFT, 3, 0)
        source, target = held.at[kind, 0, 1, pl.ds(0, half)], last_in.at[kind]
        copies.send((kind, OVER_X, last, last), source, target, target, me.x_peer)

    def home_out(kind):
        out = outs[kind]
        out[pl.ds(half, half), :] = held[kind, 0, 0, pl.ds(half, half), :].astype(out.dtype)
        copies.arrive(kind, OVER_X, last, last)
        out[pl.ds(0, half), :] = (
            held[kind, 0, 0, pl.ds(0, half), :].astype(jnp.float32)
            + last_in[kind].astype(jnp.float32)
        ).astype(out.dtype)

    experts = slot_rows.shape[0]
    jobs = []
    for expert in range(experts):
        for index in range(2):
            jobs.append(
                (grad_pre.at[index, expert], slot_rows.at[expert], grad_experts.at[expert, index])
            )
        jobs.append((gated.at[expert], slot_cotangent.at[expert], grad_experts.at[expert, 2]))
    for index in range(2):
        jobs.append((grad_shared_pre.at[index], all_rows, grad_shared.at[:, index]))
    jobs.append((scaled, all_cotangent, grad_shared.at[:, 2]))
    prepare(0, 4, 3, 5)
    over_x(0, 4)
    hop_on(0, 0)
    prepare(0, 2, 6)
    for k in range(RING):
        for slot in (0, 1):
            copies.arrive(SCALARS, LOCAL, k, slot)
            copies.arrive(SCALARS, OVER_CORE, k, slot)
    s_held[...] += s_core[...]
    copies.send((SCALARS, OVER_X), s_held.at[1], s_x, s_x, me.x_peer)
    over_x(0, 3, 5)
    hop_on(0, 1)
    copies.arrive(SCALARS, OVER_X)
    s_held[0] += s_x[...]
    pass_scalars(RIGHT, 0, 4)
    prepare(0, 1, 7, 0)
    pl.semaphore_signal(free, inc=1, device_id=me.core_peer, device_id_type=MESH_ID)
    load(1)
    lefts = {job_left.shape[2]: job_left, job_short.shape[2]: job_short}
    grads = WeightGrads(jobs, lefts, job_right, job_sums, job_low, job_sems, job_out_sems)
    over_x(0, 2, 6)
    hop_on(0, 2)
    take_scalars(RIGHT, 0, 3)
    pass_scalars(RIGHT, 1, 3)
    pass_scalars(LEFT, 1, 5)
    pl.semaphore_wait(free, 1)
    swap_cores(1)
    over_x(0, 1, 7)
    grads.run(1)
    prepare(1, 4, 3, 5)
    hop_on(0, 3)
    take_scalars(RIGHT, 1, 2)
    take_scalars(LEFT, 1, 6)
    pass_scalars(RIGHT, 2, 2)
    pass_scalars(LEFT, 2, 6)
    over_x(0, 0)
    over_x(1, 4)
    hop_on(1, 0)
    prepare(1, 2, 6)
    over_x(1, 3, 5)
    grads.run(2)
    home(0)
    for side, k in ((RIGHT, 1), (LEFT, 7)):
        take_scalars(side, 2, k)
        pass_scalars(side, 3, k)
    hop_on(1, 1)
    home_out(0)
    prepare(1, 1, 7, 0)
    over_x(1, 2, 6)
    grads.run(2)
    hop_on(1, 2)
    over_x(1, 1, 7, 0)
    grads.run(2)
    hop_on(1, 3)
    take_scalars(RIGHT, 3, 0)
    take_scalars(LEFT, 3, 0)
    out_scalars[...] = s_held[0, 0]
    grads.finish()
    home(1)
    home_out(1)
    copies.finish()


def scatter_rows(back_part, ffn_part, scalars, fed, collective_id):
    slot_rows, slot_cotangent, grad_pre, gated, all_rows, all_cotangent, grad_shared_pre, scaled = fed
    _, _, count, width = back_part.shape
    half = count // 2
    dtype, f32 = back_part.dtype, jnp.float32
    s_shape = scalars.shape[2:]
    experts, hidden = gated.shape[0], gated.shape[2]
    shared_hidden = scaled.shape[1]
    shape = jax.ShapeDtypeStruct
    return pl.pallas_call(
        scatter_kernel,
        out_shape=(
            shape((count, width), f32),
            shape((count, width), f32),
            shape(s_shape, f32),
            shape((experts, 3, hidden, width), dtype),
            shape((RING, 3, shared_hidden, width // RING), dtype),
        ),
        in_specs=[IN_PLACE] * 11,
        out_specs=(IN_VMEM,) * 3 + (IN_PLACE,) * 2,
        scratch_shapes=[
            pltpu.VMEM((2, RING, 2, count, width), dtype),
            pltpu.VMEM((RING, 2, count, width), dtype),
            pltpu.VMEM((2, RING, half, width), dtype),
            pltpu.VMEM((2, 2, 4, count, width), dtype),
            pltpu.VMEM((2, 2, 4, half, width), dtype),
            pltpu.VMEM((2, half, width), dtype),
            pltpu.VMEM((2, RING) + s_shape, f32),
            pltpu.VMEM((2, RING) + s_shape, f32),
            pltpu.VMEM((RING,) + s_shape, f32),
            pltpu.VMEM((2, 4) + s_shape, f32),
            pltpu.VMEM((2, 640, hidden), dtype),
            pltpu.VMEM((2, 640, shared_hidden), dtype),
            pltpu.VMEM((2, 640, width), dtype),
            pltpu.VMEM((2, hidden, width), f32),
            pltpu.VMEM((2, hidden, width), dtype),
            pltpu.SemaphoreType.DMA((2, 2)),
            pltpu.SemaphoreType.DMA((2, RING)),
            pltpu.SemaphoreType.REGULAR,
        ]
        + semaphores(168),
        compiler_params=remote_params(collective_id, 62),
        name="scatter_rows",
    )(back_part, ffn_part, scalars, *fed)


def open_kernel(
    shard_in, shard_out, routes, rows, gain, bias, cosine, sine, shared_in, shared_down,
    full_in, full_out, full_routes, normed, queries, keys_values, shared_shards,
    sums, share_send, share_recv, send_sems, recv_sems,
):
    me = Peers()
    copies = Copies(send_sems, recv_sems)
    bf16, f32 = jnp.bfloat16, jnp.float32
    kinds, depth, width = shard_in.shape
    out_rows, columns = shard_out.shape
    tokens = rows.shape[0]
    sides = ((RIGHT, me.right, -1), (LEFT, me.left, 1))
    greet_along_z(me)

    def cell(kind, step, part, parts):
        block = me.block(step)
        if kind < kinds:
            return full_in.at[kind, block, pl.ds(part * (depth // parts), depth // parts)]
        if kind > kinds:
            return full_routes.at[block]
        across = pl.ds(pl.multiple_of(block * columns, columns), columns)
        return full_out.at[pl.ds(part * (out_rows // parts), out_rows // parts), across]

    def pass_on(side, peer, sign, kind, hop, source=None):
        if kind > kinds and hop == 3 and side == LEFT:
            return
        parts = 2 if hop == 3 else 1
        part = side if hop == 3 else 0
        step = sign * hop
        here = cell(kind, step, part, parts)
        copies.send(
            (side, kind, hop + 1),
            here if source is None else source,
            here,
            cell(kind, step + sign, part, parts),
            peer,
        )

    def hop_on(hop, order):
        for kind in order:
            source = None
            if hop == 0:
                source = shard_in.at[kind] if kind < kinds else shard_out if kind == kinds else routes
                cell(kind, 0, 0, 1)[...] = source[...]
            for side, peer, sign in sides:
                if hop > 0:
                    copies.arrive(side, kind, hop)
                pass_on(side, peer, sign, kind, hop, source)

    def multiply(kind, step):
        block = me.block(step)
        features = normed[:, pl.ds(pl.multiple_of(block * depth, depth), depth)]
        term = product(features, full_in[kind, block])
        if step == 0:
            sums[kind] = term + bias[kind : kind + 1, :]
        else:
            sums[kind] += term

    def go_round(order):
        taken = [kind for kind in order if kind < kinds]
        for hop in (1, 2, 3):
            hop_on(hop, order)
            for kind in taken:
                for step in (-hop, hop):
                    multiply(kind, step)
        for kind in order:
            for side, _, _ in sides:
                if kind <= kinds or side == RIGHT:
                    copies.arrive(side, kind, 4)
        for kind in taken:
            multiply(kind, 4)

    def heads_of(kind, turn):
        for start in range(0, width, HD):
            head = slice(start, start + HD)
            part = sums[kind, :, head]
            if turn:
                part = turned(part, cosine[...], sine[...])
            yield head, part.astype(bf16)

    first, second = (kinds + 1,) + tuple(range(kinds - 1, 0, -1)), (0, kinds)
    hop_on(0, first)
    _, scaled = rms_parts(rows[...].astype(f32))
    normed[...] = (scaled * gain[...]).astype(bf16)
    for kind in range(kinds):
        if kind:
            multiply(kind, 0)
    places, _, slice_hidden, across = shared_shards.shape
    for index in range(2):
        turned_shard = jnp.swapaxes(shared_in[index].astype(f32), 0, 1).astype(bf16)
        shared_shards[:, index] = turned_shard.reshape(places, slice_hidden, across)
    shared_shards[:, 2] = shared_down[...].reshape(places, slice_hidden, across)
    go_round(first)
    for index in range(2):
        for head, part in heads_of(index + 1, index == 0):
            keys_values[index, 2, :, head] = part
    pieces = 2
    size = tokens // pieces
    parts = [(kind, pl.ds(piece * size, size)) for kind in range(2) for piece in range(pieces)]
    count = len(parts)
    share = Copies(share_send, share_recv)

    def upward(index, kind, at):
        target = keys_values.at[kind, 0, at]
        peer = ((me.ep + 2) % RING, me.tp)
        return share.describe(keys_values.at[kind, 2, at], target, peer, index)

    def sideways(index, kind, at):
        target = keys_values.at[kind, 1, at]
        return share.describe(keys_values.at[kind, 2, at], target, me.y_peer, count + index)

    def onward(index, kind, at):
        target = keys_values.at[kind, 1, at]
        return share.describe(keys_values.at[kind, 0, at], target, me.y_peer, count + index)

    def each(copy, action):
        for index, (kind, at) in enumerate(parts):
            action(copy(index, kind, at))

    @pl.when(me.z < 3)
    def _():
        each(upward, lambda copy: copy.start())

    @pl.when(me.y == 0)
    def _():
        each(sideways, lambda copy: copy.start())

    hop_on(0, second)
    multiply(0, 0)

    @pl.when(me.z == 0)
    def _():
        keys_values[:, 0] = jnp.zeros((2, tokens, width), bf16)

    @pl.when((me.z == 0) & (me.y == 0))
    def _():
        keys_values[:, 1] = jnp.zeros((2, tokens, width), bf16)

    @pl.when(me.z > 0)
    def _():
        for index, (kind, at) in enumerate(parts):
            upward(index, kind, at).wait_recv()

            @pl.when(me.y == 1)
            def _():
                onward(index, kind, at).start()

    go_round(second)
    for head, part in heads_of(0, True):
        queries[:, head] = part

    @pl.when((me.y == 1) | (me.z > 0))
    def _():
        each(sideways, lambda copy: copy.wait_recv())

    @pl.when(me.z < 3)
    def _():
        each(upward, lambda copy: copy.wait_send())

    @pl.when((me.y == 0) | (me.z > 0))
    def _():
        each(sideways, lambda copy: copy.wait_send())

    copies.finish()


def open_attention(
    shard_in, shard_out, routes, rows, gain, bias, cosine, sine, shared_in, shared_down, collective_id
):
    kinds, depth, width = shard_in.shape
    out_rows, columns = shard_out.shape
    tokens, features = rows.shape
    bf16 = jnp.bfloat16
    shape = jax.ShapeDtypeStruct
    return pl.pallas_call(
        open_kernel,
        out_shape=(
            shape((kinds, RING, depth, width), bf16),
            shape((out_rows, RING * columns), bf16),
            shape((RING,) + routes.shape, routes.dtype),
            shape((tokens, features), bf16),
            shape((tokens, width), bf16),
            shape((2, 3, tokens, width), bf16),
            shape((RING, 3, shared_in.shape[2] // RING, shared_in.shape[1]), bf16),
        ),
        in_specs=[IN_VMEM] * 10,
        out_specs=(IN_VMEM,) * 7,
        scratch_shapes=[pltpu.VMEM((kinds, tokens, width), jnp.float32)]
        + semaphores(8)
        + semaphores(8 * (kinds + 2)),
        compiler_params=remote_params(collective_id),
        name="open_attention",
    )(shard_in, shard_out, routes, rows, gain[None], bias, cosine, sine, shared_in, shared_down)


def finish_kernel(
    normed, grad_raw, heads, grad_attention, weights, gain, rows, grad_residual, tail,
    sum_in, sum_out, sum_tail, grad_input,
    held_in, held_out, ring_in, ring_out, tails, tail_sums,
    core_out, core_in, x_out, x_in, grad_rows, mine,
    send_sems, recv_sems,
):
    me = Peers()
    copies = Copies(send_sems, recv_sems)
    bf16, f32 = jnp.bfloat16, jnp.float32
    kinds = grad_raw.shape[0]
    depth, width = sum_in.shape[1], sum_in.shape[2]
    out_rows, columns = sum_out.shape
    count = rows.shape[0]
    peers = {RIGHT: me.right, LEFT: me.left}
    greet([me.right, me.left, me.x_peer, me.core_peer, me.far_peer])

    def held(kind, k):
        return held_in.at[k, kind] if kind < kinds else held_out.at[k]

    def ring(kind, side, hop):
        return ring_in.at[side, hop, kind] if kind < kinds else ring_out.at[side, hop]

    def span(kind, side, hop):
        whole = depth if kind < kinds else out_rows
        return (side * (whole // 2), whole // 2) if hop == 0 else (0, whole)

    def pass_on(side, hop, k, kind):
        at = pl.ds(*span(kind, side, hop))
        target = ring(kind, side, hop).at[at]
        copies.send((side, kind, hop), held(kind, k).at[at], target, target, peers[side])

    def take_in(side, hop, k, kind):
        copies.arrive(side, kind, hop)
        start, size = span(kind, side, hop)
        at = pl.ds(start, size)
        add_into(held(kind, k).at[at], ring(kind, side, hop).at[at], size)

    def work_out(*blocks):
        for k in blocks:
            block = me.block(k)
            features = normed[:, pl.ds(pl.multiple_of(block * depth, depth), depth)]
            for kind in range(kinds):
                held_in[k, kind] = product(features, grad_raw[kind], TN).astype(bf16)
            across = grad_attention[:, pl.ds(pl.multiple_of(block * columns, columns), columns)]
            held_out[k] = product(heads[...], across, TN).astype(bf16)

    def hop_on(hop):
        if hop == 0:
            for kind in range(kinds + 1):
                for side in (RIGHT, LEFT):
                    pass_on(side, 0, 4, kind)
            return
        for kind in range(kinds + 1):
            for side, k in ((RIGHT, 4 - hop), (LEFT, 4 + hop)):
                take_in(side, hop - 1, k, kind)
                pass_on(side, hop, k, kind)

    def quarter(index):
        here = pl.ds(pl.multiple_of(index * count, count), count)
        total = None
        for kind in range(kinds):
            term = product(grad_raw[kind, here, :], weights[kind], NT)
            total = term if total is None else total + term
        return total

    work_out(4)
    hop_on(0)
    for slot, index in ((1, me.far_quarter), (0, me.core_quarter)):
        core_out[slot] = quarter(index).astype(bf16)
        target = core_in.at[slot]
        copies.send((SCALARS, OVER_CORE, slot), core_out.at[slot], target, target, me.core_peer)
    mine[...] = quarter(me.x_quarter)
    copies.arrive(SCALARS, OVER_CORE, 1)
    x_out[...] = (mine[...] + core_in[1].astype(f32)).astype(bf16)
    copies.send((SCALARS, OVER_X), x_out, x_in, x_in, me.x_peer)
    work_out(3, 5)
    hop_on(1)
    mine[...] = quarter(me.quarter)
    copies.arrive(SCALARS, OVER_CORE, 0)
    work_out(2, 6)
    copies.arrive(SCALARS, OVER_X)
    total = mine[...] + core_in[0].astype(f32) + x_in[...].astype(f32)
    inverse, scaled_rows = rms_parts(rows[...].astype(f32))
    scaled = total * gain[...]
    slope = inverse * (
        scaled - scaled_rows * jnp.mean(scaled * scaled_rows, axis=-1, keepdims=True)
    )
    grad_rows[...] = (grad_residual[...] + slope).astype(bf16)
    here = grad_input.at[me.quarter]
    copies.send((SCALARS, RIGHT, OVER_X), grad_rows, here, grad_input.at[me.x_quarter], me.x_peer)
    copies.send(
        (SCALARS, RIGHT, OVER_CORE), grad_rows, here, grad_input.at[me.core_quarter], me.core_peer
    )
    copies.local((LOCAL,), grad_rows, here)
    gain_grad = jnp.sum(total * scaled_rows, axis=0, keepdims=True)
    tails[0, 0:kinds, :] = tail[...]
    for index in range(gain_grad.shape[1] // width):
        part = slice(index * width, (index + 1) * width)
        tails[0, kinds + index : kinds + index + 1, :] = gain_grad[:, part]
    tail_kind = kinds + 1

    def pass_tail(side, hop, place):
        sign = -1 if side == RIGHT else 1
        target = tails.at[(place + sign) % RING]
        copies.send((side, tail_kind, hop), tails.at[place], target, target, peers[side])

    pass_tail(RIGHT, 0, 0)
    pass_tail(LEFT, 0, 0)
    hop_on(2)
    work_out(1, 7)
    copies.arrive(SCALARS, RIGHT, OVER_X)
    beside = grad_input.at[me.x_quarter]
    copies.send(
        (SCALARS, LEFT, OVER_CORE), beside, beside, grad_input.at[me.far_quarter], me.core_peer
    )
    for side, place in ((RIGHT, 7), (LEFT, 1)):
        copies.arrive(side, tail_kind, 0)
        pass_tail(side, 1, place)
    hop_on(3)
    for side, place in ((RIGHT, 6), (LEFT, 2)):
        copies.arrive(side, tail_kind, 1)
        pass_tail(side, 2, place)
    work_out(0)
    copies.arrive(RIGHT, tail_kind, 2)
    pass_tail(RIGHT, 3, 5)
    copies.arrive(LEFT, tail_kind, 2)
    for kind in range(kinds + 1):
        for side in (RIGHT, LEFT):
            take_in(side, 3, 0, kind)
        if kind < kinds:
            sum_in[kind] = held_in[0, kind].astype(f32)
    sum_out[...] = held_out[0].astype(f32)
    copies.arrive(RIGHT, tail_kind, 3)
    total = tails[0]
    for place in range(1, RING):
        total = total + tails[place]
    tail_sums[me.tp] = total
    for way, peer, index in (
        (OVER_X, me.x_peer, me.x_quarter),
        (OVER_CORE, me.core_peer, me.core_quarter),
        (OVER_FAR, me.far_peer, me.far_quarter),
    ):
        copies.send(
            (way, tail_kind), tail_sums.at[me.tp], tail_sums.at[me.tp], tail_sums.at[index], peer
        )
    for way in (OVER_X, OVER_CORE, OVER_FAR):
        copies.arrive(way, tail_kind)
    sum_tail[...] = tail_sums[...]
    copies.finish()


def finish(
    normed, grad_raw, heads, grad_attention, weights, gain, rows, grad_residual, bias, collective_id
):
    tokens, width = normed.shape
    kinds, _, columns = grad_raw.shape
    count = rows.shape[0]
    depth = width // RING
    bf16, f32 = jnp.bfloat16, jnp.float32
    shape = jax.ShapeDtypeStruct
    tail_shape = (-(-(kinds + width // columns) // 8) * 8, columns)
    return pl.pallas_call(
        finish_kernel,
        out_shape=(
            shape((kinds, depth, columns), f32),
            shape((columns, depth), f32),
            shape((4,) + tail_shape, f32),
            shape((4, count, width), bf16),
        ),
        in_specs=[IN_VMEM] * 9,
        out_specs=(IN_VMEM,) * 3 + (IN_PLACE,),
        scratch_shapes=[
            pltpu.VMEM((RING, kinds, depth, columns), bf16),
            pltpu.VMEM((RING, columns, depth), bf16),
            pltpu.VMEM((2, 4, kinds, depth, columns), bf16),
            pltpu.VMEM((2, 4, columns, depth), bf16),
            pltpu.VMEM((RING,) + tail_shape, f32),
            pltpu.VMEM((4,) + tail_shape, f32),
            pltpu.VMEM((2, count, width), bf16),
            pltpu.VMEM((2, count, width), bf16),
            pltpu.VMEM((count, width), bf16),
            pltpu.VMEM((count, width), bf16),
            pltpu.VMEM((count, width), bf16),
            pltpu.VMEM((count, width), f32),
        ]
        + semaphores(56),
        compiler_params=remote_params(collective_id, 60),
        name="finish",
    )(normed, grad_raw, heads, grad_attention, weights, gain[None], rows, grad_residual, bias)


def widen_kernel(
    experts, shared, rows, expert_in, expert_down, shared_in, shared_down, rows_out
):
    f32 = jnp.float32
    expert_in[...] = experts[:, :2].astype(f32)
    expert_down[...] = experts[:, 2].astype(f32)
    rows_out[...] = rows[0]

    @pl.when(pl.program_id(0) == 0)
    def _():
        places, _, hidden, across = shared.shape
        for index in range(2):
            slices = shared[:, index].astype(f32).reshape(places * hidden, across)
            shared_in[index] = jnp.swapaxes(slices, 0, 1)
        shared_down[...] = shared[:, 2].astype(f32).reshape(places * hidden, across)


def widen(experts, shared, rows):
    count, _, hidden, width = experts.shape
    places, _, slice_hidden, across = shared.shape
    quarters, own, _ = rows.shape
    parts = places // count
    columns = width // parts
    step = quarters * own // places
    f32 = jnp.float32
    shape = jax.ShapeDtypeStruct
    shared_hidden = places * slice_hidden
    return pl.pallas_call(
        widen_kernel,
        grid=(places,),
        in_specs=[
            pl.BlockSpec((1, 3, hidden, columns), lambda i: (i // parts, 0, 0, i % parts)),
            pl.BlockSpec(shared.shape, lambda i: (0, 0, 0, 0)),
            pl.BlockSpec((1, step, width), lambda i: (i * step // own, i % (own // step), 0)),
        ],
        out_specs=(
            pl.BlockSpec((1, 2, hidden, columns), lambda i: (i // parts, 0, 0, i % parts)),
            pl.BlockSpec((1, hidden, columns), lambda i: (i // parts, 0, i % parts)),
            pl.BlockSpec((2, across, shared_hidden), lambda i: (0, 0, 0)),
            pl.BlockSpec((shared_hidden, across), lambda i: (0, 0)),
            pl.BlockSpec((step, width), lambda i: (i, 0)),
        ),
        out_shape=(
            shape((count, 2, hidden, width), f32),
            shape((count, hidden, width), f32),
            shape((2, across, shared_hidden), f32),
            shape((shared_hidden, across), f32),
            shape((quarters * own, width), rows.dtype),
        ),
        compiler_params=pltpu.CompilerParams(vmem_limit_bytes=60 * 2**20),
        name="widen",
    )(experts, shared, rows)


def greet_along_z(me, others=()):
    barrier = pltpu.get_barrier_semaphore()
    for peer in (me.y_peer,) + others:
        pl.semaphore_signal(barrier, inc=1, device_id=peer, device_id_type=MESH_ID)

    @pl.when(me.z > 0)
    def _():
        peer = (me.ep - 2, me.tp)
        pl.semaphore_signal(barrier, inc=1, device_id=peer, device_id_type=MESH_ID)

    @pl.when(me.z < 3)
    def _():
        peer = (me.ep + 2, me.tp)
        pl.semaphore_signal(barrier, inc=1, device_id=peer, device_id_type=MESH_ID)

    pl.semaphore_wait(barrier, 1 + len(others) + (me.z + 2) // 3 + (5 - me.z) // 3)


def back_kernel(
    rows, weights, valid, queries, keys_values, query_doc, key_doc, log_totals, cosine, sine,
    grad_attention, grad_raw,
    grad_heads, grads, total, from_y, from_z,
    y_send, y_recv, z_send, z_recv, send_sems, recv_sems,
):
    me = Peers()
    copies = Copies(send_sems, recv_sems)
    bf16, f32 = jnp.bfloat16, jnp.float32
    count = rows.shape[0]
    tokens, width = queries.shape
    blocks = keys_values.shape[1]
    head_count = width // HD
    greet_along_z(me, (me.x_peer, me.core_peer))

    mine = grad_attention.at[me.quarter]
    copies.send((OVER_X,), rows, mine, grad_attention.at[me.x_quarter], me.x_peer)
    copies.send((OVER_CORE, 0), rows, mine, grad_attention.at[me.core_quarter], me.core_peer)
    mine[...] = rows[...]

    def heads_of(quarter):
        at = pl.ds(pl.multiple_of(quarter * count, count), count)
        part = product(grad_attention[quarter], weights[...], NT) * valid[at, :]
        grad_heads[at, :] = part.astype(bf16)

    heads_of(me.quarter)
    copies.arrive(OVER_CORE, 0)
    heads_of(me.core_quarter)
    copies.arrive(OVER_X)
    beside = grad_attention.at[me.x_quarter]
    copies.send((OVER_CORE, 1), beside, beside, grad_attention.at[me.far_quarter], me.core_peer)
    heads_of(me.x_quarter)
    copies.arrive(OVER_CORE, 1)
    heads_of(me.far_quarter)

    across = Copies(y_send, y_recv)
    along = Copies(z_send, z_recv)

    def columns(head):
        return pl.ds(pl.multiple_of(head * HD, HD), HD)

    def sideways(head, kind):
        at = columns(head)
        source, target = grads.at[kind, 1, :, at], from_y.at[kind, :, at]
        return across.describe(source, target, me.y_peer, 2 * head + kind)

    def downward(head, kind, source):
        at = columns(head)
        peer = ((me.ep + RING - 2) % RING, me.tp)
        return along.describe(source.at[kind, :, at], from_z.at[kind, :, at], peer, 2 * head + kind)

    scale = 1.0 / math.sqrt(HD)

    def one_head(head, carry):
        at = columns(head)
        keys = keys_values[0, :, :, at].reshape(blocks * tokens, HD)
        values = keys_values[1, :, :, at].reshape(blocks * tokens, HD)
        query = queries[:, at]
        out_grads = grad_heads[:, at]
        scores = masked_scores(query, keys, query_doc[...], key_doc[...])
        probs = jnp.exp(scores - log_totals[head])
        slopes = product(out_grads, values, NT)
        slopes = probs * (slopes - jnp.sum(probs * slopes, axis=1, keepdims=True))
        grad_scores = slopes.astype(bf16)
        grad_keys = product(grad_scores, query, TN) * scale
        grads[0, :, :, at] = grad_keys.astype(bf16).reshape(blocks, tokens, HD)
        grad_values = product(probs.astype(bf16), out_grads, TN)
        grads[1, :, :, at] = grad_values.astype(bf16).reshape(blocks, tokens, HD)
        for kind in range(2):
            sideways(head, kind).start()

        @pl.when((me.z > 0) & (me.y == 0))
        def _():
            for kind in range(2):
                downward(head, kind, grads.at[:, 0]).start()

        turned_back = turned(product(grad_scores, keys) * scale, cosine[...], -sine[...])
        grad_raw[0, :, at] = turned_back.astype(bf16)
        return carry

    lax.fori_loop(0, head_count, one_head, 0)

    def from_beside(head, carry):
        at = columns(head)
        for kind in range(2):
            sideways(head, kind).wait_recv()
            here = grads[kind, 2, :, at].astype(f32)

            @pl.when(me.y == 0)
            def _():
                total[kind, :, at] = here + from_y[kind, :, at].astype(f32)

            @pl.when(me.y == 1)
            def _():
                total[kind, :, at] = here
                two_back = grads[kind, 0, :, at].astype(f32)
                summed = two_back + from_y[kind, :, at].astype(f32)
                from_y[kind, :, at] = summed.astype(bf16)

            @pl.when((me.z > 0) & (me.y == 1))
            def _():
                downward(head, kind, from_y).start()

        return carry

    lax.fori_loop(0, head_count, from_beside, 0)

    def from_above(head, carry):
        at = columns(head)

        @pl.when(me.z < 3)
        def _():
            for kind in range(2):
                downward(head, kind, from_y).wait_recv()
                total[kind, :, at] += from_z[kind, :, at].astype(f32)

        grad_raw[1, :, at] = turned(total[0, :, at], cosine[...], -sine[...]).astype(bf16)
        grad_raw[2, :, at] = total[1, :, at].astype(bf16)
        return carry

    lax.fori_loop(0, head_count, from_above, 0)

    def sent(head, carry):
        for kind in range(2):
            sideways(head, kind).wait_send()

        @pl.when(me.z > 0)
        def _():
            for kind in range(2):
                downward(head, kind, from_y).wait_send()

        return carry

    lax.fori_loop(0, head_count, sent, 0)
    copies.finish()


def back_attention(
    rows, weights, valid, queries, keys_values, query_doc, key_doc, log_totals, cosine, sine,
    collective_id,
):
    count, features = rows.shape
    tokens, width = queries.shape
    bf16, f32 = jnp.bfloat16, jnp.float32
    shape = jax.ShapeDtypeStruct
    pieces = 2 * (width // HD)
    return pl.pallas_call(
        back_kernel,
        out_shape=(shape((4, count, features), bf16), shape((3, tokens, width), bf16)),
        in_specs=[IN_VMEM] * 10,
        out_specs=(IN_VMEM,) * 2,
        scratch_shapes=[
            pltpu.VMEM((tokens, width), bf16),
            pltpu.VMEM(keys_values.shape, bf16),
            pltpu.VMEM((2, tokens, width), f32),
            pltpu.VMEM((2, tokens, width), bf16),
            pltpu.VMEM((2, tokens, width), bf16),
        ]
        + semaphores(pieces)
        + semaphores(pieces)
        + semaphores(3),
        compiler_params=remote_params(collective_id, 60),
        name="back_attention",
    )(rows, weights, valid, queries, keys_values, query_doc, key_doc, log_totals, cosine, sine)


def reduce_kernel(flip, left, right, out, core_out, core_in, x_out, x_in, send_sems, recv_sems):
    me = Peers()
    copies = Copies(send_sems, recv_sems)
    terms = left.shape[0]
    count = out.shape[0]
    f32 = jnp.float32
    greet([me.x_peer, me.core_peer])

    def quarter(index):
        rows = pl.ds(pl.multiple_of(index * count, count), count)
        total = None
        for term in range(terms):
            one = product(left[term, rows, :], right[term], NT if flip else NN)
            total = one if total is None else total + one
        return total

    for slot, index in ((1, me.far_quarter), (0, me.core_quarter)):
        core_out[slot] = quarter(index).astype(core_out.dtype)
        target = core_in.at[slot]
        copies.send((OVER_CORE, slot), core_out.at[slot], target, target, me.core_peer)
    mine = quarter(me.x_quarter)
    copies.arrive(OVER_CORE, 1)
    x_out[...] = (mine + core_in[1].astype(f32)).astype(x_out.dtype)
    copies.send((OVER_X,), x_out, x_in, x_in, me.x_peer)
    mine = quarter(me.quarter)
    copies.arrive(OVER_CORE, 0)
    out[...] = mine + core_in[0].astype(f32)
    copies.arrive(OVER_X)
    out[...] += x_in[...].astype(f32)
    copies.finish()


def product_to_owner(left, right, flip, collective_id):
    tokens = left.shape[1]
    width = right.shape[1] if flip else right.shape[2]
    count = tokens // 4
    bf16 = jnp.bfloat16
    return pl.pallas_call(
        functools.partial(reduce_kernel, flip),
        out_shape=jax.ShapeDtypeStruct((count, width), jnp.float32),
        in_specs=[IN_VMEM] * 2,
        out_specs=IN_VMEM,
        scratch_shapes=[
            pltpu.VMEM((2, count, width), bf16),
            pltpu.VMEM((2, count, width), bf16),
            pltpu.VMEM((count, width), bf16),
            pltpu.VMEM((count, width), bf16),
        ]
        + semaphores(3),
        compiler_params=remote_params(collective_id),
        name="product_to_owner",
    )(left, right)


def own_rows(block, tp_index, count):
    return lax.dynamic_slice_in_dim(block, tp_index * count, count, 0)


def per_device_dense(
    layer_input,
    attention_gain,
    attention_in,
    attention_bias,
    attention_out,
    feedforward_gain,
    shared_in,
    shared_down,
    shared_gate,
    router,
    expert_in,
    expert_down,
    routes,
    document_lengths,
    cotangent,
):
    bf16 = jnp.bfloat16
    f32 = jnp.float32
    both = (EP, TP)
    tok_count, model_width = layer_input.shape
    expert_count = router.shape[1]
    top_count = routes.shape[1]
    ep_size = lax.axis_size(EP)
    tp_size = lax.axis_size(TP)
    ep_index = lax.axis_index(EP)
    tp_index = lax.axis_index(TP)
    own_count = tok_count // tp_size
    all_count = tok_count * ep_size
    capacity = tp_size * (
        (5 * tok_count * top_count + 4 * expert_count * tp_size - 1) // (4 * expert_count * tp_size)
    )
    reach_back = min((WINDOW + tok_count - 2) // tok_count, ep_size - 1)
    local_experts = expert_in.shape[0]
    route_rows = jnp.concatenate(
        [routes.T, jnp.full((-top_count % 8, tok_count), -1, routes.dtype)]
    )
    positions = ep_index * tok_count + jnp.arange(tok_count, dtype=jnp.int32)
    key_count = (reach_back + 1) * tok_count
    key_positions = (ep_index - reach_back) * tok_count + jnp.arange(key_count, dtype=jnp.int32)
    query_doc, rope_pos, valid_mask = doc_table(document_lengths, positions)
    query_doc = query_doc[:, None]
    key_doc = doc_table(document_lengths, key_positions)[0][None, :]
    valid_rows = valid_mask.astype(f32)[:, None]
    cosine, sine = (part[:, 0] for part in rope_angles(rope_pos, HD))
    cosine = jnp.concatenate([cosine, cosine], axis=1)
    sine = jnp.concatenate([-sine, sine], axis=1)
    (
        in_blocks,
        out_full,
        all_routes,
        normed_attention,
        queries,
        keys_values,
        shared_shards,
    ) = open_attention(
        attention_in,
        attention_out,
        route_rows,
        layer_input,
        attention_gain,
        attention_bias,
        cosine,
        sine,
        shared_in,
        shared_down,
        0,
    )
    in_full = in_blocks.reshape(3, model_width, -1)
    shard_width = shared_in.shape[1]
    slice_hidden = shared_in.shape[2] // ep_size
    shared_slices = lax.all_to_all(shared_shards, EP, split_axis=0, concat_axis=0, tiled=True)
    heads_low, log_totals = attend(queries, keys_values, query_doc, key_doc, valid_rows)
    attention_sum = product_to_owner(heads_low[None], out_full[None], False, 2)
    input_rows = own_rows(layer_input, tp_index, own_count).astype(f32)
    residual = input_rows + attention_sum
    inverse_two, normed_two = rms_parts(residual)
    normed_ffn = normed_two * feedforward_gain
    normed_low = normed_ffn.astype(bf16)
    shared_scale = jax.nn.sigmoid(jnp.dot(normed_ffn, shared_gate, precision=HIGHEST))
    router_probs = jax.nn.softmax(jnp.dot(normed_ffn, router, precision=HIGHEST), axis=-1)
    routes_own = own_rows(routes, tp_index, own_count)
    expert_ids = jnp.arange(expert_count, dtype=jnp.int32)
    picked = jnp.any(routes_own[:, :, None] == expert_ids[None, None, :], axis=1)
    chosen = jnp.where(picked, router_probs, 0.0)
    chosen_total = jnp.sum(chosen, axis=1, keepdims=True)
    gates = chosen / chosen_total
    scale_count = -(-(expert_count + 1) // 8) * 8
    spare = jnp.zeros((scale_count - expert_count - 1, own_count), f32)
    scale_rows = jnp.concatenate([gates.T, shared_scale[None], spare])
    (
        all_rows,
        all_cotangent,
        all_scales,
        ffn_part,
        back_part,
        slot_rows,
        slot_cotangent,
        grad_pre,
        gated,
        grad_shared_pre,
        scaled_hidden,
        scalar_part,
    ) = gather_feed(
        normed_low,
        cotangent.reshape(tp_size, own_count, model_width),
        scale_rows,
        all_routes,
        jnp.swapaxes(expert_in, 2, 3).reshape(local_experts, -1, model_width),
        expert_down,
        shared_slices,
        capacity,
        3,
    )
    part_shape = (ep_size, tp_size, own_count, model_width)
    slot_count = ep_size * capacity
    fed = (
        slot_rows.reshape(local_experts, slot_count, model_width),
        slot_cotangent.reshape(local_experts, slot_count, model_width),
        grad_pre.reshape(2, local_experts, slot_count, -1),
        gated.reshape(local_experts, slot_count, -1),
        all_rows.reshape(all_count, model_width),
        all_cotangent.reshape(all_count, model_width),
        grad_shared_pre.reshape(2, all_count, slice_hidden),
        scaled_hidden.reshape(all_count, slice_hidden),
    )
    back_sum, ffn_sum, scalar_sum, grad_experts, shared_grads = scatter_rows(
        back_part.reshape(part_shape), ffn_part.reshape(part_shape), scalar_part, fed, 4
    )
    scalar_sum = scalar_sum.T
    layer_output = lax.all_gather((residual + ffn_sum).astype(bf16), TP, axis=0, tiled=True)
    shared_grads = lax.all_to_all(shared_grads, EP, split_axis=0, concat_axis=0, tiled=True)
    grad_gates = scalar_sum[:, :expert_count]
    grad_probs = jnp.where(
        picked,
        (grad_gates - jnp.sum(grad_gates * gates, axis=1, keepdims=True)) / chosen_total,
        0.0,
    )
    grad_logits = router_probs * (
        grad_probs - jnp.sum(grad_probs * router_probs, axis=1, keepdims=True)
    )
    grad_router = jnp.einsum("td,te->de", normed_ffn, grad_logits, precision=HIGHEST)
    grad_scale_pre = scalar_sum[:, expert_count] * shared_scale * (1.0 - shared_scale)
    grad_shared_gate = jnp.dot(grad_scale_pre, normed_ffn, precision=HIGHEST)
    grad_normed = (
        back_sum
        + jnp.einsum("te,de->td", grad_logits, router, precision=HIGHEST)
        + grad_scale_pre[:, None] * shared_gate[None, :]
    )
    grad_mid_norm, grad_feedforward_gain = norm_back(
        grad_normed, feedforward_gain, inverse_two, normed_two
    )
    small = jnp.concatenate([grad_feedforward_gain[None], grad_shared_gate[None], grad_router.T])
    small = lax.psum(small, both)
    grad_residual = own_rows(cotangent, tp_index, own_count).astype(f32) + grad_mid_norm
    grad_attention, grad_raw = back_attention(
        grad_residual.astype(bf16),
        out_full,
        valid_rows,
        queries,
        keys_values,
        query_doc,
        key_doc,
        log_totals,
        cosine,
        sine,
        5,
    )
    grad_attention = grad_attention.reshape(tok_count, model_width)
    grad_attention_bias = jnp.sum(grad_raw.astype(f32), axis=1)
    grad_attention_in, grad_attention_out, tails, grad_input = finish(
        normed_attention,
        grad_raw,
        heads_low,
        grad_attention,
        in_full,
        attention_gain,
        own_rows(layer_input, tp_index, own_count),
        grad_residual,
        grad_attention_bias,
        7,
    )
    grad_attention_bias = lax.dynamic_index_in_dim(tails, tp_index, 0, keepdims=False)[:3]
    grad_attention_gain = jnp.sum(tails[:, 3:], axis=0)[: model_width // tails.shape[2]].reshape(-1)
    grad_expert_in, grad_expert_down, grad_shared_in, grad_shared_down, grad_input = widen(
        grad_experts, shared_grads, grad_input
    )
    return (
        layer_output,
        grad_input,
        grad_attention_gain,
        grad_attention_in,
        grad_attention_bias,
        grad_attention_out,
        small[0],
        grad_shared_in,
        grad_shared_down,
        small[1],
        small[2:].T,
        jnp.swapaxes(grad_expert_in, 2, 3),
        grad_expert_down,
    )


def per_device(*arguments):
    small_slice = lax.axis_size(EP) == RING and lax.axis_size(TP) == 4
    return (per_device_dense if small_slice else per_device_sparse)(*arguments)


def per_device_sparse(
    layer_input,
    attention_gain,
    attention_in,
    attention_bias,
    attention_out,
    feedforward_gain,
    shared_in,
    shared_down,
    shared_gate,
    router,
    expert_in,
    expert_down,
    routes,
    document_lengths,
    cotangent,
):
    bf16 = jnp.bfloat16
    f32 = jnp.float32
    tok_count = layer_input.shape[0]
    model_width = layer_input.shape[1]
    expert_count = router.shape[1]
    top_count = routes.shape[1]
    ep_size = lax.axis_size(EP)
    tp_size = lax.axis_size(TP)
    capacity = tp_size * (
        (5 * tok_count * top_count + 4 * expert_count * tp_size - 1) // (4 * expert_count * tp_size)
    )
    reach_back = min((WINDOW + tok_count - 2) // tok_count, ep_size - 1)
    head_dim = HD
    local_heads = attention_in.shape[2] // head_dim
    score_scale = 1.0 / math.sqrt(head_dim)
    in_full, out_full, shared_in_full, shared_down_full = (
        lax.all_gather(attention_in, EP, axis=1, tiled=True),
        lax.all_gather(attention_out, EP, axis=1, tiled=True),
        lax.all_gather(shared_in, EP, axis=1, tiled=True),
        lax.all_gather(shared_down, EP, axis=1, tiled=True),
    )
    ep_index = lax.axis_index(EP)
    positions = ep_index * tok_count + jnp.arange(tok_count, dtype=jnp.int32)
    key_count = (reach_back + 1) * tok_count
    key_positions = (ep_index - reach_back) * tok_count + jnp.arange(key_count, dtype=jnp.int32)
    query_doc, rope_pos, valid_mask = doc_table(document_lengths, positions)
    key_doc = doc_table(document_lengths, key_positions)[0]
    distance = positions[:, None] - key_positions[None, :]
    allowed = (query_doc[:, None] == key_doc[None, :]) & (distance >= 0) & (distance < WINDOW)
    valid_rows = valid_mask.astype(f32)[:, None]
    cosine, sine_part = rope_angles(rope_pos, head_dim)
    input_rows = layer_input.astype(f32)
    inverse_one, normed_one = rms_parts(input_rows)
    normed_attention = (normed_one * attention_gain).astype(bf16)
    raw_proj = (
        jnp.einsum("td,sde->ste", normed_attention, in_full, preferred_element_type=f32)
        + attention_bias[:, None, :]
    )
    queries = rotate(
        raw_proj[0].reshape(tok_count, local_heads, head_dim), cosine, sine_part, 1.0
    ).astype(bf16)
    keys_own = rotate(
        raw_proj[1].reshape(tok_count, local_heads, head_dim), cosine, sine_part, 1.0
    ).astype(bf16)
    values_own = raw_proj[2].reshape(tok_count, local_heads, head_dim).astype(bf16)
    key_value = jnp.stack([keys_own, values_own])
    earlier = []
    for hop_count in range(reach_back, 0, -1):
        earlier.append(shifted(key_value, EP, hop_count))
    all_kv = jnp.concatenate(earlier + [key_value], axis=1)
    all_keys = all_kv[0]
    all_values = all_kv[1]
    scores = jnp.einsum("qhe,khe->hqk", queries, all_keys, preferred_element_type=f32) * score_scale
    scores = jnp.where(allowed[None], scores, MASKED)
    row_max = jnp.max(scores, axis=-1, keepdims=True)
    exp_terms = jnp.exp(scores - row_max)
    row_total = jnp.sum(exp_terms, axis=-1, keepdims=True)
    log_total = row_max + jnp.log(row_total)
    weights = (exp_terms / row_total).astype(bf16)
    heads_out = jnp.einsum("hqk,khe->qhe", weights, all_values, preferred_element_type=f32).reshape(
        tok_count, -1
    )
    heads_low = (heads_out * valid_rows).astype(bf16)
    attention_sum = tensor_total(jnp.dot(heads_low, out_full, preferred_element_type=f32))
    residual = input_rows + attention_sum
    inverse_two, normed_two = rms_parts(residual)
    normed_ffn = normed_two * feedforward_gain
    normed_low = normed_ffn.astype(bf16)
    shared_pre = jnp.einsum("td,sdf->stf", normed_low, shared_in_full, preferred_element_type=f32)
    shared_silu, shared_slope = silu_parts(shared_pre[0])
    shared_hidden = (shared_silu * shared_pre[1]).astype(bf16)
    shared_out = tensor_total(jnp.dot(shared_hidden, shared_down_full, preferred_element_type=f32))
    shared_scale = jax.nn.sigmoid(jnp.dot(normed_ffn, shared_gate, precision=HIGHEST))
    router_probs = jax.nn.softmax(jnp.dot(normed_ffn, router, precision=HIGHEST), axis=-1)
    chosen = jnp.take_along_axis(router_probs, routes, axis=1)
    chosen_total = jnp.sum(chosen, axis=1, keepdims=True)
    gate_values = chosen / chosen_total
    assign_count = tok_count * top_count
    flat_routes = routes.reshape(-1)
    expert_ids = jnp.arange(expert_count, dtype=jnp.int32)
    one_hot = (flat_routes[:, None] == expert_ids[None, :]).astype(jnp.int32)
    arrival_rank = jnp.sum((jnp.cumsum(one_hot, axis=0) - one_hot) * one_hot, axis=1)
    slot_count = expert_count * capacity
    slot_index = jnp.where(
        arrival_rank < capacity, flat_routes * capacity + arrival_rank, slot_count
    )
    slot_assign = (
        jnp.full((slot_count + 1,), assign_count, jnp.int32)
        .at[slot_index]
        .set(jnp.arange(assign_count, dtype=jnp.int32))[:slot_count]
    )
    slot_token = slot_assign // top_count
    padded_rows = jnp.concatenate([normed_low, jnp.zeros((1, model_width), bf16)])
    send_rows = padded_rows[slot_token].reshape(expert_count, capacity, model_width)

    def expert_trip(outgoing, work):
        row_block = lax.all_to_all(outgoing, EP, split_axis=0, concat_axis=1, tiled=True)
        partial_rows, extras = work(row_block)
        share_rows = lax.psum_scatter(partial_rows, TP, scatter_dimension=1, tiled=True).astype(
            bf16
        )
        whole_rows = lax.all_gather(share_rows, TP, axis=1, tiled=True)
        return (lax.all_to_all(whole_rows, EP, split_axis=1, concat_axis=0, tiled=True), extras)

    def expert_forward(row_block):
        pre_acts = jnp.einsum("erd,esdf->serf", row_block, expert_in, preferred_element_type=f32)
        gate_silu, gate_slope = silu_parts(pre_acts[0])
        hidden = (gate_silu * pre_acts[1]).astype(bf16)
        partial_rows = jnp.einsum("erf,efd->erd", hidden, expert_down, preferred_element_type=f32)
        return (partial_rows, (row_block, pre_acts, hidden, gate_silu, gate_slope))

    returned_rows, kept_state = expert_trip(send_rows, expert_forward)
    expert_rows, expert_pre, expert_hidden, expert_silu, expert_slope = kept_state
    padded_back = jnp.concatenate(
        [returned_rows.reshape(slot_count, model_width), jnp.zeros((1, model_width), bf16)]
    )
    picked = padded_back[slot_index].reshape(tok_count, top_count, model_width).astype(f32)
    moe_sum = jnp.sum(gate_values[:, :, None] * picked, axis=1)
    layer_output = (residual + shared_scale[:, None] * shared_out + moe_sum).astype(bf16)
    grad_rows = cotangent.astype(f32)
    padded_grad = jnp.concatenate([grad_rows, jnp.zeros((1, model_width), f32)])
    padded_gates = jnp.concatenate([gate_values.reshape(-1), jnp.zeros((1,), f32)])
    grad_send = (padded_gates[slot_assign][:, None] * padded_grad[slot_token]).astype(bf16)
    grad_send = grad_send.reshape(expert_count, capacity, model_width)

    def expert_backward(grad_block):
        grad_down = jnp.einsum(
            "erf,erd->efd", expert_hidden, grad_block, preferred_element_type=f32
        )
        grad_hidden = jnp.einsum(
            "erd,efd->erf", grad_block, expert_down, preferred_element_type=f32
        )
        grad_pre = jnp.stack(
            [grad_hidden * expert_pre[1] * expert_slope, grad_hidden * expert_silu]
        ).astype(bf16)
        grad_weights_in = jnp.einsum(
            "erd,serf->esdf", expert_rows, grad_pre, preferred_element_type=f32
        )
        grad_back_rows = jnp.einsum(
            "serf,esdf->erd", grad_pre, expert_in, preferred_element_type=f32
        )
        return (grad_back_rows, (grad_weights_in, grad_down))

    grad_returned, expert_grads = expert_trip(grad_send, expert_backward)
    grad_expert_in, grad_expert_down = expert_grads
    grad_gate_values = jnp.sum(picked * grad_rows[:, None, :], axis=2)
    grad_chosen = (
        grad_gate_values - jnp.sum(grad_gate_values * gate_values, axis=1, keepdims=True)
    ) / chosen_total
    grad_probs = jnp.sum(
        jnp.where(routes[:, :, None] == expert_ids[None, None, :], grad_chosen[:, :, None], 0.0),
        axis=1,
    )
    grad_logits = router_probs * (
        grad_probs - jnp.sum(grad_probs * router_probs, axis=1, keepdims=True)
    )
    grad_router = jnp.einsum("td,te->de", normed_ffn, grad_logits, precision=HIGHEST)
    grad_shared_out = (shared_scale[:, None] * grad_rows).astype(bf16)
    grad_shared_down = jnp.einsum(
        "tf,td->fd", shared_hidden, grad_shared_out, preferred_element_type=f32
    )
    grad_shared_hidden = jnp.einsum(
        "td,fd->tf", grad_shared_out, shared_down_full, preferred_element_type=f32
    )
    grad_shared_pre = jnp.stack(
        [grad_shared_hidden * shared_pre[1] * shared_slope, grad_shared_hidden * shared_silu]
    ).astype(bf16)
    grad_shared_in = jnp.einsum(
        "td,stf->sdf", normed_low, grad_shared_pre, preferred_element_type=f32
    )
    shared_back = jnp.einsum(
        "stf,sdf->td", grad_shared_pre, shared_in_full, preferred_element_type=f32
    )
    grad_scale_pre = jnp.sum(grad_rows * shared_out, axis=1) * shared_scale * (1.0 - shared_scale)
    grad_shared_gate = jnp.dot(grad_scale_pre, normed_ffn, precision=HIGHEST)
    padded_return = jnp.concatenate(
        [grad_returned.reshape(slot_count, model_width), jnp.zeros((1, model_width), bf16)]
    )
    moe_back = jnp.sum(
        padded_return[slot_index].reshape(tok_count, top_count, model_width).astype(f32), axis=1
    )
    grad_normed = (
        tensor_total(shared_back)
        + moe_back
        + jnp.einsum("te,de->td", grad_logits, router, precision=HIGHEST)
        + grad_scale_pre[:, None] * shared_gate[None, :]
    )
    grad_mid_norm, grad_feedforward_gain = norm_back(
        grad_normed, feedforward_gain, inverse_two, normed_two
    )
    grad_residual = grad_rows + grad_mid_norm
    grad_attention = grad_residual.astype(bf16)
    grad_attention_out = jnp.einsum(
        "tf,td->fd", heads_low, grad_attention, preferred_element_type=f32
    )
    grad_heads = jnp.einsum(
        "td,fd->tf", grad_attention, out_full, preferred_element_type=f32
    ).astype(bf16)
    grad_heads = (grad_heads * valid_rows.astype(bf16)).reshape(tok_count, local_heads, head_dim)
    scores_again = (
        jnp.einsum("qhe,khe->hqk", queries, all_keys, preferred_element_type=f32) * score_scale
    )
    scores_again = jnp.where(allowed[None], scores_again, MASKED)
    softmax_out = jnp.exp(scores_again - log_total)
    weights_again = softmax_out.astype(bf16)
    grad_weights = jnp.einsum("qhe,khe->hqk", grad_heads, all_values, preferred_element_type=f32)
    grad_scores = (
        softmax_out * (grad_weights - jnp.sum(softmax_out * grad_weights, axis=-1, keepdims=True))
    ).astype(bf16)
    grad_queries = (
        jnp.einsum("hqk,khe->qhe", grad_scores, all_keys, preferred_element_type=f32) * score_scale
    )
    grad_keys = (
        jnp.einsum("hqk,qhe->khe", grad_scores, queries, preferred_element_type=f32) * score_scale
    )
    grad_values = jnp.einsum("hqk,qhe->khe", weights_again, grad_heads, preferred_element_type=f32)
    grad_kv = jnp.stack([grad_keys, grad_values])
    own_part = grad_kv[:, reach_back * tok_count :]
    for hop_count in range(1, reach_back + 1):
        segment_start = (reach_back - hop_count) * tok_count
        segment = grad_kv[:, segment_start : segment_start + tok_count]
        own_part = own_part + shifted(segment, EP, -hop_count)
    grad_raw = (
        jnp.stack(
            [
                rotate(grad_queries, cosine, sine_part, -1.0),
                rotate(own_part[0], cosine, sine_part, -1.0),
                own_part[1],
            ]
        )
        .reshape(3, tok_count, -1)
        .astype(bf16)
    )
    grad_attention_bias = jnp.sum(grad_raw.astype(f32), axis=1)
    grad_attention_in = jnp.einsum(
        "td,ste->sde", normed_attention, grad_raw, preferred_element_type=f32
    )
    grad_normed_attention = tensor_total(
        jnp.einsum("ste,sde->td", grad_raw, in_full, preferred_element_type=f32)
    )
    grad_in_norm, grad_attention_gain = norm_back(
        grad_normed_attention, attention_gain, inverse_one, normed_one
    )
    grad_input = (grad_residual + grad_in_norm).astype(bf16)
    grad_attention_in, grad_attention_out, grad_shared_in, grad_shared_down = (
        lax.psum_scatter(
            grad_attention_in.astype(jnp.bfloat16), EP, scatter_dimension=1, tiled=True
        ).astype(jnp.float32),
        lax.psum_scatter(
            grad_attention_out.astype(jnp.bfloat16), EP, scatter_dimension=1, tiled=True
        ).astype(jnp.float32),
        lax.psum_scatter(
            grad_shared_in.astype(jnp.bfloat16), EP, scatter_dimension=1, tiled=True
        ).astype(jnp.float32),
        lax.psum_scatter(
            grad_shared_down.astype(jnp.bfloat16), EP, scatter_dimension=1, tiled=True
        ).astype(jnp.float32),
    )
    (
        grad_attention_gain,
        grad_attention_bias,
        grad_feedforward_gain,
        grad_shared_gate,
        grad_router,
    ) = (
        lax.psum(grad_attention_gain.astype(jnp.bfloat16), EP).astype(jnp.float32),
        lax.psum(grad_attention_bias.astype(jnp.bfloat16), EP).astype(jnp.float32),
        lax.psum(grad_feedforward_gain.astype(jnp.bfloat16), EP).astype(jnp.float32),
        lax.psum(grad_shared_gate.astype(jnp.bfloat16), EP).astype(jnp.float32),
        lax.psum(grad_router.astype(jnp.bfloat16), EP).astype(jnp.float32),
    )
    return (
        layer_output,
        grad_input,
        grad_attention_gain,
        grad_attention_in,
        grad_attention_bias,
        grad_attention_out,
        grad_feedforward_gain,
        grad_shared_in,
        grad_shared_down,
        grad_shared_gate,
        grad_router,
        grad_expert_in,
        grad_expert_down,
    )


def solution(mesh):
    return jax.shard_map(
        per_device,
        mesh=mesh,
        in_specs=(
            P(EP, None),
            P(),
            P(None, EP, TP),
            P(None, TP),
            P(TP, EP),
            P(),
            P(None, EP, TP),
            P(TP, EP),
            P(),
            P(),
            P(EP, None, None, TP),
            P(EP, TP, None),
            P(EP, None),
            P(),
            P(EP, None),
        ),
        out_specs=(
            P(EP, None),
            P(EP, None),
            P(),
            P(None, EP, TP),
            P(None, TP),
            P(TP, EP),
            P(),
            P(None, EP, TP),
            P(TP, EP),
            P(),
            P(),
            P(EP, None, None, TP),
            P(EP, TP, None),
        ),
        check_vma=False,
    )
```
